32 devices in a mesh: rows: 2 (over core), ha: 4 (over y, x), ma: 4 (over z).
Axes of the slice: x: 2, y: 2, z: 4, core: 2. Of those that a mesh axis runs over, the one named last changes fastest.
Arguments:
- tokens: bfloat16 [32768, 1024], P(('rows', 'ha', 'ma')), may hold values from -6 to 6
- first_values: bfloat16 [32768, 1024], P(('rows', 'ha', 'ma')), may hold values from -6 to 6
- lengths: int32 [32], P(('rows', 'ha', 'ma')), may hold values from 128 to 1024, as said below
- w_query: bfloat16 [1024, 1024], replicated, may hold values from -0.25 to 0.25
- w_key: bfloat16 [1024, 1024], replicated, may hold values from -0.25 to 0.25
- w_value: bfloat16 [1024, 1024], replicated, may hold values from -0.1875 to 0.1875
- w_out: bfloat16 [1024, 1024], replicated, may hold values from -3 to 3
- norm_attn: float32 [1024], replicated, may hold values from 0.5 to 1.5
- norm_mlp: float32 [1024], replicated, may hold values from 0.5 to 1.5
- w_gate: bfloat16 [1024, 2816], P('ma', 'ha'), may hold values from -0.1875 to 0.1875
- w_up: bfloat16 [1024, 2816], P('ma', 'ha'), may hold values from -0.1875 to 0.1875
- w_down: bfloat16 [2816, 1024], P('ha', 'ma'), may hold values from -0.21875 to 0.21875
- grad_out: bfloat16 [32768, 1024], P(('rows', 'ha', 'ma')), may hold values from -6 to 6
Outputs:
- mixed_out: bfloat16 [32768, 1024], P(('rows', 'ha', 'ma'))
- grad_tokens: float32 [32768, 1024], P(('rows', 'ha', 'ma'))
- grad_first: float32 [32768, 1024], P(('rows', 'ha', 'ma'))
- grad_query: float32 [1024, 1024], replicated
- grad_key: float32 [1024, 1024], replicated
- grad_value: float32 [1024, 1024], replicated
- grad_wout: float32 [1024, 1024], replicated
- grad_norm_attn: float32 [1024], replicated
- grad_norm_mlp: float32 [1024], replicated
- grad_gate: float32 [1024, 2816], P('ma', 'ha')
- grad_up: float32 [1024, 2816], P('ma', 'ha')
- grad_down: float32 [2816, 1024], P('ha', 'ma')
The draws below stay inside these ranges and needn't reach their ends.
Inputs may be any that keep to these rules, and one draw needn't show every extreme that they name: `lengths`: at least one sequence has exactly 1024 valid tokens in every draw.
All inputs are finite; a program needn't handle non-finite values.
Results may differ from the reference program's by a relative error of at most 0.017.
Values may be sent and summed in bfloat16 or wider, within the bound.
A program may use at most 320 MiB of HBM per device.

```python
import math
import jax
import jax.numpy as jnp
from jax import lax

D = 1024
H = 16
HD = 64
FF = 2816
SLOT = 1024
MINLEN = 128
QBLOCK = 512
SEQS = 32
TOKENS = 32768


def draw_lengths(key, part):
    key = jax.random.fold_in(key, 7)
    key_a, key_b, key_c = jax.random.split(key, 3)
    first_draw = jax.random.randint(key_a, (SEQS,), 0, 64)
    second_draw = jax.random.randint(key_b, (SEQS,), 0, 64)
    spread_len = SLOT - MINLEN
    result = MINLEN + spread_len * first_draw * (second_draw + 128) // (63 * 191)
    chosen = jax.random.randint(key_c, (), 0, SEQS)
    result = jnp.where(jnp.arange(SEQS, dtype=jnp.int32) == chosen, SLOT, result)
    return result.astype(jnp.int32)


def levels(key, extent, cuts, smallest, largest):
    level = 1.0
    for axis_at, shards_of in cuts:
        draws = jax.random.uniform(jax.random.fold_in(jax.random.fold_in(key, 6), axis_at), (shards_of,), jnp.float32, smallest / len(cuts), largest / len(cuts))
        level = level * jnp.repeat(jnp.exp(draws), extent[axis_at] // shards_of).reshape((-1,) + (1,) * (len(extent) - 1 - axis_at))
    return level


def centred(rng, extent, deviation, most, pieces=(), held_as=jnp.bfloat16):
    values = deviation * jax.random.normal(rng, extent, jnp.float32)
    if pieces:
        values = values * levels(rng, extent, pieces, -0.22, 0.18)
    return jnp.clip(values, -most, most).astype(held_as)


def setup_inputs(seed: int = 0) -> dict:
    splits = jax.random.split(jax.random.key(seed), 14)
    tokens = centred(splits[0], (TOKENS, D), 1.0, 6.0, ((0, 32),))
    first_values = centred(splits[1], (TOKENS, D), 1.0, 6.0, ((0, 32),))
    lengths = draw_lengths(jax.random.fold_in(splits[13], 71), 0)
    w_query = centred(splits[3], (D, D), (D // 2) ** -0.5, 0.25)
    w_key = centred(splits[4], (D, D), (D // 2) ** -0.5, 0.25)
    w_value = centred(splits[5], (D, D), D ** -0.5, 0.1875)
    w_out = centred(splits[6], (D, D), (4 * D // SLOT) ** -0.5, 3.0)
    norm_attn = jnp.clip(1.0 + 0.1 * jax.random.normal(splits[7], (D,), jnp.float32), 0.5, 1.5)
    norm_mlp = jnp.clip(1.0 + 0.1 * jax.random.normal(splits[8], (D,), jnp.float32), 0.5, 1.5)
    w_gate = centred(splits[9], (D, FF), D ** -0.5, 0.1875, ((0, 4), (1, 4)))
    w_up = centred(splits[10], (D, FF), D ** -0.5, 0.1875, ((0, 4), (1, 4)))
    w_down = centred(splits[11], (FF, D), (FF // 4) ** -0.5, 0.21875, ((0, 4), (1, 4)))
    grad_out = centred(splits[12], (TOKENS, D), 1.0, 6.0, ((0, 32),))
    return {"tokens": tokens, "first_values": first_values, "lengths": lengths, "w_query": w_query, "w_key": w_key, "w_value": w_value, "w_out": w_out, "norm_attn": norm_attn, "norm_mlp": norm_mlp, "w_gate": w_gate, "w_up": w_up, "w_down": w_down, "grad_out": grad_out}


HIGH = lax.Precision.HIGHEST

@jax.custom_vjp
def low(v):
    return lax.optimization_barrier(v.astype(jnp.bfloat16)).astype(jnp.float32)

@jax.custom_vjp
def low_back(v):
    return v

def low_keep(v):
    return (low(v), None)

def low_pass(kept, grad):
    return (grad,)

def back_keep(v):
    return (v, None)

def back_low(kept, grad):
    return (low(grad),)
low.defvjp(low_keep, low_pass)
low_back.defvjp(back_keep, back_low)

def norm_rows(values, scales):
    return values * lax.rsqrt(lax.optimization_barrier(jnp.mean(values * values, axis=-1, keepdims=True)) + 1e-06) * scales

def rotate(values):
    halfway = values.shape[-1] // 2
    places = jnp.arange(values.shape[1], dtype=jnp.float32)
    frequency = 10000.0 ** (-jnp.arange(halfway, dtype=jnp.float32) * 2.0 / values.shape[-1])
    angles = places[:, None] * frequency[None, :]
    cosine = jnp.cos(angles)[None, :, None, :]
    sine_part = jnp.sin(angles)[None, :, None, :]
    first_half = values[..., :halfway]
    second_half = values[..., halfway:]
    return jnp.concatenate([first_half * cosine - second_half * sine_part, second_half * cosine + first_half * sine_part], axis=-1)

def attend_seq(queries, keys_rot, values_mix, length):
    blocks = SLOT // QBLOCK
    query_blocks = queries.reshape(blocks, QBLOCK, H, HD)
    starts = jnp.arange(blocks, dtype=jnp.int32) * QBLOCK
    scaling = 1.0 / math.sqrt(HD)

    def one_block(element):
        block_q, start = element
        scores = jnp.einsum('qhd,khd->hqk', block_q, keys_rot, precision=HIGH) * scaling
        scores = low_back(scores)
        query_pos = start + jnp.arange(QBLOCK, dtype=jnp.int32)
        key_pos = jnp.arange(SLOT, dtype=jnp.int32)
        visible = (key_pos[None, :] <= query_pos[:, None]) & (key_pos[None, :] < length)
        scores = jnp.where(visible[None], scores, -1e+30)
        probabilities = low(jax.nn.softmax(scores, axis=-1))
        return jnp.einsum('hqk,khd->qhd', probabilities, values_mix, precision=HIGH)
    result = lax.map(jax.checkpoint(one_block), (query_blocks, starts))
    return result.reshape(SLOT, H * HD)

def forward(inputs, first, seq_lengths, params):
    w_query, w_key, w_value, w_out, norm_attn, norm_mlp, w_gate, w_up, w_down = params
    group = seq_lengths.shape[0]
    normed_a = low(norm_rows(inputs, norm_attn))
    q_lin = low_back(jnp.dot(normed_a, w_query, precision=HIGH))
    k_lin = low_back(jnp.dot(normed_a, w_key, precision=HIGH))
    v_lin = low_back(jnp.dot(normed_a, w_value, precision=HIGH))
    v_mix = low(0.5 * v_lin + 0.5 * first)
    shape_four = (group, SLOT, H, HD)
    q_rot = low(rotate(q_lin.reshape(shape_four)))
    k_rot = low(rotate(k_lin.reshape(shape_four)))
    attended = jax.vmap(attend_seq)(q_rot, k_rot, v_mix.reshape(shape_four), seq_lengths)
    attn_o = low(low_back(attended.reshape(group * SLOT, D)))
    h_one = inputs + low_back(jnp.dot(attn_o, w_out, precision=HIGH))
    normed_m = low(norm_rows(h_one, norm_mlp))
    gate = low_back(jnp.dot(normed_m, w_gate, precision=HIGH))
    upper = low_back(jnp.dot(normed_m, w_up, precision=HIGH))
    hidden = low(jax.nn.silu(gate) * upper)
    return h_one + low_back(jnp.dot(hidden, w_down, precision=HIGH))

def reference(tokens, first_values, lengths, w_query, w_key, w_value, w_out, norm_attn, norm_mlp, w_gate, w_up, w_down, grad_out):
    params = tuple((p.astype(jnp.float32) for p in (w_query, w_key, w_value, w_out, norm_attn, norm_mlp, w_gate, w_up, w_down)))
    seq_total = lengths.shape[0]
    group = math.gcd(seq_total, max(1, 4096 // SLOT))
    turns = seq_total // group
    width = tokens.shape[1]
    inputs = (tokens.astype(jnp.float32).reshape(turns, group * SLOT, width), first_values.astype(jnp.float32).reshape(turns, group * SLOT, width), lengths.reshape(turns, group), grad_out.astype(jnp.float32).reshape(turns, group * SLOT, width))

    def group_step(totals, element):
        block_in, block_first, block_len, block_cot = element
        result, pullback = jax.vjp(lambda a_in, b_in, c_in: forward(a_in, b_in, block_len, c_in), block_in, block_first, params)
        grad_in, grad_fv, grad_params = pullback(block_cot)
        totals = jax.tree.map(jnp.add, totals, grad_params)
        return (totals, (result.astype(jnp.bfloat16), grad_in, grad_fv))
    start_sums = jax.tree.map(jnp.zeros_like, params)
    summed, (results, grad_in, grad_fv) = lax.scan(group_step, start_sums, inputs)
    return (results.reshape(-1, width), grad_in.reshape(-1, width), grad_fv.reshape(-1, width), summed[0], summed[1], summed[2], summed[3], summed[4], summed[5], summed[6], summed[7], summed[8])
```

```python
import functools
import math

import jax
import jax.numpy as jnp
import numpy as np
from jax import lax
from jax.experimental import pallas as pl
from jax.experimental.pallas import tpu as pltpu
from jax.sharding import PartitionSpec as P

D = 1024
H = 16
HD = 64
SLOT = 1024
EPS = 1e-06
GROUP = 4
GW = GROUP * HD
QB = 256
SCALE = 1.0 / math.sqrt(HD)
C2 = SCALE * math.log2(math.e)
F32 = jnp.float32
BF16 = jnp.bfloat16
MIB = 1 << 20


def nn(a, b):
    return lax.dot_general(a, b, (((1,), (0,)), ((), ())), preferred_element_type=F32)


def nt(a, b):
    return lax.dot_general(a, b, (((1,), (1,)), ((), ())), preferred_element_type=F32)


def tn(a, b):
    return lax.dot_general(a, b, (((0,), (0,)), ((), ())), preferred_element_type=F32)


def rope_tables():
    place = np.arange(SLOT, dtype=np.float32)
    frequency = np.float32(10000.0) ** (-np.arange(HD // 2, dtype=np.float32) * np.float32(2.0) / np.float32(HD))
    angles = place[:, None] * frequency[None, :]
    cosine, sine = np.cos(angles), np.sin(angles)
    cos_row = np.concatenate([cosine] * 4, axis=1)
    sin_row = np.concatenate([-sine, sine, -sine, sine], axis=1)
    return cos_row.astype(np.float32), sin_row.astype(np.float32)


def lanes(shape):
    return lax.broadcasted_iota(jnp.int32, shape, 1)


def partner(v):
    first = (lanes(v.shape) & 63) < 32
    return jnp.where(first, pltpu.roll(v, 96, 1), pltpu.roll(v, 32, 1))


def turn(v, cos, sin):
    parts = []
    for at in range(0, v.shape[1], 128):
        piece = v[:, at : at + 128]
        parts.append(piece * cos + partner(piece) * sin)
    return jnp.concatenate(parts, axis=1)


def low3(v):
    hi = v.astype(BF16).astype(F32)
    rest = v - hi
    mid = rest.astype(BF16).astype(F32)
    return hi, mid, rest - mid


def fwd_kernel(
    len_ref, x_ref, gain_ref, wq_ref, wk_ref, wv_ref, fv_ref, cos_ref, sin_ref, wo_ref, gain_m_ref,
    q_ref, k_ref, v_ref, o_ref, st_ref, nma_ref, h1_ref, nmm_ref,
):
    g = pl.program_id(0)

    @pl.when(g == 0)
    def _():
        x = x_ref[...].astype(F32)
        r = lax.rsqrt(jnp.mean(x * x, axis=-1, keepdims=True) + EPS)
        nma_ref[...] = (x * r * gain_ref[...]).astype(BF16)
        h1_ref[...] = x
        st_ref[...] = jnp.zeros_like(st_ref)

    nm = nma_ref[...]
    cos, sin = cos_ref[...], sin_ref[...]
    q_ref[...] = turn(nn(nm, wq_ref[...]), cos, sin).astype(BF16)
    k_ref[...] = turn(nn(nm, wk_ref[...]), cos, sin).astype(BF16)
    v_ref[...] = (0.5 * nn(nm, wv_ref[...]) + 0.5 * fv_ref[...].astype(F32)).astype(BF16)
    length = len_ref[0]
    tile = (SLOT, 128)
    lane = lanes(tile)
    row = lax.broadcasted_iota(jnp.int32, tile, 0)
    k_extra = jnp.where((lane == 0) & (row >= length), -1e30, 0.0).astype(BF16)
    q_extra = jnp.where(lane == 0, 1.0, 0.0).astype(BF16)
    ones = jnp.ones(tile, BF16)
    low_lane = lane < HD
    qlane = lanes((QB, 128))
    causal = lax.broadcasted_iota(jnp.int32, (QB, QB), 1) <= lax.broadcasted_iota(jnp.int32, (QB, QB), 0)
    for pair in range(GROUP // 2):
        cols = pl.ds(pair * 128, 128)
        qp, kp, vp = q_ref[:, cols], k_ref[:, cols], v_ref[:, cols]
        q_ext = jnp.concatenate([qp, q_extra], axis=1)
        k_exts, v_exts = [], []
        for e in range(2):
            mine = low_lane if e == 0 else ~low_lane
            k_exts.append(jnp.concatenate([jnp.where(mine, kp, 0), k_extra], axis=1))
            v_exts.append(jnp.concatenate([jnp.where(mine, vp, 0), ones], axis=1))
        for qb in range(SLOT // QB):
            rows = slice(qb * QB, (qb + 1) * QB)
            top = (qb + 1) * QB
            out = None
            stats = st_ref[rows, :].astype(F32)
            for e in range(2):
                s = nt(q_ext[rows], k_exts[e][:top])
                diag = jnp.where(causal, s[:, top - QB :], -1e30)
                s = diag if qb == 0 else jnp.concatenate([s[:, : top - QB], diag], axis=1)
                m = jnp.max(s, axis=-1, keepdims=True)
                p = jnp.exp2((s - m) * C2).astype(BF16)
                res = nn(p, v_exts[e][:top])
                total = res[:, 128:]
                part = res[:, :128] / total
                out = part if out is None else out + part
                hi, mid, rest = low3(m + jnp.log2(total) * (1.0 / C2))
                base = 8 * (g * GROUP + pair * 2 + e)
                stats = jnp.where(qlane == base, hi, stats)
                stats = jnp.where(qlane == base + 1, mid, stats)
                stats = jnp.where(qlane == base + 2, rest, stats)
                stats = jnp.where(qlane == base + 3, 1.0, stats)
            o_ref[rows, cols] = out.astype(BF16)
            st_ref[rows, :] = stats.astype(BF16)
    h1_ref[...] += nn(o_ref[...], wo_ref[...])

    @pl.when(g == pl.num_programs(0) - 1)
    def _():
        h = h1_ref[...]
        r = lax.rsqrt(jnp.mean(h * h, axis=-1, keepdims=True) + EPS)
        nmm_ref[...] = (h * r * gain_m_ref[...]).astype(BF16)


def attention_forward(length, x, gain, wq, wk, wv, fv, cos, sin, wo, gain_m):
    whole = lambda *_: (0, 0)
    col = lambda g, *_: (0, g)
    tok = x.shape[0]
    full = pl.BlockSpec((tok, D), whole)
    blk = pl.BlockSpec((tok, GW), col)
    wblk = pl.BlockSpec((D, GW), col)
    vec = pl.BlockSpec((1, D), whole)
    tab = pl.BlockSpec((tok, 128), whole)
    sds = jax.ShapeDtypeStruct
    return pl.pallas_call(
        fwd_kernel,
        grid_spec=pltpu.PrefetchScalarGridSpec(
            num_scalar_prefetch=1,
            grid=(H // GROUP,),
            in_specs=[full, vec, wblk, wblk, wblk, blk, tab, tab, pl.BlockSpec((GW, D), lambda g, *_: (g, 0)), vec],
            out_specs=[blk, blk, blk, blk, tab, full, full, full],
        ),
        out_shape=[sds((tok, D), BF16)] * 4 + [sds((tok, 128), BF16), sds((tok, D), BF16), sds((tok, D), F32), sds((tok, D), BF16)],
        compiler_params=pltpu.CompilerParams(vmem_limit_bytes=56 * MIB),
        cost_estimate=pl.CostEstimate(flops=30 * 10**9, bytes_accessed=40 * 10**6, transcendentals=10**7),
        name="attention_forward",
    )(length, x, gain, wq, wk, wv, fv, cos, sin, wo, gain_m)


def prep_kernel(n, order_ref, nma_ref, o_ref, nmm_ref, dy_ref, nmat_ref, ot_ref, nmmt_ref, dyt_ref, buf):
    nmmt_ref[...] = nmm_ref[...].T
    dyt_ref[...] = dy_ref[...].T
    size = D // n
    for src, dst in ((nma_ref, nmat_ref), (o_ref, ot_ref)):
        if n == 1:
            dst[...] = src[...].T
        else:
            buf[...] = src[...].T
            for i in range(n):
                dst[pl.ds(i * size, size), :] = buf[pl.ds(pl.multiple_of(order_ref[i] * size, size), size), :]


def prepare(order, n, nma, o, nmm, dy):
    vm = pl.BlockSpec(memory_space=pltpu.VMEM)
    return pl.pallas_call(
        functools.partial(prep_kernel, n),
        in_specs=[pl.BlockSpec(memory_space=pltpu.SMEM)] + [vm] * 4,
        out_specs=[vm] * 4,
        out_shape=[jax.ShapeDtypeStruct((D, dy.shape[0]), BF16)] * 4,
        scratch_shapes=[pltpu.VMEM((D, dy.shape[0]), BF16)],
        compiler_params=pltpu.CompilerParams(vmem_limit_bytes=30 * MIB),
        cost_estimate=pl.CostEstimate(flops=10**9, bytes_accessed=16 * 10**6, transcendentals=0),
        name="prepare",
    )(order, nma, o, nmm, dy)


def wout_kernel(ot_ref, da_ref, mine_ref, other_ref):
    mine_ref[...] = nn(ot_ref[: D // 2, :], da_ref[...]).astype(BF16)
    other_ref[...] = nn(ot_ref[D // 2 :, :], da_ref[...]).astype(BF16)


def wout_grad(ot, da):
    vm = pl.BlockSpec(memory_space=pltpu.VMEM)
    return pl.pallas_call(
        wout_kernel,
        in_specs=[vm] * 2,
        out_specs=[vm] * 2,
        out_shape=[jax.ShapeDtypeStruct((D // 2, D), BF16)] * 2,
        compiler_params=pltpu.CompilerParams(vmem_limit_bytes=30 * MIB),
        cost_estimate=pl.CostEstimate(flops=2 * 10**9, bytes_accessed=6 * 10**6, transcendentals=0),
        name="wout_grad",
    )(ot, da)


def bwd_kernel(
    first_group, len_ref, da_ref, wo_ref, q_ref, k_ref, v_ref, o_ref, st_ref, nmt_ref, cos_ref, sin_ref,
    dq_ref, dk_ref, dv_ref, gf_ref, mine_ref, other_ref, dq_acc,
):
    g = pl.program_id(0) + first_group
    do_all = nt(da_ref[...], wo_ref[...]).astype(BF16)
    prod = do_all.astype(F32) * o_ref[...].astype(F32)
    hi = prod.astype(BF16)
    lo = (prod - hi.astype(F32)).astype(BF16)
    sel_row = lax.broadcasted_iota(jnp.int32, (GW, 128), 0) // HD + g * GROUP
    sel_lane = lanes((GW, 128))
    pick = jnp.where((sel_lane // 8 == sel_row) & ((sel_lane & 7) >= 4) & ((sel_lane & 7) <= 5), 1.0, 0.0).astype(BF16)
    delta = nn(hi, pick) + nn(lo, pick)
    tile = (SLOT, 128)
    lane = lanes(tile)
    d_hi = delta.astype(BF16)
    d_ext = jnp.where((lane & 7) == 4, d_hi.astype(F32), delta - d_hi.astype(F32)).astype(BF16)
    length = len_ref[0]
    row = lax.broadcasted_iota(jnp.int32, tile, 0)
    dead = row >= length
    low_lane = lane < HD
    st = st_ref[...]
    visible = lax.broadcasted_iota(jnp.int32, (QB, QB), 0) <= lax.broadcasted_iota(jnp.int32, (QB, QB), 1)
    dq_acc[...] = jnp.zeros_like(dq_acc)
    for pair in range(GROUP // 2):
        cols = pl.ds(pair * 128, 128)
        qp, kp, vp = q_ref[:, cols], k_ref[:, cols], v_ref[:, cols]
        dop = do_all[:, pair * 128 : pair * 128 + 128]
        q_ext = jnp.concatenate([qp, st], axis=1)
        do_ext = jnp.concatenate([dop, d_ext], axis=1)
        heads = []
        for e in range(2):
            mine = low_lane if e == 0 else ~low_lane
            at = lane - 8 * (g * GROUP + pair * 2 + e)
            k_x = jnp.where((at >= 0) & (at < 3), -1.0, jnp.where((at == 3) & dead, -1e30, 0.0)).astype(BF16)
            v_x = jnp.where((at >= 4) & (at < 6), -1.0, 0.0).astype(BF16)
            k_m = jnp.where(mine, kp, 0)
            heads.append((
                k_m,
                jnp.concatenate([k_m, k_x], axis=1),
                jnp.concatenate([jnp.where(mine, vp, 0), v_x], axis=1),
                jnp.where(mine, qp, 0),
                jnp.where(mine, dop, 0),
            ))
        for kb in range(SLOT // QB):
            rows = slice(kb * QB, (kb + 1) * QB)
            start = kb * QB
            dk = dv = None
            for k_m, k_ext, v_ext, q_m, do_m in heads:
                st_ = nt(k_ext[rows], q_ext[start:])
                dp = nt(v_ext[rows], do_ext[start:])
                p = jnp.exp2(st_ * C2)
                diag = jnp.where(visible, p[:, :QB], 0.0)
                p = diag if kb == SLOT // QB - 1 else jnp.concatenate([diag, p[:, QB:]], axis=1)
                ds = (p * dp).astype(BF16)
                p = p.astype(BF16)
                dv_e = nn(p, do_m[start:])
                dk_e = nn(ds, q_m[start:])
                dk = dk_e if dk is None else dk + dk_e
                dv = dv_e if dv is None else dv + dv_e
                dq_acc[start:, cols] += tn(ds, k_m[rows])
            dk = dk * SCALE
            cos, sin = cos_ref[rows, :], sin_ref[rows, :]
            dk_ref[rows, cols] = (dk * cos - partner(dk) * sin).astype(BF16)
            half = 0.5 * dv
            gf_ref[rows, cols] = half
            dv_ref[rows, cols] = half.astype(BF16)
    cos, sin = cos_ref[...], sin_ref[...]
    for pair in range(GROUP // 2):
        cols = pl.ds(pair * 128, 128)
        dq = dq_acc[:, cols] * SCALE
        dq_ref[:, cols] = (dq * cos - partner(dq) * sin).astype(BF16)
    nmt = nmt_ref[...]
    for j, ref in enumerate((dq_ref, dk_ref, dv_ref)):
        grad = nn(nmt, ref[...]).astype(BF16)
        mine_ref[j] = grad[: D // 2]
        other_ref[j] = grad[D // 2 :]


def attention_backward(first_group, groups, length, da, wo, q, k, v, o, st, nmt, cos, sin):
    whole = lambda *_: (0, 0)
    tok = da.shape[0]
    full = pl.BlockSpec((tok, D), whole)
    blk_in = pl.BlockSpec((tok, GW), lambda g, *_: (0, g + first_group))
    blk = pl.BlockSpec((tok, GW), lambda g, *_: (0, g))
    tab = pl.BlockSpec((tok, 128), whole)
    sds = jax.ShapeDtypeStruct
    width = groups * GW
    return pl.pallas_call(
        functools.partial(bwd_kernel, first_group),
        grid_spec=pltpu.PrefetchScalarGridSpec(
            num_scalar_prefetch=1,
            grid=(groups,),
            in_specs=[full, pl.BlockSpec((GW, D), lambda g, *_: (g + first_group, 0)), blk_in, blk_in, blk_in, blk_in, tab, pl.BlockSpec((D, tok), whole), tab, tab],
            out_specs=[blk, blk, blk, blk] + [pl.BlockSpec((3, D // 2, GW), lambda g, *_: (0, 0, g))] * 2,
            scratch_shapes=[pltpu.VMEM((tok, GW), F32)],
        ),
        out_shape=[sds((tok, width), BF16)] * 3 + [sds((tok, width), F32)] + [sds((3, D // 2, width), BF16)] * 2,
        compiler_params=pltpu.CompilerParams(vmem_limit_bytes=56 * MIB),
        cost_estimate=pl.CostEstimate(flops=10 * 10**9 * groups, bytes_accessed=10 * 10**6, transcendentals=groups * 3 * 10**6),
        name="attention_backward",
    )(length, da, wo, q, k, v, o, st, nmt, cos, sin)


def sig(v):
    return 1.0 / (1.0 + jnp.exp(-v))


def mlp_kernel(nc, nz, zs_ref, *refs):
    pieces = refs[: nc * nz]
    nmt_ref, dyt_ref, nm_ref, dy_ref, h_ref, dg_ref, du_ref = refs[nc * nz : nc * nz + 7]
    outs = refs[nc * nz + 7 :]
    fs = pieces[0].shape[1]
    dz = pieces[0].shape[2]
    starts = [pl.multiple_of(zs_ref[s] * dz, dz) for s in range(nz)]
    for c in range(nc):
        gate = up = dh = None
        for s in range(nz):
            w_ref = pieces[c * nz + s]
            at = pl.ds(starts[s], dz)
            nmt, dyt = nmt_ref[at, :], dyt_ref[at, :]
            parts = nn(w_ref[0], nmt), nn(w_ref[1], nmt), nn(w_ref[2], dyt)
            gate, up, dh = parts if gate is None else (gate + parts[0], up + parts[1], dh + parts[2])
        sg = sig(gate)
        silu = gate * sg
        rows = pl.ds(c * fs, fs)
        h = (silu * up).astype(BF16)
        dg = (dh * up * (sg * (1.0 + gate * (1.0 - sg)))).astype(BF16)
        du = (dh * silu).astype(BF16)
        h_ref[rows, :], dg_ref[rows, :], du_ref[rows, :] = h, dg, du
        for s in range(nz):
            at = pl.ds(starts[s], dz)
            nm, dy = nm_ref[:, at], dy_ref[:, at]
            outs[c][s, 0] = nn(dg, nm).astype(BF16)
            outs[c][s, 1] = nn(du, nm).astype(BF16)
            outs[c][s, 2] = nn(h, dy).astype(BF16)


def mlp_block(zs, pieces, nmt, dyt, nm, dy):
    nc, nz = len(pieces), len(pieces[0])
    _, fs, dz = pieces[0][0].shape
    tok = nm.shape[0]
    sds = jax.ShapeDtypeStruct
    vm = pl.BlockSpec(memory_space=pltpu.VMEM)
    return pl.pallas_call(
        functools.partial(mlp_kernel, nc, nz),
        in_specs=[pl.BlockSpec(memory_space=pltpu.SMEM)] + [vm] * (nc * nz + 4),
        out_specs=[vm] * (3 + nc),
        out_shape=[sds((nc * fs, tok), BF16)] * 3 + [sds((nz, 3, fs, dz), BF16)] * nc,
        compiler_params=pltpu.CompilerParams(vmem_limit_bytes=44 * MIB),
        cost_estimate=pl.CostEstimate(flops=12 * nc * fs * D * tok, bytes_accessed=15 * 10**6, transcendentals=nc * fs * tok),
        name="mlp_block",
    )(zs, *[p for c in pieces for p in c], nmt, dyt, nm, dy)


def norm_back(v, gain, grad):
    ms = jnp.mean(v * v, axis=-1, keepdims=True) + EPS
    r = lax.rsqrt(ms)
    gg = grad * gain
    inner = jnp.mean(gg * v, axis=-1, keepdims=True)
    dv = r * gg - v * (inner * r * r * r)
    dgain = jnp.sum(grad * v * r, axis=0, keepdims=True)
    return dv, dgain


def mlp_out_kernel(nk, nc, nz, zs_ref, *refs):
    nw = nk * nc * nz
    pieces = refs[:nw]
    hs, dgs, dus = refs[nw : nw + nk], refs[nw + nk : nw + 2 * nk], refs[nw + 2 * nk : nw + 3 * nk]
    h1_ref, gain_ref, dy_ref, mixed_ref, dh1_ref, da_ref, dgain_ref, branch_ref, dnm_ref = refs[nw + 3 * nk :]
    fs, dz = pieces[0].shape[1:]
    i = pl.program_id(0)
    for s in range(nz):
        b = d = None
        for k in range(nk):
            for c in range(nc):
                w_ref = pieces[(k * nc + c) * nz + s]
                rows = pl.ds(c * fs, fs)
                b_one = tn(hs[k][rows, :], w_ref[2])
                d_one = tn(dgs[k][rows, :], w_ref[0]) + tn(dus[k][rows, :], w_ref[1])
                b, d = (b_one, d_one) if b is None else (b + b_one, d + d_one)
        at = pl.ds(pl.multiple_of(zs_ref[s] * dz, dz), dz)
        branch_ref[:, at] = b
        dnm_ref[:, at] = d
    h1 = h1_ref[...]
    mixed_ref[...] = (h1 + branch_ref[...]).astype(BF16)
    dv, dgain = norm_back(h1, gain_ref[...], dnm_ref[...])
    dh1 = dy_ref[...].astype(F32) + dv
    dh1_ref[...] = dh1
    da_ref[...] = dh1.astype(BF16)

    @pl.when(i == 0)
    def _():
        dgain_ref[...] = jnp.zeros_like(dgain_ref)

    dgain_ref[...] += dgain


def mlp_out(zs, blocks, hs, dgs, dus, h1, gain, dy):
    nk, nc, nz = len(blocks), len(blocks[0]), len(blocks[0][0])
    flat = [p for pieces in blocks for c in pieces for p in c]
    tok = h1.shape[0]
    tile = 256
    wspec = pl.BlockSpec(memory_space=pltpu.VMEM)
    hspec = pl.BlockSpec((hs[0].shape[0], tile), lambda i: (0, i))
    row = pl.BlockSpec((tile, D), lambda i: (i, 0))
    vec = pl.BlockSpec((1, D), lambda i: (0, 0))
    sds = jax.ShapeDtypeStruct
    return pl.pallas_call(
        functools.partial(mlp_out_kernel, nk, nc, nz),
        grid=(tok // tile,),
        in_specs=[pl.BlockSpec(memory_space=pltpu.SMEM)] + [wspec] * len(flat) + [hspec] * (3 * nk) + [row, vec, row],
        out_specs=[row, row, row, vec],
        out_shape=[sds((tok, D), BF16), sds((tok, D), F32), sds((tok, D), BF16), sds((1, D), F32)],
        scratch_shapes=[pltpu.VMEM((tile, D), F32)] * 2,
        compiler_params=pltpu.CompilerParams(vmem_limit_bytes=58 * MIB),
        cost_estimate=pl.CostEstimate(flops=18 * 10**9, bytes_accessed=45 * 10**6, transcendentals=0),
        name="mlp_out",
    )(zs, *flat, *hs, *dgs, *dus, h1, gain, dy)


def tokens_kernel(n, *refs):
    parts, (wq_ref, wk_ref, wv_ref, x_ref, gain_ref, dh1_ref, out_ref, dgain_ref) = refs[: 3 * n], refs[3 * n :]
    i = pl.program_id(0)
    total = None
    for j, w_ref in enumerate((wq_ref, wk_ref, wv_ref)):
        d = parts[j * n][...] if n == 1 else jnp.concatenate([r[...] for r in parts[j * n : (j + 1) * n]], axis=1)
        t = nt(d, w_ref[...])
        total = t if total is None else total + t
    dv, dgain = norm_back(x_ref[...].astype(F32), gain_ref[...], total)
    out_ref[...] = dh1_ref[...] + dv

    @pl.when(i == 0)
    def _():
        dgain_ref[...] = jnp.zeros_like(dgain_ref)

    dgain_ref[...] += dgain


def tokens_grad(dqs, dks, dvs, wq, wk, wv, x, gain, dh1):
    n = len(dqs)
    tok = x.shape[0]
    tile = 256
    row = pl.BlockSpec((tile, D), lambda i: (i, 0))
    full = pl.BlockSpec((D, D), lambda i: (0, 0))
    vec = pl.BlockSpec((1, D), lambda i: (0, 0))
    sds = jax.ShapeDtypeStruct
    return pl.pallas_call(
        functools.partial(tokens_kernel, n),
        grid=(tok // tile,),
        in_specs=[pl.BlockSpec((tile, d.shape[1]), lambda i: (i, 0)) for d in (*dqs, *dks, *dvs)] + [full, full, full, row, vec, row],
        out_specs=[row, vec],
        out_shape=[sds((tok, D), F32), sds((1, D), F32)],
        compiler_params=pltpu.CompilerParams(vmem_limit_bytes=40 * MIB),
        cost_estimate=pl.CostEstimate(flops=7 * 10**9, bytes_accessed=24 * 10**6, transcendentals=0),
        name="tokens_grad",
    )(*dqs, *dks, *dvs, wq, wk, wv, x, gain, dh1)
RING = (0, 1, 3, 2)


def ring_perm(step):
    n = len(RING)
    return [(RING[i], RING[(i + step) % n]) for i in range(n)]


def to_right(v):
    return lax.ppermute(v, "ha", ring_perm(1))


def to_left(v):
    return lax.ppermute(v, "ha", ring_perm(-1))


def along(v, step, n):
    return lax.ppermute(v, "ma", [(i, (i + step) % n) for i in range(n)])


def swap(v):
    return lax.ppermute(v, "rows", [(0, 1), (1, 0)])


def add(*vs):
    total = vs[0].astype(F32)
    for v in vs[1:]:
        total = total + v.astype(F32)
    return total.astype(BF16)


def gather_weights(own, nz):
    col = [own] + [along(own, s, nz) for s in range(1, nz)]
    left = [to_right(p) for p in col]
    right = [to_left(p) for p in col]
    cut = nz // 2
    far = [to_right(p) for p in left[:cut]] + [to_left(p) for p in right[cut:]]
    return [[b, [swap(p) for p in b]] for b in (col, left, far, right)]


def scatter_weights(grads, nz):
    cut = nz // 2
    mine = [g[0] for g in grads]
    got = [swap(g[1]) for g in grads]
    block = lambda k, s: (mine[k][s], got[k][s])
    far = [to_left(add(*block(2, s))) if s < cut else to_right(add(*block(2, s))) for s in range(nz)]
    from_right = [to_left(add(*block(1, s), *([far[s]] if s < cut else []))) for s in range(nz)]
    from_left = [to_right(add(*block(3, s), *([far[s]] if s >= cut else []))) for s in range(nz)]
    total = [add(*block(0, s), from_right[s], from_left[s]) for s in range(nz)]
    return add(total[0], *[along(total[s], -s, nz) for s in range(1, nz)])


def reduce_all(mine, other, nz):
    lead, width = mine.shape[:-2], mine.shape[-1]
    piece = mine.shape[-2] // (4 * nz)
    axis = len(lead)
    shape = (*lead, 4, nz, piece, width)
    mine, got = mine.reshape(shape), swap(other).reshape(shape)
    cut = nz // 2
    take = lambda v, k, lo, hi: lax.slice_in_dim(lax.index_in_dim(v, k, axis, keepdims=False), lo, hi, axis=axis)
    block = lambda k, lo=0, hi=nz: (take(mine, k, lo, hi), take(got, k, lo, hi))
    far_a = to_left(add(*block(2, 0, cut)))
    far_b = to_right(add(*block(2, cut, nz)))
    from_right = [to_left(add(*block(1, 0, cut), far_a)), to_left(add(*block(1, cut, nz)))]
    from_left = [to_right(add(*block(3, 0, cut))), to_right(add(*block(3, cut, nz), far_b))]
    total = [add(*block(0, 0, cut), from_right[0], from_left[0]), add(*block(0, cut, nz), from_right[1], from_left[1])]
    pick = lambda s: lax.index_in_dim(total[s // cut], s % cut, axis, keepdims=False)
    own = add(pick(0), *[along(pick(s), -s, nz) for s in range(1, nz)])
    col = [own] + [along(own, s, nz) for s in range(1, nz)]
    halves = jnp.stack(col[:cut]), jnp.stack(col[cut:])
    left = [to_right(v) for v in halves]
    right = [to_left(v) for v in halves]
    far = [to_right(left[0]), to_left(right[1])]
    blocks = jnp.stack([jnp.concatenate(b) for b in (halves, left, far, right)])
    return jnp.stack([blocks, swap(blocks)])


def place(order, sums):
    n = sums.shape[0] * sums.shape[1] * sums.shape[2]
    lead, piece, width = sums.shape[3:]
    flat = sums.reshape(n, lead, piece, width)

    def kernel(order_ref, in_ref, out_ref):
        for i in range(n):
            at = pl.ds(pl.multiple_of(order_ref[i] * piece, piece), piece)
            for j in range(lead):
                out_ref[j, at, :] = in_ref[i, j].astype(F32)

    vm = pl.BlockSpec(memory_space=pltpu.VMEM)
    return pl.pallas_call(
        kernel,
        in_specs=[pl.BlockSpec(memory_space=pltpu.SMEM), vm],
        out_specs=vm,
        out_shape=jax.ShapeDtypeStruct((lead, n * piece, width), F32),
        compiler_params=pltpu.CompilerParams(vmem_limit_bytes=30 * MIB),
        cost_estimate=pl.CostEstimate(flops=0, bytes_accessed=6 * flat.size, transcendentals=0),
        name="place",
    )(order, flat)


def body(
    paired, tokens, first_values, lengths, w_query, w_key, w_value, w_out, norm_attn, norm_mlp, w_gate, w_up, w_down, grad_out
):
    nz = lax.axis_size("ma")
    z = lax.axis_index("ma")
    r = lax.axis_index("rows")
    cos, sin = (jnp.asarray(t) for t in rope_tables())
    gain_a, gain_m = norm_attn[None], norm_mlp[None]
    tile = jnp.stack([w_gate.T, w_up.T, w_down])
    dz = tile.shape[2]
    if paired:
        fs = tile.shape[1] // 2
        own = lax.dynamic_slice_in_dim(tile, r * fs, fs, axis=1)
        blocks = gather_weights(own, nz)
        s = jnp.arange(nz, dtype=jnp.int32)
        zs = (z - s) % nz
        place_on_ring = jnp.asarray(np.argsort(RING), jnp.int32)[lax.axis_index("ha")]
        owners = jnp.asarray(RING, jnp.int32)[(place_on_ring - jnp.arange(4, dtype=jnp.int32)) % 4]
        halves = jnp.stack([r, 1 - r])
        order = ((halves[:, None, None] * 4 + owners[None, :, None]) * nz + zs[None, None, :]).reshape(-1)
        n = 8 * nz
    else:
        full = lax.all_gather(lax.all_gather(tile, "ma", axis=0), "ha", axis=0)
        blocks = [[[full[k, s] for s in range(nz)]] for k in range(lax.axis_size("ha"))]
        zs = jnp.arange(nz, dtype=jnp.int32)
        order, n = zs, 1
    q, k, v, o, st, nma, h1, nmm = attention_forward(
        lengths, tokens, gain_a, w_query, w_key, w_value, first_values, cos, sin, w_out, gain_m
    )
    nmat, ot, nmmt, dyt = prepare(order, n, nma, o, nmm, grad_out)
    turn_order = (0, 1, 3, 2)
    done = {i: mlp_block(zs, blocks[i], nmmt, dyt, nmm, grad_out) for i in turn_order}
    hs, dgs, dus = ([done[i][j] for i in range(4)] for j in range(3))
    mixed, dh1, da, dgain_m = mlp_out(zs, blocks, hs, dgs, dus, h1, gain_m, grad_out)
    wo_parts = wout_grad(ot, da)
    calls = [
        attention_backward(2 * i, 2, lengths, da, w_out, q, k, v, o, st, nmat, cos, sin) for i in range(2)
    ]
    dqs, dks, dvs, firsts, mines, others = zip(*calls)
    grad_tokens, dgain_a = tokens_grad(dqs, dks, dvs, w_query, w_key, w_value, tokens, gain_a, dh1)
    grad_first = jnp.concatenate(firsts, axis=1)
    if paired:
        tiles = scatter_weights([done[i][3:] for i in range(4)], nz)
        twin = swap(tiles)
        tiles = jnp.where(r == 0, jnp.concatenate([tiles, twin], axis=1), jnp.concatenate([twin, tiles], axis=1)).astype(F32)
        grad_wout = place(order, reduce_all(wo_parts[0][None], wo_parts[1][None], nz))[0]
        parts = [place(order, reduce_all(m, t, nz)) for m, t in zip(mines, others)]
        grad_q, grad_k, grad_v = (jnp.concatenate([p[j] for p in parts], axis=1) for j in range(3))
    else:
        stacked = jnp.stack([done[i][3] for i in range(4)])
        part = lax.psum_scatter(lax.psum_scatter(stacked, "ha", scatter_dimension=0), "ma", scatter_dimension=0)
        tiles = lax.psum(part, "rows").astype(F32)
        whole = [jnp.concatenate(wo_parts, axis=0)] + [
            jnp.concatenate([jnp.concatenate([m[j], t[j]], axis=0) for m, t in zip(mines, others)], axis=1) for j in range(3)
        ]
        grad_wout, grad_q, grad_k, grad_v = (g.astype(F32) for g in lax.psum(whole, ("rows", "ha", "ma")))
    gains = lax.psum((dgain_a, dgain_m), ("rows", "ha", "ma"))
    return (
        mixed, grad_tokens, grad_first, grad_q, grad_k, grad_v, grad_wout, gains[0][0], gains[1][0],
        tiles[0].T, tiles[1].T, tiles[2],
    )


def solution(mesh):
    tok = P(("rows", "ha", "ma"), None)
    gate, down = P("ma", "ha"), P("ha", "ma")
    return jax.shard_map(
        functools.partial(body, mesh.shape["rows"] == 2),
        mesh=mesh,
        in_specs=(tok, tok, P(("rows", "ha", "ma")), P(), P(), P(), P(), P(), P(), gate, gate, down, tok),
        out_specs=(tok, tok, tok, P(), P(), P(), P(), P(), P(), gate, gate, down),
        check_vma=False,
    )
```

```python
import functools
import math

import jax
import jax.numpy as jnp
import numpy as np
from jax import lax
from jax.experimental import pallas as pl
from jax.experimental.pallas import tpu as pltpu
from jax.sharding import PartitionSpec as P

D = 1024
H = 16
HD = 64
SLOT = 1024
EPS = 1e-06
GROUP = 4
GW = GROUP * HD
QB = 256
SCALE = 1.0 / math.sqrt(HD)
C2 = SCALE * math.log2(math.e)
F32 = jnp.float32
BF16 = jnp.bfloat16
MIB = 1 << 20


def nn(a, b):
    return lax.dot_general(a, b, (((1,), (0,)), ((), ())), preferred_element_type=F32)


def nt(a, b):
    return lax.dot_general(a, b, (((1,), (1,)), ((), ())), preferred_element_type=F32)


def tn(a, b):
    return lax.dot_general(a, b, (((0,), (0,)), ((), ())), preferred_element_type=F32)


def rope_tables():
    place = np.arange(SLOT, dtype=np.float32)
    frequency = np.float32(10000.0) ** (-np.arange(HD // 2, dtype=np.float32) * np.float32(2.0) / np.float32(HD))
    angles = place[:, None] * frequency[None, :]
    cosine, sine = np.cos(angles), np.sin(angles)
    cos_row = np.concatenate([cosine] * 4, axis=1)
    sin_row = np.concatenate([-sine, sine, -sine, sine], axis=1)
    return cos_row.astype(np.float32), sin_row.astype(np.float32)


def lanes(shape):
    return lax.broadcasted_iota(jnp.int32, shape, 1)


def partner(v):
    first = (lanes(v.shape) & 63) < 32
    return jnp.where(first, pltpu.roll(v, 96, 1), pltpu.roll(v, 32, 1))


def turn(v, cos, sin):
    parts = []
    for at in range(0, v.shape[1], 128):
        piece = v[:, at : at + 128]
        parts.append(piece * cos + partner(piece) * sin)
    return jnp.concatenate(parts, axis=1)


def low3(v):
    hi = v.astype(BF16).astype(F32)
    rest = v - hi
    mid = rest.astype(BF16).astype(F32)
    return hi, mid, rest - mid


def forward_start(x_ref, gain_ref, nma_ref, h1_ref, st_ref):
    x = x_ref[...].astype(F32)
    r = lax.rsqrt(jnp.mean(x * x, axis=-1, keepdims=True) + EPS)
    nma_ref[...] = (x * r * gain_ref[...]).astype(BF16)
    h1_ref[...] = x
    st_ref[...] = jnp.zeros_like(st_ref)


def forward_end(h1_ref, gain_m_ref, nmm_ref):
    h = h1_ref[...]
    r = lax.rsqrt(jnp.mean(h * h, axis=-1, keepdims=True) + EPS)
    nmm_ref[...] = (h * r * gain_m_ref[...]).astype(BF16)


def forward_group(
    g, length, nma_ref, wq_ref, wk_ref, wv_ref, fv_ref, cos_ref, sin_ref, wo_ref,
    q_ref, k_ref, v_ref, o_ref, st_ref, h1_ref, between=None,
):
    nm = nma_ref[...]
    cos, sin = cos_ref[...], sin_ref[...]
    q_ref[...] = turn(nn(nm, wq_ref[...]), cos, sin).astype(BF16)
    k_ref[...] = turn(nn(nm, wk_ref[...]), cos, sin).astype(BF16)
    v_ref[...] = (0.5 * nn(nm, wv_ref[...]) + 0.5 * fv_ref[...].astype(F32)).astype(BF16)
    tile = (SLOT, 128)
    lane = lanes(tile)
    row = lax.broadcasted_iota(jnp.int32, tile, 0)
    k_extra = jnp.where((lane == 0) & (row >= length), -1e30, 0.0).astype(BF16)
    q_extra = jnp.where(lane == 0, 1.0, 0.0).astype(BF16)
    ones = jnp.ones(tile, BF16)
    low_lane = lane < HD
    qlane = lanes((QB, 128))
    causal = lax.broadcasted_iota(jnp.int32, (QB, QB), 1) <= lax.broadcasted_iota(jnp.int32, (QB, QB), 0)
    for pair in range(GROUP // 2):
        if pair == 1 and between is not None:
            between()
        cols = pl.ds(pair * 128, 128)
        qp, kp, vp = q_ref[:, cols], k_ref[:, cols], v_ref[:, cols]
        q_ext = jnp.concatenate([qp, q_extra], axis=1)
        k_exts, v_exts = [], []
        for e in range(2):
            mine = low_lane if e == 0 else ~low_lane
            k_exts.append(jnp.concatenate([jnp.where(mine, kp, 0), k_extra], axis=1))
            v_exts.append(jnp.concatenate([jnp.where(mine, vp, 0), ones], axis=1))
        for qb in range(SLOT // QB):
            rows = slice(qb * QB, (qb + 1) * QB)
            top = (qb + 1) * QB
            out = None
            stats = st_ref[rows, :].astype(F32)
            for e in range(2):
                s = nt(q_ext[rows], k_exts[e][:top])
                diag = jnp.where(causal, s[:, top - QB :], -1e30)
                s = diag if qb == 0 else jnp.concatenate([s[:, : top - QB], diag], axis=1)
                m = jnp.max(s, axis=-1, keepdims=True)
                p = jnp.exp2((s - m) * C2).astype(BF16)
                res = nn(p, v_exts[e][:top])
                total = res[:, 128:]
                part = res[:, :128] / total
                out = part if out is None else out + part
                hi, mid, rest = low3(m + jnp.log2(total) * (1.0 / C2))
                base = 8 * (g * GROUP + pair * 2 + e)
                stats = jnp.where(qlane == base, hi, stats)
                stats = jnp.where(qlane == base + 1, mid, stats)
                stats = jnp.where(qlane == base + 2, rest, stats)
                stats = jnp.where(qlane == base + 3, 1.0, stats)
            o_ref[rows, cols] = out.astype(BF16)
            st_ref[rows, :] = stats.astype(BF16)
    h1_ref[...] += nn(o_ref[...], wo_ref[...])


def fwd_kernel(
    len_ref, x_ref, gain_ref, wq_ref, wk_ref, wv_ref, fv_ref, cos_ref, sin_ref, wo_ref, gain_m_ref,
    q_ref, k_ref, v_ref, o_ref, st_ref, nma_ref, h1_ref, nmm_ref,
):
    g = pl.program_id(0)

    @pl.when(g == 0)
    def _():
        forward_start(x_ref, gain_ref, nma_ref, h1_ref, st_ref)

    forward_group(
        g, len_ref[0], nma_ref, wq_ref, wk_ref, wv_ref, fv_ref, cos_ref, sin_ref, wo_ref,
        q_ref, k_ref, v_ref, o_ref, st_ref, h1_ref,
    )

    @pl.when(g == pl.num_programs(0) - 1)
    def _():
        forward_end(h1_ref, gain_m_ref, nmm_ref)


def attention_forward(length, x, gain, wq, wk, wv, fv, cos, sin, wo, gain_m):
    whole = lambda *_: (0, 0)
    col = lambda g, *_: (0, g)
    tok = x.shape[0]
    full = pl.BlockSpec((tok, D), whole)
    blk = pl.BlockSpec((tok, GW), col)
    wblk = pl.BlockSpec((D, GW), col)
    vec = pl.BlockSpec((1, D), whole)
    tab = pl.BlockSpec((tok, 128), whole)
    sds = jax.ShapeDtypeStruct
    return pl.pallas_call(
        fwd_kernel,
        grid_spec=pltpu.PrefetchScalarGridSpec(
            num_scalar_prefetch=1,
            grid=(H // GROUP,),
            in_specs=[full, vec, wblk, wblk, wblk, blk, tab, tab, pl.BlockSpec((GW, D), lambda g, *_: (g, 0)), vec],
            out_specs=[blk, blk, blk, blk, tab, full, full, full],
        ),
        out_shape=[sds((tok, D), BF16)] * 4 + [sds((tok, 128), BF16), sds((tok, D), BF16), sds((tok, D), F32), sds((tok, D), BF16)],
        compiler_params=pltpu.CompilerParams(vmem_limit_bytes=56 * MIB),
        cost_estimate=pl.CostEstimate(flops=30 * 10**9, bytes_accessed=40 * 10**6, transcendentals=10**7),
        name="attention_forward",
    )(length, x, gain, wq, wk, wv, fv, cos, sin, wo, gain_m)


def prep_kernel(n, ordered, plain, order_ref, *refs):
    count = ordered + plain
    srcs, dsts, buf = refs[:count], refs[count : 2 * count], refs[-1]
    size = D // n
    for i, (src, dst) in enumerate(zip(srcs, dsts)):
        if i >= ordered or n == 1:
            dst[...] = src[...].T
        else:
            buf[...] = src[...].T
            for j in range(n):
                dst[pl.ds(j * size, size), :] = buf[pl.ds(pl.multiple_of(order_ref[j] * size, size), size), :]


def prepare(order, n, ordered, plain):
    vm = pl.BlockSpec(memory_space=pltpu.VMEM)
    arrays = (*ordered, *plain)
    tok = arrays[0].shape[0]
    return pl.pallas_call(
        functools.partial(prep_kernel, n, len(ordered), len(plain)),
        in_specs=[pl.BlockSpec(memory_space=pltpu.SMEM)] + [vm] * len(arrays),
        out_specs=[vm] * len(arrays),
        out_shape=[jax.ShapeDtypeStruct((D, tok), BF16)] * len(arrays),
        scratch_shapes=[pltpu.VMEM((D, tok), BF16)],
        compiler_params=pltpu.CompilerParams(vmem_limit_bytes=30 * MIB),
        cost_estimate=pl.CostEstimate(flops=10**9, bytes_accessed=16 * 10**6, transcendentals=0),
        name="prepare",
    )(order, *arrays)


def wout_kernel(ot_ref, da_ref, mine_ref, other_ref):
    mine_ref[...] = nn(ot_ref[: D // 2, :], da_ref[...]).astype(BF16)
    other_ref[...] = nn(ot_ref[D // 2 :, :], da_ref[...]).astype(BF16)


def wout_grad(ot, da):
    vm = pl.BlockSpec(memory_space=pltpu.VMEM)
    return pl.pallas_call(
        wout_kernel,
        in_specs=[vm] * 2,
        out_specs=[vm] * 2,
        out_shape=[jax.ShapeDtypeStruct((D // 2, D), BF16)] * 2,
        compiler_params=pltpu.CompilerParams(vmem_limit_bytes=30 * MIB),
        cost_estimate=pl.CostEstimate(flops=2 * 10**9, bytes_accessed=6 * 10**6, transcendentals=0),
        name="wout_grad",
    )(ot, da)


def bwd_kernel(
    first_group, len_ref, da_ref, wo_ref, q_ref, k_ref, v_ref, o_ref, st_ref, nmt_ref, cos_ref, sin_ref,
    dq_ref, dk_ref, dv_ref, gf_ref, mine_ref, other_ref, dq_acc,
):
    g = pl.program_id(0) + first_group
    do_all = nt(da_ref[...], wo_ref[...]).astype(BF16)
    prod = do_all.astype(F32) * o_ref[...].astype(F32)
    hi = prod.astype(BF16)
    lo = (prod - hi.astype(F32)).astype(BF16)
    sel_row = lax.broadcasted_iota(jnp.int32, (GW, 128), 0) // HD + g * GROUP
    sel_lane = lanes((GW, 128))
    pick = jnp.where((sel_lane // 8 == sel_row) & ((sel_lane & 7) >= 4) & ((sel_lane & 7) <= 5), 1.0, 0.0).astype(BF16)
    delta = nn(hi, pick) + nn(lo, pick)
    tile = (SLOT, 128)
    lane = lanes(tile)
    d_hi = delta.astype(BF16)
    d_ext = jnp.where((lane & 7) == 4, d_hi.astype(F32), delta - d_hi.astype(F32)).astype(BF16)
    length = len_ref[0]
    row = lax.broadcasted_iota(jnp.int32, tile, 0)
    dead = row >= length
    low_lane = lane < HD
    st = st_ref[...]
    visible = lax.broadcasted_iota(jnp.int32, (QB, QB), 0) <= lax.broadcasted_iota(jnp.int32, (QB, QB), 1)
    dq_acc[...] = jnp.zeros_like(dq_acc)
    for pair in range(GROUP // 2):
        cols = pl.ds(pair * 128, 128)
        qp, kp, vp = q_ref[:, cols], k_ref[:, cols], v_ref[:, cols]
        dop = do_all[:, pair * 128 : pair * 128 + 128]
        q_ext = jnp.concatenate([qp, st], axis=1)
        do_ext = jnp.concatenate([dop, d_ext], axis=1)
        heads = []
        for e in range(2):
            mine = low_lane if e == 0 else ~low_lane
            at = lane - 8 * (g * GROUP + pair * 2 + e)
            k_x = jnp.where((at >= 0) & (at < 3), -1.0, jnp.where((at == 3) & dead, -1e30, 0.0)).astype(BF16)
            v_x = jnp.where((at >= 4) & (at < 6), -1.0, 0.0).astype(BF16)
            k_m = jnp.where(mine, kp, 0)
            heads.append((
                k_m,
                jnp.concatenate([k_m, k_x], axis=1),
                jnp.concatenate([jnp.where(mine, vp, 0), v_x], axis=1),
                jnp.where(mine, qp, 0),
                jnp.where(mine, dop, 0),
            ))
        for kb in range(SLOT // QB):
            rows = slice(kb * QB, (kb + 1) * QB)
            start = kb * QB
            dk = dv = None
            for k_m, k_ext, v_ext, q_m, do_m in heads:
                st_ = nt(k_ext[rows], q_ext[start:])
                dp = nt(v_ext[rows], do_ext[start:])
                p = jnp.exp2(st_ * C2)
                diag = jnp.where(visible, p[:, :QB], 0.0)
                p = diag if kb == SLOT // QB - 1 else jnp.concatenate([diag, p[:, QB:]], axis=1)
                ds = (p * dp).astype(BF16)
                p = p.astype(BF16)
                dv_e = nn(p, do_m[start:])
                dk_e = nn(ds, q_m[start:])
                dk = dk_e if dk is None else dk + dk_e
                dv = dv_e if dv is None else dv + dv_e
                dq_acc[start:, cols] += tn(ds, k_m[rows])
            dk = dk * SCALE
            cos, sin = cos_ref[rows, :], sin_ref[rows, :]
            dk_ref[rows, cols] = (dk * cos - partner(dk) * sin).astype(BF16)
            half = 0.5 * dv
            gf_ref[rows, cols] = half
            dv_ref[rows, cols] = half.astype(BF16)
    cos, sin = cos_ref[...], sin_ref[...]
    for pair in range(GROUP // 2):
        cols = pl.ds(pair * 128, 128)
        dq = dq_acc[:, cols] * SCALE
        dq_ref[:, cols] = (dq * cos - partner(dq) * sin).astype(BF16)
    nmt = nmt_ref[...]
    for j, ref in enumerate((dq_ref, dk_ref, dv_ref)):
        grad = nn(nmt, ref[...]).astype(BF16)
        mine_ref[j] = grad[: D // 2]
        other_ref[j] = grad[D // 2 :]


def attention_backward(first_group, groups, length, da, wo, q, k, v, o, st, nmt, cos, sin):
    whole = lambda *_: (0, 0)
    tok = da.shape[0]
    full = pl.BlockSpec((tok, D), whole)
    blk_in = pl.BlockSpec((tok, GW), lambda g, *_: (0, g + first_group))
    blk = pl.BlockSpec((tok, GW), lambda g, *_: (0, g))
    tab = pl.BlockSpec((tok, 128), whole)
    sds = jax.ShapeDtypeStruct
    width = groups * GW
    return pl.pallas_call(
        functools.partial(bwd_kernel, first_group),
        grid_spec=pltpu.PrefetchScalarGridSpec(
            num_scalar_prefetch=1,
            grid=(groups,),
            in_specs=[full, pl.BlockSpec((GW, D), lambda g, *_: (g + first_group, 0)), blk_in, blk_in, blk_in, blk_in, tab, pl.BlockSpec((D, tok), whole), tab, tab],
            out_specs=[blk, blk, blk, blk] + [pl.BlockSpec((3, D // 2, GW), lambda g, *_: (0, 0, g))] * 2,
            scratch_shapes=[pltpu.VMEM((tok, GW), F32)],
        ),
        out_shape=[sds((tok, width), BF16)] * 3 + [sds((tok, width), F32)] + [sds((3, D // 2, width), BF16)] * 2,
        compiler_params=pltpu.CompilerParams(vmem_limit_bytes=56 * MIB),
        cost_estimate=pl.CostEstimate(flops=10 * 10**9 * groups, bytes_accessed=10 * 10**6, transcendentals=groups * 3 * 10**6),
        name="attention_backward",
    )(length, da, wo, q, k, v, o, st, nmt, cos, sin)


def sig(v):
    return 1.0 / (1.0 + jnp.exp(-v))


def mlp_kernel(nc, nz, zs_ref, *refs):
    pieces = refs[: nc * nz]
    nmt_ref, dyt_ref, nm_ref, dy_ref, h_ref, dg_ref, du_ref = refs[nc * nz : nc * nz + 7]
    outs = refs[nc * nz + 7 :]
    fs = pieces[0].shape[1]
    dz = pieces[0].shape[2]
    starts = [pl.multiple_of(zs_ref[s] * dz, dz) for s in range(nz)]
    for c in range(nc):
        gate = up = dh = None
        for s in range(nz):
            w_ref = pieces[c * nz + s]
            at = pl.ds(starts[s], dz)
            nmt, dyt = nmt_ref[at, :], dyt_ref[at, :]
            parts = nn(w_ref[0], nmt), nn(w_ref[1], nmt), nn(w_ref[2], dyt)
            gate, up, dh = parts if gate is None else (gate + parts[0], up + parts[1], dh + parts[2])
        sg = sig(gate)
        silu = gate * sg
        rows = pl.ds(c * fs, fs)
        h = (silu * up).astype(BF16)
        dg = (dh * up * (sg * (1.0 + gate * (1.0 - sg)))).astype(BF16)
        du = (dh * silu).astype(BF16)
        h_ref[rows, :], dg_ref[rows, :], du_ref[rows, :] = h, dg, du
        for s in range(nz):
            at = pl.ds(starts[s], dz)
            nm, dy = nm_ref[:, at], dy_ref[:, at]
            outs[c][s, 0] = nn(dg, nm).astype(BF16)
            outs[c][s, 1] = nn(du, nm).astype(BF16)
            outs[c][s, 2] = nn(h, dy).astype(BF16)


def mlp_block(zs, pieces, nmt, dyt, nm, dy):
    nc, nz = len(pieces), len(pieces[0])
    _, fs, dz = pieces[0][0].shape
    tok = nm.shape[0]
    sds = jax.ShapeDtypeStruct
    vm = pl.BlockSpec(memory_space=pltpu.VMEM)
    return pl.pallas_call(
        functools.partial(mlp_kernel, nc, nz),
        in_specs=[pl.BlockSpec(memory_space=pltpu.SMEM)] + [vm] * (nc * nz + 4),
        out_specs=[vm] * (3 + nc),
        out_shape=[sds((nc * fs, tok), BF16)] * 3 + [sds((nz, 3, fs, dz), BF16)] * nc,
        compiler_params=pltpu.CompilerParams(vmem_limit_bytes=44 * MIB),
        cost_estimate=pl.CostEstimate(flops=12 * nc * fs * D * tok, bytes_accessed=15 * 10**6, transcendentals=nc * fs * tok),
        name="mlp_block",
    )(zs, *[p for c in pieces for p in c], nmt, dyt, nm, dy)


MESH = pl.DeviceIdType.MESH
RING = (0, 1, 3, 2)
STEPS = H // GROUP
TURNS = (0, 1, 3, 2)


def table(index, values):
    out = values[0]
    for i, v in enumerate(values[1:], 1):
        out = jnp.where(index == i, v, out)
    return out


class Gather:
    def __init__(self, nz, own_ref, w_ref, sems):
        self.nz, self.own, self.w = nz, own_ref, w_ref
        self.recv, self.z_send, self.right_send, self.left_send, self.far_send, self.swap_send, self.local = sems
        self.r, self.a, self.z = (lax.axis_index(n) for n in ("rows", "ha", "ma"))
        spot = table(self.a, [RING.index(i) for i in range(4)])
        self.right_to = table(spot, [RING[(i + 1) % 4] for i in range(4)])
        self.left_to = table(spot, [RING[(i + 3) % 4] for i in range(4)])
        self.arrivals = [0] + [table(self.z, v) for v in ((3, 1, 3, 1), (2, 3, 1, 2), (1, 2, 2, 3))]

    def copy(self, src, dst, send, device):
        return pltpu.make_async_remote_copy(
            src_ref=self.w.at[src], dst_ref=self.w.at[dst], send_sem=send, recv_sem=self.recv.at[dst],
            device_id=device, device_id_type=MESH,
        )

    def at(self, **moved):
        place = {"rows": self.r, "ha": self.a, "ma": self.z, **moved}
        return (place["rows"], place["ha"], place["ma"])

    def z_right(self, s):
        return self.copy((0, 0, s), (0, 0, s + 1), self.z_send.at[0, s], self.at(ma=self.z + 1))

    def z_left(self, s, new):
        return self.copy((0, 0, s), (0, 0, new), self.z_send.at[1, s], self.at(ma=self.z - 1))

    def right(self, s):
        return self.copy((0, 0, s), (1, 0, s), self.right_send.at[s], self.at(ha=self.right_to))

    def left(self, s):
        return self.copy((0, 0, s), (3, 0, s), self.left_send.at[s], self.at(ha=self.left_to))

    def far(self, i):
        s = self.arrivals[i]
        if i % 2 == 0:
            return self.copy((1, 0, s), (2, 0, s), self.far_send.at[s], self.at(ha=self.right_to))
        return self.copy((3, 0, s), (2, 0, s), self.far_send.at[s], self.at(ha=self.left_to))

    def swap(self, k, s):
        return self.copy((k, 0, s), (k, 1, s), self.swap_send.at[k, s], self.at(rows=1 - self.r))

    def z_moves(self, i, act):
        s, nz, z = self.arrivals[i], self.nz, self.z
        if i == 0:
            pl.when(z < nz - 1)(lambda: act(self.z_right(0)))
            pl.when(z >= 1)(lambda: act(self.z_left(0, nz - 1)))
        else:
            pl.when((z >= s) & (z < nz - 1))(lambda: act(self.z_right(s)))
            pl.when((z < s) & (z >= 1))(lambda: act(self.z_left(s, s - 1)))

    def arrived(self, k, s, c=0):
        self.copy((k, c, s), (k, c, s), self.local, self.at()).wait_recv()

    def begin(self):
        barrier = pltpu.get_barrier_semaphore()
        up, down = (self.z + 1) % self.nz, (self.z + self.nz - 1) % self.nz
        others = [self.at(ma=up), self.at(ma=down), self.at(ha=self.right_to), self.at(ha=self.left_to), self.at(rows=1 - self.r)]
        for other in others:
            pl.semaphore_signal(barrier, inc=1, device_id=other, device_id_type=MESH)
        mine = pltpu.make_async_copy(self.own, self.w.at[0, 0, 0], self.local)
        mine.start()
        mine.wait()
        pl.semaphore_wait(barrier, len(others))
        self.spread(0)

    def spread(self, i):
        s = self.arrivals[i]
        if i:
            self.arrived(0, s)
        self.z_moves(i, lambda c: c.start())
        self.right(s).start()
        self.left(s).start()
        self.swap(0, s).start()

    def sides(self, i):
        s = self.arrivals[i]
        self.arrived(1, s)
        self.arrived(3, s)
        self.far(i).start()
        self.swap(1, s).start()
        self.swap(3, s).start()

    def opposite(self, i):
        s = self.arrivals[i]
        self.arrived(2, s)
        self.swap(2, s).start()

    def end(self):
        for i in range(self.nz):
            s = self.arrivals[i]
            self.z_moves(i, lambda c: c.wait_send())
            self.right(s).wait_send()
            self.left(s).wait_send()
            self.far(i).wait_send()
            for k in range(4):
                self.swap(k, s).wait_send()


def first_kernel(
    nz, len_ref, x_ref, gain_ref, wq_ref, wk_ref, wv_ref, fv_ref, cos_ref, sin_ref, wo_ref, gain_m_ref, dy_ref, own_ref,
    q_ref, k_ref, v_ref, o_ref, st_ref, nma_ref, h1_ref, h_ref, dg_ref, du_ref, mine_ref, other_ref, w_ref,
    nmm_ref, nmmt_ref, dyt_ref, wbuf, wsem, *sems,
):
    g = pl.program_id(0)
    gather = Gather(nz, own_ref, w_ref, sems)
    fs, dz = own_ref.shape[1:]

    @pl.when(g == 0)
    def _():
        gather.begin()
        forward_start(x_ref, gain_ref, nma_ref, h1_ref, st_ref)

    def between():
        @pl.when(g == 1)
        def _():
            gather.spread(1)
            gather.sides(0)

        @pl.when(g == 2)
        def _():
            gather.spread(2)
            gather.sides(1)

    @pl.when(g < STEPS)
    def _():
        forward_group(
            g, len_ref[0], nma_ref, wq_ref, wk_ref, wv_ref, fv_ref, cos_ref, sin_ref, wo_ref,
            q_ref, k_ref, v_ref, o_ref, st_ref, h1_ref, between,
        )

    def load(k, c, slot):
        return pltpu.make_async_copy(w_ref.at[k, c], wbuf.at[slot], wsem.at[slot])

    def fetch(k, c, slot):
        for s in range(nz):
            if c == 1:
                gather.arrived(k, s, 1)
        load(k, c, slot).start()

    @pl.when(g == STEPS - 1)
    def _():
        forward_end(h1_ref, gain_m_ref, nmm_ref)
        gather.spread(3)
        gather.opposite(0)
        fetch(0, 0, 0)
        nmmt_ref[...] = nmm_ref[...].T
        dyt_ref[...] = dy_ref[...].T

    starts = [pl.multiple_of((gather.z + nz - s) % nz * dz, dz) for s in range(nz)]

    @pl.when(g >= STEPS)
    def _():
        turn_at = g - STEPS
        k = table(turn_at, TURNS)
        following = table(turn_at, TURNS[1:] + TURNS[-1:])
        for c in range(2):
            load(k, c, c).wait()
            gate = up = dh = None
            for s in range(nz):
                at = pl.ds(starts[s], dz)
                nmt, dyt = nmmt_ref[at, :], dyt_ref[at, :]
                parts = nn(wbuf[c, s, 0], nmt), nn(wbuf[c, s, 1], nmt), nn(wbuf[c, s, 2], dyt)
                gate, up, dh = parts if gate is None else (gate + parts[0], up + parts[1], dh + parts[2])
            sg = sig(gate)
            silu = gate * sg
            rows = pl.ds(c * fs, fs)
            h = (silu * up).astype(BF16)
            dg = (dh * up * (sg * (1.0 + gate * (1.0 - sg)))).astype(BF16)
            du = (dh * silu).astype(BF16)
            h_ref[0, rows, :], dg_ref[0, rows, :], du_ref[0, rows, :] = h, dg, du
            if c == 0:
                @pl.when(turn_at == 0)
                def _():
                    gather.sides(2)
                    gather.opposite(1)

                fetch(k, 1, 1)
            else:
                @pl.when(turn_at == 0)
                def _():
                    gather.sides(3)

                @pl.when(turn_at == 1)
                def _():
                    gather.opposite(2)
                    gather.opposite(3)

                @pl.when(turn_at < len(TURNS) - 1)
                def _():
                    fetch(following, 0, 0)

            out = mine_ref if c == 0 else other_ref
            for s in range(nz):
                at = pl.ds(starts[s], dz)
                nm, dy = nmm_ref[:, at], dy_ref[:, at]
                out[0, s, 0] = nn(dg, nm).astype(BF16)
                out[0, s, 1] = nn(du, nm).astype(BF16)
                out[0, s, 2] = nn(h, dy).astype(BF16)

    @pl.when(g == pl.num_programs(0) - 1)
    def _():
        gather.end()


def first_half(length, x, gain, wq, wk, wv, fv, cos, sin, wo, gain_m, dy, own, nz):
    tok = x.shape[0]
    fs, dz = own.shape[1:]
    sds = jax.ShapeDtypeStruct
    once = dict(pipeline_mode=pl.Buffered(1))
    step = lambda g: jnp.minimum(g, STEPS - 1)
    block = lambda g: table(jnp.maximum(g - STEPS, 0), TURNS)
    full = pl.BlockSpec((tok, D), lambda g: (0, 0), **once)
    blk = pl.BlockSpec((tok, GW), lambda g: (0, step(g)))
    wblk = pl.BlockSpec((D, GW), lambda g: (0, step(g)))
    vec = pl.BlockSpec((1, D), lambda g: (0, 0), **once)
    tab = pl.BlockSpec((tok, 128), lambda g: (0, 0), **once)
    hidden = pl.BlockSpec((1, 2 * fs, tok), lambda g: (block(g), 0, 0))
    grads = pl.BlockSpec((1, nz, 3, fs, dz), lambda g: (block(g), 0, 0, 0, 0))
    hbm = pl.BlockSpec(memory_space=pl.ANY)
    sem = pltpu.SemaphoreType.DMA
    return pl.pallas_call(
        functools.partial(first_kernel, nz),
        grid=(STEPS + len(TURNS),),
        in_specs=[
            pl.BlockSpec(memory_space=pltpu.SMEM), full, vec, wblk, wblk, wblk, blk, tab, tab,
            pl.BlockSpec((GW, D), lambda g: (step(g), 0)), vec, full, hbm,
        ],
        out_specs=[blk, blk, blk, blk, tab, full, full, hidden, hidden, hidden, grads, grads, hbm],
        out_shape=[sds((tok, D), BF16)] * 4
        + [sds((tok, 128), BF16), sds((tok, D), BF16), sds((tok, D), F32)]
        + [sds((4, 2 * fs, tok), BF16)] * 3
        + [sds((4, nz, 3, fs, dz), BF16)] * 2
        + [sds((4, 2, nz, 3, fs, dz), BF16)],
        scratch_shapes=[
            pltpu.VMEM((tok, D), BF16), pltpu.VMEM((D, tok), BF16), pltpu.VMEM((D, tok), BF16),
            pltpu.VMEM((2, nz, 3, fs, dz), BF16), sem((2,)),
            sem((4, 2, nz)), sem((2, nz)), sem((nz,)), sem((nz,)), sem((nz,)), sem((4, nz)), sem,
        ],
        compiler_params=pltpu.CompilerParams(vmem_limit_bytes=60 * MIB, collective_id=1, has_side_effects=True),
        cost_estimate=pl.CostEstimate(flops=66 * 10**9, bytes_accessed=80 * 10**6, transcendentals=10**7),
        name="first_half",
    )(length, x, gain, wq, wk, wv, fv, cos, sin, wo, gain_m, dy, own)


def norm_back(v, gain, grad):
    ms = jnp.mean(v * v, axis=-1, keepdims=True) + EPS
    r = lax.rsqrt(ms)
    gg = grad * gain
    inner = jnp.mean(gg * v, axis=-1, keepdims=True)
    dv = r * gg - v * (inner * r * r * r)
    dgain = jnp.sum(grad * v * r, axis=0, keepdims=True)
    return dv, dgain


def mlp_out_kernel(nk, nc, nz, zs_ref, w_ref, hs_ref, dgs_ref, dus_ref, h1_ref, gain_ref, dy_ref, mixed_ref, dh1_ref, da_ref, dgain_ref, branch_ref, dnm_ref):
    fs, dz = w_ref.shape[4:]
    i = pl.program_id(0)
    for s in range(nz):
        b = d = None
        for k in range(nk):
            for c in range(nc):
                rows = pl.ds(c * fs, fs)
                b_one = tn(hs_ref[k, rows, :], w_ref[k, c, s, 2])
                d_one = tn(dgs_ref[k, rows, :], w_ref[k, c, s, 0]) + tn(dus_ref[k, rows, :], w_ref[k, c, s, 1])
                b, d = (b_one, d_one) if b is None else (b + b_one, d + d_one)
        at = pl.ds(pl.multiple_of(zs_ref[s] * dz, dz), dz)
        branch_ref[:, at] = b
        dnm_ref[:, at] = d
    h1 = h1_ref[...]
    mixed_ref[...] = (h1 + branch_ref[...]).astype(BF16)
    dv, dgain = norm_back(h1, gain_ref[...], dnm_ref[...])
    dh1 = dy_ref[...].astype(F32) + dv
    dh1_ref[...] = dh1
    da_ref[...] = dh1.astype(BF16)

    @pl.when(i == 0)
    def _():
        dgain_ref[...] = jnp.zeros_like(dgain_ref)

    dgain_ref[...] += dgain


def mlp_out(zs, w, hs, dgs, dus, h1, gain, dy):
    nk, nc, nz = w.shape[:3]
    tok = h1.shape[0]
    tile = 256
    wspec = pl.BlockSpec(w.shape, lambda i: (0,) * 6, pipeline_mode=pl.Buffered(1))
    hspec = pl.BlockSpec((nk, hs.shape[1], tile), lambda i: (0, 0, i))
    row = pl.BlockSpec((tile, D), lambda i: (i, 0))
    vec = pl.BlockSpec((1, D), lambda i: (0, 0))
    sds = jax.ShapeDtypeStruct
    return pl.pallas_call(
        functools.partial(mlp_out_kernel, nk, nc, nz),
        grid=(tok // tile,),
        in_specs=[pl.BlockSpec(memory_space=pltpu.SMEM), wspec, hspec, hspec, hspec, row, vec, row],
        out_specs=[row, row, row, vec],
        out_shape=[sds((tok, D), BF16), sds((tok, D), F32), sds((tok, D), BF16), sds((1, D), F32)],
        scratch_shapes=[pltpu.VMEM((tile, D), F32)] * 2,
        compiler_params=pltpu.CompilerParams(vmem_limit_bytes=58 * MIB),
        cost_estimate=pl.CostEstimate(flops=18 * 10**9, bytes_accessed=45 * 10**6, transcendentals=0),
        name="mlp_out",
    )(zs, w, hs, dgs, dus, h1, gain, dy)


def tokens_kernel(n, *refs):
    parts, (wq_ref, wk_ref, wv_ref, x_ref, gain_ref, dh1_ref, out_ref, dgain_ref) = refs[: 3 * n], refs[3 * n :]
    i = pl.program_id(0)
    total = None
    for j, w_ref in enumerate((wq_ref, wk_ref, wv_ref)):
        d = parts[j * n][...] if n == 1 else jnp.concatenate([r[...] for r in parts[j * n : (j + 1) * n]], axis=1)
        t = nt(d, w_ref[...])
        total = t if total is None else total + t
    dv, dgain = norm_back(x_ref[...].astype(F32), gain_ref[...], total)
    out_ref[...] = dh1_ref[...] + dv

    @pl.when(i == 0)
    def _():
        dgain_ref[...] = jnp.zeros_like(dgain_ref)

    dgain_ref[...] += dgain


def tokens_grad(dqs, dks, dvs, wq, wk, wv, x, gain, dh1):
    n = len(dqs)
    tok = x.shape[0]
    tile = 256
    row = pl.BlockSpec((tile, D), lambda i: (i, 0))
    full = pl.BlockSpec((D, D), lambda i: (0, 0))
    vec = pl.BlockSpec((1, D), lambda i: (0, 0))
    sds = jax.ShapeDtypeStruct
    return pl.pallas_call(
        functools.partial(tokens_kernel, n),
        grid=(tok // tile,),
        in_specs=[pl.BlockSpec((tile, d.shape[1]), lambda i: (i, 0)) for d in (*dqs, *dks, *dvs)] + [full, full, full, row, vec, row],
        out_specs=[row, vec],
        out_shape=[sds((tok, D), F32), sds((1, D), F32)],
        compiler_params=pltpu.CompilerParams(vmem_limit_bytes=40 * MIB),
        cost_estimate=pl.CostEstimate(flops=7 * 10**9, bytes_accessed=24 * 10**6, transcendentals=0),
        name="tokens_grad",
    )(*dqs, *dks, *dvs, wq, wk, wv, x, gain, dh1)
def ring_perm(step):
    n = len(RING)
    return [(RING[i], RING[(i + step) % n]) for i in range(n)]


def to_right(v):
    return lax.ppermute(v, "ha", ring_perm(1))


def to_left(v):
    return lax.ppermute(v, "ha", ring_perm(-1))


def along(v, step, n):
    return lax.ppermute(v, "ma", [(i, (i + step) % n) for i in range(n)])


def swap(v):
    return lax.ppermute(v, "rows", [(0, 1), (1, 0)])


def add(*vs):
    total = vs[0].astype(F32)
    for v in vs[1:]:
        total = total + v.astype(F32)
    return total.astype(BF16)


def scatter_weights(mine, other, nz):
    cut = nz // 2
    got = swap(other)
    block = lambda k, s: (mine[k][s], got[k][s])
    far = [to_left(add(*block(2, s))) if s < cut else to_right(add(*block(2, s))) for s in range(nz)]
    from_right = [to_left(add(*block(1, s), *([far[s]] if s < cut else []))) for s in range(nz)]
    from_left = [to_right(add(*block(3, s), *([far[s]] if s >= cut else []))) for s in range(nz)]
    total = [add(*block(0, s), from_right[s], from_left[s]) for s in range(nz)]
    return add(total[0], *[along(total[s], -s, nz) for s in range(1, nz)])


def reduce_all(mine, other, nz):
    lead, width = mine.shape[:-2], mine.shape[-1]
    piece = mine.shape[-2] // (4 * nz)
    axis = len(lead)
    shape = (*lead, 4, nz, piece, width)
    mine, got = mine.reshape(shape), swap(other).reshape(shape)
    cut = nz // 2
    take = lambda v, k, lo, hi: lax.slice_in_dim(lax.index_in_dim(v, k, axis, keepdims=False), lo, hi, axis=axis)
    block = lambda k, lo=0, hi=nz: (take(mine, k, lo, hi), take(got, k, lo, hi))
    far_a = to_left(add(*block(2, 0, cut)))
    far_b = to_right(add(*block(2, cut, nz)))
    from_right = [to_left(add(*block(1, 0, cut), far_a)), to_left(add(*block(1, cut, nz)))]
    from_left = [to_right(add(*block(3, 0, cut))), to_right(add(*block(3, cut, nz), far_b))]
    total = [add(*block(0, 0, cut), from_right[0], from_left[0]), add(*block(0, cut, nz), from_right[1], from_left[1])]
    pick = lambda s: lax.index_in_dim(total[s // cut], s % cut, axis, keepdims=False)
    own = add(pick(0), *[along(pick(s), -s, nz) for s in range(1, nz)])
    col = [own] + [along(own, s, nz) for s in range(1, nz)]
    halves = jnp.stack(col[:cut]), jnp.stack(col[cut:])
    left = [to_right(v) for v in halves]
    right = [to_left(v) for v in halves]
    far = [to_right(left[0]), to_left(right[1])]
    blocks = jnp.stack([jnp.concatenate(b) for b in (halves, left, far, right)])
    return jnp.stack([blocks, swap(blocks)])


def place(order, sums):
    n = sums.shape[0] * sums.shape[1] * sums.shape[2]
    lead, piece, width = sums.shape[3:]
    flat = sums.reshape(n, lead, piece, width)

    def kernel(order_ref, in_ref, out_ref):
        for i in range(n):
            at = pl.ds(pl.multiple_of(order_ref[i] * piece, piece), piece)
            for j in range(lead):
                out_ref[j, at, :] = in_ref[i, j].astype(F32)

    vm = pl.BlockSpec(memory_space=pltpu.VMEM)
    return pl.pallas_call(
        kernel,
        in_specs=[pl.BlockSpec(memory_space=pltpu.SMEM), vm],
        out_specs=vm,
        out_shape=jax.ShapeDtypeStruct((lead, n * piece, width), F32),
        compiler_params=pltpu.CompilerParams(vmem_limit_bytes=30 * MIB),
        cost_estimate=pl.CostEstimate(flops=0, bytes_accessed=6 * flat.size, transcendentals=0),
        name="place",
    )(order, flat)


def body(
    paired, tokens, first_values, lengths, w_query, w_key, w_value, w_out, norm_attn, norm_mlp, w_gate, w_up, w_down, grad_out
):
    nz = lax.axis_size("ma")
    z = lax.axis_index("ma")
    r = lax.axis_index("rows")
    cos, sin = (jnp.asarray(t) for t in rope_tables())
    gain_a, gain_m = norm_attn[None], norm_mlp[None]
    tile = jnp.stack([w_gate.T, w_up.T, w_down])
    dz = tile.shape[2]
    if paired:
        fs = tile.shape[1] // 2
        own = lax.dynamic_slice_in_dim(tile, r * fs, fs, axis=1)
        s = jnp.arange(nz, dtype=jnp.int32)
        zs = (z - s) % nz
        spot = jnp.asarray(np.argsort(RING), jnp.int32)[lax.axis_index("ha")]
        owners = jnp.asarray(RING, jnp.int32)[(spot - jnp.arange(4, dtype=jnp.int32)) % 4]
        halves = jnp.stack([r, 1 - r])
        order = ((halves[:, None, None] * 4 + owners[None, :, None]) * nz + zs[None, None, :]).reshape(-1)
        q, k, v, o, st, nma, h1, hs, dgs, dus, mine, other, w = first_half(
            lengths, tokens, gain_a, w_query, w_key, w_value, first_values, cos, sin, w_out, gain_m, grad_out, own, nz
        )
        nmat, ot = prepare(order, 8 * nz, [nma, o], [])
    else:
        w = lax.all_gather(lax.all_gather(tile, "ma", axis=0), "ha", axis=0)[:, None]
        zs = jnp.arange(nz, dtype=jnp.int32)
        q, k, v, o, st, nma, h1, nmm = attention_forward(
            lengths, tokens, gain_a, w_query, w_key, w_value, first_values, cos, sin, w_out, gain_m
        )
        nmat, ot, nmmt, dyt = prepare(zs, 1, [], [nma, o, nmm, grad_out])
        done = [mlp_block(zs, [[w[i, 0, j] for j in range(nz)]], nmmt, dyt, nmm, grad_out) for i in range(w.shape[0])]
        hs, dgs, dus, mine = (jnp.stack([d[j] for d in done]) for j in range(4))
    mixed, dh1, da, dgain_m = mlp_out(zs, w, hs, dgs, dus, h1, gain_m, grad_out)
    wo_parts = wout_grad(ot, da)
    calls = [
        attention_backward(2 * i, 2, lengths, da, w_out, q, k, v, o, st, nmat, cos, sin) for i in range(2)
    ]
    dqs, dks, dvs, firsts, mines, others = zip(*calls)
    grad_tokens, dgain_a = tokens_grad(dqs, dks, dvs, w_query, w_key, w_value, tokens, gain_a, dh1)
    grad_first = jnp.concatenate(firsts, axis=1)
    if paired:
        tiles = scatter_weights(mine, other, nz)
        twin = swap(tiles)
        tiles = jnp.where(r == 0, jnp.concatenate([tiles, twin], axis=1), jnp.concatenate([twin, tiles], axis=1)).astype(F32)
        grad_wout = place(order, reduce_all(wo_parts[0][None], wo_parts[1][None], nz))[0]
        parts = [place(order, reduce_all(m, t, nz)) for m, t in zip(mines, others)]
        grad_q, grad_k, grad_v = (jnp.concatenate([p[j] for p in parts], axis=1) for j in range(3))
    else:
        part = lax.psum_scatter(lax.psum_scatter(mine, "ha", scatter_dimension=0), "ma", scatter_dimension=0)
        tiles = lax.psum(part, "rows").astype(F32)
        whole = [jnp.concatenate(wo_parts, axis=0)] + [
            jnp.concatenate([jnp.concatenate([m[j], t[j]], axis=0) for m, t in zip(mines, others)], axis=1) for j in range(3)
        ]
        grad_wout, grad_q, grad_k, grad_v = (g.astype(F32) for g in lax.psum(whole, ("rows", "ha", "ma")))
    gains = lax.psum((dgain_a, dgain_m), ("rows", "ha", "ma"))
    return (
        mixed, grad_tokens, grad_first, grad_q, grad_k, grad_v, grad_wout, gains[0][0], gains[1][0],
        tiles[0].T, tiles[1].T, tiles[2],
    )


def solution(mesh):
    tok = P(("rows", "ha", "ma"), None)
    gate, down = P("ma", "ha"), P("ha", "ma")
    return jax.shard_map(
        functools.partial(body, mesh.shape["rows"] == 2),
        mesh=mesh,
        in_specs=(tok, tok, P(("rows", "ha", "ma")), P(), P(), P(), P(), P(), P(), gate, gate, down, tok),
        out_specs=(tok, tok, tok, P(), P(), P(), P(), P(), P(), gate, gate, down),
        check_vma=False,
    )
```

```python
import functools
import math

import jax
import jax.numpy as jnp
import numpy as np
from jax import lax
from jax.experimental import pallas as pl
from jax.experimental.pallas import tpu as pltpu
from jax.sharding import PartitionSpec as P

D = 1024
H = 16
HD = 64
SLOT = 1024
EPS = 1e-06
GROUP = 4
GW = GROUP * HD
QB = 256
SCALE = 1.0 / math.sqrt(HD)
C2 = SCALE * math.log2(math.e)
F32 = jnp.float32
BF16 = jnp.bfloat16
MIB = 1 << 20


def nn(a, b):
    return lax.dot_general(a, b, (((1,), (0,)), ((), ())), preferred_element_type=F32)


def nt(a, b):
    return lax.dot_general(a, b, (((1,), (1,)), ((), ())), preferred_element_type=F32)


def tn(a, b):
    return lax.dot_general(a, b, (((0,), (0,)), ((), ())), preferred_element_type=F32)


def rope_tables():
    place = np.arange(SLOT, dtype=np.float32)
    frequency = np.float32(10000.0) ** (-np.arange(HD // 2, dtype=np.float32) * np.float32(2.0) / np.float32(HD))
    angles = place[:, None] * frequency[None, :]
    cosine, sine = np.cos(angles), np.sin(angles)
    cos_row = np.concatenate([cosine] * 4, axis=1)
    sin_row = np.concatenate([-sine, sine, -sine, sine], axis=1)
    return cos_row.astype(np.float32), sin_row.astype(np.float32)


def lanes(shape):
    return lax.broadcasted_iota(jnp.int32, shape, 1)


def partner(v):
    first = (lanes(v.shape) & 63) < 32
    return jnp.where(first, pltpu.roll(v, 96, 1), pltpu.roll(v, 32, 1))


def turn(v, cos, sin):
    parts = []
    for at in range(0, v.shape[1], 128):
        piece = v[:, at : at + 128]
        parts.append(piece * cos + partner(piece) * sin)
    return jnp.concatenate(parts, axis=1)


def low3(v):
    hi = v.astype(BF16).astype(F32)
    rest = v - hi
    mid = rest.astype(BF16).astype(F32)
    return hi, mid, rest - mid


def forward_start(x_ref, gain_ref, nma_ref, h1_ref, st_ref):
    x = x_ref[...].astype(F32)
    r = lax.rsqrt(jnp.mean(x * x, axis=-1, keepdims=True) + EPS)
    nma_ref[...] = (x * r * gain_ref[...]).astype(BF16)
    h1_ref[...] = x
    st_ref[...] = jnp.zeros_like(st_ref)


def forward_end(h1_ref, gain_m_ref, nmm_ref):
    h = h1_ref[...]
    r = lax.rsqrt(jnp.mean(h * h, axis=-1, keepdims=True) + EPS)
    nmm_ref[...] = (h * r * gain_m_ref[...]).astype(BF16)


def forward_group(
    g, length, nma_ref, wq_ref, wk_ref, wv_ref, fv_ref, cos_ref, sin_ref, wo_ref,
    q_ref, k_ref, v_ref, o_ref, st_ref, h1_ref, between=None,
):
    nm = nma_ref[...]
    cos, sin = cos_ref[...], sin_ref[...]
    q_ref[...] = turn(nn(nm, wq_ref[...]), cos, sin).astype(BF16)
    k_ref[...] = turn(nn(nm, wk_ref[...]), cos, sin).astype(BF16)
    v_ref[...] = (0.5 * nn(nm, wv_ref[...]) + 0.5 * fv_ref[...].astype(F32)).astype(BF16)
    tile = (SLOT, 128)
    lane = lanes(tile)
    row = lax.broadcasted_iota(jnp.int32, tile, 0)
    k_extra = jnp.where((lane == 0) & (row >= length), -1e30, 0.0).astype(BF16)
    q_extra = jnp.where(lane == 0, 1.0, 0.0).astype(BF16)
    ones = jnp.ones(tile, BF16)
    low_lane = lane < HD
    qlane = lanes((QB, 128))
    causal = lax.broadcasted_iota(jnp.int32, (QB, QB), 1) <= lax.broadcasted_iota(jnp.int32, (QB, QB), 0)
    for pair in range(GROUP // 2):
        if pair == 1 and between is not None:
            between()
        cols = pl.ds(pair * 128, 128)
        qp, kp, vp = q_ref[:, cols], k_ref[:, cols], v_ref[:, cols]
        q_ext = jnp.concatenate([qp, q_extra], axis=1)
        k_exts, v_exts = [], []
        for e in range(2):
            mine = low_lane if e == 0 else ~low_lane
            k_exts.append(jnp.concatenate([jnp.where(mine, kp, 0), k_extra], axis=1))
            v_exts.append(jnp.concatenate([jnp.where(mine, vp, 0), ones], axis=1))
        for qb in range(SLOT // QB):
            rows = slice(qb * QB, (qb + 1) * QB)
            top = (qb + 1) * QB
            out = None
            stats = st_ref[rows, :].astype(F32)
            for e in range(2):
                s = nt(q_ext[rows], k_exts[e][:top])
                diag = jnp.where(causal, s[:, top - QB :], -1e30)
                s = diag if qb == 0 else jnp.concatenate([s[:, : top - QB], diag], axis=1)
                m = jnp.max(s, axis=-1, keepdims=True)
                p = jnp.exp2((s - m) * C2).astype(BF16)
                res = nn(p, v_exts[e][:top])
                total = res[:, 128:]
                part = res[:, :128] / total
                out = part if out is None else out + part
                hi, mid, rest = low3(m + jnp.log2(total) * (1.0 / C2))
                base = 8 * (g * GROUP + pair * 2 + e)
                stats = jnp.where(qlane == base, hi, stats)
                stats = jnp.where(qlane == base + 1, mid, stats)
                stats = jnp.where(qlane == base + 2, rest, stats)
                stats = jnp.where(qlane == base + 3, 1.0, stats)
            o_ref[rows, cols] = out.astype(BF16)
            st_ref[rows, :] = stats.astype(BF16)
    h1_ref[...] += nn(o_ref[...], wo_ref[...])


def fwd_kernel(
    len_ref, x_ref, gain_ref, wq_ref, wk_ref, wv_ref, fv_ref, cos_ref, sin_ref, wo_ref, gain_m_ref,
    q_ref, k_ref, v_ref, o_ref, st_ref, nma_ref, h1_ref, nmm_ref,
):
    g = pl.program_id(0)

    @pl.when(g == 0)
    def _():
        forward_start(x_ref, gain_ref, nma_ref, h1_ref, st_ref)

    forward_group(
        g, len_ref[0], nma_ref, wq_ref, wk_ref, wv_ref, fv_ref, cos_ref, sin_ref, wo_ref,
        q_ref, k_ref, v_ref, o_ref, st_ref, h1_ref,
    )

    @pl.when(g == pl.num_programs(0) - 1)
    def _():
        forward_end(h1_ref, gain_m_ref, nmm_ref)


def attention_forward(length, x, gain, wq, wk, wv, fv, cos, sin, wo, gain_m):
    whole = lambda *_: (0, 0)
    col = lambda g, *_: (0, g)
    tok = x.shape[0]
    full = pl.BlockSpec((tok, D), whole)
    blk = pl.BlockSpec((tok, GW), col)
    wblk = pl.BlockSpec((D, GW), col)
    vec = pl.BlockSpec((1, D), whole)
    tab = pl.BlockSpec((tok, 128), whole)
    sds = jax.ShapeDtypeStruct
    return pl.pallas_call(
        fwd_kernel,
        grid_spec=pltpu.PrefetchScalarGridSpec(
            num_scalar_prefetch=1,
            grid=(H // GROUP,),
            in_specs=[full, vec, wblk, wblk, wblk, blk, tab, tab, pl.BlockSpec((GW, D), lambda g, *_: (g, 0)), vec],
            out_specs=[blk, blk, blk, blk, tab, full, full, full],
        ),
        out_shape=[sds((tok, D), BF16)] * 4 + [sds((tok, 128), BF16), sds((tok, D), BF16), sds((tok, D), F32), sds((tok, D), BF16)],
        compiler_params=pltpu.CompilerParams(vmem_limit_bytes=56 * MIB),
        cost_estimate=pl.CostEstimate(flops=30 * 10**9, bytes_accessed=40 * 10**6, transcendentals=10**7),
        name="attention_forward",
    )(length, x, gain, wq, wk, wv, fv, cos, sin, wo, gain_m)


def prep_kernel(*refs):
    count = len(refs) // 2
    for src, dst in zip(refs[:count], refs[count:]):
        dst[...] = src[...].T


def prepare(*arrays):
    vm = pl.BlockSpec(memory_space=pltpu.VMEM)
    tok = arrays[0].shape[0]
    return pl.pallas_call(
        prep_kernel,
        in_specs=[vm] * len(arrays),
        out_specs=[vm] * len(arrays),
        out_shape=[jax.ShapeDtypeStruct((D, tok), BF16)] * len(arrays),
        compiler_params=pltpu.CompilerParams(vmem_limit_bytes=30 * MIB),
        cost_estimate=pl.CostEstimate(flops=10**9, bytes_accessed=4 * len(arrays) * 10**6, transcendentals=0),
        name="prepare",
    )(*arrays)


def wout_kernel(ot_ref, da_ref, out_ref):
    out_ref[...] = nn(ot_ref[...], da_ref[...]).astype(BF16)


def wout_grad(ot, da):
    vm = pl.BlockSpec(memory_space=pltpu.VMEM)
    return pl.pallas_call(
        wout_kernel,
        in_specs=[vm] * 2,
        out_specs=vm,
        out_shape=jax.ShapeDtypeStruct((D, D), BF16),
        compiler_params=pltpu.CompilerParams(vmem_limit_bytes=30 * MIB),
        cost_estimate=pl.CostEstimate(flops=2 * 10**9, bytes_accessed=6 * 10**6, transcendentals=0),
        name="wout_grad",
    )(ot, da)


def backward_group(
    g, length, da_ref, wo_ref, q_ref, k_ref, v_ref, o_ref, st_ref, cos_ref, sin_ref, dq_ref, dk_ref, dv_ref, gf_ref, dq_acc, between=None
):
    do_all = nt(da_ref[...], wo_ref[...]).astype(BF16)
    prod = do_all.astype(F32) * o_ref[...].astype(F32)
    hi = prod.astype(BF16)
    lo = (prod - hi.astype(F32)).astype(BF16)
    sel_row = lax.broadcasted_iota(jnp.int32, (GW, 128), 0) // HD + g * GROUP
    sel_lane = lanes((GW, 128))
    pick = jnp.where((sel_lane // 8 == sel_row) & ((sel_lane & 7) >= 4) & ((sel_lane & 7) <= 5), 1.0, 0.0).astype(BF16)
    delta = nn(hi, pick) + nn(lo, pick)
    tile = (SLOT, 128)
    lane = lanes(tile)
    d_hi = delta.astype(BF16)
    d_ext = jnp.where((lane & 7) == 4, d_hi.astype(F32), delta - d_hi.astype(F32)).astype(BF16)
    row = lax.broadcasted_iota(jnp.int32, tile, 0)
    dead = row >= length
    low_lane = lane < HD
    st = st_ref[...]
    visible = lax.broadcasted_iota(jnp.int32, (QB, QB), 0) <= lax.broadcasted_iota(jnp.int32, (QB, QB), 1)
    dq_acc[...] = jnp.zeros_like(dq_acc)
    for pair in range(GROUP // 2):
        cols = pl.ds(pair * 128, 128)
        qp, kp, vp = q_ref[:, cols], k_ref[:, cols], v_ref[:, cols]
        dop = do_all[:, pair * 128 : pair * 128 + 128]
        q_ext = jnp.concatenate([qp, st], axis=1)
        do_ext = jnp.concatenate([dop, d_ext], axis=1)
        heads = []
        for e in range(2):
            mine = low_lane if e == 0 else ~low_lane
            at = lane - 8 * (g * GROUP + pair * 2 + e)
            k_x = jnp.where((at >= 0) & (at < 3), -1.0, jnp.where((at == 3) & dead, -1e30, 0.0)).astype(BF16)
            v_x = jnp.where((at >= 4) & (at < 6), -1.0, 0.0).astype(BF16)
            k_m = jnp.where(mine, kp, 0)
            heads.append((
                k_m,
                jnp.concatenate([k_m, k_x], axis=1),
                jnp.concatenate([jnp.where(mine, vp, 0), v_x], axis=1),
                jnp.where(mine, qp, 0),
                jnp.where(mine, dop, 0),
            ))
        for kb in range(SLOT // QB):
            if between is not None:
                between(pair, kb)
            rows = slice(kb * QB, (kb + 1) * QB)
            start = kb * QB
            dk = dv = None
            for k_m, k_ext, v_ext, q_m, do_m in heads:
                st_ = nt(k_ext[rows], q_ext[start:])
                dp = nt(v_ext[rows], do_ext[start:])
                p = jnp.exp2(st_ * C2)
                diag = jnp.where(visible, p[:, :QB], 0.0)
                p = diag if kb == SLOT // QB - 1 else jnp.concatenate([diag, p[:, QB:]], axis=1)
                ds = (p * dp).astype(BF16)
                p = p.astype(BF16)
                dv_e = nn(p, do_m[start:])
                dk_e = nn(ds, q_m[start:])
                dk = dk_e if dk is None else dk + dk_e
                dv = dv_e if dv is None else dv + dv_e
                dq_acc[start:, cols] += tn(ds, k_m[rows])
            dk = dk * SCALE
            cos, sin = cos_ref[rows, :], sin_ref[rows, :]
            dk_ref[rows, cols] = (dk * cos - partner(dk) * sin).astype(BF16)
            half = 0.5 * dv
            gf_ref[rows, cols] = half
            dv_ref[rows, cols] = half.astype(BF16)
    cos, sin = cos_ref[...], sin_ref[...]
    for pair in range(GROUP // 2):
        cols = pl.ds(pair * 128, 128)
        dq = dq_acc[:, cols] * SCALE
        dq_ref[:, cols] = (dq * cos - partner(dq) * sin).astype(BF16)


def bwd_kernel(
    first_group, len_ref, da_ref, wo_ref, q_ref, k_ref, v_ref, o_ref, st_ref, nmt_ref, cos_ref, sin_ref,
    dq_ref, dk_ref, dv_ref, gf_ref, gw_ref, dq_acc,
):
    g = pl.program_id(0) + first_group
    backward_group(
        g, len_ref[0], da_ref, wo_ref, q_ref, k_ref, v_ref, o_ref, st_ref, cos_ref, sin_ref, dq_ref, dk_ref, dv_ref, gf_ref, dq_acc
    )
    for j, ref in enumerate((dq_ref, dk_ref, dv_ref)):
        gw_ref[j] = nn(nmt_ref[...], ref[...]).astype(BF16)


def attention_backward(first_group, groups, length, da, wo, q, k, v, o, st, nmt, cos, sin):
    whole = lambda *_: (0, 0)
    tok = da.shape[0]
    full = pl.BlockSpec((tok, D), whole)
    blk_in = pl.BlockSpec((tok, GW), lambda g, *_: (0, g + first_group))
    blk = pl.BlockSpec((tok, GW), lambda g, *_: (0, g))
    tab = pl.BlockSpec((tok, 128), whole)
    sds = jax.ShapeDtypeStruct
    width = groups * GW
    return pl.pallas_call(
        functools.partial(bwd_kernel, first_group),
        grid_spec=pltpu.PrefetchScalarGridSpec(
            num_scalar_prefetch=1,
            grid=(groups,),
            in_specs=[full, pl.BlockSpec((GW, D), lambda g, *_: (g + first_group, 0)), blk_in, blk_in, blk_in, blk_in, tab, pl.BlockSpec((D, tok), whole), tab, tab],
            out_specs=[blk, blk, blk, blk, pl.BlockSpec((3, D, GW), lambda g, *_: (0, 0, g))],
            scratch_shapes=[pltpu.VMEM((tok, GW), F32)],
        ),
        out_shape=[sds((tok, width), BF16)] * 3 + [sds((tok, width), F32), sds((3, D, width), BF16)],
        compiler_params=pltpu.CompilerParams(vmem_limit_bytes=56 * MIB),
        cost_estimate=pl.CostEstimate(flops=10 * 10**9 * groups, bytes_accessed=10 * 10**6, transcendentals=groups * 3 * 10**6),
        name="attention_backward",
    )(length, da, wo, q, k, v, o, st, nmt, cos, sin)


def sig(v):
    return 1.0 / (1.0 + jnp.exp(-v))


def mlp_kernel(nc, nz, zs_ref, *refs):
    pieces = refs[: nc * nz]
    nmt_ref, dyt_ref, nm_ref, dy_ref, h_ref, dg_ref, du_ref = refs[nc * nz : nc * nz + 7]
    outs = refs[nc * nz + 7 :]
    fs = pieces[0].shape[1]
    dz = pieces[0].shape[2]
    starts = [pl.multiple_of(zs_ref[s] * dz, dz) for s in range(nz)]
    for c in range(nc):
        gate = up = dh = None
        for s in range(nz):
            w_ref = pieces[c * nz + s]
            at = pl.ds(starts[s], dz)
            nmt, dyt = nmt_ref[at, :], dyt_ref[at, :]
            parts = nn(w_ref[0], nmt), nn(w_ref[1], nmt), nn(w_ref[2], dyt)
            gate, up, dh = parts if gate is None else (gate + parts[0], up + parts[1], dh + parts[2])
        sg = sig(gate)
        silu = gate * sg
        rows = pl.ds(c * fs, fs)
        h = (silu * up).astype(BF16)
        dg = (dh * up * (sg * (1.0 + gate * (1.0 - sg)))).astype(BF16)
        du = (dh * silu).astype(BF16)
        h_ref[rows, :], dg_ref[rows, :], du_ref[rows, :] = h, dg, du
        for s in range(nz):
            at = pl.ds(starts[s], dz)
            nm, dy = nm_ref[:, at], dy_ref[:, at]
            outs[c][s, 0] = nn(dg, nm).astype(BF16)
            outs[c][s, 1] = nn(du, nm).astype(BF16)
            outs[c][s, 2] = nn(h, dy).astype(BF16)


def mlp_block(zs, pieces, nmt, dyt, nm, dy):
    nc, nz = len(pieces), len(pieces[0])
    _, fs, dz = pieces[0][0].shape
    tok = nm.shape[0]
    sds = jax.ShapeDtypeStruct
    vm = pl.BlockSpec(memory_space=pltpu.VMEM)
    return pl.pallas_call(
        functools.partial(mlp_kernel, nc, nz),
        in_specs=[pl.BlockSpec(memory_space=pltpu.SMEM)] + [vm] * (nc * nz + 4),
        out_specs=[vm] * (3 + nc),
        out_shape=[sds((nc * fs, tok), BF16)] * 3 + [sds((nz, 3, fs, dz), BF16)] * nc,
        compiler_params=pltpu.CompilerParams(vmem_limit_bytes=44 * MIB),
        cost_estimate=pl.CostEstimate(flops=12 * nc * fs * D * tok, bytes_accessed=15 * 10**6, transcendentals=nc * fs * tok),
        name="mlp_block",
    )(zs, *[p for c in pieces for p in c], nmt, dyt, nm, dy)


MESH = pl.DeviceIdType.MESH
RING = (0, 1, 3, 2)
STEPS = H // GROUP
TURNS = (0, 1, 3, 2)


def table(index, values):
    out = values[0]
    for i, v in enumerate(values[1:], 1):
        out = jnp.where(index == i, v, out)
    return out


def norm_back(v, gain, grad):
    ms = jnp.mean(v * v, axis=-1, keepdims=True) + EPS
    r = lax.rsqrt(ms)
    gg = grad * gain
    inner = jnp.mean(gg * v, axis=-1, keepdims=True)
    dv = r * gg - v * (inner * r * r * r)
    dgain = jnp.sum(grad * v * r, axis=0, keepdims=True)
    return dv, dgain


class Places:
    def __init__(self, nz):
        self.nz = nz
        self.r, self.a, self.z = (lax.axis_index(n) for n in ("rows", "ha", "ma"))
        self.spot = table(self.a, [RING.index(i) for i in range(4)])
        self.right_to = table(self.spot, [RING[(i + 1) % 4] for i in range(4)])
        self.left_to = table(self.spot, [RING[(i + 3) % 4] for i in range(4)])
        self.far_to = table(self.spot, [RING[(i + 2) % 4] for i in range(4)])
        self.arrivals = [0] + [table(self.z, v) for v in ((3, 1, 3, 1), (2, 3, 1, 2), (1, 2, 2, 3))]

    def at(self, **moved):
        place = {"rows": self.r, "ha": self.a, "ma": self.z, **moved}
        return (place["rows"], place["ha"], place["ma"])

    def meet(self, others):
        barrier = pltpu.get_barrier_semaphore()
        for other in others:
            pl.semaphore_signal(barrier, inc=1, device_id=other, device_id_type=MESH)
        return lambda: pl.semaphore_wait(barrier, len(others))


def remote(src, dst, send, recv, device):
    return pltpu.make_async_remote_copy(
        src_ref=src, dst_ref=dst, send_sem=send, recv_sem=recv, device_id=device, device_id_type=MESH
    )


class Gather:
    def __init__(self, places, own_ref, w_ref, sems):
        self.p, self.own, self.w = places, own_ref, w_ref
        self.recv, self.z_send, self.right_send, self.left_send, self.far_send, self.swap_send, self.local = sems

    def copy(self, src, dst, send, device):
        return remote(self.w.at[src], self.w.at[dst], send, self.recv.at[dst], device)

    def right(self, s):
        return self.copy((0, 0, s), (1, 0, s), self.right_send.at[s], self.p.at(ha=self.p.right_to))

    def left(self, s):
        return self.copy((0, 0, s), (3, 0, s), self.left_send.at[s], self.p.at(ha=self.p.left_to))

    def far_copy(self, i):
        s = self.p.arrivals[i]
        if i % 2 == 0:
            return self.copy((1, 0, s), (2, 0, s), self.far_send.at[s], self.p.at(ha=self.p.right_to))
        return self.copy((3, 0, s), (2, 0, s), self.far_send.at[s], self.p.at(ha=self.p.left_to))

    def swap(self, k, s):
        return self.copy((k, 0, s), (k, 1, s), self.swap_send.at[k, s], self.p.at(rows=1 - self.p.r))

    def arrived(self, k, s, c=0):
        self.copy((k, c, s), (k, c, s), self.local, self.p.at(rows=1 - self.p.r)).wait_recv()

    def line(self, d, act, wait):
        nz, z = self.p.nz, self.p.z

        def up(cond):
            pl.when(cond & (z < nz - 1))(
                lambda: act(self.copy((0, 0, d), (0, 0, d + 1), self.z_send.at[0, d], self.p.at(ma=z + 1)))
            )

        def down(cond):
            pl.when(cond & (z >= 1))(
                lambda: act(self.copy((0, 0, (nz - d) % nz), (0, 0, nz - d - 1), self.z_send.at[1, d], self.p.at(ma=z - 1)))
            )

        if d and wait:
            pl.when(z >= d)(lambda: self.arrived(0, d))
            pl.when(z + d <= nz - 1)(lambda: self.arrived(0, nz - d))
        if d < nz - 1:
            up(z >= d)
            down(z + d <= nz - 1)

    def begin(self):
        p = self.p
        wait = p.meet([
            p.at(ma=(p.z + 1) % p.nz), p.at(ma=(p.z + p.nz - 1) % p.nz), p.at(ha=p.right_to), p.at(ha=p.left_to), p.at(rows=1 - p.r)
        ])
        mine = pltpu.make_async_copy(self.own, self.w.at[0, 0, 0], self.local)
        mine.start()
        mine.wait()
        wait()
        self.pass_line(0)
        self.spread(0)

    def pass_line(self, d):
        self.line(d, lambda c: c.start(), True)

    def spread(self, i):
        s = self.p.arrivals[i]
        self.right(s).start()
        self.left(s).start()
        self.swap(0, s).start()

    def sides(self, i):
        s = self.p.arrivals[i]
        self.arrived(1, s)
        self.arrived(3, s)
        self.swap(1, s).start()
        self.swap(3, s).start()

    def far(self, i):
        self.far_copy(i).start()

    def opposite(self, i):
        s = self.p.arrivals[i]
        self.arrived(2, s)
        self.swap(2, s).start()

    def end(self):
        for i in range(self.p.nz):
            s = self.p.arrivals[i]
            self.line(i, lambda c: c.wait_send(), False)
            self.right(s).wait_send()
            self.left(s).wait_send()
            self.far_copy(i).wait_send()
            for k in range(4):
                self.swap(k, s).wait_send()


def first_kernel(
    nz, len_ref, x_ref, gain_ref, wq_ref, wk_ref, wv_ref, fv_ref, cos_ref, sin_ref, wo_ref, gain_m_ref, dy_ref, own_ref,
    q_ref, k_ref, v_ref, o_ref, st_ref, nma_ref, mixed_ref, dh1_ref, da_ref, dgain_ref, mine_ref, got_ref, w_ref,
    h1_ref, branch_ref, nmm_ref, nmmt_ref, dyt_ref, wbuf, gbuf, wsem, gsem, gsend, grecv, *sems,
):
    g = pl.program_id(0)
    places = Places(nz)
    gather = Gather(places, own_ref, w_ref, sems)
    fs, dz = own_ref.shape[1:]

    @pl.when(g == 0)
    def _():
        gather.begin()
        forward_start(x_ref, gain_ref, nma_ref, h1_ref, st_ref)

    def between():
        @pl.when(g == 1)
        def _():
            gather.pass_line(1)
            gather.spread(1)

    @pl.when(g < STEPS)
    def _():
        forward_group(
            g, len_ref[0], nma_ref, wq_ref, wk_ref, wv_ref, fv_ref, cos_ref, sin_ref, wo_ref,
            q_ref, k_ref, v_ref, o_ref, st_ref, h1_ref, between,
        )

    @pl.when(g == 2)
    def _():
        gather.pass_line(2)
        gather.spread(2)
        gather.sides(0)

    def load(k, c, slot):
        return pltpu.make_async_copy(w_ref.at[k, c], wbuf.at[slot], wsem.at[slot])

    def fetch(k, c, slot):
        for s in range(nz):
            if c == 1:
                gather.arrived(k, s, 1)
        load(k, c, slot).start()

    def keep(k):
        return pltpu.make_async_copy(gbuf.at[0], mine_ref.at[k], gsem)

    def push(k):
        return remote(gbuf.at[1], got_ref.at[k], gsend, grecv.at[k], places.at(rows=1 - places.r))

    @pl.when(g == STEPS - 1)
    def _():
        gather.pass_line(3)
        gather.spread(3)
        gather.sides(1)
        gather.far(0)
        gather.far(1)
        forward_end(h1_ref, gain_m_ref, nmm_ref)
        fetch(0, 0, 0)
        nmmt_ref[...] = nmm_ref[...].T
        dyt_ref[...] = dy_ref[...].T
        branch_ref[...] = jnp.zeros_like(branch_ref)
        dh1_ref[...] = jnp.zeros_like(dh1_ref)

    starts = [pl.multiple_of((places.z + nz - s) % nz * dz, dz) for s in range(nz)]

    @pl.when(g >= STEPS)
    def _():
        turn_at = g - STEPS
        k = table(turn_at, TURNS)
        before = table(turn_at, TURNS[:1] + TURNS[:-1])
        following = table(turn_at, TURNS[1:] + TURNS[-1:])
        for c in range(2):
            load(k, c, c).wait()
            gate = up = dh = None
            for s in range(nz):
                at = pl.ds(starts[s], dz)
                nmt, dyt = nmmt_ref[at, :], dyt_ref[at, :]
                parts = nn(wbuf[c, s, 0], nmt), nn(wbuf[c, s, 1], nmt), nn(wbuf[c, s, 2], dyt)
                gate, up, dh = parts if gate is None else (gate + parts[0], up + parts[1], dh + parts[2])
            sg = sig(gate)
            silu = gate * sg
            h = (silu * up).astype(BF16)
            dg = (dh * up * (sg * (1.0 + gate * (1.0 - sg)))).astype(BF16)
            du = (dh * silu).astype(BF16)
            if c == 0:
                @pl.when(turn_at == 0)
                def _():
                    gather.sides(2)

                fetch(k, 1, 1)
            else:
                @pl.when(turn_at == 0)
                def _():
                    gather.sides(3)
                    gather.far(2)
                    gather.far(3)
                    gather.opposite(0)

                @pl.when(turn_at == 1)
                def _():
                    gather.opposite(1)
                    gather.opposite(2)
                    gather.opposite(3)

            @pl.when(turn_at > 0)
            def _():
                if c == 0:
                    keep(before).wait()
                else:
                    push(before).wait_send()

            for s in range(nz):
                at = pl.ds(starts[s], dz)
                nm, dy = nmm_ref[:, at], dy_ref[:, at]
                gbuf[c, s, 0] = nn(dg, nm).astype(BF16)
                gbuf[c, s, 1] = nn(du, nm).astype(BF16)
                gbuf[c, s, 2] = nn(h, dy).astype(BF16)
            if c == 0:
                keep(k).start()
            else:
                push(k).start()
            for s in range(nz):
                at = pl.ds(starts[s], dz)
                branch_ref[:, at] += tn(h, wbuf[c, s, 2])
                dh1_ref[:, at] += tn(dg, wbuf[c, s, 0]) + tn(du, wbuf[c, s, 1])
            if c == 1:
                @pl.when(turn_at < len(TURNS) - 1)
                def _():
                    fetch(following, 0, 0)

    @pl.when(g == pl.num_programs(0) - 1)
    def _():
        total = jnp.zeros(dgain_ref.shape, F32)
        for at in range(0, SLOT, QB):
            rows = slice(at, at + QB)
            h1 = h1_ref[rows, :]
            mixed_ref[rows, :] = (h1 + branch_ref[rows, :]).astype(BF16)
            dv, dgain = norm_back(h1, gain_m_ref[...], dh1_ref[rows, :])
            dh1 = dy_ref[rows, :].astype(F32) + dv
            dh1_ref[rows, :] = dh1
            da_ref[rows, :] = dh1.astype(BF16)
            total = total + dgain
        dgain_ref[...] = total
        last = TURNS[-1]
        keep(last).wait()
        push(last).wait_send()
        for k in range(4):
            push(k).wait_recv()
        gather.end()


def first_half(length, x, gain, wq, wk, wv, fv, cos, sin, wo, gain_m, dy, own, nz):
    tok = x.shape[0]
    fs, dz = own.shape[1:]
    sds = jax.ShapeDtypeStruct
    once = dict(pipeline_mode=pl.Buffered(1))
    step = lambda g: jnp.minimum(g, STEPS - 1)
    full = pl.BlockSpec((tok, D), lambda g: (0, 0), **once)
    blk = pl.BlockSpec((tok, GW), lambda g: (0, step(g)))
    wblk = pl.BlockSpec((D, GW), lambda g: (0, step(g)))
    vec = pl.BlockSpec((1, D), lambda g: (0, 0), **once)
    tab = pl.BlockSpec((tok, 128), lambda g: (0, 0), **once)
    hbm = pl.BlockSpec(memory_space=pl.ANY)
    sem = pltpu.SemaphoreType.DMA
    return pl.pallas_call(
        functools.partial(first_kernel, nz),
        grid=(STEPS + len(TURNS),),
        in_specs=[
            pl.BlockSpec(memory_space=pltpu.SMEM), full, vec, wblk, wblk, wblk, blk, tab, tab,
            pl.BlockSpec((GW, D), lambda g: (step(g), 0)), vec, full, hbm,
        ],
        out_specs=[blk, blk, blk, blk, tab, full, full, full, full, vec, hbm, hbm, hbm],
        out_shape=[sds((tok, D), BF16)] * 4
        + [sds((tok, 128), BF16), sds((tok, D), BF16), sds((tok, D), BF16), sds((tok, D), F32), sds((tok, D), BF16), sds((1, D), F32)]
        + [sds((4, nz, 3, fs, dz), BF16)] * 2
        + [sds((4, 2, nz, 3, fs, dz), BF16)],
        scratch_shapes=[
            pltpu.VMEM((tok, D), F32), pltpu.VMEM((tok, D), F32),
            pltpu.VMEM((tok, D), BF16), pltpu.VMEM((D, tok), BF16), pltpu.VMEM((D, tok), BF16),
            pltpu.VMEM((2, nz, 3, fs, dz), BF16), pltpu.VMEM((2, nz, 3, fs, dz), BF16), sem((2,)), sem, sem, sem((4,)),
            sem((4, 2, nz)), sem((2, nz)), sem((nz,)), sem((nz,)), sem((nz,)), sem((4, nz)), sem,
        ],
        compiler_params=pltpu.CompilerParams(vmem_limit_bytes=63 * MIB, collective_id=1, has_side_effects=True),
        cost_estimate=pl.CostEstimate(flops=84 * 10**9, bytes_accessed=80 * 10**6, transcendentals=10**7),
        name="first_half",
    )(length, x, gain, wq, wk, wv, fv, cos, sin, wo, gain_m, dy, own)


MOVES = {
    (0, 0, 0): [("pass", 2, 1), ("pass", 2, 2)],
    (0, 0, 3): [(4, 1)],
    (0, 1, 0): [("pass", 1, 2), ("pass", 3, 1)],
    (0, 1, 3): [(4, 2)],
    (0, 2, 0): [(0, 0)],
    (1, 0, 0): [("pass", 1, 1), ("pass", 3, 2)],
    (1, 0, 2): [(4, 3), (0, 1)],
    (1, 1, 0): [("pass", 2, 3), ("pass", 2, 0)],
    (1, 1, 2): [(4, 4), (0, 2)],
    (1, 2, 0): [(1, 0), (4, 5)],
    (2, 0, 0): [("pass", 1, 0), ("pass", 3, 3)],
    (2, 0, 2): [(0, 3), (1, 1), (4, 6)],
    (2, 1, 0): [("total", 1), ("total", 2)],
    (2, 1, 2): [(0, 4), (1, 2), (4, 7)],
    (2, 2, 0): [(2, 0), (0, 5)],
    (3, 0, 0): [("pass", 1, 3), ("pass", 3, 0)],
    (3, 0, 2): [(1, 3), (2, 1), (0, 6)],
    (3, 1, 0): [(1, 4), (2, 2), (0, 7)],
    (3, 1, 2): [(1, 5), (2, 3)],
    (3, 2, 0): [(3, 0)],
}
TAIL = [
    [(2, 4), (1, 6), ("total", 3), ("total", 0)],
    [(3, 1), (2, 5), (1, 7)],
    [(3, 2), (2, 6)],
    [(3, 3), (2, 7)],
]
SEQUENCE = [what for at in sorted(MOVES) for what in MOVES[at]] + [what for moves in TAIL for what in moves]


class Reduce:
    BY_LEFT = (1, 3)
    def __init__(self, places, mine_ref, got_ref, tiles_ref, bufs, sems):
        self.p, self.mine, self.got, self.tiles = places, mine_ref, got_ref, tiles_ref
        self.inb, self.pool, self.tot, self.far_in, self.b1_in, self.b3_in, self.z_in = bufs
        self.load_sem, self.send, self.z_send, self.far_recv, self.b1_recv, self.b3_recv, self.z_recv, self.out_sem, self.swap_send, self.swap_recv = sems
        self.order = [w[1:] if w[0] == "pass" else (0, w[1]) for w in SEQUENCE if w[0] in ("pass", "total")]
        self.sent = [w for w in self.order if w[0]]

    def loads(self, i):
        k, s = self.order[i]
        slot = i % 2
        return [
            pltpu.make_async_copy(src.at[k, s], self.inb.at[slot, j], self.load_sem.at[slot, j])
            for j, src in enumerate((self.mine, self.got))
        ]

    def begin(self):
        for i in range(2):
            for c in self.loads(i):
                c.start()

    def sum_of(self, k, s, out, extra):
        i = self.order.index((k, s))
        for c in self.loads(i):
            c.wait()
        for j in range(3):
            total = self.inb[i % 2, 0, j].astype(F32) + self.inb[i % 2, 1, j].astype(F32)
            for e in extra:
                total = total + e[s, j].astype(F32)
            out[j] = total.astype(BF16)
        if i + 2 < len(self.order):
            for c in self.loads(i + 2):
                c.start()

    def sender(self, n, k, s):
        slot = n % self.pool.shape[0]
        if k == 2:
            dst, sem, left = self.far_in, self.far_recv, s in self.BY_LEFT
        elif k == 1:
            dst, sem, left = self.b1_in, self.b1_recv, True
        else:
            dst, sem, left = self.b3_in, self.b3_recv, False
        to = self.p.at(ha=self.p.left_to if left else self.p.right_to)
        return remote(self.pool.at[slot], dst.at[s], self.send.at[slot], sem.at[s], to)

    def got_in(self, which, s):
        ref, sem = {2: (self.far_in, self.far_recv), 1: (self.b1_in, self.b1_recv), 3: (self.b3_in, self.b3_recv)}[which]
        remote(ref.at[s], ref.at[s], self.out_sem, sem.at[s], self.p.at(ha=self.p.right_to)).wait_recv()

    def pass_on(self, k, s):
        n = self.sent.index((k, s))
        size = self.pool.shape[0]
        if n >= size:
            self.sender(n - size, *self.sent[n - size]).wait_send()
        relayed = k != 2 and ((s in self.BY_LEFT) == (k == 1))
        if relayed:
            self.got_in(2, s)
        self.sum_of(k, s, self.pool.at[n % size], [self.far_in] if relayed else [])
        self.sender(n, k, s).start()

    def to_owner(self, s):
        nz, z = self.p.nz, self.p.z
        return remote(self.tot.at[s], self.z_in.at[s], self.z_send.at[s], self.z_recv.at[s], self.p.at(ma=(z + nz - s) % nz))

    def total(self, s):
        self.got_in(1, s)
        self.got_in(3, s)
        self.sum_of(0, s, self.tot.at[s], [self.b1_in, self.b3_in])
        if s:
            self.to_owner(s).start()

    def last_copies(self):
        p = self.p
        return (
            pltpu.make_async_copy(self.tot.at[0], self.tiles.at[p.r], self.out_sem),
            remote(self.tot.at[0], self.tiles.at[p.r], self.swap_send, self.swap_recv, p.at(rows=1 - p.r)),
        )

    def finish(self):
        nz = self.p.nz
        for s in range(1, nz):
            self.to_owner(s).wait_recv()
        for j in range(3):
            total = self.tot[0, j].astype(F32)
            for s in range(1, nz):
                total = total + self.z_in[s, j].astype(F32)
            self.tot[0, j] = total.astype(BF16)
        for c in self.last_copies():
            c.start()

    def end(self):
        for c in self.last_copies():
            c.wait()
        for n in range(max(0, len(self.sent) - self.pool.shape[0]), len(self.sent)):
            self.sender(n, *self.sent[n]).wait_send()
        for s in range(1, self.p.nz):
            self.to_owner(s).wait_send()


class Spread:
    def __init__(self, places, m, x, far, r1, r3, zin, piece, y, send, recv, local):
        self.p, self.m, self.x, self.far, self.r1, self.r3, self.zin, self.piece, self.y = places, m, x, far, r1, r3, zin, piece, y
        self.send, self.recv, self.local = send, recv, local
        self.half = D // 2
        self.block = self.half // 4
        self.small = self.block // places.nz

    def own_half(self):
        return pl.multiple_of(self.p.r * self.half, self.half)

    def place_of(self, k):
        return (self.p.a, self.p.left_to, self.p.far_to, self.p.right_to)[k]

    def in_x(self, k, at=0, size=None):
        return pl.ds(pl.multiple_of(self.place_of(k) * self.block + at, self.small), size or self.block)

    def rows(self, k, at=0, size=None):
        return pl.ds(pl.multiple_of(self.p.r * self.half + self.place_of(k) * self.block + at, self.small), size or self.block)

    def small_rows(self, z):
        return pl.ds(pl.multiple_of(self.p.r * self.half + self.p.a * self.block + z * self.small, self.small), self.small)

    def copy(self, n, src, dst, device):
        return remote(src, dst, self.send.at[n], self.recv.at[n], device)

    def left(self):
        return self.p.at(ha=self.p.left_to)

    def right(self):
        return self.p.at(ha=self.p.right_to)

    def sibling(self):
        return self.p.at(rows=1 - self.p.r)

    def copies(self, stage):
        p, m, y = self.p, self.m, self.y
        h = self.block // 2
        if stage == 0:
            other = pl.ds(pl.multiple_of((1 - p.r) * self.half, self.half), self.half)
            return [(0, m.at[:, other], self.x, self.sibling())]
        if stage == 1:
            return [
                (1, m.at[:, self.rows(2, 0, h)], self.far.at[:, pl.ds(0, h)], self.left()),
                (2, m.at[:, self.rows(2, h, h)], self.far.at[:, pl.ds(h, h)], self.right()),
            ]
        if stage == 2:
            return [(3, m.at[:, self.rows(1)], self.r1, self.left()), (4, m.at[:, self.rows(3)], self.r3, self.right())]
        if stage == 3:
            return [
                (4 + s, m.at[:, self.small_rows((p.z + p.nz - s) % p.nz)], self.zin.at[s], p.at(ma=(p.z + p.nz - s) % p.nz))
                for s in range(1, p.nz)
            ]
        if stage == 4:
            at = self.small_rows(p.z)
            return [(7 + s, self.piece, y.at[:, at], p.at(ma=(p.z + s) % p.nz)) for s in range(1, p.nz)]
        if stage == 5:
            at = self.rows(0)
            return [(n, y.at[:, at], y.at[:, at], to) for n, to in ((11, self.right()), (12, self.left()), (13, self.sibling()))]
        if stage == 6:
            first, second = self.rows(1, 0, h), self.rows(3, h, h)
            return [(14, y.at[:, first], y.at[:, first], self.right()), (15, y.at[:, second], y.at[:, second], self.left())] + [
                (n, y.at[:, self.rows(k)], y.at[:, self.rows(k)], self.sibling()) for n, k in ((16, 1), (17, 3))
            ]
        return [(18, y.at[:, self.rows(2)], y.at[:, self.rows(2)], self.sibling())]

    def keep(self):
        return pltpu.make_async_copy(self.piece, self.y.at[:, self.small_rows(self.p.z)], self.local)

    def wait_for(self, stage, which=None):
        copies = self.copies(stage)
        for i in which if which is not None else range(len(copies)):
            self.copy(*copies[i]).wait_recv()

    def add(self, at, *others):
        for j in range(self.m.shape[0]):
            total = self.m[j, at, :].astype(F32)
            for ref, place in others:
                total = total + ref[j, place, :].astype(F32)
            self.m[j, at, :] = total.astype(BF16)

    def run(self, stage):
        p = self.p
        h = self.block // 2
        if stage == 1:
            self.wait_for(0)
            self.add(self.rows(2), (self.x, self.in_x(2)))
        elif stage == 2:
            self.wait_for(1)
            self.add(self.rows(1, 0, h), (self.x, self.in_x(1, 0, h)), (self.far, pl.ds(0, h)))
            self.add(self.rows(1, h, h), (self.x, self.in_x(1, h, h)))
            self.add(self.rows(3, 0, h), (self.x, self.in_x(3, 0, h)))
            self.add(self.rows(3, h, h), (self.x, self.in_x(3, h, h)), (self.far, pl.ds(h, h)))
        elif stage == 3:
            self.wait_for(2)
            whole = pl.ds(0, self.block)
            self.add(self.rows(0), (self.x, self.in_x(0)), (self.r1, whole), (self.r3, whole))
        elif stage == 4:
            self.wait_for(3)
            for j in range(self.m.shape[0]):
                total = self.m[j, self.small_rows(p.z), :].astype(F32)
                for s in range(1, p.nz):
                    total = total + self.zin[s, j].astype(F32)
                self.piece[j] = total.astype(BF16)
            self.keep().start()
        elif stage == 5:
            self.wait_for(4)
            self.keep().wait()
        elif stage == 6:
            self.wait_for(5, (0, 1))
        elif stage == 7:
            self.wait_for(6, (0, 1))
        for c in self.copies(stage):
            self.copy(*c).start()

    def end(self):
        self.wait_for(5, (2,))
        self.wait_for(6, (2, 3))
        self.wait_for(7)
        for stage in range(8):
            for c in self.copies(stage):
                self.copy(*c).wait_send()


class Gains:
    def __init__(self, places, own, twin, ring, line, send, recv):
        self.p, self.own, self.twin, self.ring, self.line, self.send, self.recv = places, own, twin, ring, line, send, recv

    def to_twin(self):
        return [remote(self.own, self.twin, self.send.at[0], self.recv.at[0], self.p.at(rows=1 - self.p.r))]

    def round_ring(self):
        p, at = self.p, self.ring.at[self.p.a]
        return [remote(at, at, self.send.at[i], self.recv.at[i], p.at(ha=to)) for i, to in ((1, p.right_to), (2, p.left_to), (3, p.far_to))]

    def along_line(self):
        p, at = self.p, self.line.at[self.p.z]
        return [remote(at, at, self.send.at[3 + s], self.recv.at[3 + s], p.at(ma=(p.z + s) % p.nz)) for s in range(1, p.nz)]

    def run(self, stage):
        if stage == 0:
            sends = self.to_twin()
        elif stage == 1:
            for c in self.to_twin():
                c.wait_recv()
            self.ring[pl.ds(self.p.a, 1)] = (self.own[...] + self.twin[...])[None]
            sends = self.round_ring()
        else:
            for c in self.round_ring():
                c.wait_recv()
            self.line[pl.ds(self.p.z, 1)] = (self.ring[0] + self.ring[1] + self.ring[2] + self.ring[3])[None]
            sends = self.along_line()
        for c in sends:
            c.start()

    def end(self, out_ref):
        for c in self.along_line():
            c.wait_recv()
        total = self.line[0]
        for s in range(1, self.p.nz):
            total = total + self.line[s]
        out_ref[...] = total
        for c in self.to_twin() + self.round_ring() + self.along_line():
            c.wait_send()


def second_kernel(
    nz, len_ref, da_ref, wo_ref, q_ref, k_ref, v_ref, o_ref, st_ref, nmt_ref, cos_ref, sin_ref, wq_ref, wk_ref, wv_ref,
    gain_ref, dgm_ref, x_ref, dh1_ref, gwo_ref, mine_ref, got_ref,
    gt_ref, gf_ref, gains_ref, ywo_ref, y_ref, tiles_ref,
    dq_acc, dq_ref, dk_ref, dv_ref, xbuf, hbuf, tile_sem,
    mo, xo, faro, r1o, r3o, zo, po, mg, xg, farg, r1g, r3g, zg, pg,
    inb, pool, tot, far_in, b1_in, b3_in, z_in, gown, gtwin, gring, gline,
    ar_send, ar_recv, ar_local, g_send, g_recv, *rs_sems,
):
    g = pl.program_id(0)
    p = Places(nz)
    reduce = Reduce(p, mine_ref, got_ref, tiles_ref, (inb, pool, tot, far_in, b1_in, b3_in, z_in), rs_sems)
    sets = mg.shape[0]
    width = mg.shape[3]
    chunks = [
        Spread(
            p, *(v.at[i % sets] for v in (mg, xg, farg, r1g, r3g, zg, pg)), y_ref.at[:, :, pl.ds(i * width, width)],
            ar_send.at[i], ar_recv.at[i], ar_local.at[i],
        )
        for i in range(STEPS)
    ]
    chunks.append(Spread(p, mo, xo, faro, r1o, r3o, zo, po, ywo_ref, ar_send.at[STEPS], ar_recv.at[STEPS], ar_local.at[STEPS]))
    gains = Gains(p, gown, gtwin, gring, gline, g_send, g_recv)

    def move(what):
        if what[0] == "pass":
            reduce.pass_on(*what[1:])
        elif what[0] == "total":
            reduce.total(what[1])
        else:
            chunks[what[0]].run(what[1])

    def between(pair, kb):
        for at in range(STEPS):
            moves = MOVES.get((at, pair, kb))
            if moves:
                @pl.when(g == at)
                def _():
                    for what in moves:
                        move(what)

    @pl.when(g == 0)
    def _():
        wait = p.meet(
            [p.at(ma=(p.z + s) % nz) for s in range(1, nz)] + [p.at(ha=to) for to in (p.right_to, p.left_to, p.far_to)] + [p.at(rows=1 - p.r)]
        )
        reduce.begin()
        load = pltpu.make_async_copy(gwo_ref, mo, ar_local.at[STEPS])
        load.start()
        gt_ref[...] = jnp.zeros_like(gt_ref)
        load.wait()
        wait()
        chunks[STEPS].run(0)

    backward_group(
        g, len_ref[0], da_ref, wo_ref, q_ref, k_ref, v_ref, o_ref, st_ref, cos_ref, sin_ref,
        dq_ref, dk_ref, dv_ref, gf_ref, dq_acc, between,
    )
    for i in range(sets, STEPS):
        @pl.when(g == i)
        def _():
            chunks[i - sets].end()

    for j, ref in enumerate((dq_ref, dk_ref, dv_ref)):
        mg[g % sets, j] = nn(nmt_ref[...], ref[...]).astype(BF16)

    between(2, 0)
    gt_ref[...] += nt(dq_ref[...], wq_ref[...]) + nt(dk_ref[...], wk_ref[...]) + nt(dv_ref[...], wv_ref[...])

    @pl.when(g == STEPS - 1)
    def _():
        def loads(i):
            rows = pl.ds(i * QB, QB)
            return [
                pltpu.make_async_copy(src.at[rows], buf.at[i % 2], tile_sem.at[i % 2, j])
                for j, (src, buf) in enumerate(((x_ref, xbuf), (dh1_ref, hbuf)))
            ]

        tiles = SLOT // QB
        for c in loads(0):
            c.start()
        total = jnp.zeros(gain_ref.shape, F32)
        for i in range(tiles):
            if i + 1 < tiles:
                for c in loads(i + 1):
                    c.start()
            for what in TAIL[i]:
                move(what)
            for c in loads(i):
                c.wait()
            rows = slice(i * QB, (i + 1) * QB)
            dv, dgain = norm_back(xbuf[i % 2].astype(F32), gain_ref[...], gt_ref[rows, :])
            gt_ref[rows, :] = hbuf[i % 2] + dv
            total = total + dgain
        gown[...] = jnp.concatenate([total, dgm_ref[...], jnp.zeros((6, D), F32)], axis=0)
        gains.run(0)
        move((3, 4))
        gains.run(1)
        move((3, 5))
        gains.run(2)
        reduce.finish()
        move((3, 6))
        move((3, 7))
        gains.end(gains_ref)
        for i in [STEPS] + list(range(max(0, STEPS - sets), STEPS)):
            chunks[i].end()
        reduce.end()


def second_half(length, da, wo, q, k, v, o, st, nmt, cos, sin, wq, wk, wv, gain, dgm, x, dh1, gwo, mine, got):
    tok = x.shape[0]
    _, nz, _, fs, dz = mine.shape
    sds = jax.ShapeDtypeStruct
    once = dict(pipeline_mode=pl.Buffered(1))
    full = pl.BlockSpec((tok, D), lambda g: (0, 0), **once)
    blk = pl.BlockSpec((tok, GW), lambda g: (0, g))
    wblk = pl.BlockSpec((D, GW), lambda g: (0, g))
    vec = pl.BlockSpec((1, D), lambda g: (0, 0), **once)
    tab = pl.BlockSpec((tok, 128), lambda g: (0, 0), **once)
    hbm = pl.BlockSpec(memory_space=pl.ANY)
    sem = pltpu.SemaphoreType.DMA
    vmem = lambda *shape: pltpu.VMEM(shape, BF16)
    half = D // 2
    block = half // 4
    small = block // nz
    sets = 3
    piece = (3, fs, dz)

    def buffers(n, lead, width):
        return [
            vmem(*n, lead, D, width), vmem(*n, lead, half, width), vmem(*n, lead, block, width), vmem(*n, lead, block, width),
            vmem(*n, lead, block, width), vmem(*n, nz, lead, small, width), vmem(*n, lead, small, width),
        ]

    return pl.pallas_call(
        functools.partial(second_kernel, nz),
        grid=(STEPS,),
        in_specs=[
            pl.BlockSpec(memory_space=pltpu.SMEM), full, pl.BlockSpec((GW, D), lambda g: (g, 0)), blk, blk, blk, blk, tab, full,
            tab, tab, wblk, wblk, wblk, vec, vec, hbm, hbm, hbm, hbm, hbm,
        ],
        out_specs=[full, blk, pl.BlockSpec((8, D), lambda g: (0, 0), **once), hbm, hbm, hbm],
        out_shape=[
            sds((tok, D), F32), sds((tok, D), F32), sds((8, D), F32), sds((1, D, D), BF16), sds((3, D, D), BF16), sds((2, *piece), BF16),
        ],
        scratch_shapes=[
            pltpu.VMEM((tok, GW), F32), vmem(tok, GW), vmem(tok, GW), vmem(tok, GW), vmem(2, QB, D), pltpu.VMEM((2, QB, D), F32), sem((2, 2)),
            *buffers((), 1, D), *buffers((sets,), 3, GW),
            vmem(2, 2, *piece), vmem(5, *piece), vmem(nz, *piece), vmem(nz, *piece), vmem(nz, *piece), vmem(nz, *piece), vmem(nz, *piece),
            pltpu.VMEM((8, D), F32), pltpu.VMEM((8, D), F32), pltpu.VMEM((4, 8, D), F32), pltpu.VMEM((nz, 8, D), F32),
            sem((STEPS + 1, 19)), sem((STEPS + 1, 19)), sem((STEPS + 1,)), sem((3 + nz,)), sem((3 + nz,)),
            sem((2, 2)), sem((5,)), sem((nz,)), sem((nz,)), sem((nz,)), sem((nz,)), sem((nz,)), sem, sem, sem,
        ],
        compiler_params=pltpu.CompilerParams(vmem_limit_bytes=63 * MIB, collective_id=2, has_side_effects=True),
        cost_estimate=pl.CostEstimate(flops=50 * 10**9, bytes_accessed=80 * 10**6, transcendentals=10**7),
        name="second_half",
    )(length, da, wo, q, k, v, o, st, nmt, cos, sin, wq, wk, wv, gain, dgm, x, dh1, gwo, mine, got)


def mlp_out_kernel(nk, nc, nz, zs_ref, w_ref, hs_ref, dgs_ref, dus_ref, h1_ref, gain_ref, dy_ref, mixed_ref, dh1_ref, da_ref, dgain_ref, branch_ref, dnm_ref):
    fs, dz = w_ref.shape[4:]
    i = pl.program_id(0)
    for s in range(nz):
        b = d = None
        for k in range(nk):
            for c in range(nc):
                rows = pl.ds(c * fs, fs)
                b_one = tn(hs_ref[k, rows, :], w_ref[k, c, s, 2])
                d_one = tn(dgs_ref[k, rows, :], w_ref[k, c, s, 0]) + tn(dus_ref[k, rows, :], w_ref[k, c, s, 1])
                b, d = (b_one, d_one) if b is None else (b + b_one, d + d_one)
        at = pl.ds(pl.multiple_of(zs_ref[s] * dz, dz), dz)
        branch_ref[:, at] = b
        dnm_ref[:, at] = d
    h1 = h1_ref[...]
    mixed_ref[...] = (h1 + branch_ref[...]).astype(BF16)
    dv, dgain = norm_back(h1, gain_ref[...], dnm_ref[...])
    dh1 = dy_ref[...].astype(F32) + dv
    dh1_ref[...] = dh1
    da_ref[...] = dh1.astype(BF16)

    @pl.when(i == 0)
    def _():
        dgain_ref[...] = jnp.zeros_like(dgain_ref)

    dgain_ref[...] += dgain


def mlp_out(zs, w, hs, dgs, dus, h1, gain, dy):
    nk, nc, nz = w.shape[:3]
    tok = h1.shape[0]
    tile = 256
    wspec = pl.BlockSpec(w.shape, lambda i: (0,) * 6, pipeline_mode=pl.Buffered(1))
    hspec = pl.BlockSpec((nk, hs.shape[1], tile), lambda i: (0, 0, i))
    row = pl.BlockSpec((tile, D), lambda i: (i, 0))
    vec = pl.BlockSpec((1, D), lambda i: (0, 0))
    sds = jax.ShapeDtypeStruct
    return pl.pallas_call(
        functools.partial(mlp_out_kernel, nk, nc, nz),
        grid=(tok // tile,),
        in_specs=[pl.BlockSpec(memory_space=pltpu.SMEM), wspec, hspec, hspec, hspec, row, vec, row],
        out_specs=[row, row, row, vec],
        out_shape=[sds((tok, D), BF16), sds((tok, D), F32), sds((tok, D), BF16), sds((1, D), F32)],
        scratch_shapes=[pltpu.VMEM((tile, D), F32)] * 2,
        compiler_params=pltpu.CompilerParams(vmem_limit_bytes=58 * MIB),
        cost_estimate=pl.CostEstimate(flops=18 * 10**9, bytes_accessed=45 * 10**6, transcendentals=0),
        name="mlp_out",
    )(zs, w, hs, dgs, dus, h1, gain, dy)


def tokens_kernel(n, *refs):
    parts, (wq_ref, wk_ref, wv_ref, x_ref, gain_ref, dh1_ref, out_ref, dgain_ref) = refs[: 3 * n], refs[3 * n :]
    i = pl.program_id(0)
    total = None
    for j, w_ref in enumerate((wq_ref, wk_ref, wv_ref)):
        d = parts[j * n][...] if n == 1 else jnp.concatenate([r[...] for r in parts[j * n : (j + 1) * n]], axis=1)
        t = nt(d, w_ref[...])
        total = t if total is None else total + t
    dv, dgain = norm_back(x_ref[...].astype(F32), gain_ref[...], total)
    out_ref[...] = dh1_ref[...] + dv

    @pl.when(i == 0)
    def _():
        dgain_ref[...] = jnp.zeros_like(dgain_ref)

    dgain_ref[...] += dgain


def tokens_grad(dqs, dks, dvs, wq, wk, wv, x, gain, dh1):
    n = len(dqs)
    tok = x.shape[0]
    tile = 256
    row = pl.BlockSpec((tile, D), lambda i: (i, 0))
    full = pl.BlockSpec((D, D), lambda i: (0, 0))
    vec = pl.BlockSpec((1, D), lambda i: (0, 0))
    sds = jax.ShapeDtypeStruct
    return pl.pallas_call(
        functools.partial(tokens_kernel, n),
        grid=(tok // tile,),
        in_specs=[pl.BlockSpec((tile, d.shape[1]), lambda i: (i, 0)) for d in (*dqs, *dks, *dvs)] + [full, full, full, row, vec, row],
        out_specs=[row, vec],
        out_shape=[sds((tok, D), F32), sds((1, D), F32)],
        compiler_params=pltpu.CompilerParams(vmem_limit_bytes=40 * MIB),
        cost_estimate=pl.CostEstimate(flops=7 * 10**9, bytes_accessed=24 * 10**6, transcendentals=0),
        name="tokens_grad",
    )(*dqs, *dks, *dvs, wq, wk, wv, x, gain, dh1)
def body(
    paired, tokens, first_values, lengths, w_query, w_key, w_value, w_out, norm_attn, norm_mlp, w_gate, w_up, w_down, grad_out
):
    nz = lax.axis_size("ma")
    r = lax.axis_index("rows")
    cos, sin = (jnp.asarray(t) for t in rope_tables())
    gain_a, gain_m = norm_attn[None], norm_mlp[None]
    tile = jnp.stack([w_gate.T, w_up.T, w_down])
    if paired:
        fs = tile.shape[1] // 2
        own = lax.dynamic_slice_in_dim(tile, r * fs, fs, axis=1)
        q, k, v, o, st, nma, mixed, dh1, da, dgain_m, mine, got, _ = first_half(
            lengths, tokens, gain_a, w_query, w_key, w_value, first_values, cos, sin, w_out, gain_m, grad_out, own, nz
        )
        nmat, ot = prepare(nma, o)
        grad_tokens, grad_first, gains, grad_wout, grads, tiles = second_half(
            lengths, da, w_out, q, k, v, o, st, nmat, cos, sin, w_query, w_key, w_value, gain_a, dgain_m, tokens, dh1,
            wout_grad(ot, da)[None], mine, got,
        )
        gain_grads = gains[0], gains[1]
        grad_wout = grad_wout[0].astype(F32)
        grad_q, grad_k, grad_v = (grads[j].astype(F32) for j in range(3))
        tiles = tiles.transpose(1, 0, 2, 3).reshape(tile.shape).astype(F32)
    else:
        w = lax.all_gather(lax.all_gather(tile, "ma", axis=0), "ha", axis=0)[:, None]
        zs = jnp.arange(nz, dtype=jnp.int32)
        q, k, v, o, st, nma, h1, nmm = attention_forward(
            lengths, tokens, gain_a, w_query, w_key, w_value, first_values, cos, sin, w_out, gain_m
        )
        nmat, ot, nmmt, dyt = prepare(nma, o, nmm, grad_out)
        done = [mlp_block(zs, [[w[i, 0, j] for j in range(nz)]], nmmt, dyt, nmm, grad_out) for i in range(w.shape[0])]
        hs, dgs, dus, mine = (jnp.stack([d[j] for d in done]) for j in range(4))
        mixed, dh1, da, dgain_m = mlp_out(zs, w, hs, dgs, dus, h1, gain_m, grad_out)
        dq, dk, dv, grad_first, grads = attention_backward(
            0, H // GROUP, lengths, da, w_out, q, k, v, o, st, nmat, cos, sin
        )
        grad_tokens, dgain_a = tokens_grad([dq], [dk], [dv], w_query, w_key, w_value, tokens, gain_a, dh1)
        part = lax.psum_scatter(lax.psum_scatter(mine, "ha", scatter_dimension=0), "ma", scatter_dimension=0)
        tiles = lax.psum(part, "rows").astype(F32)
        grad_wout, grads, *gains = lax.psum((wout_grad(ot, da), grads, dgain_a, dgain_m), ("rows", "ha", "ma"))
        grad_wout = grad_wout.astype(F32)
        grad_q, grad_k, grad_v = (grads[j].astype(F32) for j in range(3))
        gain_grads = [v[0] for v in gains]
    return (
        mixed, grad_tokens, grad_first, grad_q, grad_k, grad_v, grad_wout, gain_grads[0], gain_grads[1],
        tiles[0].T, tiles[1].T, tiles[2],
    )


def solution(mesh):
    tok = P(("rows", "ha", "ma"), None)
    gate, down = P("ma", "ha"), P("ha", "ma")
    return jax.shard_map(
        functools.partial(body, mesh.shape["rows"] == 2),
        mesh=mesh,
        in_specs=(tok, tok, P(("rows", "ha", "ma")), P(), P(), P(), P(), P(), P(), gate, gate, down, tok),
        out_specs=(tok, tok, tok, P(), P(), P(), P(), P(), P(), gate, gate, down),
        check_vma=False,
    )
```

```python
import functools
import math

import jax
import jax.numpy as jnp
import numpy as np
from jax import lax
from jax.experimental import pallas as pl
from jax.experimental.pallas import tpu as pltpu
from jax.sharding import PartitionSpec as P

D = 1024
H = 16
HD = 64
SLOT = 1024
EPS = 1e-06
GROUP = 4
GW = GROUP * HD
QB = 256
SCALE = 1.0 / math.sqrt(HD)
C2 = SCALE * math.log2(math.e)
F32 = jnp.float32
BF16 = jnp.bfloat16
MIB = 1 << 20


def nn(a, b):
    return lax.dot_general(a, b, (((1,), (0,)), ((), ())), preferred_element_type=F32)


def nt(a, b):
    return lax.dot_general(a, b, (((1,), (1,)), ((), ())), preferred_element_type=F32)


def tn(a, b):
    return lax.dot_general(a, b, (((0,), (0,)), ((), ())), preferred_element_type=F32)


def rope_tables():
    place = np.arange(SLOT, dtype=np.float32)
    frequency = np.float32(10000.0) ** (-np.arange(HD // 2, dtype=np.float32) * np.float32(2.0) / np.float32(HD))
    angles = place[:, None] * frequency[None, :]
    cosine, sine = np.cos(angles), np.sin(angles)
    cos_row = np.concatenate([cosine] * 4, axis=1)
    sin_row = np.concatenate([-sine, sine, -sine, sine], axis=1)
    return cos_row.astype(np.float32), sin_row.astype(np.float32)


def lanes(shape):
    return lax.broadcasted_iota(jnp.int32, shape, 1)


def partner(v):
    first = (lanes(v.shape) & 63) < 32
    return jnp.where(first, pltpu.roll(v, 96, 1), pltpu.roll(v, 32, 1))


def turn(v, cos, sin):
    parts = []
    for at in range(0, v.shape[1], 128):
        piece = v[:, at : at + 128]
        parts.append(piece * cos + partner(piece) * sin)
    return jnp.concatenate(parts, axis=1)


def low3(v):
    hi = v.astype(BF16).astype(F32)
    rest = v - hi
    mid = rest.astype(BF16).astype(F32)
    return hi, mid, rest - mid


def forward_start(x_ref, gain_ref, nma_ref, h1_ref, st_ref):
    x = x_ref[...].astype(F32)
    r = lax.rsqrt(jnp.mean(x * x, axis=-1, keepdims=True) + EPS)
    nma_ref[...] = (x * r * gain_ref[...]).astype(BF16)
    h1_ref[...] = x
    st_ref[...] = jnp.zeros_like(st_ref)


def forward_end(h1_ref, gain_m_ref, nmm_ref):
    h = h1_ref[...]
    r = lax.rsqrt(jnp.mean(h * h, axis=-1, keepdims=True) + EPS)
    nmm_ref[...] = (h * r * gain_m_ref[...]).astype(BF16)


def forward_group(
    g, length, nma_ref, wq_ref, wk_ref, wv_ref, fv_ref, cos_ref, sin_ref, wo_ref,
    q_ref, k_ref, v_ref, o_ref, st_ref, h1_ref, between=None,
):
    nm = nma_ref[...]
    cos, sin = cos_ref[...], sin_ref[...]
    q_ref[...] = turn(nn(nm, wq_ref[...]), cos, sin).astype(BF16)
    k_ref[...] = turn(nn(nm, wk_ref[...]), cos, sin).astype(BF16)
    v_ref[...] = (0.5 * nn(nm, wv_ref[...]) + 0.5 * fv_ref[...].astype(F32)).astype(BF16)
    tile = (SLOT, 128)
    lane = lanes(tile)
    row = lax.broadcasted_iota(jnp.int32, tile, 0)
    k_extra = jnp.where((lane == 0) & (row >= length), -1e30, 0.0).astype(BF16)
    q_extra = jnp.where(lane == 0, 1.0, 0.0).astype(BF16)
    ones = jnp.ones(tile, BF16)
    low_lane = lane < HD
    qlane = lanes((QB, 128))
    causal = lax.broadcasted_iota(jnp.int32, (QB, QB), 1) <= lax.broadcasted_iota(jnp.int32, (QB, QB), 0)
    for pair in range(GROUP // 2):
        cols = pl.ds(pair * 128, 128)
        qp, kp, vp = q_ref[:, cols], k_ref[:, cols], v_ref[:, cols]
        q_ext = jnp.concatenate([qp, q_extra], axis=1)
        k_exts, v_exts = [], []
        for e in range(2):
            mine = low_lane if e == 0 else ~low_lane
            k_exts.append(jnp.concatenate([jnp.where(mine, kp, 0), k_extra], axis=1))
            v_exts.append(jnp.concatenate([jnp.where(mine, vp, 0), ones], axis=1))
        for qb in range(SLOT // QB):
            if between is not None:
                between(pair, qb)
            rows = slice(qb * QB, (qb + 1) * QB)
            top = (qb + 1) * QB
            out = None
            stats = st_ref[rows, :].astype(F32)
            for e in range(2):
                s = nt(q_ext[rows], k_exts[e][:top])
                diag = jnp.where(causal, s[:, top - QB :], -1e30)
                s = diag if qb == 0 else jnp.concatenate([s[:, : top - QB], diag], axis=1)
                m = jnp.max(s, axis=-1, keepdims=True)
                p = jnp.exp2((s - m) * C2).astype(BF16)
                res = nn(p, v_exts[e][:top])
                total = res[:, 128:]
                part = res[:, :128] / total
                out = part if out is None else out + part
                hi, mid, rest = low3(m + jnp.log2(total) * (1.0 / C2))
                base = 8 * (g * GROUP + pair * 2 + e)
                stats = jnp.where(qlane == base, hi, stats)
                stats = jnp.where(qlane == base + 1, mid, stats)
                stats = jnp.where(qlane == base + 2, rest, stats)
                stats = jnp.where(qlane == base + 3, 1.0, stats)
            o_ref[rows, cols] = out.astype(BF16)
            st_ref[rows, :] = stats.astype(BF16)
    h1_ref[...] += nn(o_ref[...], wo_ref[...])


def fwd_kernel(
    len_ref, x_ref, gain_ref, wq_ref, wk_ref, wv_ref, fv_ref, cos_ref, sin_ref, wo_ref, gain_m_ref,
    q_ref, k_ref, v_ref, o_ref, st_ref, nma_ref, h1_ref, nmm_ref,
):
    g = pl.program_id(0)

    @pl.when(g == 0)
    def _():
        forward_start(x_ref, gain_ref, nma_ref, h1_ref, st_ref)

    forward_group(
        g, len_ref[0], nma_ref, wq_ref, wk_ref, wv_ref, fv_ref, cos_ref, sin_ref, wo_ref,
        q_ref, k_ref, v_ref, o_ref, st_ref, h1_ref,
    )

    @pl.when(g == pl.num_programs(0) - 1)
    def _():
        forward_end(h1_ref, gain_m_ref, nmm_ref)


def attention_forward(length, x, gain, wq, wk, wv, fv, cos, sin, wo, gain_m):
    whole = lambda *_: (0, 0)
    col = lambda g, *_: (0, g)
    tok = x.shape[0]
    full = pl.BlockSpec((tok, D), whole)
    blk = pl.BlockSpec((tok, GW), col)
    wblk = pl.BlockSpec((D, GW), col)
    vec = pl.BlockSpec((1, D), whole)
    tab = pl.BlockSpec((tok, 128), whole)
    sds = jax.ShapeDtypeStruct
    return pl.pallas_call(
        fwd_kernel,
        grid_spec=pltpu.PrefetchScalarGridSpec(
            num_scalar_prefetch=1,
            grid=(H // GROUP,),
            in_specs=[full, vec, wblk, wblk, wblk, blk, tab, tab, pl.BlockSpec((GW, D), lambda g, *_: (g, 0)), vec],
            out_specs=[blk, blk, blk, blk, tab, full, full, full],
        ),
        out_shape=[sds((tok, D), BF16)] * 4 + [sds((tok, 128), BF16), sds((tok, D), BF16), sds((tok, D), F32), sds((tok, D), BF16)],
        compiler_params=pltpu.CompilerParams(vmem_limit_bytes=56 * MIB),
        cost_estimate=pl.CostEstimate(flops=30 * 10**9, bytes_accessed=40 * 10**6, transcendentals=10**7),
        name="attention_forward",
    )(length, x, gain, wq, wk, wv, fv, cos, sin, wo, gain_m)


def prep_kernel(*refs):
    count = len(refs) // 2
    for src, dst in zip(refs[:count], refs[count:]):
        dst[...] = src[...].T


def prepare(*arrays):
    vm = pl.BlockSpec(memory_space=pltpu.VMEM)
    tok = arrays[0].shape[0]
    return pl.pallas_call(
        prep_kernel,
        in_specs=[vm] * len(arrays),
        out_specs=[vm] * len(arrays),
        out_shape=[jax.ShapeDtypeStruct((D, tok), BF16)] * len(arrays),
        compiler_params=pltpu.CompilerParams(vmem_limit_bytes=30 * MIB),
        cost_estimate=pl.CostEstimate(flops=10**9, bytes_accessed=4 * len(arrays) * 10**6, transcendentals=0),
        name="prepare",
    )(*arrays)


def wout_kernel(ot_ref, da_ref, out_ref):
    out_ref[...] = nn(ot_ref[...], da_ref[...]).astype(BF16)


def wout_grad(ot, da):
    vm = pl.BlockSpec(memory_space=pltpu.VMEM)
    return pl.pallas_call(
        wout_kernel,
        in_specs=[vm] * 2,
        out_specs=vm,
        out_shape=jax.ShapeDtypeStruct((D, D), BF16),
        compiler_params=pltpu.CompilerParams(vmem_limit_bytes=30 * MIB),
        cost_estimate=pl.CostEstimate(flops=2 * 10**9, bytes_accessed=6 * 10**6, transcendentals=0),
        name="wout_grad",
    )(ot, da)


def backward_group(
    g, length, da_ref, wo_ref, q_ref, k_ref, v_ref, o_ref, st_ref, cos_ref, sin_ref, dq_ref, dk_ref, dv_ref, gf_ref, dq_acc, between=None
):
    do_all = nt(da_ref[...], wo_ref[...]).astype(BF16)
    prod = do_all.astype(F32) * o_ref[...].astype(F32)
    hi = prod.astype(BF16)
    lo = (prod - hi.astype(F32)).astype(BF16)
    sel_row = lax.broadcasted_iota(jnp.int32, (GW, 128), 0) // HD + g * GROUP
    sel_lane = lanes((GW, 128))
    pick = jnp.where((sel_lane // 8 == sel_row) & ((sel_lane & 7) >= 4) & ((sel_lane & 7) <= 5), 1.0, 0.0).astype(BF16)
    delta = nn(hi, pick) + nn(lo, pick)
    tile = (SLOT, 128)
    lane = lanes(tile)
    d_hi = delta.astype(BF16)
    d_ext = jnp.where((lane & 7) == 4, d_hi.astype(F32), delta - d_hi.astype(F32)).astype(BF16)
    row = lax.broadcasted_iota(jnp.int32, tile, 0)
    dead = row >= length
    low_lane = lane < HD
    st = st_ref[...]
    visible = lax.broadcasted_iota(jnp.int32, (QB, QB), 0) <= lax.broadcasted_iota(jnp.int32, (QB, QB), 1)
    dq_acc[...] = jnp.zeros_like(dq_acc)
    for pair in range(GROUP // 2):
        cols = pl.ds(pair * 128, 128)
        qp, kp, vp = q_ref[:, cols], k_ref[:, cols], v_ref[:, cols]
        dop = do_all[:, pair * 128 : pair * 128 + 128]
        q_ext = jnp.concatenate([qp, st], axis=1)
        do_ext = jnp.concatenate([dop, d_ext], axis=1)
        heads = []
        for e in range(2):
            mine = low_lane if e == 0 else ~low_lane
            at = lane - 8 * (g * GROUP + pair * 2 + e)
            k_x = jnp.where((at >= 0) & (at < 3), -1.0, jnp.where((at == 3) & dead, -1e30, 0.0)).astype(BF16)
            v_x = jnp.where((at >= 4) & (at < 6), -1.0, 0.0).astype(BF16)
            k_m = jnp.where(mine, kp, 0)
            heads.append((
                k_m,
                jnp.concatenate([k_m, k_x], axis=1),
                jnp.concatenate([jnp.where(mine, vp, 0), v_x], axis=1),
                jnp.where(mine, qp, 0),
                jnp.where(mine, dop, 0),
            ))
        for kb in range(SLOT // QB):
            if between is not None:
                between(pair, kb)
            rows = slice(kb * QB, (kb + 1) * QB)
            start = kb * QB
            dk = dv = None
            for k_m, k_ext, v_ext, q_m, do_m in heads:
                st_ = nt(k_ext[rows], q_ext[start:])
                dp = nt(v_ext[rows], do_ext[start:])
                p = jnp.exp2(st_ * C2)
                diag = jnp.where(visible, p[:, :QB], 0.0)
                p = diag if kb == SLOT // QB - 1 else jnp.concatenate([diag, p[:, QB:]], axis=1)
                ds = (p * dp).astype(BF16)
                p = p.astype(BF16)
                dv_e = nn(p, do_m[start:])
                dk_e = nn(ds, q_m[start:])
                dk = dk_e if dk is None else dk + dk_e
                dv = dv_e if dv is None else dv + dv_e
                dq_acc[start:, cols] += tn(ds, k_m[rows])
            dk = dk * SCALE
            cos, sin = cos_ref[rows, :], sin_ref[rows, :]
            dk_ref[rows, cols] = (dk * cos - partner(dk) * sin).astype(BF16)
            half = 0.5 * dv
            gf_ref[rows, cols] = half
            dv_ref[rows, cols] = half.astype(BF16)
    cos, sin = cos_ref[...], sin_ref[...]
    for pair in range(GROUP // 2):
        cols = pl.ds(pair * 128, 128)
        dq = dq_acc[:, cols] * SCALE
        dq_ref[:, cols] = (dq * cos - partner(dq) * sin).astype(BF16)


def bwd_kernel(
    first_group, len_ref, da_ref, wo_ref, q_ref, k_ref, v_ref, o_ref, st_ref, nmt_ref, cos_ref, sin_ref,
    dq_ref, dk_ref, dv_ref, gf_ref, gw_ref, dq_acc,
):
    g = pl.program_id(0) + first_group
    backward_group(
        g, len_ref[0], da_ref, wo_ref, q_ref, k_ref, v_ref, o_ref, st_ref, cos_ref, sin_ref, dq_ref, dk_ref, dv_ref, gf_ref, dq_acc
    )
    for j, ref in enumerate((dq_ref, dk_ref, dv_ref)):
        gw_ref[j] = nn(nmt_ref[...], ref[...]).astype(BF16)


def attention_backward(first_group, groups, length, da, wo, q, k, v, o, st, nmt, cos, sin):
    whole = lambda *_: (0, 0)
    tok = da.shape[0]
    full = pl.BlockSpec((tok, D), whole)
    blk_in = pl.BlockSpec((tok, GW), lambda g, *_: (0, g + first_group))
    blk = pl.BlockSpec((tok, GW), lambda g, *_: (0, g))
    tab = pl.BlockSpec((tok, 128), whole)
    sds = jax.ShapeDtypeStruct
    width = groups * GW
    return pl.pallas_call(
        functools.partial(bwd_kernel, first_group),
        grid_spec=pltpu.PrefetchScalarGridSpec(
            num_scalar_prefetch=1,
            grid=(groups,),
            in_specs=[full, pl.BlockSpec((GW, D), lambda g, *_: (g + first_group, 0)), blk_in, blk_in, blk_in, blk_in, tab, pl.BlockSpec((D, tok), whole), tab, tab],
            out_specs=[blk, blk, blk, blk, pl.BlockSpec((3, D, GW), lambda g, *_: (0, 0, g))],
            scratch_shapes=[pltpu.VMEM((tok, GW), F32)],
        ),
        out_shape=[sds((tok, width), BF16)] * 3 + [sds((tok, width), F32), sds((3, D, width), BF16)],
        compiler_params=pltpu.CompilerParams(vmem_limit_bytes=56 * MIB),
        cost_estimate=pl.CostEstimate(flops=10 * 10**9 * groups, bytes_accessed=10 * 10**6, transcendentals=groups * 3 * 10**6),
        name="attention_backward",
    )(length, da, wo, q, k, v, o, st, nmt, cos, sin)


def sig(v):
    return 1.0 / (1.0 + jnp.exp(-v))


def mlp_kernel(nc, nz, zs_ref, *refs):
    pieces = refs[: nc * nz]
    nmt_ref, dyt_ref, nm_ref, dy_ref, h_ref, dg_ref, du_ref = refs[nc * nz : nc * nz + 7]
    outs = refs[nc * nz + 7 :]
    fs = pieces[0].shape[1]
    dz = pieces[0].shape[2]
    starts = [pl.multiple_of(zs_ref[s] * dz, dz) for s in range(nz)]
    for c in range(nc):
        gate = up = dh = None
        for s in range(nz):
            w_ref = pieces[c * nz + s]
            at = pl.ds(starts[s], dz)
            nmt, dyt = nmt_ref[at, :], dyt_ref[at, :]
            parts = nn(w_ref[0], nmt), nn(w_ref[1], nmt), nn(w_ref[2], dyt)
            gate, up, dh = parts if gate is None else (gate + parts[0], up + parts[1], dh + parts[2])
        sg = sig(gate)
        silu = gate * sg
        rows = pl.ds(c * fs, fs)
        h = (silu * up).astype(BF16)
        dg = (dh * up * (sg * (1.0 + gate * (1.0 - sg)))).astype(BF16)
        du = (dh * silu).astype(BF16)
        h_ref[rows, :], dg_ref[rows, :], du_ref[rows, :] = h, dg, du
        for s in range(nz):
            at = pl.ds(starts[s], dz)
            nm, dy = nm_ref[:, at], dy_ref[:, at]
            outs[c][s, 0] = nn(dg, nm).astype(BF16)
            outs[c][s, 1] = nn(du, nm).astype(BF16)
            outs[c][s, 2] = nn(h, dy).astype(BF16)


def mlp_block(zs, pieces, nmt, dyt, nm, dy):
    nc, nz = len(pieces), len(pieces[0])
    _, fs, dz = pieces[0][0].shape
    tok = nm.shape[0]
    sds = jax.ShapeDtypeStruct
    vm = pl.BlockSpec(memory_space=pltpu.VMEM)
    return pl.pallas_call(
        functools.partial(mlp_kernel, nc, nz),
        in_specs=[pl.BlockSpec(memory_space=pltpu.SMEM)] + [vm] * (nc * nz + 4),
        out_specs=[vm] * (3 + nc),
        out_shape=[sds((nc * fs, tok), BF16)] * 3 + [sds((nz, 3, fs, dz), BF16)] * nc,
        compiler_params=pltpu.CompilerParams(vmem_limit_bytes=44 * MIB),
        cost_estimate=pl.CostEstimate(flops=12 * nc * fs * D * tok, bytes_accessed=15 * 10**6, transcendentals=nc * fs * tok),
        name="mlp_block",
    )(zs, *[p for c in pieces for p in c], nmt, dyt, nm, dy)


MESH = pl.DeviceIdType.MESH
RING = (0, 1, 3, 2)
STEPS = H // GROUP
TURNS = (0, 1, 3, 2)


def table(index, values):
    out = values[0]
    for i, v in enumerate(values[1:], 1):
        out = jnp.where(index == i, v, out)
    return out


def norm_back(v, gain, grad):
    ms = jnp.mean(v * v, axis=-1, keepdims=True) + EPS
    r = lax.rsqrt(ms)
    gg = grad * gain
    inner = jnp.mean(gg * v, axis=-1, keepdims=True)
    dv = r * gg - v * (inner * r * r * r)
    dgain = jnp.sum(grad * v * r, axis=0, keepdims=True)
    return dv, dgain


class Places:
    def __init__(self, nz):
        self.nz = nz
        self.r, self.a, self.z = (lax.axis_index(n) for n in ("rows", "ha", "ma"))
        self.spot = table(self.a, [RING.index(i) for i in range(4)])
        self.right_to = table(self.spot, [RING[(i + 1) % 4] for i in range(4)])
        self.left_to = table(self.spot, [RING[(i + 3) % 4] for i in range(4)])
        self.far_to = table(self.spot, [RING[(i + 2) % 4] for i in range(4)])
        self.arrivals = [0] + [table(self.z, v) for v in ((3, 1, 3, 1), (2, 3, 1, 2), (1, 2, 2, 3))]

    def at(self, **moved):
        place = {"rows": self.r, "ha": self.a, "ma": self.z, **moved}
        return (place["rows"], place["ha"], place["ma"])

    def meet(self, others):
        barrier = pltpu.get_barrier_semaphore()
        for other in others:
            pl.semaphore_signal(barrier, inc=1, device_id=other, device_id_type=MESH)
        return lambda: pl.semaphore_wait(barrier, len(others))


def remote(src, dst, send, recv, device):
    return pltpu.make_async_remote_copy(
        src_ref=src, dst_ref=dst, send_sem=send, recv_sem=recv, device_id=device, device_id_type=MESH
    )


class Gather:
    def __init__(self, places, own_ref, w_ref, sems):
        self.p, self.own, self.w = places, own_ref, w_ref
        self.recv, self.z_send, self.right_send, self.left_send, self.far_send, self.swap_send, self.local = sems

    def copy(self, src, dst, send, device):
        return remote(self.w.at[src], self.w.at[dst], send, self.recv.at[dst], device)

    def right(self, s):
        return self.copy((0, 0, s), (1, 0, s), self.right_send.at[s], self.p.at(ha=self.p.right_to))

    def left(self, s):
        return self.copy((0, 0, s), (3, 0, s), self.left_send.at[s], self.p.at(ha=self.p.left_to))

    def far_copy(self, i):
        s = self.p.arrivals[i]
        if i % 2 == 0:
            return self.copy((1, 0, s), (2, 0, s), self.far_send.at[s], self.p.at(ha=self.p.right_to))
        return self.copy((3, 0, s), (2, 0, s), self.far_send.at[s], self.p.at(ha=self.p.left_to))

    def swap(self, k, s):
        return self.copy((k, 0, s), (k, 1, s), self.swap_send.at[k, s], self.p.at(rows=1 - self.p.r))

    def arrived(self, k, s, c=0):
        self.copy((k, c, s), (k, c, s), self.local, self.p.at(rows=1 - self.p.r)).wait_recv()

    def line(self, d, act, wait):
        nz, z = self.p.nz, self.p.z

        def up(cond):
            pl.when(cond & (z < nz - 1))(
                lambda: act(self.copy((0, 0, d), (0, 0, d + 1), self.z_send.at[0, d], self.p.at(ma=z + 1)))
            )

        def down(cond):
            pl.when(cond & (z >= 1))(
                lambda: act(self.copy((0, 0, (nz - d) % nz), (0, 0, nz - d - 1), self.z_send.at[1, d], self.p.at(ma=z - 1)))
            )

        if d and wait:
            pl.when(z >= d)(lambda: self.arrived(0, d))
            pl.when(z + d <= nz - 1)(lambda: self.arrived(0, nz - d))
        if d < nz - 1:
            up(z >= d)
            down(z + d <= nz - 1)

    def begin(self):
        p = self.p
        wait = p.meet([
            p.at(ma=(p.z + 1) % p.nz), p.at(ma=(p.z + p.nz - 1) % p.nz), p.at(ha=p.right_to), p.at(ha=p.left_to), p.at(rows=1 - p.r)
        ])
        mine = pltpu.make_async_copy(self.own, self.w.at[0, 0, 0], self.local)
        mine.start()
        mine.wait()
        wait()
        self.pass_line(0)
        self.spread(0)

    def pass_line(self, d):
        self.line(d, lambda c: c.start(), True)

    def spread(self, i):
        s = self.p.arrivals[i]
        self.right(s).start()
        self.left(s).start()
        self.swap(0, s).start()

    def sides(self, i):
        s = self.p.arrivals[i]
        self.arrived(1, s)
        self.arrived(3, s)
        self.swap(1, s).start()
        self.swap(3, s).start()

    def far(self, i):
        self.far_copy(i).start()

    def opposite(self, i):
        s = self.p.arrivals[i]
        self.arrived(2, s)
        self.swap(2, s).start()

    def end(self):
        for i in range(self.p.nz):
            s = self.p.arrivals[i]
            self.line(i, lambda c: c.wait_send(), False)
            self.right(s).wait_send()
            self.left(s).wait_send()
            self.far_copy(i).wait_send()
            for k in range(4):
                self.swap(k, s).wait_send()


class Reduce:
    BY_LEFT = (1, 3)

    def __init__(self, places, mine_ref, got_ref, steps, inb, pool, sinks, extras, sems):
        self.p, self.mine, self.got, self.steps, self.inb, self.pool = places, mine_ref, got_ref, steps, inb, pool
        self.sinks, self.extras = sinks, extras
        self.load_sem, self.send, self.spare = sems
        self.order = [at for group in steps for at in group]
        self.sent = [at for at in self.order if at[0]]
        self.first = {group[0] for group in steps}
        self.last = {group[-1] for group in steps}

    def columns(self, s):
        nz, dz = self.p.nz, self.inb.shape[4]
        return pl.ds(pl.multiple_of((self.p.z + nz - s) % nz * dz, dz), dz)

    def loads(self, i):
        k, s = self.order[i]
        slot = i % 2
        at = self.columns(s)
        sources = [self.mine.at[k, :, :, at], self.got.at[k, :, :, at]] + self.extras(k, s)[0]
        return [pltpu.make_async_copy(src, self.inb.at[slot, j], self.load_sem.at[slot, j]) for j, src in enumerate(sources)]

    def begin(self, group):
        at = self.order.index(self.steps[group][0])
        for i in range(at, min(at + 2, at + len(self.steps[group]))):
            for c in self.loads(i):
                c.start()

    def sum_of(self, k, s, out):
        i = self.order.index((k, s))
        loads = self.loads(i)
        for c in loads:
            c.wait()
        for j in range(3):
            total = self.inb[i % 2, 0, j].astype(F32)
            for n in range(1, len(loads)):
                total = total + self.inb[i % 2, n, j].astype(F32)
            for ref in self.extras(k, s)[1]:
                total = total + ref[j].astype(F32)
            out[j] = total.astype(BF16)
        group = next(g for g in self.steps if (k, s) in g)
        if group.index((k, s)) + 2 < len(group):
            for c in self.loads(i + 2):
                c.start()

    def sender(self, n):
        k, s = self.sent[n]
        slot = n % self.pool.shape[0]
        left = k == 1 or (k == 2 and s in self.BY_LEFT)
        ref, recv = self.sinks[k]
        to = self.p.at(ha=self.p.left_to if left else self.p.right_to)
        return remote(self.pool.at[slot], ref.at[s], self.send.at[slot], recv.at[s], to)

    def wait_in(self, k, s):
        ref, recv = self.sinks[k]
        remote(ref.at[s], ref.at[s], self.spare, recv.at[s], self.p.at(ha=self.p.right_to)).wait_recv()

    def pass_on(self, k, s):
        n = self.sent.index((k, s))
        size = self.pool.shape[0]
        if n >= size:
            self.sender(n - size).wait_send()
        self.sum_of(k, s, self.pool.at[n % size])
        self.sender(n).start()

    def end(self):
        for n in range(max(0, len(self.sent) - self.pool.shape[0]), len(self.sent)):
            self.sender(n).wait_send()


EARLY = [[(1, 2), (1, 0)], [(2, 1), (2, 2), (2, 3), (2, 0)]]


def first_kernel(
    nz, len_ref, x_ref, gain_ref, wq_ref, wk_ref, wv_ref, fv_ref, cos_ref, sin_ref, wo_ref, gain_m_ref, dy_ref, own_ref,
    q_ref, k_ref, v_ref, o_ref, st_ref, nma_ref, mixed_ref, dh1_ref, da_ref, dgain_ref, mine_ref, got_ref, far_ref, b1_ref, w_ref,
    h1_ref, branch_ref, nmm_ref, nmmt_ref, dyt_ref, hbuf, wbuf, gbuf, inb, pool,
    wsem, gsem, gsend, grecv, load_sem, rsend, spare, far_recv, b1_recv, *sems,
):
    g = pl.program_id(0)
    places = Places(nz)
    gather = Gather(places, own_ref, w_ref, sems)
    fs, dz = own_ref.shape[1:]
    reduce = Reduce(
        places, mine_ref, got_ref, EARLY, inb, pool, {1: (b1_ref, b1_recv), 2: (far_ref, far_recv)}, lambda k, s: ([], []),
        (load_sem, rsend, spare),
    )

    @pl.when(g == 0)
    def _():
        gather.begin()
        forward_start(x_ref, gain_ref, nma_ref, h1_ref, st_ref)

    def between(pair, qb):
        if (pair, qb) == (1, 0):
            @pl.when(g == 1)
            def _():
                gather.pass_line(1)
                gather.spread(1)

        if (pair, qb) == (1, 2):
            @pl.when(g == 2)
            def _():
                gather.pass_line(2)
                gather.spread(2)
                gather.sides(0)

    @pl.when(g < STEPS)
    def _():
        forward_group(
            g, len_ref[0], nma_ref, wq_ref, wk_ref, wv_ref, fv_ref, cos_ref, sin_ref, wo_ref,
            q_ref, k_ref, v_ref, o_ref, st_ref, h1_ref, between,
        )

    starts = [pl.multiple_of((places.z + nz - s) % nz * dz, dz) for s in range(nz)]

    def loads(k):
        return [
            pltpu.make_async_copy(w_ref.at[k, c, s], wbuf.at[:, pl.ds(c * fs, fs), pl.ds(starts[s], dz)], wsem.at[c, s])
            for c in range(2)
            for s in range(nz)
        ]

    def fetch(k):
        for s in range(nz):
            gather.arrived(k, s, 1)
        for c in loads(k):
            c.start()

    def keep(k):
        return pltpu.make_async_copy(gbuf.at[0], mine_ref.at[k], gsem)

    def push(k):
        return remote(gbuf.at[1], got_ref.at[k], gsend, grecv.at[k], places.at(rows=1 - places.r))

    @pl.when(g == STEPS - 1)
    def _():
        gather.pass_line(3)
        gather.spread(3)
        gather.sides(1)
        forward_end(h1_ref, gain_m_ref, nmm_ref)
        nmmt_ref[...] = nmm_ref[...].T
        dyt_ref[...] = dy_ref[...].T
        fetch(0)
        gather.far(0)
        gather.far(1)
        branch_ref[...] = jnp.zeros_like(branch_ref)
        dh1_ref[...] = jnp.zeros_like(dh1_ref)

    @pl.when(g >= STEPS)
    def _():
        k = g - STEPS
        for c in loads(k):
            c.wait()

        @pl.when(k > 0)
        def _():
            keep(k - 1).wait()

        for c in range(2):
            rows = slice(c * fs, (c + 1) * fs)
            gate = nn(wbuf[0, rows, :], nmmt_ref[...])
            up = nn(wbuf[1, rows, :], nmmt_ref[...])
            dh = nn(wbuf[2, rows, :], dyt_ref[...])
            sg = sig(gate)
            silu = gate * sg
            hbuf[2, rows, :] = (silu * up).astype(BF16)
            hbuf[0, rows, :] = (dh * up * (sg * (1.0 + gate * (1.0 - sg)))).astype(BF16)
            hbuf[1, rows, :] = (dh * silu).astype(BF16)
            if c == 0:
                @pl.when(k == 0)
                def _():
                    gather.sides(2)

                @pl.when(k == 1)
                def _():
                    gather.opposite(0)
                    gather.opposite(1)

                for group, at in enumerate((2, 3)):
                    @pl.when(k == at)
                    def _():
                        push(at - 1).wait_recv()
                        reduce.begin(group)
                        for step in EARLY[group]:
                            reduce.pass_on(*step)

        for at in range(0, SLOT, QB):
            rows = slice(at, at + QB)
            branch_ref[rows, :] += tn(hbuf[2, :, rows], wbuf[2])
            dh1_ref[rows, :] += tn(hbuf[0, :, rows], wbuf[0]) + tn(hbuf[1, :, rows], wbuf[1])

        @pl.when(k == 0)
        def _():
            gather.sides(3)
            gather.far(2)
            gather.far(3)
            fetch(1)

        @pl.when(k == 1)
        def _():
            gather.opposite(2)
            gather.opposite(3)
            fetch(2)

        @pl.when(k == 2)
        def _():
            fetch(3)

        @pl.when(k > 0)
        def _():
            push(k - 1).wait_send()

        for c in range(2):
            rows = slice(c * fs, (c + 1) * fs)
            gbuf[c, 0] = nn(hbuf[0, rows, :], nmm_ref[...]).astype(BF16)
            gbuf[c, 1] = nn(hbuf[1, rows, :], nmm_ref[...]).astype(BF16)
            gbuf[c, 2] = nn(hbuf[2, rows, :], dy_ref[...]).astype(BF16)
            if c == 0:
                keep(k).start()
            else:
                push(k).start()

    @pl.when(g == pl.num_programs(0) - 1)
    def _():
        total = jnp.zeros(dgain_ref.shape, F32)
        for at in range(0, SLOT, QB):
            rows = slice(at, at + QB)
            h1 = h1_ref[rows, :]
            mixed_ref[rows, :] = (h1 + branch_ref[rows, :]).astype(BF16)
            dv, dgain = norm_back(h1, gain_m_ref[...], dh1_ref[rows, :])
            dh1 = dy_ref[rows, :].astype(F32) + dv
            dh1_ref[rows, :] = dh1
            da_ref[rows, :] = dh1.astype(BF16)
            total = total + dgain
        dgain_ref[...] = total
        keep(3).wait()
        push(3).wait_send()
        push(0).wait_recv()
        push(3).wait_recv()
        for group in EARLY:
            for step in group:
                reduce.wait_in(*step)
        reduce.end()
        gather.end()


def first_half(length, x, gain, wq, wk, wv, fv, cos, sin, wo, gain_m, dy, own, nz):
    tok = x.shape[0]
    fs, dz = own.shape[1:]
    sds = jax.ShapeDtypeStruct
    once = dict(pipeline_mode=pl.Buffered(1))
    step = lambda g: jnp.minimum(g, STEPS - 1)
    full = pl.BlockSpec((tok, D), lambda g: (0, 0), **once)
    blk = pl.BlockSpec((tok, GW), lambda g: (0, step(g)))
    wblk = pl.BlockSpec((D, GW), lambda g: (0, step(g)))
    vec = pl.BlockSpec((1, D), lambda g: (0, 0), **once)
    tab = pl.BlockSpec((tok, 128), lambda g: (0, 0), **once)
    hbm = pl.BlockSpec(memory_space=pl.ANY)
    sem = pltpu.SemaphoreType.DMA
    piece = (3, fs, dz)
    return pl.pallas_call(
        functools.partial(first_kernel, nz),
        grid=(STEPS + 4,),
        in_specs=[
            pl.BlockSpec(memory_space=pltpu.SMEM), full, vec, wblk, wblk, wblk, blk, tab, tab,
            pl.BlockSpec((GW, D), lambda g: (step(g), 0)), vec, full, hbm,
        ],
        out_specs=[blk, blk, blk, blk, tab, full, full, full, full, vec, hbm, hbm, hbm, hbm, hbm],
        out_shape=[sds((tok, D), BF16)] * 4
        + [sds((tok, 128), BF16), sds((tok, D), BF16), sds((tok, D), BF16), sds((tok, D), F32), sds((tok, D), BF16), sds((1, D), F32)]
        + [sds((4, 3, fs, D), BF16)] * 2
        + [sds((nz, *piece), BF16)] * 2
        + [sds((4, 2, nz, *piece), BF16)],
        scratch_shapes=[
            pltpu.VMEM((tok, D), F32), pltpu.VMEM((tok, D), F32),
            pltpu.VMEM((tok, D), BF16), pltpu.VMEM((D, tok), BF16), pltpu.VMEM((D, tok), BF16),
            pltpu.VMEM((3, 2 * fs, tok), BF16), pltpu.VMEM((3, 2 * fs, D), BF16), pltpu.VMEM((2, 3, fs, D), BF16),
            pltpu.VMEM((2, 2, *piece), BF16), pltpu.VMEM((3, *piece), BF16),
            sem((2, nz)), sem, sem, sem((4,)), sem((2, 2)), sem((3,)), sem, sem((nz,)), sem((nz,)),
            sem((4, 2, nz)), sem((2, nz)), sem((nz,)), sem((nz,)), sem((nz,)), sem((4, nz)), sem,
        ],
        compiler_params=pltpu.CompilerParams(vmem_limit_bytes=63 * MIB, collective_id=1, has_side_effects=True),
        cost_estimate=pl.CostEstimate(flops=84 * 10**9, bytes_accessed=80 * 10**6, transcendentals=10**7),
        name="first_half",
    )(length, x, gain, wq, wk, wv, fv, cos, sin, wo, gain_m, dy, own)


MOVES = {
    (0, 0, 0): [(4, 0), ("pass", 3, 2)],
    (0, 1, 1): [("pass", 3, 1)],
    (0, 1, 2): [(4, 1)],
    (0, 2, 0): [(0, 0)],
    (1, 0, 0): [("total", 2)],
    (1, 0, 1): [(4, 2)],
    (1, 0, 2): [(0, 1)],
    (1, 0, 3): [("pass", 1, 1), ("pass", 3, 0)],
    (1, 1, 2): [(0, 2)],
    (1, 2, 0): [(4, 3), (1, 0)],
    (2, 0, 1): [("pass", 1, 3), (0, 3), (1, 1)],
    (2, 0, 2): [("pass", 3, 3)],
    (2, 1, 0): [(4, 4)],
    (2, 1, 1): [(1, 2)],
    (2, 1, 2): [(0, 4), ("total", 1)],
    (2, 2, 0): [(2, 0)],
    (3, 0, 0): [(1, 3), (0, 5)],
    (3, 0, 1): [(2, 1)],
    (3, 0, 3): [(0, 6), ("total", 0)],
    (3, 1, 0): [(2, 2)],
    (3, 1, 1): [(4, 5), (1, 4), (0, 7)],
    (3, 2, 0): [(2, 3), (1, 5), (3, 0)],
}
TAIL = [
    [("total", 3), (3, 1), (2, 4), (1, 6)],
    [(3, 2), (2, 5)],
    [(3, 3), (4, 6), (1, 7)],
    [(2, 6), (4, 7), (2, 7)],
]
SEQUENCE = [what for at in sorted(MOVES) for what in MOVES[at]] + [what for moves in TAIL for what in moves]
LATE = [[what[1:] if what[0] == "pass" else (0, what[1]) for what in SEQUENCE if what[0] in ("pass", "total")]]


class Spread:
    def __init__(self, places, m, x, far, r1, r3, zin, piece, y, send, recv, local):
        self.p, self.m, self.x, self.far, self.r1, self.r3, self.zin, self.piece, self.y = places, m, x, far, r1, r3, zin, piece, y
        self.send, self.recv, self.local = send, recv, local
        self.half = D // 2
        self.block = self.half // 4
        self.small = self.block // places.nz

    def own_half(self):
        return pl.multiple_of(self.p.r * self.half, self.half)

    def place_of(self, k):
        return (self.p.a, self.p.left_to, self.p.far_to, self.p.right_to)[k]

    def in_x(self, k, at=0, size=None):
        return pl.ds(pl.multiple_of(self.place_of(k) * self.block + at, self.small), size or self.block)

    def rows(self, k, at=0, size=None):
        return pl.ds(pl.multiple_of(self.p.r * self.half + self.place_of(k) * self.block + at, self.small), size or self.block)

    def small_rows(self, z):
        return pl.ds(pl.multiple_of(self.p.r * self.half + self.p.a * self.block + z * self.small, self.small), self.small)

    def copy(self, n, src, dst, device):
        return remote(src, dst, self.send.at[n], self.recv.at[n], device)

    def left(self):
        return self.p.at(ha=self.p.left_to)

    def right(self):
        return self.p.at(ha=self.p.right_to)

    def sibling(self):
        return self.p.at(rows=1 - self.p.r)

    def copies(self, stage):
        p, m, y = self.p, self.m, self.y
        h = self.block // 2
        if stage == 0:
            other = pl.ds(pl.multiple_of((1 - p.r) * self.half, self.half), self.half)
            return [(0, m.at[:, other], self.x, self.sibling())]
        if stage == 1:
            return [
                (1, m.at[:, self.rows(2, 0, h)], self.far.at[:, pl.ds(0, h)], self.left()),
                (2, m.at[:, self.rows(2, h, h)], self.far.at[:, pl.ds(h, h)], self.right()),
            ]
        if stage == 2:
            return [(3, m.at[:, self.rows(1)], self.r1, self.left()), (4, m.at[:, self.rows(3)], self.r3, self.right())]
        if stage == 3:
            return [
                (4 + s, m.at[:, self.small_rows((p.z + p.nz - s) % p.nz)], self.zin.at[s], p.at(ma=(p.z + p.nz - s) % p.nz))
                for s in range(1, p.nz)
            ]
        if stage == 4:
            at = self.small_rows(p.z)
            return [(7 + s, self.piece, y.at[:, at], p.at(ma=(p.z + s) % p.nz)) for s in range(1, p.nz)]
        if stage == 5:
            at = self.rows(0)
            return [(n, y.at[:, at], y.at[:, at], to) for n, to in ((11, self.right()), (12, self.left()), (13, self.sibling()))]
        if stage == 6:
            first, second = self.rows(1, 0, h), self.rows(3, h, h)
            return [(14, y.at[:, first], y.at[:, first], self.right()), (15, y.at[:, second], y.at[:, second], self.left())] + [
                (n, y.at[:, self.rows(k)], y.at[:, self.rows(k)], self.sibling()) for n, k in ((16, 1), (17, 3))
            ]
        return [(18, y.at[:, self.rows(2)], y.at[:, self.rows(2)], self.sibling())]

    def keep(self):
        return pltpu.make_async_copy(self.piece, self.y.at[:, self.small_rows(self.p.z)], self.local)

    def wait_for(self, stage, which=None):
        copies = self.copies(stage)
        for i in which if which is not None else range(len(copies)):
            self.copy(*copies[i]).wait_recv()

    def add(self, at, *others):
        for j in range(self.m.shape[0]):
            total = self.m[j, at, :].astype(F32)
            for ref, place in others:
                total = total + ref[j, place, :].astype(F32)
            self.m[j, at, :] = total.astype(BF16)

    def run(self, stage):
        p = self.p
        h = self.block // 2
        if stage == 1:
            self.wait_for(0)
            self.add(self.rows(2), (self.x, self.in_x(2)))
        elif stage == 2:
            self.wait_for(1)
            self.add(self.rows(1, 0, h), (self.x, self.in_x(1, 0, h)), (self.far, pl.ds(0, h)))
            self.add(self.rows(1, h, h), (self.x, self.in_x(1, h, h)))
            self.add(self.rows(3, 0, h), (self.x, self.in_x(3, 0, h)))
            self.add(self.rows(3, h, h), (self.x, self.in_x(3, h, h)), (self.far, pl.ds(h, h)))
        elif stage == 3:
            self.wait_for(2)
            whole = pl.ds(0, self.block)
            self.add(self.rows(0), (self.x, self.in_x(0)), (self.r1, whole), (self.r3, whole))
        elif stage == 4:
            self.wait_for(3)
            for j in range(self.m.shape[0]):
                total = self.m[j, self.small_rows(p.z), :].astype(F32)
                for s in range(1, p.nz):
                    total = total + self.zin[s, j].astype(F32)
                self.piece[j] = total.astype(BF16)
            self.keep().start()
        elif stage == 5:
            self.wait_for(4)
            self.keep().wait()
        elif stage == 6:
            self.wait_for(5, (0, 1))
        elif stage == 7:
            self.wait_for(6, (0, 1))
        for c in self.copies(stage):
            self.copy(*c).start()

    def end(self):
        self.wait_for(5, (2,))
        self.wait_for(6, (2, 3))
        self.wait_for(7)
        for stage in range(8):
            for c in self.copies(stage):
                self.copy(*c).wait_send()


class Gains:
    def __init__(self, places, own, twin, ring, line, send, recv):
        self.p, self.own, self.twin, self.ring, self.line, self.send, self.recv = places, own, twin, ring, line, send, recv

    def to_twin(self):
        return [remote(self.own, self.twin, self.send.at[0], self.recv.at[0], self.p.at(rows=1 - self.p.r))]

    def round_ring(self):
        p, at = self.p, self.ring.at[self.p.a]
        return [remote(at, at, self.send.at[i], self.recv.at[i], p.at(ha=to)) for i, to in ((1, p.right_to), (2, p.left_to), (3, p.far_to))]

    def along_line(self):
        p, at = self.p, self.line.at[self.p.z]
        return [remote(at, at, self.send.at[3 + s], self.recv.at[3 + s], p.at(ma=(p.z + s) % p.nz)) for s in range(1, p.nz)]

    def run(self, stage):
        if stage == 0:
            sends = self.to_twin()
        elif stage == 1:
            for c in self.to_twin():
                c.wait_recv()
            self.ring[pl.ds(self.p.a, 1)] = (self.own[...] + self.twin[...])[None]
            sends = self.round_ring()
        else:
            for c in self.round_ring():
                c.wait_recv()
            self.line[pl.ds(self.p.z, 1)] = (self.ring[0] + self.ring[1] + self.ring[2] + self.ring[3])[None]
            sends = self.along_line()
        for c in sends:
            c.start()

    def end(self, out_ref):
        for c in self.along_line():
            c.wait_recv()
        total = self.line[0]
        for s in range(1, self.p.nz):
            total = total + self.line[s]
        out_ref[...] = total
        for c in self.to_twin() + self.round_ring() + self.along_line():
            c.wait_send()


def second_kernel(
    nz, len_ref, da_ref, wo_ref, q_ref, k_ref, v_ref, o_ref, st_ref, cos_ref, sin_ref, wq_ref, wk_ref, wv_ref,
    gain_ref, dgm_ref, x_ref, dh1_ref, nma_ref, attn_ref, mine_ref, got_ref, far_ref, b1_ref,
    gt_ref, gf_ref, gains_ref, ywo_ref, y_ref, tiles_ref,
    dq_acc, dq_ref, dk_ref, dv_ref, xbuf, hbuf, tile_sem,
    mo, xo, faro, r1o, r3o, zo, po, mg, xg, farg, r1g, r3g, zg, pg,
    nmt_ref, inb, pool, tot, b1_in, b3_in, z_in, gown, gtwin, gring, gline,
    ar_send, ar_recv, ar_local, g_send, g_recv,
    first_sem, load_sem, rsend, spare, b1_recv, b3_recv, z_send, z_recv, swap_send, swap_recv,
):
    g = pl.program_id(0)
    p = Places(nz)

    def extras(block, s):
        if block == 0:
            early = (1, s) in EARLY[0]
            return [b1_ref.at[s]] if early else [], [b3_in.at[s]] if early else [b1_in.at[s], b3_in.at[s]]
        return [far_ref.at[s]] if (s in Reduce.BY_LEFT) == (block == 1) else [], []

    reduce = Reduce(
        p, mine_ref, got_ref, LATE, inb, pool, {1: (b1_in, b1_recv), 3: (b3_in, b3_recv)}, extras, (load_sem, rsend, spare)
    )

    def to_owner(s):
        return remote(tot.at[s], z_in.at[s], z_send.at[s], z_recv.at[s], p.at(ma=(p.z + nz - s) % nz))

    def total_of(s):
        if (1, s) not in EARLY[0]:
            reduce.wait_in(1, s)
        reduce.wait_in(3, s)
        reduce.sum_of(0, s, tot.at[s])
        if s:
            to_owner(s).start()

    def tile_copies():
        return (
            pltpu.make_async_copy(tot.at[0], tiles_ref.at[p.r], spare),
            remote(tot.at[0], tiles_ref.at[p.r], swap_send, swap_recv, p.at(rows=1 - p.r)),
        )

    def finish():
        for s in range(1, nz):
            to_owner(s).wait_recv()
        for j in range(3):
            total = tot[0, j].astype(F32)
            for s in range(1, nz):
                total = total + z_in[s, j].astype(F32)
            tot[0, j] = total.astype(BF16)
        for c in tile_copies():
            c.start()

    sets = mg.shape[0]
    width = mg.shape[3]
    chunks = [
        Spread(
            p, *(v.at[i % sets] for v in (mg, xg, farg, r1g, r3g, zg, pg)), y_ref.at[:, :, pl.ds(i * width, width)],
            ar_send.at[i], ar_recv.at[i], ar_local.at[i],
        )
        for i in range(STEPS)
    ]
    chunks.append(Spread(p, mo, xo, faro, r1o, r3o, zo, po, ywo_ref, ar_send.at[STEPS], ar_recv.at[STEPS], ar_local.at[STEPS]))
    gains = Gains(p, gown, gtwin, gring, gline, g_send, g_recv)

    def move(what):
        if what[0] == "pass":
            reduce.pass_on(*what[1:])
        elif what[0] == "total":
            total_of(what[1])
        else:
            chunks[what[0]].run(what[1])

    def between(pair, kb):
        for at in range(STEPS):
            moves = MOVES.get((at, pair, kb))
            if moves:
                @pl.when(g == at)
                def _():
                    for what in moves:
                        move(what)

    @pl.when(g == 0)
    def _():
        wait = p.meet(
            [p.at(ma=(p.z + s) % nz) for s in range(1, nz)] + [p.at(ha=to) for to in (p.right_to, p.left_to, p.far_to)] + [p.at(rows=1 - p.r)]
        )
        spots = [(i // 3, i % 3) for i in range(8)]
        fills = [
            pltpu.make_async_copy(src.at[:, pl.ds(i % 4 * width, width)], mg.at[spots[i]], first_sem.at[i])
            for i, src in enumerate([attn_ref] * 4 + [nma_ref] * 4)
        ]
        for c in fills:
            c.start()
        reduce.begin(0)
        gt_ref[...] = jnp.zeros_like(gt_ref)
        for i in range(4):
            fills[i].wait()
            mo[0, pl.ds(i * width, width), :] = tn(mg[spots[i]], da_ref[...]).astype(BF16)
        for i in range(4, 8):
            fills[i].wait()
            nmt_ref[pl.ds((i - 4) * width, width), :] = mg[spots[i]].T
        wait()

    backward_group(
        g, len_ref[0], da_ref, wo_ref, q_ref, k_ref, v_ref, o_ref, st_ref, cos_ref, sin_ref,
        dq_ref, dk_ref, dv_ref, gf_ref, dq_acc, between,
    )
    for i in range(sets, STEPS):
        @pl.when(g == i)
        def _():
            chunks[i - sets].end()

    for j, ref in enumerate((dq_ref, dk_ref, dv_ref)):
        mg[g % sets, j] = nn(nmt_ref[...], ref[...]).astype(BF16)

    between(2, 0)
    gt_ref[...] += nt(dq_ref[...], wq_ref[...]) + nt(dk_ref[...], wk_ref[...]) + nt(dv_ref[...], wv_ref[...])

    @pl.when(g == STEPS - 1)
    def _():
        def loads(i):
            rows = pl.ds(i * QB, QB)
            return [
                pltpu.make_async_copy(src.at[rows], buf.at[i % 2], tile_sem.at[i % 2, j])
                for j, (src, buf) in enumerate(((x_ref, xbuf), (dh1_ref, hbuf)))
            ]

        tiles = SLOT // QB
        for c in loads(0):
            c.start()
        total = jnp.zeros(gain_ref.shape, F32)
        for i in range(tiles):
            if i + 1 < tiles:
                for c in loads(i + 1):
                    c.start()
            for what in TAIL[i]:
                move(what)
            for c in loads(i):
                c.wait()
            rows = slice(i * QB, (i + 1) * QB)
            dv, dgain = norm_back(xbuf[i % 2].astype(F32), gain_ref[...], gt_ref[rows, :])
            gt_ref[rows, :] = hbuf[i % 2] + dv
            total = total + dgain
        gown[...] = jnp.concatenate([total, dgm_ref[...], jnp.zeros((6, D), F32)], axis=0)
        gains.run(0)
        move((3, 4))
        gains.run(1)
        move((3, 5))
        gains.run(2)
        finish()
        move((3, 6))
        move((3, 7))
        gains.end(gains_ref)
        for i in [STEPS] + list(range(max(0, STEPS - sets), STEPS)):
            chunks[i].end()
        for c in tile_copies():
            c.wait()
        for s in range(1, nz):
            to_owner(s).wait_send()
        reduce.end()


def second_half(length, da, wo, q, k, v, o, st, nma, cos, sin, wq, wk, wv, gain, dgm, x, dh1, mine, got, far, b1):
    tok = x.shape[0]
    nz, _, fs, dz = far.shape
    sds = jax.ShapeDtypeStruct
    once = dict(pipeline_mode=pl.Buffered(1))
    full = pl.BlockSpec((tok, D), lambda g: (0, 0), **once)
    blk = pl.BlockSpec((tok, GW), lambda g: (0, g))
    wblk = pl.BlockSpec((D, GW), lambda g: (0, g))
    vec = pl.BlockSpec((1, D), lambda g: (0, 0), **once)
    tab = pl.BlockSpec((tok, 128), lambda g: (0, 0), **once)
    hbm = pl.BlockSpec(memory_space=pl.ANY)
    sem = pltpu.SemaphoreType.DMA
    vmem = lambda *shape: pltpu.VMEM(shape, BF16)
    half = D // 2
    block = half // 4
    small = block // nz
    sets = 3
    piece = (3, fs, dz)

    def buffers(n, lead, width):
        return [
            vmem(*n, lead, D, width), vmem(*n, lead, half, width), vmem(*n, lead, block, width), vmem(*n, lead, block, width),
            vmem(*n, lead, block, width), vmem(*n, nz, lead, small, width), vmem(*n, lead, small, width),
        ]

    return pl.pallas_call(
        functools.partial(second_kernel, nz),
        grid=(STEPS,),
        in_specs=[
            pl.BlockSpec(memory_space=pltpu.SMEM), full, pl.BlockSpec((GW, D), lambda g: (g, 0)), blk, blk, blk, blk, tab,
            tab, tab, wblk, wblk, wblk, vec, vec, *[hbm] * 8,
        ],
        out_specs=[full, blk, pl.BlockSpec((8, D), lambda g: (0, 0), **once), hbm, hbm, hbm],
        out_shape=[
            sds((tok, D), F32), sds((tok, D), F32), sds((8, D), F32), sds((1, D, D), BF16), sds((3, D, D), BF16), sds((2, *piece), BF16),
        ],
        scratch_shapes=[
            pltpu.VMEM((tok, GW), F32), vmem(tok, GW), vmem(tok, GW), vmem(tok, GW), vmem(2, QB, D), pltpu.VMEM((2, QB, D), F32), sem((2, 2)),
            *buffers((), 1, D), *buffers((sets,), 3, GW),
            vmem(D, tok), vmem(2, 3, *piece), vmem(4, *piece), vmem(nz, *piece), vmem(nz, *piece), vmem(nz, *piece), vmem(nz, *piece),
            pltpu.VMEM((8, D), F32), pltpu.VMEM((8, D), F32), pltpu.VMEM((4, 8, D), F32), pltpu.VMEM((nz, 8, D), F32),
            sem((STEPS + 1, 19)), sem((STEPS + 1, 19)), sem((STEPS + 1,)), sem((3 + nz,)), sem((3 + nz,)),
            sem((8,)), sem((2, 3)), sem((4,)), sem, sem((nz,)), sem((nz,)), sem((nz,)), sem((nz,)), sem, sem,
        ],
        compiler_params=pltpu.CompilerParams(vmem_limit_bytes=63 * MIB, collective_id=2, has_side_effects=True),
        cost_estimate=pl.CostEstimate(flops=50 * 10**9, bytes_accessed=80 * 10**6, transcendentals=10**7),
        name="second_half",
    )(length, da, wo, q, k, v, o, st, cos, sin, wq, wk, wv, gain, dgm, x, dh1, nma, o, mine, got, far, b1)


def mlp_out_kernel(nk, nc, nz, zs_ref, w_ref, hs_ref, dgs_ref, dus_ref, h1_ref, gain_ref, dy_ref, mixed_ref, dh1_ref, da_ref, dgain_ref, branch_ref, dnm_ref):
    fs, dz = w_ref.shape[4:]
    i = pl.program_id(0)
    for s in range(nz):
        b = d = None
        for k in range(nk):
            for c in range(nc):
                rows = pl.ds(c * fs, fs)
                b_one = tn(hs_ref[k, rows, :], w_ref[k, c, s, 2])
                d_one = tn(dgs_ref[k, rows, :], w_ref[k, c, s, 0]) + tn(dus_ref[k, rows, :], w_ref[k, c, s, 1])
                b, d = (b_one, d_one) if b is None else (b + b_one, d + d_one)
        at = pl.ds(pl.multiple_of(zs_ref[s] * dz, dz), dz)
        branch_ref[:, at] = b
        dnm_ref[:, at] = d
    h1 = h1_ref[...]
    mixed_ref[...] = (h1 + branch_ref[...]).astype(BF16)
    dv, dgain = norm_back(h1, gain_ref[...], dnm_ref[...])
    dh1 = dy_ref[...].astype(F32) + dv
    dh1_ref[...] = dh1
    da_ref[...] = dh1.astype(BF16)

    @pl.when(i == 0)
    def _():
        dgain_ref[...] = jnp.zeros_like(dgain_ref)

    dgain_ref[...] += dgain


def mlp_out(zs, w, hs, dgs, dus, h1, gain, dy):
    nk, nc, nz = w.shape[:3]
    tok = h1.shape[0]
    tile = 256
    wspec = pl.BlockSpec(w.shape, lambda i: (0,) * 6, pipeline_mode=pl.Buffered(1))
    hspec = pl.BlockSpec((nk, hs.shape[1], tile), lambda i: (0, 0, i))
    row = pl.BlockSpec((tile, D), lambda i: (i, 0))
    vec = pl.BlockSpec((1, D), lambda i: (0, 0))
    sds = jax.ShapeDtypeStruct
    return pl.pallas_call(
        functools.partial(mlp_out_kernel, nk, nc, nz),
        grid=(tok // tile,),
        in_specs=[pl.BlockSpec(memory_space=pltpu.SMEM), wspec, hspec, hspec, hspec, row, vec, row],
        out_specs=[row, row, row, vec],
        out_shape=[sds((tok, D), BF16), sds((tok, D), F32), sds((tok, D), BF16), sds((1, D), F32)],
        scratch_shapes=[pltpu.VMEM((tile, D), F32)] * 2,
        compiler_params=pltpu.CompilerParams(vmem_limit_bytes=58 * MIB),
        cost_estimate=pl.CostEstimate(flops=18 * 10**9, bytes_accessed=45 * 10**6, transcendentals=0),
        name="mlp_out",
    )(zs, w, hs, dgs, dus, h1, gain, dy)


def tokens_kernel(n, *refs):
    parts, (wq_ref, wk_ref, wv_ref, x_ref, gain_ref, dh1_ref, out_ref, dgain_ref) = refs[: 3 * n], refs[3 * n :]
    i = pl.program_id(0)
    total = None
    for j, w_ref in enumerate((wq_ref, wk_ref, wv_ref)):
        d = parts[j * n][...] if n == 1 else jnp.concatenate([r[...] for r in parts[j * n : (j + 1) * n]], axis=1)
        t = nt(d, w_ref[...])
        total = t if total is None else total + t
    dv, dgain = norm_back(x_ref[...].astype(F32), gain_ref[...], total)
    out_ref[...] = dh1_ref[...] + dv

    @pl.when(i == 0)
    def _():
        dgain_ref[...] = jnp.zeros_like(dgain_ref)

    dgain_ref[...] += dgain


def tokens_grad(dqs, dks, dvs, wq, wk, wv, x, gain, dh1):
    n = len(dqs)
    tok = x.shape[0]
    tile = 256
    row = pl.BlockSpec((tile, D), lambda i: (i, 0))
    full = pl.BlockSpec((D, D), lambda i: (0, 0))
    vec = pl.BlockSpec((1, D), lambda i: (0, 0))
    sds = jax.ShapeDtypeStruct
    return pl.pallas_call(
        functools.partial(tokens_kernel, n),
        grid=(tok // tile,),
        in_specs=[pl.BlockSpec((tile, d.shape[1]), lambda i: (i, 0)) for d in (*dqs, *dks, *dvs)] + [full, full, full, row, vec, row],
        out_specs=[row, vec],
        out_shape=[sds((tok, D), F32), sds((1, D), F32)],
        compiler_params=pltpu.CompilerParams(vmem_limit_bytes=40 * MIB),
        cost_estimate=pl.CostEstimate(flops=7 * 10**9, bytes_accessed=24 * 10**6, transcendentals=0),
        name="tokens_grad",
    )(*dqs, *dks, *dvs, wq, wk, wv, x, gain, dh1)
def body(
    paired, tokens, first_values, lengths, w_query, w_key, w_value, w_out, norm_attn, norm_mlp, w_gate, w_up, w_down, grad_out
):
    nz = lax.axis_size("ma")
    r = lax.axis_index("rows")
    cos, sin = (jnp.asarray(t) for t in rope_tables())
    gain_a, gain_m = norm_attn[None], norm_mlp[None]
    tile = jnp.stack([w_gate.T, w_up.T, w_down])
    if paired:
        fs = tile.shape[1] // 2
        own = lax.dynamic_slice_in_dim(tile, r * fs, fs, axis=1)
        q, k, v, o, st, nma, mixed, dh1, da, dgain_m, mine, got, far, b1, _ = first_half(
            lengths, tokens, gain_a, w_query, w_key, w_value, first_values, cos, sin, w_out, gain_m, grad_out, own, nz
        )
        grad_tokens, grad_first, gains, grad_wout, grads, tiles = second_half(
            lengths, da, w_out, q, k, v, o, st, nma, cos, sin, w_query, w_key, w_value, gain_a, dgain_m, tokens, dh1,
            mine, got, far, b1,
        )
        gain_grads = gains[0], gains[1]
        grad_wout = grad_wout[0].astype(F32)
        grad_q, grad_k, grad_v = (grads[j].astype(F32) for j in range(3))
        tiles = tiles.transpose(1, 0, 2, 3).reshape(tile.shape).astype(F32)
    else:
        w = lax.all_gather(lax.all_gather(tile, "ma", axis=0), "ha", axis=0)[:, None]
        zs = jnp.arange(nz, dtype=jnp.int32)
        q, k, v, o, st, nma, h1, nmm = attention_forward(
            lengths, tokens, gain_a, w_query, w_key, w_value, first_values, cos, sin, w_out, gain_m
        )
        nmat, ot, nmmt, dyt = prepare(nma, o, nmm, grad_out)
        done = [mlp_block(zs, [[w[i, 0, j] for j in range(nz)]], nmmt, dyt, nmm, grad_out) for i in range(w.shape[0])]
        hs, dgs, dus, mine = (jnp.stack([d[j] for d in done]) for j in range(4))
        mixed, dh1, da, dgain_m = mlp_out(zs, w, hs, dgs, dus, h1, gain_m, grad_out)
        dq, dk, dv, grad_first, grads = attention_backward(
            0, H // GROUP, lengths, da, w_out, q, k, v, o, st, nmat, cos, sin
        )
        grad_tokens, dgain_a = tokens_grad([dq], [dk], [dv], w_query, w_key, w_value, tokens, gain_a, dh1)
        part = lax.psum_scatter(lax.psum_scatter(mine, "ha", scatter_dimension=0), "ma", scatter_dimension=0)
        tiles = lax.psum(part, "rows").astype(F32)
        grad_wout, grads, *gains = lax.psum((wout_grad(ot, da), grads, dgain_a, dgain_m), ("rows", "ha", "ma"))
        grad_wout = grad_wout.astype(F32)
        grad_q, grad_k, grad_v = (grads[j].astype(F32) for j in range(3))
        gain_grads = [v[0] for v in gains]
    return (
        mixed, grad_tokens, grad_first, grad_q, grad_k, grad_v, grad_wout, gain_grads[0], gain_grads[1],
        tiles[0].T, tiles[1].T, tiles[2],
    )


def solution(mesh):
    tok = P(("rows", "ha", "ma"), None)
    gate, down = P("ma", "ha"), P("ha", "ma")
    return jax.shard_map(
        functools.partial(body, mesh.shape["rows"] == 2),
        mesh=mesh,
        in_specs=(tok, tok, P(("rows", "ha", "ma")), P(), P(), P(), P(), P(), P(), gate, gate, down, tok),
        out_specs=(tok, tok, tok, P(), P(), P(), P(), P(), P(), gate, gate, down),
        check_vma=False,
    )
```

```python
import functools
import math

import jax
import jax.numpy as jnp
import numpy as np
from jax import lax
from jax.experimental import pallas as pl
from jax.experimental.pallas import tpu as pltpu
from jax.sharding import PartitionSpec as P

D = 1024
H = 16
HD = 64
SLOT = 1024
EPS = 1e-06
GROUP = 4
GW = GROUP * HD
QB = 256
SCALE = 1.0 / math.sqrt(HD)
C2 = SCALE * math.log2(math.e)
F32 = jnp.float32
BF16 = jnp.bfloat16
MIB = 1 << 20


def nn(a, b):
    return lax.dot_general(a, b, (((1,), (0,)), ((), ())), preferred_element_type=F32)


def nt(a, b):
    return lax.dot_general(a, b, (((1,), (1,)), ((), ())), preferred_element_type=F32)


def tn(a, b):
    return lax.dot_general(a, b, (((0,), (0,)), ((), ())), preferred_element_type=F32)


def rope_tables():
    place = np.arange(SLOT, dtype=np.float32)
    frequency = np.float32(10000.0) ** (-np.arange(HD // 2, dtype=np.float32) * np.float32(2.0) / np.float32(HD))
    angles = place[:, None] * frequency[None, :]
    cosine, sine = np.cos(angles), np.sin(angles)
    cos_row = np.concatenate([cosine] * 4, axis=1)
    sin_row = np.concatenate([-sine, sine, -sine, sine], axis=1)
    return cos_row.astype(np.float32), sin_row.astype(np.float32)


def lanes(shape):
    return lax.broadcasted_iota(jnp.int32, shape, 1)


def partner(v):
    first = (lanes(v.shape) & 63) < 32
    return jnp.where(first, pltpu.roll(v, 96, 1), pltpu.roll(v, 32, 1))


def turn(v, cos, sin):
    parts = []
    for at in range(0, v.shape[1], 128):
        piece = v[:, at : at + 128]
        parts.append(piece * cos + partner(piece) * sin)
    return jnp.concatenate(parts, axis=1)


def low3(v):
    hi = v.astype(BF16).astype(F32)
    rest = v - hi
    mid = rest.astype(BF16).astype(F32)
    return hi, mid, rest - mid


def forward_start(x_ref, gain_ref, nma_ref, h1_ref, st_ref):
    x = x_ref[...].astype(F32)
    r = lax.rsqrt(jnp.mean(x * x, axis=-1, keepdims=True) + EPS)
    nma_ref[...] = (x * r * gain_ref[...]).astype(BF16)
    h1_ref[...] = x
    st_ref[...] = jnp.zeros_like(st_ref)


def forward_end(h1_ref, gain_m_ref, nmm_ref):
    h = h1_ref[...]
    r = lax.rsqrt(jnp.mean(h * h, axis=-1, keepdims=True) + EPS)
    nmm_ref[...] = (h * r * gain_m_ref[...]).astype(BF16)


def forward_group(
    g, length, nma_ref, wq_ref, wk_ref, wv_ref, fv_ref, cos_ref, sin_ref, wo_ref,
    q_ref, k_ref, v_ref, o_ref, st_ref, h1_ref, between=None,
):
    nm = nma_ref[...]
    cos, sin = cos_ref[...], sin_ref[...]
    q_ref[...] = turn(nn(nm, wq_ref[...]), cos, sin).astype(BF16)
    k_ref[...] = turn(nn(nm, wk_ref[...]), cos, sin).astype(BF16)
    v_ref[...] = (0.5 * nn(nm, wv_ref[...]) + 0.5 * fv_ref[...].astype(F32)).astype(BF16)
    tile = (SLOT, 128)
    lane = lanes(tile)
    row = lax.broadcasted_iota(jnp.int32, tile, 0)
    k_extra = jnp.where((lane == 0) & (row >= length), -1e30, 0.0).astype(BF16)
    q_extra = jnp.where(lane == 0, 1.0, 0.0).astype(BF16)
    ones = jnp.ones(tile, BF16)
    low_lane = lane < HD
    qlane = lanes((QB, 128))
    causal = lax.broadcasted_iota(jnp.int32, (QB, QB), 1) <= lax.broadcasted_iota(jnp.int32, (QB, QB), 0)
    for pair in range(GROUP // 2):
        cols = pl.ds(pair * 128, 128)
        qp, kp, vp = q_ref[:, cols], k_ref[:, cols], v_ref[:, cols]
        q_ext = jnp.concatenate([qp, q_extra], axis=1)
        k_exts, v_exts = [], []
        for e in range(2):
            mine = low_lane if e == 0 else ~low_lane
            k_exts.append(jnp.concatenate([jnp.where(mine, kp, 0), k_extra], axis=1))
            v_exts.append(jnp.concatenate([jnp.where(mine, vp, 0), ones], axis=1))
        for qb in range(SLOT // QB):
            if between is not None:
                between(pair, qb)
            rows = slice(qb * QB, (qb + 1) * QB)
            top = (qb + 1) * QB
            out = None
            stats = st_ref[rows, :].astype(F32)
            for e in range(2):
                s = nt(q_ext[rows], k_exts[e][:top])
                diag = jnp.where(causal, s[:, top - QB :], -1e30)
                s = diag if qb == 0 else jnp.concatenate([s[:, : top - QB], diag], axis=1)
                m = jnp.max(s, axis=-1, keepdims=True)
                p = jnp.exp2((s - m) * C2).astype(BF16)
                res = nn(p, v_exts[e][:top])
                total = res[:, 128:]
                part = res[:, :128] / total
                out = part if out is None else out + part
                hi, mid, rest = low3(m + jnp.log2(total) * (1.0 / C2))
                base = 8 * (g * GROUP + pair * 2 + e)
                stats = jnp.where(qlane == base, hi, stats)
                stats = jnp.where(qlane == base + 1, mid, stats)
                stats = jnp.where(qlane == base + 2, rest, stats)
                stats = jnp.where(qlane == base + 3, 1.0, stats)
            o_ref[rows, cols] = out.astype(BF16)
            st_ref[rows, :] = stats.astype(BF16)
    h1_ref[...] += nn(o_ref[...], wo_ref[...])


def fwd_kernel(
    len_ref, x_ref, gain_ref, wq_ref, wk_ref, wv_ref, fv_ref, cos_ref, sin_ref, wo_ref, gain_m_ref,
    q_ref, k_ref, v_ref, o_ref, st_ref, nma_ref, h1_ref, nmm_ref,
):
    g = pl.program_id(0)

    @pl.when(g == 0)
    def _():
        forward_start(x_ref, gain_ref, nma_ref, h1_ref, st_ref)

    forward_group(
        g, len_ref[0], nma_ref, wq_ref, wk_ref, wv_ref, fv_ref, cos_ref, sin_ref, wo_ref,
        q_ref, k_ref, v_ref, o_ref, st_ref, h1_ref,
    )

    @pl.when(g == pl.num_programs(0) - 1)
    def _():
        forward_end(h1_ref, gain_m_ref, nmm_ref)


def attention_forward(length, x, gain, wq, wk, wv, fv, cos, sin, wo, gain_m):
    whole = lambda *_: (0, 0)
    col = lambda g, *_: (0, g)
    tok = x.shape[0]
    full = pl.BlockSpec((tok, D), whole)
    blk = pl.BlockSpec((tok, GW), col)
    wblk = pl.BlockSpec((D, GW), col)
    vec = pl.BlockSpec((1, D), whole)
    tab = pl.BlockSpec((tok, 128), whole)
    sds = jax.ShapeDtypeStruct
    return pl.pallas_call(
        fwd_kernel,
        grid_spec=pltpu.PrefetchScalarGridSpec(
            num_scalar_prefetch=1,
            grid=(H // GROUP,),
            in_specs=[full, vec, wblk, wblk, wblk, blk, tab, tab, pl.BlockSpec((GW, D), lambda g, *_: (g, 0)), vec],
            out_specs=[blk, blk, blk, blk, tab, full, full, full],
        ),
        out_shape=[sds((tok, D), BF16)] * 4 + [sds((tok, 128), BF16), sds((tok, D), BF16), sds((tok, D), F32), sds((tok, D), BF16)],
        compiler_params=pltpu.CompilerParams(vmem_limit_bytes=56 * MIB),
        cost_estimate=pl.CostEstimate(flops=30 * 10**9, bytes_accessed=40 * 10**6, transcendentals=10**7),
        name="attention_forward",
    )(length, x, gain, wq, wk, wv, fv, cos, sin, wo, gain_m)


def prep_kernel(*refs):
    count = len(refs) // 2
    for src, dst in zip(refs[:count], refs[count:]):
        dst[...] = src[...].T


def prepare(*arrays):
    vm = pl.BlockSpec(memory_space=pltpu.VMEM)
    tok = arrays[0].shape[0]
    return pl.pallas_call(
        prep_kernel,
        in_specs=[vm] * len(arrays),
        out_specs=[vm] * len(arrays),
        out_shape=[jax.ShapeDtypeStruct((D, tok), BF16)] * len(arrays),
        compiler_params=pltpu.CompilerParams(vmem_limit_bytes=30 * MIB),
        cost_estimate=pl.CostEstimate(flops=10**9, bytes_accessed=4 * len(arrays) * 10**6, transcendentals=0),
        name="prepare",
    )(*arrays)


def wout_kernel(ot_ref, da_ref, out_ref):
    out_ref[...] = nn(ot_ref[...], da_ref[...]).astype(BF16)


def wout_grad(ot, da):
    vm = pl.BlockSpec(memory_space=pltpu.VMEM)
    return pl.pallas_call(
        wout_kernel,
        in_specs=[vm] * 2,
        out_specs=vm,
        out_shape=jax.ShapeDtypeStruct((D, D), BF16),
        compiler_params=pltpu.CompilerParams(vmem_limit_bytes=30 * MIB),
        cost_estimate=pl.CostEstimate(flops=2 * 10**9, bytes_accessed=6 * 10**6, transcendentals=0),
        name="wout_grad",
    )(ot, da)


def backward_group(
    g, length, da_ref, wo_ref, q_ref, k_ref, v_ref, o_ref, st_ref, cos_ref, sin_ref, dq_ref, dk_ref, dv_ref, gf_ref, dq_acc, between=None
):
    do_all = nt(da_ref[...], wo_ref[...]).astype(BF16)
    prod = do_all.astype(F32) * o_ref[...].astype(F32)
    hi = prod.astype(BF16)
    lo = (prod - hi.astype(F32)).astype(BF16)
    sel_row = lax.broadcasted_iota(jnp.int32, (GW, 128), 0) // HD + g * GROUP
    sel_lane = lanes((GW, 128))
    pick = jnp.where((sel_lane // 8 == sel_row) & ((sel_lane & 7) >= 4) & ((sel_lane & 7) <= 5), 1.0, 0.0).astype(BF16)
    delta = nn(hi, pick) + nn(lo, pick)
    tile = (SLOT, 128)
    lane = lanes(tile)
    d_hi = delta.astype(BF16)
    d_ext = jnp.where((lane & 7) == 4, d_hi.astype(F32), delta - d_hi.astype(F32)).astype(BF16)
    row = lax.broadcasted_iota(jnp.int32, tile, 0)
    dead = row >= length
    low_lane = lane < HD
    st = st_ref[...]
    visible = lax.broadcasted_iota(jnp.int32, (QB, QB), 0) <= lax.broadcasted_iota(jnp.int32, (QB, QB), 1)
    dq_acc[...] = jnp.zeros_like(dq_acc)
    for pair in range(GROUP // 2):
        cols = pl.ds(pair * 128, 128)
        qp, kp, vp = q_ref[:, cols], k_ref[:, cols], v_ref[:, cols]
        dop = do_all[:, pair * 128 : pair * 128 + 128]
        q_ext = jnp.concatenate([qp, st], axis=1)
        do_ext = jnp.concatenate([dop, d_ext], axis=1)
        heads = []
        for e in range(2):
            mine = low_lane if e == 0 else ~low_lane
            at = lane - 8 * (g * GROUP + pair * 2 + e)
            k_x = jnp.where((at >= 0) & (at < 3), -1.0, jnp.where((at == 3) & dead, -1e30, 0.0)).astype(BF16)
            v_x = jnp.where((at >= 4) & (at < 6), -1.0, 0.0).astype(BF16)
            k_m = jnp.where(mine, kp, 0)
            heads.append((
                k_m,
                jnp.concatenate([k_m, k_x], axis=1),
                jnp.concatenate([jnp.where(mine, vp, 0), v_x], axis=1),
                jnp.where(mine, qp, 0),
                jnp.where(mine, dop, 0),
            ))
        for kb in range(SLOT // QB):
            if between is not None:
                between(pair, kb)
            rows = slice(kb * QB, (kb + 1) * QB)
            start = kb * QB
            dk = dv = None
            for k_m, k_ext, v_ext, q_m, do_m in heads:
                st_ = nt(k_ext[rows], q_ext[start:])
                dp = nt(v_ext[rows], do_ext[start:])
                p = jnp.exp2(st_ * C2)
                diag = jnp.where(visible, p[:, :QB], 0.0)
                p = diag if kb == SLOT // QB - 1 else jnp.concatenate([diag, p[:, QB:]], axis=1)
                ds = (p * dp).astype(BF16)
                p = p.astype(BF16)
                dv_e = nn(p, do_m[start:])
                dk_e = nn(ds, q_m[start:])
                dk = dk_e if dk is None else dk + dk_e
                dv = dv_e if dv is None else dv + dv_e
                dq_acc[start:, cols] += tn(ds, k_m[rows])
            dk = dk * SCALE
            cos, sin = cos_ref[rows, :], sin_ref[rows, :]
            dk_ref[rows, cols] = (dk * cos - partner(dk) * sin).astype(BF16)
            half = 0.5 * dv
            gf_ref[rows, cols] = half
            dv_ref[rows, cols] = half.astype(BF16)
    cos, sin = cos_ref[...], sin_ref[...]
    for pair in range(GROUP // 2):
        cols = pl.ds(pair * 128, 128)
        dq = dq_acc[:, cols] * SCALE
        dq_ref[:, cols] = (dq * cos - partner(dq) * sin).astype(BF16)


def bwd_kernel(
    first_group, len_ref, da_ref, wo_ref, q_ref, k_ref, v_ref, o_ref, st_ref, nmt_ref, cos_ref, sin_ref,
    dq_ref, dk_ref, dv_ref, gf_ref, gw_ref, dq_acc,
):
    g = pl.program_id(0) + first_group
    backward_group(
        g, len_ref[0], da_ref, wo_ref, q_ref, k_ref, v_ref, o_ref, st_ref, cos_ref, sin_ref, dq_ref, dk_ref, dv_ref, gf_ref, dq_acc
    )
    for j, ref in enumerate((dq_ref, dk_ref, dv_ref)):
        gw_ref[j] = nn(nmt_ref[...], ref[...]).astype(BF16)


def attention_backward(first_group, groups, length, da, wo, q, k, v, o, st, nmt, cos, sin):
    whole = lambda *_: (0, 0)
    tok = da.shape[0]
    full = pl.BlockSpec((tok, D), whole)
    blk_in = pl.BlockSpec((tok, GW), lambda g, *_: (0, g + first_group))
    blk = pl.BlockSpec((tok, GW), lambda g, *_: (0, g))
    tab = pl.BlockSpec((tok, 128), whole)
    sds = jax.ShapeDtypeStruct
    width = groups * GW
    return pl.pallas_call(
        functools.partial(bwd_kernel, first_group),
        grid_spec=pltpu.PrefetchScalarGridSpec(
            num_scalar_prefetch=1,
            grid=(groups,),
            in_specs=[full, pl.BlockSpec((GW, D), lambda g, *_: (g + first_group, 0)), blk_in, blk_in, blk_in, blk_in, tab, pl.BlockSpec((D, tok), whole), tab, tab],
            out_specs=[blk, blk, blk, blk, pl.BlockSpec((3, D, GW), lambda g, *_: (0, 0, g))],
            scratch_shapes=[pltpu.VMEM((tok, GW), F32)],
        ),
        out_shape=[sds((tok, width), BF16)] * 3 + [sds((tok, width), F32), sds((3, D, width), BF16)],
        compiler_params=pltpu.CompilerParams(vmem_limit_bytes=56 * MIB),
        cost_estimate=pl.CostEstimate(flops=10 * 10**9 * groups, bytes_accessed=10 * 10**6, transcendentals=groups * 3 * 10**6),
        name="attention_backward",
    )(length, da, wo, q, k, v, o, st, nmt, cos, sin)


def sig(v):
    return 1.0 / (1.0 + jnp.exp(-v))


def mlp_kernel(nc, nz, zs_ref, *refs):
    pieces = refs[: nc * nz]
    nmt_ref, dyt_ref, nm_ref, dy_ref, h_ref, dg_ref, du_ref = refs[nc * nz : nc * nz + 7]
    outs = refs[nc * nz + 7 :]
    fs = pieces[0].shape[1]
    dz = pieces[0].shape[2]
    starts = [pl.multiple_of(zs_ref[s] * dz, dz) for s in range(nz)]
    for c in range(nc):
        gate = up = dh = None
        for s in range(nz):
            w_ref = pieces[c * nz + s]
            at = pl.ds(starts[s], dz)
            nmt, dyt = nmt_ref[at, :], dyt_ref[at, :]
            parts = nn(w_ref[0], nmt), nn(w_ref[1], nmt), nn(w_ref[2], dyt)
            gate, up, dh = parts if gate is None else (gate + parts[0], up + parts[1], dh + parts[2])
        sg = sig(gate)
        silu = gate * sg
        rows = pl.ds(c * fs, fs)
        h = (silu * up).astype(BF16)
        dg = (dh * up * (sg * (1.0 + gate * (1.0 - sg)))).astype(BF16)
        du = (dh * silu).astype(BF16)
        h_ref[rows, :], dg_ref[rows, :], du_ref[rows, :] = h, dg, du
        for s in range(nz):
            at = pl.ds(starts[s], dz)
            nm, dy = nm_ref[:, at], dy_ref[:, at]
            outs[c][s, 0] = nn(dg, nm).astype(BF16)
            outs[c][s, 1] = nn(du, nm).astype(BF16)
            outs[c][s, 2] = nn(h, dy).astype(BF16)


def mlp_block(zs, pieces, nmt, dyt, nm, dy):
    nc, nz = len(pieces), len(pieces[0])
    _, fs, dz = pieces[0][0].shape
    tok = nm.shape[0]
    sds = jax.ShapeDtypeStruct
    vm = pl.BlockSpec(memory_space=pltpu.VMEM)
    return pl.pallas_call(
        functools.partial(mlp_kernel, nc, nz),
        in_specs=[pl.BlockSpec(memory_space=pltpu.SMEM)] + [vm] * (nc * nz + 4),
        out_specs=[vm] * (3 + nc),
        out_shape=[sds((nc * fs, tok), BF16)] * 3 + [sds((nz, 3, fs, dz), BF16)] * nc,
        compiler_params=pltpu.CompilerParams(vmem_limit_bytes=44 * MIB),
        cost_estimate=pl.CostEstimate(flops=12 * nc * fs * D * tok, bytes_accessed=15 * 10**6, transcendentals=nc * fs * tok),
        name="mlp_block",
    )(zs, *[p for c in pieces for p in c], nmt, dyt, nm, dy)


MESH = pl.DeviceIdType.MESH
RING = (0, 1, 3, 2)
STEPS = H // GROUP
TURNS = (0, 1, 3, 2)


def table(index, values):
    out = values[0]
    for i, v in enumerate(values[1:], 1):
        out = jnp.where(index == i, v, out)
    return out


def norm_back(v, gain, grad):
    ms = jnp.mean(v * v, axis=-1, keepdims=True) + EPS
    r = lax.rsqrt(ms)
    gg = grad * gain
    inner = jnp.mean(gg * v, axis=-1, keepdims=True)
    dv = r * gg - v * (inner * r * r * r)
    dgain = jnp.sum(grad * v * r, axis=0, keepdims=True)
    return dv, dgain


class Places:
    def __init__(self, nz):
        self.nz = nz
        self.r, self.a, self.z = (lax.axis_index(n) for n in ("rows", "ha", "ma"))
        self.spot = table(self.a, [RING.index(i) for i in range(4)])
        self.right_to = table(self.spot, [RING[(i + 1) % 4] for i in range(4)])
        self.left_to = table(self.spot, [RING[(i + 3) % 4] for i in range(4)])
        self.far_to = table(self.spot, [RING[(i + 2) % 4] for i in range(4)])
        self.arrivals = [0] + [table(self.z, v) for v in ((3, 1, 3, 1), (2, 3, 1, 2), (1, 2, 2, 3))]

    def at(self, **moved):
        place = {"rows": self.r, "ha": self.a, "ma": self.z, **moved}
        return (place["rows"], place["ha"], place["ma"])

    def meet(self, others):
        barrier = pltpu.get_barrier_semaphore()
        for other in others:
            pl.semaphore_signal(barrier, inc=1, device_id=other, device_id_type=MESH)
        return lambda: pl.semaphore_wait(barrier, len(others))


def remote(src, dst, send, recv, device):
    return pltpu.make_async_remote_copy(
        src_ref=src, dst_ref=dst, send_sem=send, recv_sem=recv, device_id=device, device_id_type=MESH
    )


class Gather:
    def __init__(self, places, own_ref, w_ref, sems):
        self.p, self.own, self.w = places, own_ref, w_ref
        self.recv, self.swap_recv, self.z_send, self.right_send, self.left_send, self.far_send, self.swap_send, self.local = sems
        self.fs = own_ref.shape[1]

    def part(self, k, s, c=0):
        return self.w.at[k, s, :, pl.ds(c * self.fs, self.fs)]

    def copy(self, src, dst, send, device):
        return remote(self.part(*src), self.part(*dst), send, self.recv.at[dst], device)

    def right(self, s):
        return self.copy((0, s), (1, s), self.right_send, self.p.at(ha=self.p.right_to))

    def left(self, s):
        return self.copy((0, s), (3, s), self.left_send, self.p.at(ha=self.p.left_to))

    def far_copy(self, i):
        s = self.p.arrivals[i]
        if i % 2 == 0:
            return self.copy((1, s), (2, s), self.far_send, self.p.at(ha=self.p.right_to))
        return self.copy((3, s), (2, s), self.far_send, self.p.at(ha=self.p.left_to))

    def swap(self, k, s):
        return remote(self.part(k, s), self.part(k, s, 1), self.swap_send, self.swap_recv.at[k], self.p.at(rows=1 - self.p.r))

    def arrived(self, k, s):
        self.copy((k, s), (k, s), self.local, self.p.at(rows=1 - self.p.r)).wait_recv()

    def all_swapped(self, k):
        half = self.w.at[k, :, :, pl.ds(self.fs, self.fs)]
        remote(half, half, self.local, self.swap_recv.at[k], self.p.at(rows=1 - self.p.r)).wait_recv()

    def line(self, d, act, wait):
        nz, z = self.p.nz, self.p.z

        def up(cond):
            pl.when(cond & (z < nz - 1))(
                lambda: act(self.copy((0, d), (0, d + 1), self.z_send.at[0, d], self.p.at(ma=z + 1)))
            )

        def down(cond):
            pl.when(cond & (z >= 1))(
                lambda: act(self.copy((0, (nz - d) % nz), (0, nz - d - 1), self.z_send.at[1, d], self.p.at(ma=z - 1)))
            )

        if d and wait:
            pl.when(z >= d)(lambda: self.arrived(0, d))
            pl.when(z + d <= nz - 1)(lambda: self.arrived(0, nz - d))
        if d < nz - 1:
            up(z >= d)
            down(z + d <= nz - 1)

    def begin(self):
        p = self.p
        wait = p.meet([
            p.at(ma=(p.z + 1) % p.nz), p.at(ma=(p.z + p.nz - 1) % p.nz), p.at(ha=p.right_to), p.at(ha=p.left_to), p.at(rows=1 - p.r)
        ])
        mine = pltpu.make_async_copy(self.own, self.part(0, 0), self.local)
        mine.start()
        mine.wait()
        wait()
        self.pass_line(0)
        self.spread(0)

    def pass_line(self, d):
        self.line(d, lambda c: c.start(), True)

    def spread(self, i):
        s = self.p.arrivals[i]
        self.right(s).start()
        self.left(s).start()
        self.swap(0, s).start()

    def sides(self, i):
        s = self.p.arrivals[i]
        self.arrived(1, s)
        self.arrived(3, s)
        self.swap(1, s).start()
        self.swap(3, s).start()

    def far(self, i):
        self.far_copy(i).start()

    def opposite(self, i):
        s = self.p.arrivals[i]
        self.arrived(2, s)
        self.swap(2, s).start()

    def end(self):
        for i in range(self.p.nz):
            self.line(i, lambda c: c.wait_send(), False)
        here = self.p.at(rows=1 - self.p.r)
        column = self.w.at[0, :, :, pl.ds(0, self.fs)]
        for send in (self.right_send, self.left_send, self.far_send):
            remote(column, column, send, self.local, here).wait_send()
        whole = self.w.at[:, :, :, pl.ds(0, self.fs)]
        remote(whole, whole, self.swap_send, self.local, here).wait_send()


class Reduce:
    BY_LEFT = (1, 3)

    def __init__(self, places, mine_ref, got_ref, steps, inb, pool, sinks, extras, sems):
        self.p, self.mine, self.got, self.steps, self.inb, self.pool = places, mine_ref, got_ref, steps, inb, pool
        self.sinks, self.extras = sinks, extras
        self.load_sem, self.send, self.spare = sems
        self.order = [at for group in steps for at in group]
        self.sent = [at for at in self.order if at[0]]
        self.first = {group[0] for group in steps}
        self.last = {group[-1] for group in steps}

    def columns(self, s):
        nz, dz = self.p.nz, self.inb.shape[4]
        return pl.ds(pl.multiple_of((self.p.z + nz - s) % nz * dz, dz), dz)

    def loads(self, i):
        k, s = self.order[i]
        slot = i % 2
        at = self.columns(s)
        sources = [self.mine.at[k, :, :, at], self.got.at[k, :, :, at]] + self.extras(k, s)[0]
        return [pltpu.make_async_copy(src, self.inb.at[slot, j], self.load_sem.at[slot, j]) for j, src in enumerate(sources)]

    def begin(self, group):
        at = self.order.index(self.steps[group][0])
        for i in range(at, min(at + 2, at + len(self.steps[group]))):
            for c in self.loads(i):
                c.start()

    def sum_of(self, k, s, out):
        i = self.order.index((k, s))
        loads = self.loads(i)
        for c in loads:
            c.wait()
        for j in range(3):
            total = self.inb[i % 2, 0, j].astype(F32)
            for n in range(1, len(loads)):
                total = total + self.inb[i % 2, n, j].astype(F32)
            for ref in self.extras(k, s)[1]:
                total = total + ref[j].astype(F32)
            out[j] = total.astype(BF16)
        group = next(g for g in self.steps if (k, s) in g)
        if group.index((k, s)) + 2 < len(group):
            for c in self.loads(i + 2):
                c.start()

    def sender(self, n):
        k, s = self.sent[n]
        slot = n % self.pool.shape[0]
        left = k == 1 or (k == 2 and s in self.BY_LEFT)
        ref, recv = self.sinks[k]
        to = self.p.at(ha=self.p.left_to if left else self.p.right_to)
        return remote(self.pool.at[slot], ref.at[s], self.send.at[slot], recv.at[s], to)

    def wait_in(self, k, s):
        ref, recv = self.sinks[k]
        remote(ref.at[s], ref.at[s], self.spare, recv.at[s], self.p.at(ha=self.p.right_to)).wait_recv()

    def pass_on(self, k, s):
        n = self.sent.index((k, s))
        size = self.pool.shape[0]
        if n >= size:
            self.sender(n - size).wait_send()
        self.sum_of(k, s, self.pool.at[n % size])
        self.sender(n).start()

    def end(self):
        for n in range(max(0, len(self.sent) - self.pool.shape[0]), len(self.sent)):
            self.sender(n).wait_send()


EARLY = [[(1, 2), (1, 0)], [(2, 1), (2, 2), (2, 3), (2, 0)]]


def first_kernel(
    nz, len_ref, x_ref, gain_ref, wq_ref, wk_ref, wv_ref, fv_ref, cos_ref, sin_ref, wo_ref, gain_m_ref, dy_ref, own_ref,
    q_ref, k_ref, v_ref, o_ref, st_ref, nmmt_ref, mixed_ref, dh1_ref, da_ref, dgain_ref, mine_ref, got_ref, far_ref, b1_ref, w_ref,
    h1_ref, branch_ref, nmm_ref, nma_ref, dyt_ref, hbuf, wbuf, gbuf, inb, pool,
    wsem, gsem, gsend, grecv, load_sem, rsend, spare, far_recv, b1_recv, *sems,
):
    g = pl.program_id(0)
    places = Places(nz)
    gather = Gather(places, own_ref, w_ref, sems)
    fs, dz = own_ref.shape[1:]
    reduce = Reduce(
        places, mine_ref, got_ref, EARLY, inb, pool, {1: (b1_ref, b1_recv), 2: (far_ref, far_recv)}, lambda k, s: ([], []),
        (load_sem, rsend, spare),
    )

    @pl.when(g == 0)
    def _():
        gather.begin()
        forward_start(x_ref, gain_ref, nma_ref, h1_ref, st_ref)

    @pl.when(g == 1)
    def _():
        gather.pass_line(1)
        gather.spread(1)

    @pl.when(g == 3)
    def _():
        gather.pass_line(2)
        gather.spread(2)
        gather.sides(0)

    @pl.when(g < STEPS)
    def _():
        forward_group(
            g, len_ref[0], nma_ref, wq_ref, wk_ref, wv_ref, fv_ref, cos_ref, sin_ref, wo_ref,
            q_ref, k_ref, v_ref, o_ref, st_ref, h1_ref,
        )

    starts = [pl.multiple_of((places.z + nz - s) % nz * dz, dz) for s in range(nz)]

    def loads(k):
        return [
            pltpu.make_async_copy(w_ref.at[k, s], wbuf.at[:, :, pl.ds(starts[s], dz)], wsem.at[s])
            for s in range(nz)
        ]

    def fetch(k):
        gather.all_swapped(k)
        for c in loads(k):
            c.start()

    def keep(k):
        return pltpu.make_async_copy(gbuf.at[0], mine_ref.at[k], gsem)

    def push(k):
        return remote(gbuf.at[1], got_ref.at[k], gsend, grecv.at[k], places.at(rows=1 - places.r))

    @pl.when(g == STEPS - 1)
    def _():
        gather.pass_line(3)
        gather.spread(3)
        gather.sides(1)
        forward_end(h1_ref, gain_m_ref, nmm_ref)
        nmmt_ref[...] = nmm_ref[...].T
        dyt_ref[...] = dy_ref[...].T
        fetch(0)
        gather.far(0)
        gather.far(1)
        branch_ref[...] = jnp.zeros_like(branch_ref)
        dh1_ref[...] = jnp.zeros_like(dh1_ref)

    @pl.when(g >= STEPS)
    def _():
        k = g - STEPS
        for c in loads(k):
            c.wait()

        @pl.when(k > 0)
        def _():
            keep(k - 1).wait()

        for group, at in enumerate((2, 3)):
            @pl.when(k == at)
            def _():
                push(at - 1).wait_recv()
                reduce.begin(group)
                for step in EARLY[group]:
                    reduce.pass_on(*step)

        for c in range(2):
            rows = slice(c * fs, (c + 1) * fs)
            gate = nn(wbuf[0, rows, :], nmmt_ref[...])
            up = nn(wbuf[1, rows, :], nmmt_ref[...])
            dh = nn(wbuf[2, rows, :], dyt_ref[...])
            sg = sig(gate)
            silu = gate * sg
            hbuf[2, rows, :] = (silu * up).astype(BF16)
            hbuf[0, rows, :] = (dh * up * (sg * (1.0 + gate * (1.0 - sg)))).astype(BF16)
            hbuf[1, rows, :] = (dh * silu).astype(BF16)
        for at in range(0, SLOT, QB):
            rows = slice(at, at + QB)
            branch_ref[rows, :] += tn(hbuf[2, :, rows], wbuf[2])
            dh1_ref[rows, :] += tn(hbuf[0, :, rows], wbuf[0]) + tn(hbuf[1, :, rows], wbuf[1])

        @pl.when(k == 0)
        def _():
            gather.sides(2)
            gather.sides(3)
            gather.far(2)
            gather.far(3)
            fetch(1)

        @pl.when(k == 1)
        def _():
            for i in range(4):
                gather.opposite(i)
            fetch(2)

        @pl.when(k == 2)
        def _():
            fetch(3)

        @pl.when(k > 0)
        def _():
            push(k - 1).wait_send()

        for c in (1, 0):
            rows = slice(c * fs, (c + 1) * fs)
            gbuf[c, 0] = nn(hbuf[0, rows, :], nmm_ref[...]).astype(BF16)
            gbuf[c, 1] = nn(hbuf[1, rows, :], nmm_ref[...]).astype(BF16)
            gbuf[c, 2] = nn(hbuf[2, rows, :], dy_ref[...]).astype(BF16)
            if c == 0:
                keep(k).start()
            else:
                push(k).start()

    @pl.when(g == pl.num_programs(0) - 1)
    def _():
        total = jnp.zeros(dgain_ref.shape, F32)
        for at in range(0, SLOT, QB):
            rows = slice(at, at + QB)
            h1 = h1_ref[rows, :]
            mixed_ref[rows, :] = (h1 + branch_ref[rows, :]).astype(BF16)
            dv, dgain = norm_back(h1, gain_m_ref[...], dh1_ref[rows, :])
            dh1 = dy_ref[rows, :].astype(F32) + dv
            dh1_ref[rows, :] = dh1
            da_ref[rows, :] = dh1.astype(BF16)
            total = total + dgain
        dgain_ref[...] = total
        nmmt_ref[...] = nma_ref[...].T
        keep(3).wait()
        push(3).wait_send()
        push(0).wait_recv()
        push(3).wait_recv()
        for group in EARLY:
            for step in group:
                reduce.wait_in(*step)
        reduce.end()
        gather.end()


def first_half(length, x, gain, wq, wk, wv, fv, cos, sin, wo, gain_m, dy, own, nz):
    tok = x.shape[0]
    fs, dz = own.shape[1:]
    sds = jax.ShapeDtypeStruct
    once = dict(pipeline_mode=pl.Buffered(1))
    step = lambda g: jnp.minimum(g, STEPS - 1)
    full = pl.BlockSpec((tok, D), lambda g: (0, 0), **once)
    blk = pl.BlockSpec((tok, GW), lambda g: (0, step(g)))
    wblk = pl.BlockSpec((D, GW), lambda g: (0, step(g)))
    vec = pl.BlockSpec((1, D), lambda g: (0, 0), **once)
    tab = pl.BlockSpec((tok, 128), lambda g: (0, 0), **once)
    hbm = pl.BlockSpec(memory_space=pl.ANY)
    sem = pltpu.SemaphoreType.DMA
    piece = (3, fs, dz)
    return pl.pallas_call(
        functools.partial(first_kernel, nz),
        grid=(STEPS + 4,),
        in_specs=[
            pl.BlockSpec(memory_space=pltpu.SMEM), full, vec, wblk, wblk, wblk, blk, tab, tab,
            pl.BlockSpec((GW, D), lambda g: (step(g), 0)), vec, full, hbm,
        ],
        out_specs=[blk, blk, blk, blk, tab, full, full, full, full, vec, hbm, hbm, hbm, hbm, hbm],
        out_shape=[sds((tok, D), BF16)] * 4
        + [sds((tok, 128), BF16), sds((D, tok), BF16), sds((tok, D), BF16), sds((tok, D), F32), sds((tok, D), BF16), sds((1, D), F32)]
        + [sds((4, 3, fs, D), BF16)] * 2
        + [sds((nz, *piece), BF16)] * 2
        + [sds((4, nz, 3, 2 * fs, dz), BF16)],
        scratch_shapes=[
            pltpu.VMEM((tok, D), F32), pltpu.VMEM((tok, D), F32),
            pltpu.VMEM((tok, D), BF16), pltpu.VMEM((D, tok), BF16), pltpu.VMEM((D, tok), BF16),
            pltpu.VMEM((3, 2 * fs, tok), BF16), pltpu.VMEM((3, 2 * fs, D), BF16), pltpu.VMEM((2, 3, fs, D), BF16),
            pltpu.VMEM((2, 2, *piece), BF16), pltpu.VMEM((3, *piece), BF16),
            sem((nz,)), sem, sem, sem((4,)), sem((2, 2)), sem((3,)), sem, sem((nz,)), sem((nz,)),
            sem((4, nz)), sem((4,)), sem((2, nz)), sem, sem, sem, sem, sem,
        ],
        compiler_params=pltpu.CompilerParams(vmem_limit_bytes=63 * MIB, collective_id=1, has_side_effects=True),
        cost_estimate=pl.CostEstimate(flops=84 * 10**9, bytes_accessed=80 * 10**6, transcendentals=10**7),
        name="first_half",
    )(length, x, gain, wq, wk, wv, fv, cos, sin, wo, gain_m, dy, own)


MOVES = {
    (0, 0, 0): [("pass", 3, 1), ("pass", 1, 1), (4, 0)],
    (0, 1, 0): [("pass", 3, 2)],
    (0, 2, 0): [(4, 1), (0, 0)],
    (1, 0, 0): [(0, 1), ("total", 1)],
    (1, 1, 0): [(0, 2), (4, 2)],
    (1, 2, 0): [(1, 0)],
    (2, 0, 0): [(0, 3), (1, 1), ("pass", 3, 3), ("pass", 1, 3), (4, 3)],
    (2, 1, 0): [(0, 4), (1, 2)],
    (2, 2, 0): [(4, 4), (0, 5), (2, 0), ("total", 2)],
    (3, 0, 0): [(2, 1), (1, 3), ("pass", 3, 0), (0, 6), (2, 2)],
    (3, 1, 0): [(1, 4), (4, 5), (0, 7)],
    (3, 2, 0): [(2, 3), (3, 0), (1, 5), (4, 6), (3, 1)],
}
TAIL = [
    [("total", 0), (2, 4)],
    [(1, 6)],
    [("total", 3), (3, 2), (2, 5), (4, 7)],
    [(1, 7), (3, 3), (2, 6), (2, 7)],
]
SEQUENCE = [what for at in sorted(MOVES) for what in MOVES[at]] + [what for moves in TAIL for what in moves]
LATE = [[what[1:] if what[0] == "pass" else (0, what[1]) for what in SEQUENCE if what[0] in ("pass", "total")]]


class Spread:
    def __init__(self, places, m, x, far, r1, r3, zin, piece, y, send, recv, local):
        self.p, self.m, self.x, self.far, self.r1, self.r3, self.zin, self.piece, self.y = places, m, x, far, r1, r3, zin, piece, y
        self.send, self.recv, self.local = send, recv, local
        self.half = D // 2
        self.block = self.half // 4
        self.small = self.block // places.nz
        self.to_left = self.block - self.small

    def own_half(self):
        return pl.multiple_of(self.p.r * self.half, self.half)

    def place_of(self, k):
        return (self.p.a, self.p.left_to, self.p.far_to, self.p.right_to)[k]

    def in_x(self, k, at=0, size=None):
        return pl.ds(pl.multiple_of(self.place_of(k) * self.block + at, self.small), size or self.block)

    def rows(self, k, at=0, size=None):
        return pl.ds(pl.multiple_of(self.p.r * self.half + self.place_of(k) * self.block + at, self.small), size or self.block)

    def small_rows(self, z):
        return pl.ds(pl.multiple_of(self.p.r * self.half + self.p.a * self.block + z * self.small, self.small), self.small)

    def copy(self, stage, src, dst, device):
        return remote(src, dst, self.send, self.recv.at[stage], device)

    def left(self):
        return self.p.at(ha=self.p.left_to)

    def right(self):
        return self.p.at(ha=self.p.right_to)

    def sibling(self):
        return self.p.at(rows=1 - self.p.r)

    def copies(self, stage):
        p, m, y = self.p, self.m, self.y
        h = self.to_left
        others = range(1, p.nz)
        if stage == 0:
            other = pl.ds(pl.multiple_of((1 - p.r) * self.half, self.half), self.half)
            return [(m.at[:, other], self.x, self.sibling())]
        if stage == 1:
            return [
                (m.at[:, self.rows(2, 0, h)], self.far.at[:, pl.ds(0, h)], self.left()),
                (m.at[:, self.rows(2, h, self.block - h)], self.far.at[:, pl.ds(h, self.block - h)], self.right()),
            ]
        if stage == 2:
            return [(m.at[:, self.rows(1)], self.r1, self.left()), (m.at[:, self.rows(3)], self.r3, self.right())]
        if stage == 3:
            to = [(p.z + p.nz - s) % p.nz for s in others]
            return [(m.at[:, self.small_rows(z)], self.zin.at[s], p.at(ma=z)) for s, z in zip(others, to)]
        if stage == 4:
            return [(self.piece, y.at[:, self.small_rows(p.z)], p.at(ma=(p.z + s) % p.nz)) for s in others]
        if stage == 5:
            here = y.at[:, self.rows(0)]
            return [(here, here, self.right()), (here, here, self.left())]
        if stage == 6:
            cut = self.block - h
            first, second = y.at[:, self.rows(1, 0, cut)], y.at[:, self.rows(3, cut, h)]
            return [(first, first, self.right()), (second, second, self.left())]
        here = y.at[:, pl.ds(self.own_half(), self.half)]
        return [(here, here, self.sibling())]

    def amount(self, stage):
        return (self.half, self.block, 2 * self.block, self.block - self.small, self.block - self.small, 2 * self.block, self.block, self.half)[stage]

    def keep(self):
        return pltpu.make_async_copy(self.piece, self.y.at[:, self.small_rows(self.p.z)], self.local)

    def wait_for(self, stage):
        these = self.m.at[:, pl.ds(0, self.amount(stage))]
        self.copy(stage, these, these, self.sibling()).wait_recv()

    def add(self, at, *others):
        for j in range(self.m.shape[0]):
            total = self.m[j, at, :].astype(F32)
            for ref, place in others:
                total = total + ref[j, place, :].astype(F32)
            self.m[j, at, :] = total.astype(BF16)

    def run(self, stage):
        p = self.p
        h = self.to_left
        rest = self.block - h
        if stage == 1:
            self.wait_for(0)
            self.add(self.rows(2), (self.x, self.in_x(2)))
        elif stage == 2:
            self.wait_for(1)
            self.add(self.rows(1, 0, h), (self.x, self.in_x(1, 0, h)), (self.far, pl.ds(0, h)))
            self.add(self.rows(1, h, rest), (self.x, self.in_x(1, h, rest)))
            self.add(self.rows(3, 0, h), (self.x, self.in_x(3, 0, h)))
            self.add(self.rows(3, h, rest), (self.x, self.in_x(3, h, rest)), (self.far, pl.ds(h, rest)))
        elif stage == 3:
            self.wait_for(2)
            whole = pl.ds(0, self.block)
            self.add(self.rows(0), (self.x, self.in_x(0)), (self.r1, whole), (self.r3, whole))
        elif stage == 4:
            self.wait_for(3)
            for j in range(self.m.shape[0]):
                total = self.m[j, self.small_rows(p.z), :].astype(F32)
                for s in range(1, p.nz):
                    total = total + self.zin[s, j].astype(F32)
                self.piece[j] = total.astype(BF16)
            self.keep().start()
        elif stage == 5:
            self.wait_for(4)
            self.keep().wait()
        elif stage == 6:
            self.wait_for(5)
        elif stage == 7:
            self.wait_for(6)
        for c in self.copies(stage):
            self.copy(stage, *c).start()

    def end(self):
        self.wait_for(7)
        left = sum(self.amount(stage) for stage in range(8))
        while left:
            these = self.m.at[:, pl.ds(0, min(left, D))]
            self.copy(0, these, these, self.sibling()).wait_send()
            left -= min(left, D)


class Gains:
    def __init__(self, places, own, twin, ring, line, send, recv):
        self.p, self.own, self.twin, self.ring, self.line, self.send, self.recv = places, own, twin, ring, line, send, recv

    def to_twin(self):
        return [remote(self.own, self.twin, self.send.at[0], self.recv.at[0], self.p.at(rows=1 - self.p.r))]

    def round_ring(self):
        p, at = self.p, self.ring.at[self.p.a]
        return [remote(at, at, self.send.at[i], self.recv.at[i], p.at(ha=to)) for i, to in ((1, p.right_to), (2, p.left_to), (3, p.far_to))]

    def along_line(self):
        p, at = self.p, self.line.at[self.p.z]
        return [remote(at, at, self.send.at[3 + s], self.recv.at[3 + s], p.at(ma=(p.z + s) % p.nz)) for s in range(1, p.nz)]

    def run(self, stage):
        if stage == 0:
            sends = self.to_twin()
        elif stage == 1:
            for c in self.to_twin():
                c.wait_recv()
            self.ring[pl.ds(self.p.a, 1)] = (self.own[...] + self.twin[...])[None]
            sends = self.round_ring()
        else:
            for c in self.round_ring():
                c.wait_recv()
            self.line[pl.ds(self.p.z, 1)] = (self.ring[0] + self.ring[1] + self.ring[2] + self.ring[3])[None]
            sends = self.along_line()
        for c in sends:
            c.start()

    def end(self, out_ref):
        for c in self.along_line():
            c.wait_recv()
        total = self.line[0]
        for s in range(1, self.p.nz):
            total = total + self.line[s]
        out_ref[...] = total
        for c in self.to_twin() + self.round_ring() + self.along_line():
            c.wait_send()


def second_kernel(
    nz, len_ref, da_ref, wo_ref, q_ref, k_ref, v_ref, o_ref, st_ref, nmt_ref, cos_ref, sin_ref, wq_ref, wk_ref, wv_ref,
    gain_ref, dgm_ref, x_ref, dh1_ref, attn_ref, mine_ref, got_ref, far_ref, b1_ref,
    gt_ref, gf_ref, gains_ref, ywo_ref, y_ref, tiles_ref,
    dq_acc, dq_ref, dk_ref, dv_ref, xbuf, hbuf, tile_sem,
    mo, xo, faro, r1o, r3o, zo, po, mg, xg, farg, r1g, r3g, zg, pg,
    inb, pool, tot, b1_in, b3_in, z_in, gown, gtwin, gring, gline,
    ar_send, ar_recv, ar_local, g_send, g_recv,
    first_sem, load_sem, rsend, spare, b1_recv, b3_recv, z_send, z_recv, swap_send, swap_recv,
):
    g = pl.program_id(0)
    p = Places(nz)

    def extras(block, s):
        if block == 0:
            early = (1, s) in EARLY[0]
            return [b1_ref.at[s]] if early else [], [b3_in.at[s]] if early else [b1_in.at[s], b3_in.at[s]]
        return [far_ref.at[s]] if (s in Reduce.BY_LEFT) == (block == 1) else [], []

    reduce = Reduce(
        p, mine_ref, got_ref, LATE, inb, pool, {1: (b1_in, b1_recv), 3: (b3_in, b3_recv)}, extras, (load_sem, rsend, spare)
    )

    def to_owner(s):
        return remote(tot.at[s], z_in.at[s], z_send.at[s], z_recv.at[s], p.at(ma=(p.z + nz - s) % nz))

    def total_of(s):
        if (1, s) not in EARLY[0]:
            reduce.wait_in(1, s)
        reduce.wait_in(3, s)
        reduce.sum_of(0, s, tot.at[s])
        if s:
            to_owner(s).start()

    def tile_copies():
        return (
            pltpu.make_async_copy(tot.at[0], tiles_ref.at[p.r], spare),
            remote(tot.at[0], tiles_ref.at[p.r], swap_send, swap_recv, p.at(rows=1 - p.r)),
        )

    def finish():
        for s in range(1, nz):
            to_owner(s).wait_recv()
        for j in range(3):
            total = tot[0, j].astype(F32)
            for s in range(1, nz):
                total = total + z_in[s, j].astype(F32)
            tot[0, j] = total.astype(BF16)
        for c in tile_copies():
            c.start()

    sets = mg.shape[0]
    width = mg.shape[3]
    chunks = [
        Spread(
            p, *(v.at[i % sets] for v in (mg, xg, farg, r1g, r3g, zg, pg)), y_ref.at[i],
            ar_send.at[i], ar_recv.at[i], ar_local.at[i],
        )
        for i in range(STEPS)
    ]
    chunks.append(Spread(p, mo, xo, faro, r1o, r3o, zo, po, ywo_ref, ar_send.at[STEPS], ar_recv.at[STEPS], ar_local.at[STEPS]))
    gains = Gains(p, gown, gtwin, gring, gline, g_send, g_recv)

    def move(what):
        if what[0] == "pass":
            reduce.pass_on(*what[1:])
        elif what[0] == "total":
            total_of(what[1])
        else:
            chunks[what[0]].run(what[1])

    def between(pair, kb):
        for at in range(STEPS):
            moves = MOVES.get((at, pair, kb))
            if moves:
                @pl.when(g == at)
                def _():
                    for what in moves:
                        move(what)

    @pl.when(g == 0)
    def _():
        wait = p.meet(
            [p.at(ma=(p.z + s) % nz) for s in range(1, nz)] + [p.at(ha=to) for to in (p.right_to, p.left_to, p.far_to)] + [p.at(rows=1 - p.r)]
        )
        spots = [(i // 3, i % 3) for i in range(4)]
        fills = [
            pltpu.make_async_copy(attn_ref.at[:, pl.ds(i * width, width)], mg.at[spots[i]], first_sem.at[i])
            for i in range(4)
        ]
        for c in fills:
            c.start()
        reduce.begin(0)
        gt_ref[...] = jnp.zeros_like(gt_ref)
        for i in range(4):
            fills[i].wait()
            mo[0, pl.ds(i * width, width), :] = tn(mg[spots[i]], da_ref[...]).astype(BF16)
        wait()

    backward_group(
        g, len_ref[0], da_ref, wo_ref, q_ref, k_ref, v_ref, o_ref, st_ref, cos_ref, sin_ref,
        dq_ref, dk_ref, dv_ref, gf_ref, dq_acc, between,
    )
    for i in range(sets, STEPS):
        @pl.when(g == i)
        def _():
            chunks[i - sets].end()

    for j, ref in enumerate((dq_ref, dk_ref, dv_ref)):
        mg[g % sets, j] = nn(nmt_ref[...], ref[...]).astype(BF16)

    between(2, 0)
    gt_ref[...] += nt(dq_ref[...], wq_ref[...]) + nt(dk_ref[...], wk_ref[...]) + nt(dv_ref[...], wv_ref[...])

    @pl.when(g == STEPS - 1)
    def _():
        def loads(i):
            rows = pl.ds(i * QB, QB)
            return [
                pltpu.make_async_copy(src.at[rows], buf.at[i % 2], tile_sem.at[i % 2, j])
                for j, (src, buf) in enumerate(((x_ref, xbuf), (dh1_ref, hbuf)))
            ]

        tiles = SLOT // QB
        for c in loads(0):
            c.start()
        total = jnp.zeros(gain_ref.shape, F32)
        for i in range(tiles):
            if i + 1 < tiles:
                for c in loads(i + 1):
                    c.start()
            for what in TAIL[i]:
                move(what)
            for c in loads(i):
                c.wait()
            rows = slice(i * QB, (i + 1) * QB)
            dv, dgain = norm_back(xbuf[i % 2].astype(F32), gain_ref[...], gt_ref[rows, :])
            gt_ref[rows, :] = hbuf[i % 2] + dv
            total = total + dgain
        gown[...] = jnp.concatenate([total, dgm_ref[...], jnp.zeros((6, D), F32)], axis=0)
        gains.run(0)
        move((3, 4))
        gains.run(1)
        move((3, 5))
        gains.run(2)
        finish()
        move((3, 6))
        move((3, 7))
        gains.end(gains_ref)
        for i in [STEPS] + list(range(max(0, STEPS - sets), STEPS)):
            chunks[i].end()
        for c in tile_copies():
            c.wait()
        for s in range(1, nz):
            to_owner(s).wait_send()
        reduce.end()


def second_half(length, da, wo, q, k, v, o, st, nmat, cos, sin, wq, wk, wv, gain, dgm, x, dh1, mine, got, far, b1):
    tok = x.shape[0]
    nz, _, fs, dz = far.shape
    sds = jax.ShapeDtypeStruct
    once = dict(pipeline_mode=pl.Buffered(1))
    full = pl.BlockSpec((tok, D), lambda g: (0, 0), **once)
    blk = pl.BlockSpec((tok, GW), lambda g: (0, g))
    wblk = pl.BlockSpec((D, GW), lambda g: (0, g))
    vec = pl.BlockSpec((1, D), lambda g: (0, 0), **once)
    tab = pl.BlockSpec((tok, 128), lambda g: (0, 0), **once)
    hbm = pl.BlockSpec(memory_space=pl.ANY)
    sem = pltpu.SemaphoreType.DMA
    vmem = lambda *shape: pltpu.VMEM(shape, BF16)
    half = D // 2
    block = half // 4
    small = block // nz
    sets = 3
    piece = (3, fs, dz)

    def buffers(n, lead, width):
        return [
            vmem(*n, lead, D, width), vmem(*n, lead, half, width), vmem(*n, lead, block, width), vmem(*n, lead, block, width),
            vmem(*n, lead, block, width), vmem(*n, nz, lead, small, width), vmem(*n, lead, small, width),
        ]

    return pl.pallas_call(
        functools.partial(second_kernel, nz),
        grid=(STEPS,),
        in_specs=[
            pl.BlockSpec(memory_space=pltpu.SMEM), full, pl.BlockSpec((GW, D), lambda g: (g, 0)), blk, blk, blk, blk, tab, full,
            tab, tab, wblk, wblk, wblk, vec, vec, *[hbm] * 7,
        ],
        out_specs=[full, blk, pl.BlockSpec((8, D), lambda g: (0, 0), **once), hbm, hbm, hbm],
        out_shape=[
            sds((tok, D), F32), sds((tok, D), F32), sds((8, D), F32), sds((1, D, D), BF16), sds((STEPS, 3, D, GW), BF16), sds((2, *piece), BF16),
        ],
        scratch_shapes=[
            pltpu.VMEM((tok, GW), F32), vmem(tok, GW), vmem(tok, GW), vmem(tok, GW), vmem(2, QB, D), pltpu.VMEM((2, QB, D), F32), sem((2, 2)),
            *buffers((), 1, D), *buffers((sets,), 3, GW),
            vmem(2, 3, *piece), vmem(4, *piece), vmem(nz, *piece), vmem(nz, *piece), vmem(nz, *piece), vmem(nz, *piece),
            pltpu.VMEM((8, D), F32), pltpu.VMEM((8, D), F32), pltpu.VMEM((4, 8, D), F32), pltpu.VMEM((nz, 8, D), F32),
            sem((STEPS + 1,)), sem((STEPS + 1, 8)), sem((STEPS + 1,)), sem((3 + nz,)), sem((3 + nz,)),
            sem((4,)), sem((2, 3)), sem((4,)), sem, sem((nz,)), sem((nz,)), sem((nz,)), sem((nz,)), sem, sem,
        ],
        compiler_params=pltpu.CompilerParams(vmem_limit_bytes=63 * MIB, collective_id=2, has_side_effects=True),
        cost_estimate=pl.CostEstimate(flops=50 * 10**9, bytes_accessed=80 * 10**6, transcendentals=10**7),
        name="second_half",
    )(length, da, wo, q, k, v, o, st, nmat, cos, sin, wq, wk, wv, gain, dgm, x, dh1, o, mine, got, far, b1)


def mlp_out_kernel(nk, nc, nz, zs_ref, w_ref, hs_ref, dgs_ref, dus_ref, h1_ref, gain_ref, dy_ref, mixed_ref, dh1_ref, da_ref, dgain_ref, branch_ref, dnm_ref):
    fs, dz = w_ref.shape[4:]
    i = pl.program_id(0)
    for s in range(nz):
        b = d = None
        for k in range(nk):
            for c in range(nc):
                rows = pl.ds(c * fs, fs)
                b_one = tn(hs_ref[k, rows, :], w_ref[k, c, s, 2])
                d_one = tn(dgs_ref[k, rows, :], w_ref[k, c, s, 0]) + tn(dus_ref[k, rows, :], w_ref[k, c, s, 1])
                b, d = (b_one, d_one) if b is None else (b + b_one, d + d_one)
        at = pl.ds(pl.multiple_of(zs_ref[s] * dz, dz), dz)
        branch_ref[:, at] = b
        dnm_ref[:, at] = d
    h1 = h1_ref[...]
    mixed_ref[...] = (h1 + branch_ref[...]).astype(BF16)
    dv, dgain = norm_back(h1, gain_ref[...], dnm_ref[...])
    dh1 = dy_ref[...].astype(F32) + dv
    dh1_ref[...] = dh1
    da_ref[...] = dh1.astype(BF16)

    @pl.when(i == 0)
    def _():
        dgain_ref[...] = jnp.zeros_like(dgain_ref)

    dgain_ref[...] += dgain


def mlp_out(zs, w, hs, dgs, dus, h1, gain, dy):
    nk, nc, nz = w.shape[:3]
    tok = h1.shape[0]
    tile = 256
    wspec = pl.BlockSpec(w.shape, lambda i: (0,) * 6, pipeline_mode=pl.Buffered(1))
    hspec = pl.BlockSpec((nk, hs.shape[1], tile), lambda i: (0, 0, i))
    row = pl.BlockSpec((tile, D), lambda i: (i, 0))
    vec = pl.BlockSpec((1, D), lambda i: (0, 0))
    sds = jax.ShapeDtypeStruct
    return pl.pallas_call(
        functools.partial(mlp_out_kernel, nk, nc, nz),
        grid=(tok // tile,),
        in_specs=[pl.BlockSpec(memory_space=pltpu.SMEM), wspec, hspec, hspec, hspec, row, vec, row],
        out_specs=[row, row, row, vec],
        out_shape=[sds((tok, D), BF16), sds((tok, D), F32), sds((tok, D), BF16), sds((1, D), F32)],
        scratch_shapes=[pltpu.VMEM((tile, D), F32)] * 2,
        compiler_params=pltpu.CompilerParams(vmem_limit_bytes=58 * MIB),
        cost_estimate=pl.CostEstimate(flops=18 * 10**9, bytes_accessed=45 * 10**6, transcendentals=0),
        name="mlp_out",
    )(zs, w, hs, dgs, dus, h1, gain, dy)


def tokens_kernel(n, *refs):
    parts, (wq_ref, wk_ref, wv_ref, x_ref, gain_ref, dh1_ref, out_ref, dgain_ref) = refs[: 3 * n], refs[3 * n :]
    i = pl.program_id(0)
    total = None
    for j, w_ref in enumerate((wq_ref, wk_ref, wv_ref)):
        d = parts[j * n][...] if n == 1 else jnp.concatenate([r[...] for r in parts[j * n : (j + 1) * n]], axis=1)
        t = nt(d, w_ref[...])
        total = t if total is None else total + t
    dv, dgain = norm_back(x_ref[...].astype(F32), gain_ref[...], total)
    out_ref[...] = dh1_ref[...] + dv

    @pl.when(i == 0)
    def _():
        dgain_ref[...] = jnp.zeros_like(dgain_ref)

    dgain_ref[...] += dgain


def tokens_grad(dqs, dks, dvs, wq, wk, wv, x, gain, dh1):
    n = len(dqs)
    tok = x.shape[0]
    tile = 256
    row = pl.BlockSpec((tile, D), lambda i: (i, 0))
    full = pl.BlockSpec((D, D), lambda i: (0, 0))
    vec = pl.BlockSpec((1, D), lambda i: (0, 0))
    sds = jax.ShapeDtypeStruct
    return pl.pallas_call(
        functools.partial(tokens_kernel, n),
        grid=(tok // tile,),
        in_specs=[pl.BlockSpec((tile, d.shape[1]), lambda i: (i, 0)) for d in (*dqs, *dks, *dvs)] + [full, full, full, row, vec, row],
        out_specs=[row, vec],
        out_shape=[sds((tok, D), F32), sds((1, D), F32)],
        compiler_params=pltpu.CompilerParams(vmem_limit_bytes=40 * MIB),
        cost_estimate=pl.CostEstimate(flops=7 * 10**9, bytes_accessed=24 * 10**6, transcendentals=0),
        name="tokens_grad",
    )(*dqs, *dks, *dvs, wq, wk, wv, x, gain, dh1)
def body(
    paired, tokens, first_values, lengths, w_query, w_key, w_value, w_out, norm_attn, norm_mlp, w_gate, w_up, w_down, grad_out
):
    nz = lax.axis_size("ma")
    r = lax.axis_index("rows")
    cos, sin = (jnp.asarray(t) for t in rope_tables())
    gain_a, gain_m = norm_attn[None], norm_mlp[None]
    tile = jnp.stack([w_gate.T, w_up.T, w_down])
    if paired:
        fs = tile.shape[1] // 2
        own = lax.dynamic_slice_in_dim(tile, r * fs, fs, axis=1)
        q, k, v, o, st, nmat, mixed, dh1, da, dgain_m, mine, got, far, b1, _ = first_half(
            lengths, tokens, gain_a, w_query, w_key, w_value, first_values, cos, sin, w_out, gain_m, grad_out, own, nz
        )
        grad_tokens, grad_first, gains, grad_wout, grads, tiles = second_half(
            lengths, da, w_out, q, k, v, o, st, nmat, cos, sin, w_query, w_key, w_value, gain_a, dgain_m, tokens, dh1,
            mine, got, far, b1,
        )
        gain_grads = gains[0], gains[1]
        grad_wout = grad_wout[0].astype(F32)
        grad_q, grad_k, grad_v = (jnp.concatenate(list(grads[:, j]), axis=1).astype(F32) for j in range(3))
        tiles = tiles.transpose(1, 0, 2, 3).reshape(tile.shape).astype(F32)
    else:
        w = lax.all_gather(lax.all_gather(tile, "ma", axis=0), "ha", axis=0)[:, None]
        zs = jnp.arange(nz, dtype=jnp.int32)
        q, k, v, o, st, nma, h1, nmm = attention_forward(
            lengths, tokens, gain_a, w_query, w_key, w_value, first_values, cos, sin, w_out, gain_m
        )
        nmat, ot, nmmt, dyt = prepare(nma, o, nmm, grad_out)
        done = [mlp_block(zs, [[w[i, 0, j] for j in range(nz)]], nmmt, dyt, nmm, grad_out) for i in range(w.shape[0])]
        hs, dgs, dus, mine = (jnp.stack([d[j] for d in done]) for j in range(4))
        mixed, dh1, da, dgain_m = mlp_out(zs, w, hs, dgs, dus, h1, gain_m, grad_out)
        dq, dk, dv, grad_first, grads = attention_backward(
            0, H // GROUP, lengths, da, w_out, q, k, v, o, st, nmat, cos, sin
        )
        grad_tokens, dgain_a = tokens_grad([dq], [dk], [dv], w_query, w_key, w_value, tokens, gain_a, dh1)
        part = lax.psum_scatter(lax.psum_scatter(mine, "ha", scatter_dimension=0), "ma", scatter_dimension=0)
        tiles = lax.psum(part, "rows").astype(F32)
        grad_wout, grads, *gains = lax.psum((wout_grad(ot, da), grads, dgain_a, dgain_m), ("rows", "ha", "ma"))
        grad_wout = grad_wout.astype(F32)
        grad_q, grad_k, grad_v = (grads[j].astype(F32) for j in range(3))
        gain_grads = [v[0] for v in gains]
    return (
        mixed, grad_tokens, grad_first, grad_q, grad_k, grad_v, grad_wout, gain_grads[0], gain_grads[1],
        tiles[0].T, tiles[1].T, tiles[2],
    )


def solution(mesh):
    tok = P(("rows", "ha", "ma"), None)
    gate, down = P("ma", "ha"), P("ha", "ma")
    return jax.shard_map(
        functools.partial(body, mesh.shape["rows"] == 2),
        mesh=mesh,
        in_specs=(tok, tok, P(("rows", "ha", "ma")), P(), P(), P(), P(), P(), P(), gate, gate, down, tok),
        out_specs=(tok, tok, tok, P(), P(), P(), P(), P(), P(), gate, gate, down),
        check_vma=False,
    )
```

```python
import functools
import math

import jax
import jax.numpy as jnp
import numpy as np
from jax import lax
from jax.experimental import pallas as pl
from jax.experimental.pallas import tpu as pltpu
from jax.sharding import PartitionSpec as P

D = 1024
H = 16
HD = 64
SLOT = 1024
EPS = 1e-06
GROUP = 4
GW = GROUP * HD
QB = 256
SCALE = 1.0 / math.sqrt(HD)
C2 = SCALE * math.log2(math.e)
F32 = jnp.float32
BF16 = jnp.bfloat16
MIB = 1 << 20


def nn(a, b):
    return lax.dot_general(a, b, (((1,), (0,)), ((), ())), preferred_element_type=F32)


def nt(a, b):
    return lax.dot_general(a, b, (((1,), (1,)), ((), ())), preferred_element_type=F32)


def tn(a, b):
    return lax.dot_general(a, b, (((0,), (0,)), ((), ())), preferred_element_type=F32)


def rope_tables():
    place = np.arange(SLOT, dtype=np.float32)
    frequency = np.float32(10000.0) ** (-np.arange(HD // 2, dtype=np.float32) * np.float32(2.0) / np.float32(HD))
    angles = place[:, None] * frequency[None, :]
    cosine, sine = np.cos(angles), np.sin(angles)
    cos_row = np.concatenate([cosine] * 4, axis=1)
    sin_row = np.concatenate([-sine, sine, -sine, sine], axis=1)
    return cos_row.astype(np.float32), sin_row.astype(np.float32)


def lanes(shape):
    return lax.broadcasted_iota(jnp.int32, shape, 1)


def partner(v):
    first = (lanes(v.shape) & 63) < 32
    return jnp.where(first, pltpu.roll(v, 96, 1), pltpu.roll(v, 32, 1))


def turn(v, cos, sin):
    parts = []
    for at in range(0, v.shape[1], 128):
        piece = v[:, at : at + 128]
        parts.append(piece * cos + partner(piece) * sin)
    return jnp.concatenate(parts, axis=1)


def low3(v):
    hi = v.astype(BF16).astype(F32)
    rest = v - hi
    mid = rest.astype(BF16).astype(F32)
    return hi, mid, rest - mid


def forward_start(x_ref, gain_ref, nma_ref, h1_ref, st_ref):
    x = x_ref[...].astype(F32)
    r = lax.rsqrt(jnp.mean(x * x, axis=-1, keepdims=True) + EPS)
    nma_ref[...] = (x * r * gain_ref[...]).astype(BF16)
    h1_ref[...] = x
    st_ref[...] = jnp.zeros_like(st_ref)


def forward_end(h1_ref, gain_m_ref, nmm_ref):
    h = h1_ref[...]
    r = lax.rsqrt(jnp.mean(h * h, axis=-1, keepdims=True) + EPS)
    nmm_ref[...] = (h * r * gain_m_ref[...]).astype(BF16)


def forward_group(
    g, length, nma_ref, wq_ref, wk_ref, wv_ref, fv_ref, cos_ref, sin_ref, wo_ref,
    q_ref, k_ref, v_ref, o_ref, st_ref, h1_ref, between=None,
):
    nm = nma_ref[...]
    cos, sin = cos_ref[...], sin_ref[...]
    q_ref[...] = turn(nn(nm, wq_ref[...]), cos, sin).astype(BF16)
    k_ref[...] = turn(nn(nm, wk_ref[...]), cos, sin).astype(BF16)
    v_ref[...] = (0.5 * nn(nm, wv_ref[...]) + 0.5 * fv_ref[...].astype(F32)).astype(BF16)
    tile = (SLOT, 128)
    lane = lanes(tile)
    row = lax.broadcasted_iota(jnp.int32, tile, 0)
    k_extra = jnp.where((lane == 0) & (row >= length), -1e30, 0.0).astype(BF16)
    q_extra = jnp.where(lane == 0, 1.0, 0.0).astype(BF16)
    ones = jnp.ones(tile, BF16)
    low_lane = lane < HD
    qlane = lanes((QB, 128))
    causal = lax.broadcasted_iota(jnp.int32, (QB, QB), 1) <= lax.broadcasted_iota(jnp.int32, (QB, QB), 0)
    for pair in range(GROUP // 2):
        cols = pl.ds(pair * 128, 128)
        qp, kp, vp = q_ref[:, cols], k_ref[:, cols], v_ref[:, cols]
        q_ext = jnp.concatenate([qp, q_extra], axis=1)
        k_exts, v_exts = [], []
        for e in range(2):
            mine = low_lane if e == 0 else ~low_lane
            k_exts.append(jnp.concatenate([jnp.where(mine, kp, 0), k_extra], axis=1))
            v_exts.append(jnp.concatenate([jnp.where(mine, vp, 0), ones], axis=1))
        for qb in range(SLOT // QB):
            if between is not None:
                between(pair, qb)
            rows = slice(qb * QB, (qb + 1) * QB)
            top = (qb + 1) * QB
            out = None
            stats = st_ref[rows, :].astype(F32)
            for e in range(2):
                s = nt(q_ext[rows], k_exts[e][:top])
                diag = jnp.where(causal, s[:, top - QB :], -1e30)
                s = diag if qb == 0 else jnp.concatenate([s[:, : top - QB], diag], axis=1)
                m = jnp.max(s, axis=-1, keepdims=True)
                p = jnp.exp2((s - m) * C2).astype(BF16)
                res = nn(p, v_exts[e][:top])
                total = res[:, 128:]
                part = res[:, :128] / total
                out = part if out is None else out + part
                hi, mid, rest = low3(m + jnp.log2(total) * (1.0 / C2))
                base = 8 * (g * GROUP + pair * 2 + e)
                stats = jnp.where(qlane == base, hi, stats)
                stats = jnp.where(qlane == base + 1, mid, stats)
                stats = jnp.where(qlane == base + 2, rest, stats)
                stats = jnp.where(qlane == base + 3, 1.0, stats)
            o_ref[rows, cols] = out.astype(BF16)
            st_ref[rows, :] = stats.astype(BF16)
    h1_ref[...] += nn(o_ref[...], wo_ref[...])


def fwd_kernel(
    len_ref, x_ref, gain_ref, wq_ref, wk_ref, wv_ref, fv_ref, cos_ref, sin_ref, wo_ref, gain_m_ref,
    q_ref, k_ref, v_ref, o_ref, st_ref, nma_ref, h1_ref, nmm_ref,
):
    g = pl.program_id(0)

    @pl.when(g == 0)
    def _():
        forward_start(x_ref, gain_ref, nma_ref, h1_ref, st_ref)

    forward_group(
        g, len_ref[0], nma_ref, wq_ref, wk_ref, wv_ref, fv_ref, cos_ref, sin_ref, wo_ref,
        q_ref, k_ref, v_ref, o_ref, st_ref, h1_ref,
    )

    @pl.when(g == pl.num_programs(0) - 1)
    def _():
        forward_end(h1_ref, gain_m_ref, nmm_ref)


def attention_forward(length, x, gain, wq, wk, wv, fv, cos, sin, wo, gain_m):
    whole = lambda *_: (0, 0)
    col = lambda g, *_: (0, g)
    tok = x.shape[0]
    full = pl.BlockSpec((tok, D), whole)
    blk = pl.BlockSpec((tok, GW), col)
    wblk = pl.BlockSpec((D, GW), col)
    vec = pl.BlockSpec((1, D), whole)
    tab = pl.BlockSpec((tok, 128), whole)
    sds = jax.ShapeDtypeStruct
    return pl.pallas_call(
        fwd_kernel,
        grid_spec=pltpu.PrefetchScalarGridSpec(
            num_scalar_prefetch=1,
            grid=(H // GROUP,),
            in_specs=[full, vec, wblk, wblk, wblk, blk, tab, tab, pl.BlockSpec((GW, D), lambda g, *_: (g, 0)), vec],
            out_specs=[blk, blk, blk, blk, tab, full, full, full],
        ),
        out_shape=[sds((tok, D), BF16)] * 4 + [sds((tok, 128), BF16), sds((tok, D), BF16), sds((tok, D), F32), sds((tok, D), BF16)],
        compiler_params=pltpu.CompilerParams(vmem_limit_bytes=56 * MIB),
        cost_estimate=pl.CostEstimate(flops=30 * 10**9, bytes_accessed=40 * 10**6, transcendentals=10**7),
        name="attention_forward",
    )(length, x, gain, wq, wk, wv, fv, cos, sin, wo, gain_m)


def prep_kernel(*refs):
    count = len(refs) // 2
    for src, dst in zip(refs[:count], refs[count:]):
        dst[...] = src[...].T


def prepare(*arrays):
    vm = pl.BlockSpec(memory_space=pltpu.VMEM)
    tok = arrays[0].shape[0]
    return pl.pallas_call(
        prep_kernel,
        in_specs=[vm] * len(arrays),
        out_specs=[vm] * len(arrays),
        out_shape=[jax.ShapeDtypeStruct((D, tok), BF16)] * len(arrays),
        compiler_params=pltpu.CompilerParams(vmem_limit_bytes=30 * MIB),
        cost_estimate=pl.CostEstimate(flops=10**9, bytes_accessed=4 * len(arrays) * 10**6, transcendentals=0),
        name="prepare",
    )(*arrays)


def wout_kernel(ot_ref, da_ref, out_ref):
    out_ref[...] = nn(ot_ref[...], da_ref[...]).astype(BF16)


def wout_grad(ot, da):
    vm = pl.BlockSpec(memory_space=pltpu.VMEM)
    return pl.pallas_call(
        wout_kernel,
        in_specs=[vm] * 2,
        out_specs=vm,
        out_shape=jax.ShapeDtypeStruct((D, D), BF16),
        compiler_params=pltpu.CompilerParams(vmem_limit_bytes=30 * MIB),
        cost_estimate=pl.CostEstimate(flops=2 * 10**9, bytes_accessed=6 * 10**6, transcendentals=0),
        name="wout_grad",
    )(ot, da)


def backward_group(
    g, length, da_ref, wo_ref, q_ref, k_ref, v_ref, o_ref, st_ref, cos_ref, sin_ref, dq_ref, dk_ref, dv_ref, gf_ref, dq_acc, between=None
):
    do_all = nt(da_ref[...], wo_ref[...]).astype(BF16)
    prod = do_all.astype(F32) * o_ref[...].astype(F32)
    hi = prod.astype(BF16)
    lo = (prod - hi.astype(F32)).astype(BF16)
    sel_row = lax.broadcasted_iota(jnp.int32, (GW, 128), 0) // HD + g * GROUP
    sel_lane = lanes((GW, 128))
    pick = jnp.where((sel_lane // 8 == sel_row) & ((sel_lane & 7) >= 4) & ((sel_lane & 7) <= 5), 1.0, 0.0).astype(BF16)
    delta = nn(hi, pick) + nn(lo, pick)
    tile = (SLOT, 128)
    lane = lanes(tile)
    d_hi = delta.astype(BF16)
    d_ext = jnp.where((lane & 7) == 4, d_hi.astype(F32), delta - d_hi.astype(F32)).astype(BF16)
    row = lax.broadcasted_iota(jnp.int32, tile, 0)
    dead = row >= length
    low_lane = lane < HD
    st = st_ref[...]
    visible = lax.broadcasted_iota(jnp.int32, (QB, QB), 0) <= lax.broadcasted_iota(jnp.int32, (QB, QB), 1)
    dq_acc[...] = jnp.zeros_like(dq_acc)
    for pair in range(GROUP // 2):
        cols = pl.ds(pair * 128, 128)
        qp, kp, vp = q_ref[:, cols], k_ref[:, cols], v_ref[:, cols]
        dop = do_all[:, pair * 128 : pair * 128 + 128]
        q_ext = jnp.concatenate([qp, st], axis=1)
        do_ext = jnp.concatenate([dop, d_ext], axis=1)
        heads = []
        for e in range(2):
            mine = low_lane if e == 0 else ~low_lane
            at = lane - 8 * (g * GROUP + pair * 2 + e)
            k_x = jnp.where((at >= 0) & (at < 3), -1.0, jnp.where((at == 3) & dead, -1e30, 0.0)).astype(BF16)
            v_x = jnp.where((at >= 4) & (at < 6), -1.0, 0.0).astype(BF16)
            k_m = jnp.where(mine, kp, 0)
            heads.append((
                k_m,
                jnp.concatenate([k_m, k_x], axis=1),
                jnp.concatenate([jnp.where(mine, vp, 0), v_x], axis=1),
                jnp.where(mine, qp, 0),
                jnp.where(mine, dop, 0),
            ))
        for kb in range(SLOT // QB):
            if between is not None:
                between(pair, kb)
            rows = slice(kb * QB, (kb + 1) * QB)
            start = kb * QB
            dk = dv = None
            for k_m, k_ext, v_ext, q_m, do_m in heads:
                st_ = nt(k_ext[rows], q_ext[start:])
                dp = nt(v_ext[rows], do_ext[start:])
                p = jnp.exp2(st_ * C2)
                diag = jnp.where(visible, p[:, :QB], 0.0)
                p = diag if kb == SLOT // QB - 1 else jnp.concatenate([diag, p[:, QB:]], axis=1)
                ds = (p * dp).astype(BF16)
                p = p.astype(BF16)
                dv_e = nn(p, do_m[start:])
                dk_e = nn(ds, q_m[start:])
                dk = dk_e if dk is None else dk + dk_e
                dv = dv_e if dv is None else dv + dv_e
                dq_acc[start:, cols] += tn(ds, k_m[rows])
            dk = dk * SCALE
            cos, sin = cos_ref[rows, :], sin_ref[rows, :]
            dk_ref[rows, cols] = (dk * cos - partner(dk) * sin).astype(BF16)
            half = 0.5 * dv
            gf_ref[rows, cols] = dv
            dv_ref[rows, cols] = half.astype(BF16)
    cos, sin = cos_ref[...], sin_ref[...]
    for pair in range(GROUP // 2):
        cols = pl.ds(pair * 128, 128)
        dq = dq_acc[:, cols] * SCALE
        dq_ref[:, cols] = (dq * cos - partner(dq) * sin).astype(BF16)


def bwd_kernel(
    first_group, len_ref, da_ref, wo_ref, q_ref, k_ref, v_ref, o_ref, st_ref, nmt_ref, cos_ref, sin_ref,
    dq_ref, dk_ref, dv_ref, gf_ref, gw_ref, dq_acc,
):
    g = pl.program_id(0) + first_group
    backward_group(
        g, len_ref[0], da_ref, wo_ref, q_ref, k_ref, v_ref, o_ref, st_ref, cos_ref, sin_ref, dq_ref, dk_ref, dv_ref, gf_ref, dq_acc
    )
    for j, ref in enumerate((dq_ref, dk_ref, dv_ref)):
        gw_ref[j] = nn(nmt_ref[...], ref[...]).astype(BF16)


def attention_backward(first_group, groups, length, da, wo, q, k, v, o, st, nmt, cos, sin):
    whole = lambda *_: (0, 0)
    tok = da.shape[0]
    full = pl.BlockSpec((tok, D), whole)
    blk_in = pl.BlockSpec((tok, GW), lambda g, *_: (0, g + first_group))
    blk = pl.BlockSpec((tok, GW), lambda g, *_: (0, g))
    tab = pl.BlockSpec((tok, 128), whole)
    sds = jax.ShapeDtypeStruct
    width = groups * GW
    return pl.pallas_call(
        functools.partial(bwd_kernel, first_group),
        grid_spec=pltpu.PrefetchScalarGridSpec(
            num_scalar_prefetch=1,
            grid=(groups,),
            in_specs=[full, pl.BlockSpec((GW, D), lambda g, *_: (g + first_group, 0)), blk_in, blk_in, blk_in, blk_in, tab, pl.BlockSpec((D, tok), whole), tab, tab],
            out_specs=[blk, blk, blk, blk, pl.BlockSpec((3, D, GW), lambda g, *_: (0, 0, g))],
            scratch_shapes=[pltpu.VMEM((tok, GW), F32)],
        ),
        out_shape=[sds((tok, width), BF16)] * 3 + [sds((tok, width), F32), sds((3, D, width), BF16)],
        compiler_params=pltpu.CompilerParams(vmem_limit_bytes=56 * MIB),
        cost_estimate=pl.CostEstimate(flops=10 * 10**9 * groups, bytes_accessed=10 * 10**6, transcendentals=groups * 3 * 10**6),
        name="attention_backward",
    )(length, da, wo, q, k, v, o, st, nmt, cos, sin)


def sig(v):
    return 1.0 / (1.0 + jnp.exp(-v))


def mlp_kernel(nc, nz, zs_ref, *refs):
    pieces = refs[: nc * nz]
    nmt_ref, dyt_ref, nm_ref, dy_ref, h_ref, dg_ref, du_ref = refs[nc * nz : nc * nz + 7]
    outs = refs[nc * nz + 7 :]
    fs = pieces[0].shape[1]
    dz = pieces[0].shape[2]
    starts = [pl.multiple_of(zs_ref[s] * dz, dz) for s in range(nz)]
    for c in range(nc):
        gate = up = dh = None
        for s in range(nz):
            w_ref = pieces[c * nz + s]
            at = pl.ds(starts[s], dz)
            nmt, dyt = nmt_ref[at, :], dyt_ref[at, :]
            parts = nn(w_ref[0], nmt), nn(w_ref[1], nmt), nn(w_ref[2], dyt)
            gate, up, dh = parts if gate is None else (gate + parts[0], up + parts[1], dh + parts[2])
        sg = sig(gate)
        silu = gate * sg
        rows = pl.ds(c * fs, fs)
        h = (silu * up).astype(BF16)
        dg = (dh * up * (sg * (1.0 + gate * (1.0 - sg)))).astype(BF16)
        du = (dh * silu).astype(BF16)
        h_ref[rows, :], dg_ref[rows, :], du_ref[rows, :] = h, dg, du
        for s in range(nz):
            at = pl.ds(starts[s], dz)
            nm, dy = nm_ref[:, at], dy_ref[:, at]
            outs[c][s, 0] = nn(dg, nm).astype(BF16)
            outs[c][s, 1] = nn(du, nm).astype(BF16)
            outs[c][s, 2] = nn(h, dy).astype(BF16)


def mlp_block(zs, pieces, nmt, dyt, nm, dy):
    nc, nz = len(pieces), len(pieces[0])
    _, fs, dz = pieces[0][0].shape
    tok = nm.shape[0]
    sds = jax.ShapeDtypeStruct
    vm = pl.BlockSpec(memory_space=pltpu.VMEM)
    return pl.pallas_call(
        functools.partial(mlp_kernel, nc, nz),
        in_specs=[pl.BlockSpec(memory_space=pltpu.SMEM)] + [vm] * (nc * nz + 4),
        out_specs=[vm] * (3 + nc),
        out_shape=[sds((nc * fs, tok), BF16)] * 3 + [sds((nz, 3, fs, dz), BF16)] * nc,
        compiler_params=pltpu.CompilerParams(vmem_limit_bytes=44 * MIB),
        cost_estimate=pl.CostEstimate(flops=12 * nc * fs * D * tok, bytes_accessed=15 * 10**6, transcendentals=nc * fs * tok),
        name="mlp_block",
    )(zs, *[p for c in pieces for p in c], nmt, dyt, nm, dy)


MESH = pl.DeviceIdType.MESH
RING = (0, 1, 3, 2)
STEPS = H // GROUP
TURNS = (0, 1, 3, 2)


def table(index, values):
    out = values[0]
    for i, v in enumerate(values[1:], 1):
        out = jnp.where(index == i, v, out)
    return out


def norm_back(v, gain, grad):
    ms = jnp.mean(v * v, axis=-1, keepdims=True) + EPS
    r = lax.rsqrt(ms)
    gg = grad * gain
    inner = jnp.mean(gg * v, axis=-1, keepdims=True)
    dv = r * gg - v * (inner * r * r * r)
    dgain = jnp.sum(grad * v * r, axis=0, keepdims=True)
    return dv, dgain


class Places:
    def __init__(self, nz):
        self.nz = nz
        self.r, self.a, self.z = (lax.axis_index(n) for n in ("rows", "ha", "ma"))
        self.spot = table(self.a, [RING.index(i) for i in range(4)])
        self.right_to = table(self.spot, [RING[(i + 1) % 4] for i in range(4)])
        self.left_to = table(self.spot, [RING[(i + 3) % 4] for i in range(4)])
        self.far_to = table(self.spot, [RING[(i + 2) % 4] for i in range(4)])
        self.arrivals = [0] + [table(self.z, v) for v in ((3, 1, 3, 1), (2, 3, 1, 2), (1, 2, 2, 3))]

    def at(self, **moved):
        place = {"rows": self.r, "ha": self.a, "ma": self.z, **moved}
        return (place["rows"], place["ha"], place["ma"])

    def meet(self, others):
        barrier = pltpu.get_barrier_semaphore()
        for other in others:
            pl.semaphore_signal(barrier, inc=1, device_id=other, device_id_type=MESH)
        return lambda: pl.semaphore_wait(barrier, len(others))


def remote(src, dst, send, recv, device):
    return pltpu.make_async_remote_copy(
        src_ref=src, dst_ref=dst, send_sem=send, recv_sem=recv, device_id=device, device_id_type=MESH
    )


class Gather:
    def __init__(self, places, own_ref, w_ref, sems):
        self.p, self.own, self.w = places, own_ref, w_ref
        self.recv, self.swap_recv, self.z_send, self.right_send, self.left_send, self.far_send, self.swap_send, self.local = sems
        self.fs = own_ref.shape[1]

    def part(self, k, s, c=0):
        return self.w.at[k, s, :, pl.ds(c * self.fs, self.fs)]

    def copy(self, src, dst, send, device):
        return remote(self.part(*src), self.part(*dst), send, self.recv.at[dst], device)

    def right(self, s):
        return self.copy((0, s), (1, s), self.right_send, self.p.at(ha=self.p.right_to))

    def left(self, s):
        return self.copy((0, s), (3, s), self.left_send, self.p.at(ha=self.p.left_to))

    def far_copy(self, i):
        s = self.p.arrivals[i]
        if i % 2 == 0:
            return self.copy((1, s), (2, s), self.far_send, self.p.at(ha=self.p.right_to))
        return self.copy((3, s), (2, s), self.far_send, self.p.at(ha=self.p.left_to))

    def swap(self, k, s):
        return remote(self.part(k, s), self.part(k, s, 1), self.swap_send, self.swap_recv.at[k], self.p.at(rows=1 - self.p.r))

    def arrived(self, k, s):
        self.copy((k, s), (k, s), self.local, self.p.at(rows=1 - self.p.r)).wait_recv()

    def all_swapped(self, k):
        half = self.w.at[k, :, :, pl.ds(self.fs, self.fs)]
        remote(half, half, self.local, self.swap_recv.at[k], self.p.at(rows=1 - self.p.r)).wait_recv()

    def line(self, d, act, wait):
        nz, z = self.p.nz, self.p.z

        def up(cond):
            pl.when(cond & (z < nz - 1))(
                lambda: act(self.copy((0, d), (0, d + 1), self.z_send.at[0, d], self.p.at(ma=z + 1)))
            )

        def down(cond):
            pl.when(cond & (z >= 1))(
                lambda: act(self.copy((0, (nz - d) % nz), (0, nz - d - 1), self.z_send.at[1, d], self.p.at(ma=z - 1)))
            )

        if d and wait:
            pl.when(z >= d)(lambda: self.arrived(0, d))
            pl.when(z + d <= nz - 1)(lambda: self.arrived(0, nz - d))
        if d < nz - 1:
            up(z >= d)
            down(z + d <= nz - 1)

    def begin(self):
        p = self.p
        wait = p.meet([
            p.at(ma=(p.z + 1) % p.nz), p.at(ma=(p.z + p.nz - 1) % p.nz), p.at(ha=p.right_to), p.at(ha=p.left_to), p.at(rows=1 - p.r)
        ])
        mine = pltpu.make_async_copy(self.own, self.part(0, 0), self.local)
        mine.start()
        mine.wait()
        wait()
        self.pass_line(0)
        self.spread(0)

    def pass_line(self, d):
        self.line(d, lambda c: c.start(), True)

    def spread(self, i):
        s = self.p.arrivals[i]
        self.right(s).start()
        self.left(s).start()
        self.swap(0, s).start()

    def sides(self, i):
        s = self.p.arrivals[i]
        self.arrived(1, s)
        self.arrived(3, s)
        self.swap(1, s).start()
        self.swap(3, s).start()

    def far(self, i):
        self.far_copy(i).start()

    def opposite(self, i):
        s = self.p.arrivals[i]
        self.arrived(2, s)
        self.swap(2, s).start()

    def end(self):
        for i in range(self.p.nz):
            self.line(i, lambda c: c.wait_send(), False)
        here = self.p.at(rows=1 - self.p.r)
        column = self.w.at[0, :, :, pl.ds(0, self.fs)]
        for send in (self.right_send, self.left_send, self.far_send):
            remote(column, column, send, self.local, here).wait_send()
        whole = self.w.at[:, :, :, pl.ds(0, self.fs)]
        remote(whole, whole, self.swap_send, self.local, here).wait_send()


class Reduce:
    BY_LEFT = (1, 3)

    def __init__(self, places, mine_ref, got_ref, steps, inb, pool, sinks, extras, sems):
        self.p, self.mine, self.got, self.steps, self.inb, self.pool = places, mine_ref, got_ref, steps, inb, pool
        self.sinks, self.extras = sinks, extras
        self.load_sem, self.send, self.spare = sems
        self.order = [at for group in steps for at in group]
        self.sent = [at for at in self.order if at[0]]
        self.first = {group[0] for group in steps}
        self.last = {group[-1] for group in steps}

    def columns(self, s):
        nz, dz = self.p.nz, self.inb.shape[4]
        return pl.ds(pl.multiple_of((self.p.z + nz - s) % nz * dz, dz), dz)

    def loads(self, i):
        k, s = self.order[i]
        slot = i % 2
        at = self.columns(s)
        sources = [self.mine.at[k, :, :, at], self.got.at[k, :, :, at]] + self.extras(k, s)[0]
        return [pltpu.make_async_copy(src, self.inb.at[slot, j], self.load_sem.at[slot, j]) for j, src in enumerate(sources)]

    def begin(self, group):
        at = self.order.index(self.steps[group][0])
        for i in range(at, min(at + 2, at + len(self.steps[group]))):
            for c in self.loads(i):
                c.start()

    def sum_of(self, k, s, out):
        i = self.order.index((k, s))
        loads = self.loads(i)
        for c in loads:
            c.wait()
        for j in range(3):
            total = self.inb[i % 2, 0, j].astype(F32)
            for n in range(1, len(loads)):
                total = total + self.inb[i % 2, n, j].astype(F32)
            for ref in self.extras(k, s)[1]:
                total = total + ref[j].astype(F32)
            out[j] = total.astype(BF16)
        group = next(g for g in self.steps if (k, s) in g)
        if group.index((k, s)) + 2 < len(group):
            for c in self.loads(i + 2):
                c.start()

    def sender(self, n):
        k, s = self.sent[n]
        slot = n % self.pool.shape[0]
        left = k == 1 or (k == 2 and s in self.BY_LEFT)
        ref, recv = self.sinks[k]
        to = self.p.at(ha=self.p.left_to if left else self.p.right_to)
        return remote(self.pool.at[slot], ref.at[s], self.send.at[slot], recv.at[s], to)

    def wait_in(self, k, s):
        ref, recv = self.sinks[k]
        remote(ref.at[s], ref.at[s], self.spare, recv.at[s], self.p.at(ha=self.p.right_to)).wait_recv()

    def pass_on(self, k, s):
        n = self.sent.index((k, s))
        size = self.pool.shape[0]
        if n >= size:
            self.sender(n - size).wait_send()
        self.sum_of(k, s, self.pool.at[n % size])
        self.sender(n).start()

    def end(self):
        for n in range(max(0, len(self.sent) - self.pool.shape[0]), len(self.sent)):
            self.sender(n).wait_send()


EARLY = [[(1, 2), (1, 0)], [(2, 1), (2, 2), (2, 3), (2, 0)]]


def first_kernel(
    nz, len_ref, x_ref, gain_ref, wq_ref, wk_ref, wv_ref, fv_ref, cos_ref, sin_ref, wo_ref, gain_m_ref, dy_ref, own_ref,
    q_ref, k_ref, v_ref, o_ref, st_ref, nmmt_ref, mixed_ref, dh1_ref, da_ref, dgain_ref, mine_ref, got_ref, far_ref, b1_ref, w_ref,
    h1_ref, branch_ref, nmm_ref, nma_ref, dyt_ref, hbuf, wbuf, gbuf, inb, pool,
    wsem, gsem, gsend, grecv, load_sem, rsend, spare, far_recv, b1_recv, *sems,
):
    g = pl.program_id(0)
    places = Places(nz)
    gather = Gather(places, own_ref, w_ref, sems)
    fs, dz = own_ref.shape[1:]
    reduce = Reduce(
        places, mine_ref, got_ref, EARLY, inb, pool, {1: (b1_ref, b1_recv), 2: (far_ref, far_recv)}, lambda k, s: ([], []),
        (load_sem, rsend, spare),
    )

    @pl.when(g == 0)
    def _():
        gather.begin()
        forward_start(x_ref, gain_ref, nma_ref, h1_ref, st_ref)

    @pl.when(g == 1)
    def _():
        gather.pass_line(1)
        gather.spread(1)

    @pl.when(g == 3)
    def _():
        gather.pass_line(2)
        gather.spread(2)
        gather.sides(0)

    @pl.when(g < STEPS)
    def _():
        forward_group(
            g, len_ref[0], nma_ref, wq_ref, wk_ref, wv_ref, fv_ref, cos_ref, sin_ref, wo_ref,
            q_ref, k_ref, v_ref, o_ref, st_ref, h1_ref,
        )

    starts = [pl.multiple_of((places.z + nz - s) % nz * dz, dz) for s in range(nz)]

    def loads(k):
        return [
            pltpu.make_async_copy(w_ref.at[k, s], wbuf.at[:, :, pl.ds(starts[s], dz)], wsem.at[s])
            for s in range(nz)
        ]

    def fetch(k):
        gather.all_swapped(k)
        for c in loads(k):
            c.start()

    def keep(k):
        return pltpu.make_async_copy(gbuf.at[0], mine_ref.at[k], gsem)

    def push(k):
        return remote(gbuf.at[1], got_ref.at[k], gsend, grecv.at[k], places.at(rows=1 - places.r))

    @pl.when(g == STEPS - 1)
    def _():
        gather.pass_line(3)
        gather.spread(3)
        gather.sides(1)
        forward_end(h1_ref, gain_m_ref, nmm_ref)
        nmmt_ref[...] = nmm_ref[...].T
        dyt_ref[...] = dy_ref[...].T
        fetch(0)
        gather.far(0)
        gather.far(1)
        branch_ref[...] = jnp.zeros_like(branch_ref)
        dh1_ref[...] = jnp.zeros_like(dh1_ref)

    @pl.when(g >= STEPS)
    def _():
        k = g - STEPS
        for c in loads(k):
            c.wait()

        @pl.when(k > 0)
        def _():
            keep(k - 1).wait()

        for group, at in enumerate((2, 3)):
            @pl.when(k == at)
            def _():
                push(at - 1).wait_recv()
                reduce.begin(group)
                for step in EARLY[group]:
                    reduce.pass_on(*step)

        for c in range(2):
            rows = slice(c * fs, (c + 1) * fs)
            gate = nn(wbuf[0, rows, :], nmmt_ref[...])
            up = nn(wbuf[1, rows, :], nmmt_ref[...])
            dh = nn(wbuf[2, rows, :], dyt_ref[...])
            sg = sig(gate)
            silu = gate * sg
            hbuf[2, rows, :] = (silu * up).astype(BF16)
            hbuf[0, rows, :] = (dh * up * (sg * (1.0 + gate * (1.0 - sg)))).astype(BF16)
            hbuf[1, rows, :] = (dh * silu).astype(BF16)
        for at in range(0, SLOT, QB):
            rows = slice(at, at + QB)
            branch_ref[rows, :] += tn(hbuf[2, :, rows], wbuf[2])
            dh1_ref[rows, :] += tn(hbuf[0, :, rows], wbuf[0]) + tn(hbuf[1, :, rows], wbuf[1])

        @pl.when(k == 0)
        def _():
            gather.sides(2)
            gather.sides(3)
            gather.far(2)
            gather.far(3)
            fetch(1)

        @pl.when(k == 1)
        def _():
            for i in range(4):
                gather.opposite(i)
            fetch(2)

        @pl.when(k == 2)
        def _():
            fetch(3)

        @pl.when(k > 0)
        def _():
            push(k - 1).wait_send()

        for c in (1, 0):
            rows = slice(c * fs, (c + 1) * fs)
            gbuf[c, 0] = nn(hbuf[0, rows, :], nmm_ref[...]).astype(BF16)
            gbuf[c, 1] = nn(hbuf[1, rows, :], nmm_ref[...]).astype(BF16)
            gbuf[c, 2] = nn(hbuf[2, rows, :], dy_ref[...]).astype(BF16)
            if c == 0:
                keep(k).start()
            else:
                push(k).start()

    @pl.when(g == pl.num_programs(0) - 1)
    def _():
        total = jnp.zeros(dgain_ref.shape, F32)
        for at in range(0, SLOT, QB):
            rows = slice(at, at + QB)
            h1 = h1_ref[rows, :]
            mixed_ref[rows, :] = (h1 + branch_ref[rows, :]).astype(BF16)
            dv, dgain = norm_back(h1, gain_m_ref[...], dh1_ref[rows, :])
            dh1 = dy_ref[rows, :].astype(F32) + dv
            dh1_ref[rows, :] = dh1
            da_ref[rows, :] = dh1.astype(BF16)
            total = total + dgain
        dgain_ref[...] = total
        nmmt_ref[...] = nma_ref[...].T
        keep(3).wait()
        push(3).wait_send()
        push(0).wait_recv()
        push(3).wait_recv()
        for group in EARLY:
            for step in group:
                reduce.wait_in(*step)
        reduce.end()
        gather.end()


def first_half(length, x, gain, wq, wk, wv, fv, cos, sin, wo, gain_m, dy, own, nz):
    tok = x.shape[0]
    fs, dz = own.shape[1:]
    sds = jax.ShapeDtypeStruct
    once = dict(pipeline_mode=pl.Buffered(1))
    step = lambda g: jnp.minimum(g, STEPS - 1)
    full = pl.BlockSpec((tok, D), lambda g: (0, 0), **once)
    blk = pl.BlockSpec((tok, GW), lambda g: (0, step(g)))
    wblk = pl.BlockSpec((D, GW), lambda g: (0, step(g)))
    vec = pl.BlockSpec((1, D), lambda g: (0, 0), **once)
    tab = pl.BlockSpec((tok, 128), lambda g: (0, 0), **once)
    hbm = pl.BlockSpec(memory_space=pl.ANY)
    sem = pltpu.SemaphoreType.DMA
    piece = (3, fs, dz)
    return pl.pallas_call(
        functools.partial(first_kernel, nz),
        grid=(STEPS + 4,),
        in_specs=[
            pl.BlockSpec(memory_space=pltpu.SMEM), full, vec, wblk, wblk, wblk, blk, tab, tab,
            pl.BlockSpec((GW, D), lambda g: (step(g), 0)), vec, full, hbm,
        ],
        out_specs=[blk, blk, blk, blk, tab, full, full, full, full, vec, hbm, hbm, hbm, hbm, hbm],
        out_shape=[sds((tok, D), BF16)] * 4
        + [sds((tok, 128), BF16), sds((D, tok), BF16), sds((tok, D), BF16), sds((tok, D), F32), sds((tok, D), BF16), sds((1, D), F32)]
        + [sds((4, 3, fs, D), BF16)] * 2
        + [sds((nz, *piece), BF16)] * 2
        + [sds((4, nz, 3, 2 * fs, dz), BF16)],
        scratch_shapes=[
            pltpu.VMEM((tok, D), F32), pltpu.VMEM((tok, D), F32),
            pltpu.VMEM((tok, D), BF16), pltpu.VMEM((D, tok), BF16), pltpu.VMEM((D, tok), BF16),
            pltpu.VMEM((3, 2 * fs, tok), BF16), pltpu.VMEM((3, 2 * fs, D), BF16), pltpu.VMEM((2, 3, fs, D), BF16),
            pltpu.VMEM((2, 2, *piece), BF16), pltpu.VMEM((3, *piece), BF16),
            sem((nz,)), sem, sem, sem((4,)), sem((2, 2)), sem((3,)), sem, sem((nz,)), sem((nz,)),
            sem((4, nz)), sem((4,)), sem((2, nz)), sem, sem, sem, sem, sem,
        ],
        compiler_params=pltpu.CompilerParams(vmem_limit_bytes=63 * MIB, collective_id=1, has_side_effects=True),
        cost_estimate=pl.CostEstimate(flops=84 * 10**9, bytes_accessed=80 * 10**6, transcendentals=10**7),
        name="first_half",
    )(length, x, gain, wq, wk, wv, fv, cos, sin, wo, gain_m, dy, own)


MOVES = {
    (0, 0, 0): [("pass", 3, 1), ("pass", 1, 1), (4, 0)],
    (0, 1, 0): [("pass", 3, 2)],
    (0, 2, 0): [(4, 1), (0, 0)],
    (1, 0, 0): [(0, 1), ("total", 1)],
    (1, 1, 0): [(0, 2), (4, 2)],
    (1, 2, 0): [(1, 0)],
    (2, 0, 0): [(0, 3), (1, 1), ("pass", 3, 3), ("pass", 1, 3), (4, 3)],
    (2, 1, 0): [(0, 4), (1, 2)],
    (2, 2, 0): [(4, 4), (0, 5), (2, 0), ("total", 2)],
    (3, 0, 0): [(2, 1), (1, 3), ("pass", 3, 0), (0, 6), (2, 2)],
    (3, 1, 0): [(1, 4), (4, 5), (0, 7)],
    (3, 2, 0): [(2, 3), (3, 0), (1, 5), (4, 6), (3, 1)],
}
TAIL = [
    [("total", 0), (2, 4)],
    [(1, 6)],
    [("total", 3), (3, 2), (2, 5), (4, 7)],
    [(1, 7), (3, 3), (2, 6), (2, 7)],
]
SEQUENCE = [what for at in sorted(MOVES) for what in MOVES[at]] + [what for moves in TAIL for what in moves]
LATE = [[what[1:] if what[0] == "pass" else (0, what[1]) for what in SEQUENCE if what[0] in ("pass", "total")]]


class Spread:
    def __init__(self, places, m, x, far, r1, r3, zin, piece, y, send, recv, local):
        self.p, self.m, self.x, self.far, self.r1, self.r3, self.zin, self.piece, self.y = places, m, x, far, r1, r3, zin, piece, y
        self.send, self.recv, self.local = send, recv, local
        self.half = D // 2
        self.block = self.half // 4
        self.small = self.block // places.nz
        self.to_left = self.block - self.small

    def own_half(self):
        return pl.multiple_of(self.p.r * self.half, self.half)

    def place_of(self, k):
        return (self.p.a, self.p.left_to, self.p.far_to, self.p.right_to)[k]

    def in_x(self, k, at=0, size=None):
        return pl.ds(pl.multiple_of(self.place_of(k) * self.block + at, self.small), size or self.block)

    def rows(self, k, at=0, size=None):
        return pl.ds(pl.multiple_of(self.p.r * self.half + self.place_of(k) * self.block + at, self.small), size or self.block)

    def small_rows(self, z):
        return pl.ds(pl.multiple_of(self.p.r * self.half + self.p.a * self.block + z * self.small, self.small), self.small)

    def copy(self, stage, src, dst, device):
        return remote(src, dst, self.send, self.recv.at[stage], device)

    def left(self):
        return self.p.at(ha=self.p.left_to)

    def right(self):
        return self.p.at(ha=self.p.right_to)

    def sibling(self):
        return self.p.at(rows=1 - self.p.r)

    def copies(self, stage):
        p, m, y = self.p, self.m, self.y
        h = self.to_left
        others = range(1, p.nz)
        if stage == 0:
            other = pl.ds(pl.multiple_of((1 - p.r) * self.half, self.half), self.half)
            return [(m.at[:, other], self.x, self.sibling())]
        if stage == 1:
            return [
                (m.at[:, self.rows(2, 0, h)], self.far.at[:, pl.ds(0, h)], self.left()),
                (m.at[:, self.rows(2, h, self.block - h)], self.far.at[:, pl.ds(h, self.block - h)], self.right()),
            ]
        if stage == 2:
            return [(m.at[:, self.rows(1)], self.r1, self.left()), (m.at[:, self.rows(3)], self.r3, self.right())]
        if stage == 3:
            to = [(p.z + p.nz - s) % p.nz for s in others]
            return [(m.at[:, self.small_rows(z)], self.zin.at[s], p.at(ma=z)) for s, z in zip(others, to)]
        if stage == 4:
            return [(self.piece, y.at[:, self.small_rows(p.z)], p.at(ma=(p.z + s) % p.nz)) for s in others]
        if stage == 5:
            here = y.at[:, self.rows(0)]
            return [(here, here, self.right()), (here, here, self.left())]
        if stage == 6:
            cut = self.block - h
            first, second = y.at[:, self.rows(1, 0, cut)], y.at[:, self.rows(3, cut, h)]
            return [(first, first, self.right()), (second, second, self.left())]
        here = y.at[:, pl.ds(self.own_half(), self.half)]
        return [(here, here, self.sibling())]

    def amount(self, stage):
        return (self.half, self.block, 2 * self.block, self.block - self.small, self.block - self.small, 2 * self.block, self.block, self.half)[stage]

    def keep(self):
        return pltpu.make_async_copy(self.piece, self.y.at[:, self.small_rows(self.p.z)], self.local)

    def wait_for(self, stage):
        these = self.m.at[:, pl.ds(0, self.amount(stage))]
        self.copy(stage, these, these, self.sibling()).wait_recv()

    def add(self, at, *others):
        for j in range(self.m.shape[0]):
            total = self.m[j, at, :].astype(F32)
            for ref, place in others:
                total = total + ref[j, place, :].astype(F32)
            self.m[j, at, :] = total.astype(BF16)

    def run(self, stage):
        p = self.p
        h = self.to_left
        rest = self.block - h
        if stage == 1:
            self.wait_for(0)
            self.add(self.rows(2), (self.x, self.in_x(2)))
        elif stage == 2:
            self.wait_for(1)
            self.add(self.rows(1, 0, h), (self.x, self.in_x(1, 0, h)), (self.far, pl.ds(0, h)))
            self.add(self.rows(1, h, rest), (self.x, self.in_x(1, h, rest)))
            self.add(self.rows(3, 0, h), (self.x, self.in_x(3, 0, h)))
            self.add(self.rows(3, h, rest), (self.x, self.in_x(3, h, rest)), (self.far, pl.ds(h, rest)))
        elif stage == 3:
            self.wait_for(2)
            whole = pl.ds(0, self.block)
            self.add(self.rows(0), (self.x, self.in_x(0)), (self.r1, whole), (self.r3, whole))
        elif stage == 4:
            self.wait_for(3)
            for j in range(self.m.shape[0]):
                total = self.m[j, self.small_rows(p.z), :].astype(F32)
                for s in range(1, p.nz):
                    total = total + self.zin[s, j].astype(F32)
                self.piece[j] = total.astype(BF16)
            self.keep().start()
        elif stage == 5:
            self.wait_for(4)
            self.keep().wait()
        elif stage == 6:
            self.wait_for(5)
        elif stage == 7:
            self.wait_for(6)
        for c in self.copies(stage):
            self.copy(stage, *c).start()

    def end(self):
        self.wait_for(7)
        left = sum(self.amount(stage) for stage in range(8))
        while left:
            these = self.m.at[:, pl.ds(0, min(left, D))]
            self.copy(0, these, these, self.sibling()).wait_send()
            left -= min(left, D)


class Gains:
    def __init__(self, places, own, twin, ring, line, send, recv):
        self.p, self.own, self.twin, self.ring, self.line, self.send, self.recv = places, own, twin, ring, line, send, recv

    def to_twin(self):
        return [remote(self.own, self.twin, self.send.at[0], self.recv.at[0], self.p.at(rows=1 - self.p.r))]

    def round_ring(self):
        p, at = self.p, self.ring.at[self.p.a]
        return [remote(at, at, self.send.at[i], self.recv.at[i], p.at(ha=to)) for i, to in ((1, p.right_to), (2, p.left_to), (3, p.far_to))]

    def along_line(self):
        p, at = self.p, self.line.at[self.p.z]
        return [remote(at, at, self.send.at[3 + s], self.recv.at[3 + s], p.at(ma=(p.z + s) % p.nz)) for s in range(1, p.nz)]

    def run(self, stage):
        if stage == 0:
            sends = self.to_twin()
        elif stage == 1:
            for c in self.to_twin():
                c.wait_recv()
            self.ring[pl.ds(self.p.a, 1)] = (self.own[...] + self.twin[...])[None]
            sends = self.round_ring()
        else:
            for c in self.round_ring():
                c.wait_recv()
            self.line[pl.ds(self.p.z, 1)] = (self.ring[0] + self.ring[1] + self.ring[2] + self.ring[3])[None]
            sends = self.along_line()
        for c in sends:
            c.start()

    def end(self, out_ref):
        for c in self.along_line():
            c.wait_recv()
        total = self.line[0]
        for s in range(1, self.p.nz):
            total = total + self.line[s]
        out_ref[...] = total
        for c in self.to_twin() + self.round_ring() + self.along_line():
            c.wait_send()


def second_kernel(
    nz, len_ref, da_ref, wo_ref, q_ref, k_ref, v_ref, o_ref, st_ref, nmt_ref, cos_ref, sin_ref, wq_ref, wk_ref, wv_ref,
    gain_ref, dgm_ref, x_ref, dh1_ref, attn_ref, mine_ref, got_ref, far_ref, b1_ref,
    gt_ref, gf_ref, gains_ref, ywo_ref, y_ref, tiles_ref,
    dq_acc, dq_ref, dk_ref, dv_ref, xbuf, hbuf, tile_sem,
    mo, xo, faro, r1o, r3o, zo, po, mg, xg, farg, r1g, r3g, zg, pg,
    inb, pool, tot, b1_in, b3_in, z_in, gown, gtwin, gring, gline,
    ar_send, ar_recv, ar_local, g_send, g_recv,
    first_sem, load_sem, rsend, spare, b1_recv, b3_recv, z_send, z_recv, swap_send, swap_recv,
):
    g = pl.program_id(0)
    p = Places(nz)

    def extras(block, s):
        if block == 0:
            early = (1, s) in EARLY[0]
            return [b1_ref.at[s]] if early else [], [b3_in.at[s]] if early else [b1_in.at[s], b3_in.at[s]]
        return [far_ref.at[s]] if (s in Reduce.BY_LEFT) == (block == 1) else [], []

    reduce = Reduce(
        p, mine_ref, got_ref, LATE, inb, pool, {1: (b1_in, b1_recv), 3: (b3_in, b3_recv)}, extras, (load_sem, rsend, spare)
    )

    def to_owner(s):
        return remote(tot.at[s], z_in.at[s], z_send.at[s], z_recv.at[s], p.at(ma=(p.z + nz - s) % nz))

    def total_of(s):
        if (1, s) not in EARLY[0]:
            reduce.wait_in(1, s)
        reduce.wait_in(3, s)
        reduce.sum_of(0, s, tot.at[s])
        if s:
            to_owner(s).start()

    def tile_copies():
        return (
            pltpu.make_async_copy(tot.at[0], tiles_ref.at[p.r], spare),
            remote(tot.at[0], tiles_ref.at[p.r], swap_send, swap_recv, p.at(rows=1 - p.r)),
        )

    def finish():
        for s in range(1, nz):
            to_owner(s).wait_recv()
        for j in range(3):
            total = tot[0, j].astype(F32)
            for s in range(1, nz):
                total = total + z_in[s, j].astype(F32)
            tot[0, j] = total.astype(BF16)
        for c in tile_copies():
            c.start()

    sets = mg.shape[0]
    width = mg.shape[3]
    chunks = [
        Spread(
            p, *(v.at[i % sets] for v in (mg, xg, farg, r1g, r3g, zg, pg)), y_ref.at[i],
            ar_send.at[i], ar_recv.at[i], ar_local.at[i],
        )
        for i in range(STEPS)
    ]
    chunks.append(Spread(p, mo, xo, faro, r1o, r3o, zo, po, ywo_ref, ar_send.at[STEPS], ar_recv.at[STEPS], ar_local.at[STEPS]))
    gains = Gains(p, gown, gtwin, gring, gline, g_send, g_recv)

    def move(what):
        if what[0] == "pass":
            reduce.pass_on(*what[1:])
        elif what[0] == "total":
            total_of(what[1])
        else:
            chunks[what[0]].run(what[1])

    def between(pair, kb):
        for at in range(STEPS):
            moves = MOVES.get((at, pair, kb))
            if moves:
                @pl.when(g == at)
                def _():
                    for what in moves:
                        move(what)

    @pl.when(g == 0)
    def _():
        wait = p.meet(
            [p.at(ma=(p.z + s) % nz) for s in range(1, nz)] + [p.at(ha=to) for to in (p.right_to, p.left_to, p.far_to)] + [p.at(rows=1 - p.r)]
        )
        spots = [(i // 3, i % 3) for i in range(4)]
        fills = [
            pltpu.make_async_copy(attn_ref.at[:, pl.ds(i * width, width)], mg.at[spots[i]], first_sem.at[i])
            for i in range(4)
        ]
        for c in fills:
            c.start()
        reduce.begin(0)
        gt_ref[...] = jnp.zeros_like(gt_ref)
        for i in range(4):
            fills[i].wait()
            mo[0, pl.ds(i * width, width), :] = tn(mg[spots[i]], da_ref[...]).astype(BF16)
        wait()

    backward_group(
        g, len_ref[0], da_ref, wo_ref, q_ref, k_ref, v_ref, o_ref, st_ref, cos_ref, sin_ref,
        dq_ref, dk_ref, dv_ref, gf_ref, dq_acc, between,
    )
    for i in range(sets, STEPS):
        @pl.when(g == i)
        def _():
            chunks[i - sets].end()

    for j, ref in enumerate((dq_ref, dk_ref, dv_ref)):
        mg[g % sets, j] = nn(nmt_ref[...], ref[...]).astype(BF16)

    between(2, 0)
    gt_ref[...] += nt(dq_ref[...], wq_ref[...]) + nt(dk_ref[...], wk_ref[...]) + nt(dv_ref[...], wv_ref[...])

    @pl.when(g == STEPS - 1)
    def _():
        def loads(i):
            rows = pl.ds(i * QB, QB)
            return [
                pltpu.make_async_copy(src.at[rows], buf.at[i % 2], tile_sem.at[i % 2, j])
                for j, (src, buf) in enumerate(((x_ref, xbuf), (dh1_ref, hbuf)))
            ]

        tiles = SLOT // QB
        for c in loads(0):
            c.start()
        total = jnp.zeros(gain_ref.shape, F32)
        for i in range(tiles):
            if i + 1 < tiles:
                for c in loads(i + 1):
                    c.start()
            for what in TAIL[i]:
                move(what)
            for c in loads(i):
                c.wait()
            rows = slice(i * QB, (i + 1) * QB)
            dv, dgain = norm_back(xbuf[i % 2].astype(F32), gain_ref[...], gt_ref[rows, :])
            gt_ref[rows, :] = hbuf[i % 2] + dv
            total = total + dgain
        gown[...] = jnp.concatenate([total, dgm_ref[...], jnp.zeros((6, D), F32)], axis=0)
        gains.run(0)
        move((3, 4))
        gains.run(1)
        move((3, 5))
        gains.run(2)
        finish()
        move((3, 6))
        move((3, 7))
        gains.end(gains_ref)
        for i in [STEPS] + list(range(max(0, STEPS - sets), STEPS)):
            chunks[i].end()
        for c in tile_copies():
            c.wait()
        for s in range(1, nz):
            to_owner(s).wait_send()
        reduce.end()


def second_half(length, da, wo, q, k, v, o, st, nmat, cos, sin, wq, wk, wv, gain, dgm, x, dh1, mine, got, far, b1):
    tok = x.shape[0]
    nz, _, fs, dz = far.shape
    sds = jax.ShapeDtypeStruct
    once = dict(pipeline_mode=pl.Buffered(1))
    full = pl.BlockSpec((tok, D), lambda g: (0, 0), **once)
    blk = pl.BlockSpec((tok, GW), lambda g: (0, g))
    wblk = pl.BlockSpec((D, GW), lambda g: (0, g))
    vec = pl.BlockSpec((1, D), lambda g: (0, 0), **once)
    tab = pl.BlockSpec((tok, 128), lambda g: (0, 0), **once)
    hbm = pl.BlockSpec(memory_space=pl.ANY)
    sem = pltpu.SemaphoreType.DMA
    vmem = lambda *shape: pltpu.VMEM(shape, BF16)
    half = D // 2
    block = half // 4
    small = block // nz
    sets = 3
    piece = (3, fs, dz)

    def buffers(n, lead, width):
        return [
            vmem(*n, lead, D, width), vmem(*n, lead, half, width), vmem(*n, lead, block, width), vmem(*n, lead, block, width),
            vmem(*n, lead, block, width), vmem(*n, nz, lead, small, width), vmem(*n, lead, small, width),
        ]

    return pl.pallas_call(
        functools.partial(second_kernel, nz),
        grid=(STEPS,),
        in_specs=[
            pl.BlockSpec(memory_space=pltpu.SMEM), full, pl.BlockSpec((GW, D), lambda g: (g, 0)), blk, blk, blk, blk, tab, full,
            tab, tab, wblk, wblk, wblk, vec, vec, *[hbm] * 7,
        ],
        out_specs=[full, blk, pl.BlockSpec((8, D), lambda g: (0, 0), **once), hbm, hbm, hbm],
        out_shape=[
            sds((tok, D), F32), sds((tok, D), F32), sds((8, D), F32), sds((1, D, D), BF16), sds((STEPS, 3, D, GW), BF16), sds((2, *piece), BF16),
        ],
        scratch_shapes=[
            pltpu.VMEM((tok, GW), F32), vmem(tok, GW), vmem(tok, GW), vmem(tok, GW), vmem(2, QB, D), pltpu.VMEM((2, QB, D), F32), sem((2, 2)),
            *buffers((), 1, D), *buffers((sets,), 3, GW),
            vmem(2, 3, *piece), vmem(4, *piece), vmem(nz, *piece), vmem(nz, *piece), vmem(nz, *piece), vmem(nz, *piece),
            pltpu.VMEM((8, D), F32), pltpu.VMEM((8, D), F32), pltpu.VMEM((4, 8, D), F32), pltpu.VMEM((nz, 8, D), F32),
            sem((STEPS + 1,)), sem((STEPS + 1, 8)), sem((STEPS + 1,)), sem((3 + nz,)), sem((3 + nz,)),
            sem((4,)), sem((2, 3)), sem((4,)), sem, sem((nz,)), sem((nz,)), sem((nz,)), sem((nz,)), sem, sem,
        ],
        compiler_params=pltpu.CompilerParams(vmem_limit_bytes=63 * MIB, collective_id=2, has_side_effects=True),
        cost_estimate=pl.CostEstimate(flops=50 * 10**9, bytes_accessed=80 * 10**6, transcendentals=10**7),
        name="second_half",
    )(length, da, wo, q, k, v, o, st, nmat, cos, sin, wq, wk, wv, gain, dgm, x, dh1, o, mine, got, far, b1)


def mlp_out_kernel(nk, nc, nz, zs_ref, w_ref, hs_ref, dgs_ref, dus_ref, h1_ref, gain_ref, dy_ref, mixed_ref, dh1_ref, da_ref, dgain_ref, branch_ref, dnm_ref):
    fs, dz = w_ref.shape[4:]
    i = pl.program_id(0)
    for s in range(nz):
        b = d = None
        for k in range(nk):
            for c in range(nc):
                rows = pl.ds(c * fs, fs)
                b_one = tn(hs_ref[k, rows, :], w_ref[k, c, s, 2])
                d_one = tn(dgs_ref[k, rows, :], w_ref[k, c, s, 0]) + tn(dus_ref[k, rows, :], w_ref[k, c, s, 1])
                b, d = (b_one, d_one) if b is None else (b + b_one, d + d_one)
        at = pl.ds(pl.multiple_of(zs_ref[s] * dz, dz), dz)
        branch_ref[:, at] = b
        dnm_ref[:, at] = d
    h1 = h1_ref[...]
    mixed_ref[...] = (h1 + branch_ref[...]).astype(BF16)
    dv, dgain = norm_back(h1, gain_ref[...], dnm_ref[...])
    dh1 = dy_ref[...].astype(F32) + dv
    dh1_ref[...] = dh1
    da_ref[...] = dh1.astype(BF16)

    @pl.when(i == 0)
    def _():
        dgain_ref[...] = jnp.zeros_like(dgain_ref)

    dgain_ref[...] += dgain


def mlp_out(zs, w, hs, dgs, dus, h1, gain, dy):
    nk, nc, nz = w.shape[:3]
    tok = h1.shape[0]
    tile = 256
    wspec = pl.BlockSpec(w.shape, lambda i: (0,) * 6, pipeline_mode=pl.Buffered(1))
    hspec = pl.BlockSpec((nk, hs.shape[1], tile), lambda i: (0, 0, i))
    row = pl.BlockSpec((tile, D), lambda i: (i, 0))
    vec = pl.BlockSpec((1, D), lambda i: (0, 0))
    sds = jax.ShapeDtypeStruct
    return pl.pallas_call(
        functools.partial(mlp_out_kernel, nk, nc, nz),
        grid=(tok // tile,),
        in_specs=[pl.BlockSpec(memory_space=pltpu.SMEM), wspec, hspec, hspec, hspec, row, vec, row],
        out_specs=[row, row, row, vec],
        out_shape=[sds((tok, D), BF16), sds((tok, D), F32), sds((tok, D), BF16), sds((1, D), F32)],
        scratch_shapes=[pltpu.VMEM((tile, D), F32)] * 2,
        compiler_params=pltpu.CompilerParams(vmem_limit_bytes=58 * MIB),
        cost_estimate=pl.CostEstimate(flops=18 * 10**9, bytes_accessed=45 * 10**6, transcendentals=0),
        name="mlp_out",
    )(zs, w, hs, dgs, dus, h1, gain, dy)


def tokens_kernel(n, *refs):
    parts, (wq_ref, wk_ref, wv_ref, x_ref, gain_ref, dh1_ref, out_ref, dgain_ref) = refs[: 3 * n], refs[3 * n :]
    i = pl.program_id(0)
    total = None
    for j, w_ref in enumerate((wq_ref, wk_ref, wv_ref)):
        d = parts[j * n][...] if n == 1 else jnp.concatenate([r[...] for r in parts[j * n : (j + 1) * n]], axis=1)
        t = nt(d, w_ref[...])
        total = t if total is None else total + t
    dv, dgain = norm_back(x_ref[...].astype(F32), gain_ref[...], total)
    out_ref[...] = dh1_ref[...] + dv

    @pl.when(i == 0)
    def _():
        dgain_ref[...] = jnp.zeros_like(dgain_ref)

    dgain_ref[...] += dgain


def tokens_grad(dqs, dks, dvs, wq, wk, wv, x, gain, dh1):
    n = len(dqs)
    tok = x.shape[0]
    tile = 256
    row = pl.BlockSpec((tile, D), lambda i: (i, 0))
    full = pl.BlockSpec((D, D), lambda i: (0, 0))
    vec = pl.BlockSpec((1, D), lambda i: (0, 0))
    sds = jax.ShapeDtypeStruct
    return pl.pallas_call(
        functools.partial(tokens_kernel, n),
        grid=(tok // tile,),
        in_specs=[pl.BlockSpec((tile, d.shape[1]), lambda i: (i, 0)) for d in (*dqs, *dks, *dvs)] + [full, full, full, row, vec, row],
        out_specs=[row, vec],
        out_shape=[sds((tok, D), F32), sds((1, D), F32)],
        compiler_params=pltpu.CompilerParams(vmem_limit_bytes=40 * MIB),
        cost_estimate=pl.CostEstimate(flops=7 * 10**9, bytes_accessed=24 * 10**6, transcendentals=0),
        name="tokens_grad",
    )(*dqs, *dks, *dvs, wq, wk, wv, x, gain, dh1)
def body(
    paired, tokens, first_values, lengths, w_query, w_key, w_value, w_out, norm_attn, norm_mlp, w_gate, w_up, w_down, grad_out
):
    nz = lax.axis_size("ma")
    r = lax.axis_index("rows")
    cos, sin = (jnp.asarray(t) for t in rope_tables())
    gain_a, gain_m = norm_attn[None], norm_mlp[None]
    tile = jnp.stack([w_gate.T, w_up.T, w_down])
    if paired:
        fs = tile.shape[1] // 2
        own = lax.dynamic_slice_in_dim(tile, r * fs, fs, axis=1)
        q, k, v, o, st, nmat, mixed, dh1, da, dgain_m, mine, got, far, b1, _ = first_half(
            lengths, tokens, gain_a, w_query, w_key, w_value, first_values, cos, sin, w_out, gain_m, grad_out, own, nz
        )
        grad_tokens, grad_first, gains, grad_wout, grads, tiles = second_half(
            lengths, da, w_out, q, k, v, o, st, nmat, cos, sin, w_query, w_key, w_value, gain_a, dgain_m, tokens, dh1,
            mine, got, far, b1,
        )
        gain_grads = gains[0], gains[1]
        grad_wout = grad_wout[0].astype(F32)
        grad_q, grad_k, grad_v = (jnp.concatenate(list(grads[:, j]), axis=1).astype(F32) for j in range(3))
        tiles = tiles.transpose(1, 0, 2, 3).reshape(tile.shape).astype(F32)
    else:
        w = lax.all_gather(lax.all_gather(tile, "ma", axis=0), "ha", axis=0)[:, None]
        zs = jnp.arange(nz, dtype=jnp.int32)
        q, k, v, o, st, nma, h1, nmm = attention_forward(
            lengths, tokens, gain_a, w_query, w_key, w_value, first_values, cos, sin, w_out, gain_m
        )
        nmat, ot, nmmt, dyt = prepare(nma, o, nmm, grad_out)
        done = [mlp_block(zs, [[w[i, 0, j] for j in range(nz)]], nmmt, dyt, nmm, grad_out) for i in range(w.shape[0])]
        hs, dgs, dus, mine = (jnp.stack([d[j] for d in done]) for j in range(4))
        mixed, dh1, da, dgain_m = mlp_out(zs, w, hs, dgs, dus, h1, gain_m, grad_out)
        dq, dk, dv, grad_first, grads = attention_backward(
            0, H // GROUP, lengths, da, w_out, q, k, v, o, st, nmat, cos, sin
        )
        grad_tokens, dgain_a = tokens_grad([dq], [dk], [dv], w_query, w_key, w_value, tokens, gain_a, dh1)
        part = lax.psum_scatter(lax.psum_scatter(mine, "ha", scatter_dimension=0), "ma", scatter_dimension=0)
        tiles = lax.psum(part, "rows").astype(F32)
        grad_wout, grads, *gains = lax.psum((wout_grad(ot, da), grads, dgain_a, dgain_m), ("rows", "ha", "ma"))
        grad_wout = grad_wout.astype(F32)
        grad_q, grad_k, grad_v = (grads[j].astype(F32) for j in range(3))
        gain_grads = [v[0] for v in gains]
    return (
        mixed, grad_tokens, 0.5 * grad_first, grad_q, grad_k, grad_v, grad_wout, gain_grads[0], gain_grads[1],
        tiles[0].T, tiles[1].T, tiles[2],
    )


def solution(mesh):
    tok = P(("rows", "ha", "ma"), None)
    gate, down = P("ma", "ha"), P("ha", "ma")
    return jax.shard_map(
        functools.partial(body, mesh.shape["rows"] == 2),
        mesh=mesh,
        in_specs=(tok, tok, P(("rows", "ha", "ma")), P(), P(), P(), P(), P(), P(), gate, gate, down, tok),
        out_specs=(tok, tok, tok, P(), P(), P(), P(), P(), P(), gate, gate, down),
        check_vma=False,
    )
```

```python
import functools
import math

import jax
import jax.numpy as jnp
import numpy as np
from jax import lax
from jax.experimental import pallas as pl
from jax.experimental.pallas import tpu as pltpu
from jax.sharding import PartitionSpec as P

D = 1024
H = 16
HD = 64
SLOT = 1024
EPS = 1e-06
GROUP = 4
GW = GROUP * HD
QB = 256
SCALE = 1.0 / math.sqrt(HD)
C2 = SCALE * math.log2(math.e)
F32 = jnp.float32
BF16 = jnp.bfloat16
MIB = 1 << 20


def nn(a, b):
    return lax.dot_general(a, b, (((1,), (0,)), ((), ())), preferred_element_type=F32)


def nt(a, b):
    return lax.dot_general(a, b, (((1,), (1,)), ((), ())), preferred_element_type=F32)


def tn(a, b):
    return lax.dot_general(a, b, (((0,), (0,)), ((), ())), preferred_element_type=F32)


def rope_tables():
    place = np.arange(SLOT, dtype=np.float32)
    frequency = np.float32(10000.0) ** (-np.arange(HD // 2, dtype=np.float32) * np.float32(2.0) / np.float32(HD))
    angles = place[:, None] * frequency[None, :]
    cosine, sine = np.cos(angles), np.sin(angles)
    cos_row = np.concatenate([cosine] * 4, axis=1)
    sin_row = np.concatenate([-sine, sine, -sine, sine], axis=1)
    return cos_row.astype(np.float32), sin_row.astype(np.float32)


def lanes(shape):
    return lax.broadcasted_iota(jnp.int32, shape, 1)


def partner(v):
    first = (lanes(v.shape) & 63) < 32
    return jnp.where(first, pltpu.roll(v, 96, 1), pltpu.roll(v, 32, 1))


def turn(v, cos, sin):
    parts = []
    for at in range(0, v.shape[1], 128):
        piece = v[:, at : at + 128]
        parts.append(piece * cos + partner(piece) * sin)
    return jnp.concatenate(parts, axis=1)


def low3(v):
    hi = v.astype(BF16).astype(F32)
    rest = v - hi
    mid = rest.astype(BF16).astype(F32)
    return hi, mid, rest - mid


def forward_start(x_ref, gain_ref, nma_ref, h1_ref, st_ref):
    x = x_ref[...].astype(F32)
    r = lax.rsqrt(jnp.mean(x * x, axis=-1, keepdims=True) + EPS)
    nma_ref[...] = (x * r * gain_ref[...]).astype(BF16)
    h1_ref[...] = x
    st_ref[...] = jnp.zeros_like(st_ref)


def forward_end(h1_ref, gain_m_ref, nmm_ref):
    h = h1_ref[...]
    r = lax.rsqrt(jnp.mean(h * h, axis=-1, keepdims=True) + EPS)
    nmm_ref[...] = (h * r * gain_m_ref[...]).astype(BF16)


def forward_group(
    g, length, nma_ref, wq_ref, wk_ref, wv_ref, fv_ref, cos_ref, sin_ref, wo_ref,
    q_ref, k_ref, v_ref, o_ref, st_ref, h1_ref, between=None,
):
    nm = nma_ref[...]
    cos, sin = cos_ref[...], sin_ref[...]
    q_ref[...] = turn(nn(nm, wq_ref[...]), cos, sin).astype(BF16)
    k_ref[...] = turn(nn(nm, wk_ref[...]), cos, sin).astype(BF16)
    v_ref[...] = (0.5 * nn(nm, wv_ref[...]) + 0.5 * fv_ref[...].astype(F32)).astype(BF16)
    tile = (SLOT, 128)
    lane = lanes(tile)
    row = lax.broadcasted_iota(jnp.int32, tile, 0)
    k_extra = jnp.where((lane == 0) & (row >= length), -1e30, 0.0).astype(BF16)
    q_extra = jnp.where(lane == 0, 1.0, 0.0).astype(BF16)
    ones = jnp.ones(tile, BF16)
    low_lane = lane < HD
    qlane = lanes((QB, 128))
    causal = lax.broadcasted_iota(jnp.int32, (QB, QB), 1) <= lax.broadcasted_iota(jnp.int32, (QB, QB), 0)
    for pair in range(GROUP // 2):
        cols = pl.ds(pair * 128, 128)
        qp, kp, vp = q_ref[:, cols], k_ref[:, cols], v_ref[:, cols]
        q_ext = jnp.concatenate([qp, q_extra], axis=1)
        k_exts, v_exts = [], []
        for e in range(2):
            mine = low_lane if e == 0 else ~low_lane
            k_exts.append(jnp.concatenate([jnp.where(mine, kp, 0), k_extra], axis=1))
            v_exts.append(jnp.concatenate([jnp.where(mine, vp, 0), ones], axis=1))
        for qb in range(SLOT // QB):
            if between is not None:
                between(pair, qb)
            rows = slice(qb * QB, (qb + 1) * QB)
            top = (qb + 1) * QB
            out = None
            stats = st_ref[rows, :].astype(F32)
            for e in range(2):
                s = nt(q_ext[rows], k_exts[e][:top])
                diag = jnp.where(causal, s[:, top - QB :], -1e30)
                s = diag if qb == 0 else jnp.concatenate([s[:, : top - QB], diag], axis=1)
                m = jnp.max(s, axis=-1, keepdims=True)
                p = jnp.exp2((s - m) * C2).astype(BF16)
                res = nn(p, v_exts[e][:top])
                total = res[:, 128:]
                part = res[:, :128] / total
                out = part if out is None else out + part
                hi, mid, rest = low3(m + jnp.log2(total) * (1.0 / C2))
                base = 8 * (g * GROUP + pair * 2 + e)
                stats = jnp.where(qlane == base, hi, stats)
                stats = jnp.where(qlane == base + 1, mid, stats)
                stats = jnp.where(qlane == base + 2, rest, stats)
                stats = jnp.where(qlane == base + 3, 1.0, stats)
            o_ref[rows, cols] = out.astype(BF16)
            st_ref[rows, :] = stats.astype(BF16)
    h1_ref[...] += nn(o_ref[...], wo_ref[...])


def fwd_kernel(
    len_ref, x_ref, gain_ref, wq_ref, wk_ref, wv_ref, fv_ref, cos_ref, sin_ref, wo_ref, gain_m_ref,
    q_ref, k_ref, v_ref, o_ref, st_ref, nma_ref, h1_ref, nmm_ref,
):
    g = pl.program_id(0)

    @pl.when(g == 0)
    def _():
        forward_start(x_ref, gain_ref, nma_ref, h1_ref, st_ref)

    forward_group(
        g, len_ref[0], nma_ref, wq_ref, wk_ref, wv_ref, fv_ref, cos_ref, sin_ref, wo_ref,
        q_ref, k_ref, v_ref, o_ref, st_ref, h1_ref,
    )

    @pl.when(g == pl.num_programs(0) - 1)
    def _():
        forward_end(h1_ref, gain_m_ref, nmm_ref)


def attention_forward(length, x, gain, wq, wk, wv, fv, cos, sin, wo, gain_m):
    whole = lambda *_: (0, 0)
    col = lambda g, *_: (0, g)
    tok = x.shape[0]
    full = pl.BlockSpec((tok, D), whole)
    blk = pl.BlockSpec((tok, GW), col)
    wblk = pl.BlockSpec((D, GW), col)
    vec = pl.BlockSpec((1, D), whole)
    tab = pl.BlockSpec((tok, 128), whole)
    sds = jax.ShapeDtypeStruct
    return pl.pallas_call(
        fwd_kernel,
        grid_spec=pltpu.PrefetchScalarGridSpec(
            num_scalar_prefetch=1,
            grid=(H // GROUP,),
            in_specs=[full, vec, wblk, wblk, wblk, blk, tab, tab, pl.BlockSpec((GW, D), lambda g, *_: (g, 0)), vec],
            out_specs=[blk, blk, blk, blk, tab, full, full, full],
        ),
        out_shape=[sds((tok, D), BF16)] * 4 + [sds((tok, 128), BF16), sds((tok, D), BF16), sds((tok, D), F32), sds((tok, D), BF16)],
        compiler_params=pltpu.CompilerParams(vmem_limit_bytes=56 * MIB),
        cost_estimate=pl.CostEstimate(flops=30 * 10**9, bytes_accessed=40 * 10**6, transcendentals=10**7),
        name="attention_forward",
    )(length, x, gain, wq, wk, wv, fv, cos, sin, wo, gain_m)


def prep_kernel(*refs):
    count = len(refs) // 2
    for src, dst in zip(refs[:count], refs[count:]):
        dst[...] = src[...].T


def prepare(*arrays):
    vm = pl.BlockSpec(memory_space=pltpu.VMEM)
    tok = arrays[0].shape[0]
    return pl.pallas_call(
        prep_kernel,
        in_specs=[vm] * len(arrays),
        out_specs=[vm] * len(arrays),
        out_shape=[jax.ShapeDtypeStruct((D, tok), BF16)] * len(arrays),
        compiler_params=pltpu.CompilerParams(vmem_limit_bytes=30 * MIB),
        cost_estimate=pl.CostEstimate(flops=10**9, bytes_accessed=4 * len(arrays) * 10**6, transcendentals=0),
        name="prepare",
    )(*arrays)


def wout_kernel(ot_ref, da_ref, out_ref):
    out_ref[...] = nn(ot_ref[...], da_ref[...]).astype(BF16)


def wout_grad(ot, da):
    vm = pl.BlockSpec(memory_space=pltpu.VMEM)
    return pl.pallas_call(
        wout_kernel,
        in_specs=[vm] * 2,
        out_specs=vm,
        out_shape=jax.ShapeDtypeStruct((D, D), BF16),
        compiler_params=pltpu.CompilerParams(vmem_limit_bytes=30 * MIB),
        cost_estimate=pl.CostEstimate(flops=2 * 10**9, bytes_accessed=6 * 10**6, transcendentals=0),
        name="wout_grad",
    )(ot, da)


def backward_group(
    g, length, da_ref, wo_ref, q_ref, k_ref, v_ref, o_ref, st_ref, cos_ref, sin_ref, dq_ref, dk_ref, dv_ref, gf_ref, dq_acc, between=None
):
    do_all = nt(da_ref[...], wo_ref[...]).astype(BF16)
    prod = do_all.astype(F32) * o_ref[...].astype(F32)
    hi = prod.astype(BF16)
    lo = (prod - hi.astype(F32)).astype(BF16)
    sel_row = lax.broadcasted_iota(jnp.int32, (GW, 128), 0) // HD + g * GROUP
    sel_lane = lanes((GW, 128))
    pick = jnp.where((sel_lane // 8 == sel_row) & ((sel_lane & 7) >= 4) & ((sel_lane & 7) <= 5), 1.0, 0.0).astype(BF16)
    delta = nn(hi, pick) + nn(lo, pick)
    tile = (SLOT, 128)
    lane = lanes(tile)
    d_hi = delta.astype(BF16)
    d_ext = jnp.where((lane & 7) == 4, d_hi.astype(F32), delta - d_hi.astype(F32)).astype(BF16)
    row = lax.broadcasted_iota(jnp.int32, tile, 0)
    dead = row >= length
    low_lane = lane < HD
    st = st_ref[...]
    visible = lax.broadcasted_iota(jnp.int32, (QB, QB), 0) <= lax.broadcasted_iota(jnp.int32, (QB, QB), 1)
    dq_acc[...] = jnp.zeros_like(dq_acc)
    for pair in range(GROUP // 2):
        cols = pl.ds(pair * 128, 128)
        qp, kp, vp = q_ref[:, cols], k_ref[:, cols], v_ref[:, cols]
        dop = do_all[:, pair * 128 : pair * 128 + 128]
        q_ext = jnp.concatenate([qp, st], axis=1)
        do_ext = jnp.concatenate([dop, d_ext], axis=1)
        heads = []
        for e in range(2):
            mine = low_lane if e == 0 else ~low_lane
            at = lane - 8 * (g * GROUP + pair * 2 + e)
            k_x = jnp.where((at >= 0) & (at < 3), -1.0, jnp.where((at == 3) & dead, -1e30, 0.0)).astype(BF16)
            v_x = jnp.where((at >= 4) & (at < 6), -1.0, 0.0).astype(BF16)
            k_m = jnp.where(mine, kp, 0)
            heads.append((
                k_m,
                jnp.concatenate([k_m, k_x], axis=1),
                jnp.concatenate([jnp.where(mine, vp, 0), v_x], axis=1),
                jnp.where(mine, qp, 0),
                jnp.where(mine, dop, 0),
            ))
        for kb in range(SLOT // QB):
            if between is not None:
                between(pair, kb)
            rows = slice(kb * QB, (kb + 1) * QB)
            start = kb * QB
            dk = dv = None
            for k_m, k_ext, v_ext, q_m, do_m in heads:
                st_ = nt(k_ext[rows], q_ext[start:])
                dp = nt(v_ext[rows], do_ext[start:])
                p = jnp.exp2(st_ * C2)
                diag = jnp.where(visible, p[:, :QB], 0.0)
                p = diag if kb == SLOT // QB - 1 else jnp.concatenate([diag, p[:, QB:]], axis=1)
                ds = (p * dp).astype(BF16)
                p = p.astype(BF16)
                dv_e = nn(p, do_m[start:])
                dk_e = nn(ds, q_m[start:])
                dk = dk_e if dk is None else dk + dk_e
                dv = dv_e if dv is None else dv + dv_e
                dq_acc[start:, cols] += tn(ds, k_m[rows])
            dk = dk * SCALE
            cos, sin = cos_ref[rows, :], sin_ref[rows, :]
            dk_ref[rows, cols] = (dk * cos - partner(dk) * sin).astype(BF16)
            half = 0.5 * dv
            gf_ref[rows, cols] = dv
            dv_ref[rows, cols] = half.astype(BF16)
    cos, sin = cos_ref[...], sin_ref[...]
    for pair in range(GROUP // 2):
        cols = pl.ds(pair * 128, 128)
        dq = dq_acc[:, cols] * SCALE
        dq_ref[:, cols] = (dq * cos - partner(dq) * sin).astype(BF16)


def bwd_kernel(
    first_group, len_ref, da_ref, wo_ref, q_ref, k_ref, v_ref, o_ref, st_ref, nmt_ref, cos_ref, sin_ref,
    dq_ref, dk_ref, dv_ref, gf_ref, gw_ref, dq_acc,
):
    g = pl.program_id(0) + first_group
    backward_group(
        g, len_ref[0], da_ref, wo_ref, q_ref, k_ref, v_ref, o_ref, st_ref, cos_ref, sin_ref, dq_ref, dk_ref, dv_ref, gf_ref, dq_acc
    )
    for j, ref in enumerate((dq_ref, dk_ref, dv_ref)):
        gw_ref[j] = nn(nmt_ref[...], ref[...]).astype(BF16)


def attention_backward(first_group, groups, length, da, wo, q, k, v, o, st, nmt, cos, sin):
    whole = lambda *_: (0, 0)
    tok = da.shape[0]
    full = pl.BlockSpec((tok, D), whole)
    blk_in = pl.BlockSpec((tok, GW), lambda g, *_: (0, g + first_group))
    blk = pl.BlockSpec((tok, GW), lambda g, *_: (0, g))
    tab = pl.BlockSpec((tok, 128), whole)
    sds = jax.ShapeDtypeStruct
    width = groups * GW
    return pl.pallas_call(
        functools.partial(bwd_kernel, first_group),
        grid_spec=pltpu.PrefetchScalarGridSpec(
            num_scalar_prefetch=1,
            grid=(groups,),
            in_specs=[full, pl.BlockSpec((GW, D), lambda g, *_: (g + first_group, 0)), blk_in, blk_in, blk_in, blk_in, tab, pl.BlockSpec((D, tok), whole), tab, tab],
            out_specs=[blk, blk, blk, blk, pl.BlockSpec((3, D, GW), lambda g, *_: (0, 0, g))],
            scratch_shapes=[pltpu.VMEM((tok, GW), F32)],
        ),
        out_shape=[sds((tok, width), BF16)] * 3 + [sds((tok, width), F32), sds((3, D, width), BF16)],
        compiler_params=pltpu.CompilerParams(vmem_limit_bytes=56 * MIB),
        cost_estimate=pl.CostEstimate(flops=10 * 10**9 * groups, bytes_accessed=10 * 10**6, transcendentals=groups * 3 * 10**6),
        name="attention_backward",
    )(length, da, wo, q, k, v, o, st, nmt, cos, sin)


def sig(v):
    return 1.0 / (1.0 + jnp.exp(-v))


def mlp_kernel(nc, nz, zs_ref, *refs):
    pieces = refs[: nc * nz]
    nmt_ref, dyt_ref, nm_ref, dy_ref, h_ref, dg_ref, du_ref = refs[nc * nz : nc * nz + 7]
    outs = refs[nc * nz + 7 :]
    fs = pieces[0].shape[1]
    dz = pieces[0].shape[2]
    starts = [pl.multiple_of(zs_ref[s] * dz, dz) for s in range(nz)]
    for c in range(nc):
        gate = up = dh = None
        for s in range(nz):
            w_ref = pieces[c * nz + s]
            at = pl.ds(starts[s], dz)
            nmt, dyt = nmt_ref[at, :], dyt_ref[at, :]
            parts = nn(w_ref[0], nmt), nn(w_ref[1], nmt), nn(w_ref[2], dyt)
            gate, up, dh = parts if gate is None else (gate + parts[0], up + parts[1], dh + parts[2])
        sg = sig(gate)
        silu = gate * sg
        rows = pl.ds(c * fs, fs)
        h = (silu * up).astype(BF16)
        dg = (dh * up * (sg * (1.0 + gate * (1.0 - sg)))).astype(BF16)
        du = (dh * silu).astype(BF16)
        h_ref[rows, :], dg_ref[rows, :], du_ref[rows, :] = h, dg, du
        for s in range(nz):
            at = pl.ds(starts[s], dz)
            nm, dy = nm_ref[:, at], dy_ref[:, at]
            outs[c][s, 0] = nn(dg, nm).astype(BF16)
            outs[c][s, 1] = nn(du, nm).astype(BF16)
            outs[c][s, 2] = nn(h, dy).astype(BF16)


def mlp_block(zs, pieces, nmt, dyt, nm, dy):
    nc, nz = len(pieces), len(pieces[0])
    _, fs, dz = pieces[0][0].shape
    tok = nm.shape[0]
    sds = jax.ShapeDtypeStruct
    vm = pl.BlockSpec(memory_space=pltpu.VMEM)
    return pl.pallas_call(
        functools.partial(mlp_kernel, nc, nz),
        in_specs=[pl.BlockSpec(memory_space=pltpu.SMEM)] + [vm] * (nc * nz + 4),
        out_specs=[vm] * (3 + nc),
        out_shape=[sds((nc * fs, tok), BF16)] * 3 + [sds((nz, 3, fs, dz), BF16)] * nc,
        compiler_params=pltpu.CompilerParams(vmem_limit_bytes=44 * MIB),
        cost_estimate=pl.CostEstimate(flops=12 * nc * fs * D * tok, bytes_accessed=15 * 10**6, transcendentals=nc * fs * tok),
        name="mlp_block",
    )(zs, *[p for c in pieces for p in c], nmt, dyt, nm, dy)


MESH = pl.DeviceIdType.MESH
RING = (0, 1, 3, 2)
STEPS = H // GROUP
TURNS = (0, 1, 3, 2)


def table(index, values):
    out = values[0]
    for i, v in enumerate(values[1:], 1):
        out = jnp.where(index == i, v, out)
    return out


def norm_back(v, gain, grad):
    ms = jnp.mean(v * v, axis=-1, keepdims=True) + EPS
    r = lax.rsqrt(ms)
    gg = grad * gain
    inner = jnp.mean(gg * v, axis=-1, keepdims=True)
    dv = r * gg - v * (inner * r * r * r)
    dgain = jnp.sum(grad * v * r, axis=0, keepdims=True)
    return dv, dgain


class Places:
    def __init__(self, nz):
        self.nz = nz
        self.r, self.a, self.z = (lax.axis_index(n) for n in ("rows", "ha", "ma"))
        self.spot = table(self.a, [RING.index(i) for i in range(4)])
        self.right_to = table(self.spot, [RING[(i + 1) % 4] for i in range(4)])
        self.left_to = table(self.spot, [RING[(i + 3) % 4] for i in range(4)])
        self.far_to = table(self.spot, [RING[(i + 2) % 4] for i in range(4)])
        self.arrivals = [0] + [table(self.z, v) for v in ((3, 1, 3, 1), (2, 3, 1, 2), (1, 2, 2, 3))]

    def at(self, **moved):
        place = {"rows": self.r, "ha": self.a, "ma": self.z, **moved}
        return (place["rows"], place["ha"], place["ma"])

    def meet(self, others):
        barrier = pltpu.get_barrier_semaphore()
        for other in others:
            pl.semaphore_signal(barrier, inc=1, device_id=other, device_id_type=MESH)
        return lambda: pl.semaphore_wait(barrier, len(others))


def remote(src, dst, send, recv, device):
    return pltpu.make_async_remote_copy(
        src_ref=src, dst_ref=dst, send_sem=send, recv_sem=recv, device_id=device, device_id_type=MESH
    )


class Gather:
    def __init__(self, places, own_ref, w_ref, sems):
        self.p, self.own, self.w = places, own_ref, w_ref
        self.recv, self.swap_recv, self.z_send, self.right_send, self.left_send, self.far_send, self.swap_send, self.local = sems
        self.fs = own_ref.shape[1]

    def part(self, k, s, c=0):
        return self.w.at[k, s, :, pl.ds(c * self.fs, self.fs)]

    def copy(self, src, dst, send, device):
        return remote(self.part(*src), self.part(*dst), send, self.recv.at[dst], device)

    def right(self, s):
        return self.copy((0, s), (1, s), self.right_send, self.p.at(ha=self.p.right_to))

    def left(self, s):
        return self.copy((0, s), (3, s), self.left_send, self.p.at(ha=self.p.left_to))

    def far_copy(self, i):
        s = self.p.arrivals[i]
        if i % 2 == 0:
            return self.copy((1, s), (2, s), self.far_send, self.p.at(ha=self.p.right_to))
        return self.copy((3, s), (2, s), self.far_send, self.p.at(ha=self.p.left_to))

    def swap(self, k, s):
        return remote(self.part(k, s), self.part(k, s, 1), self.swap_send, self.swap_recv.at[k], self.p.at(rows=1 - self.p.r))

    def arrived(self, k, s):
        self.copy((k, s), (k, s), self.local, self.p.at(rows=1 - self.p.r)).wait_recv()

    def all_swapped(self, k):
        half = self.w.at[k, :, :, pl.ds(self.fs, self.fs)]
        remote(half, half, self.local, self.swap_recv.at[k], self.p.at(rows=1 - self.p.r)).wait_recv()

    def line(self, d, act, wait):
        nz, z = self.p.nz, self.p.z

        def up(cond):
            pl.when(cond & (z < nz - 1))(
                lambda: act(self.copy((0, d), (0, d + 1), self.z_send.at[0, d], self.p.at(ma=z + 1)))
            )

        def down(cond):
            pl.when(cond & (z >= 1))(
                lambda: act(self.copy((0, (nz - d) % nz), (0, nz - d - 1), self.z_send.at[1, d], self.p.at(ma=z - 1)))
            )

        if d and wait:
            pl.when(z >= d)(lambda: self.arrived(0, d))
            pl.when(z + d <= nz - 1)(lambda: self.arrived(0, nz - d))
        if d < nz - 1:
            up(z >= d)
            down(z + d <= nz - 1)

    def begin(self):
        p = self.p
        wait = p.meet([
            p.at(ma=(p.z + 1) % p.nz), p.at(ma=(p.z + p.nz - 1) % p.nz), p.at(ha=p.right_to), p.at(ha=p.left_to), p.at(rows=1 - p.r)
        ])
        mine = pltpu.make_async_copy(self.own, self.part(0, 0), self.local)
        mine.start()
        mine.wait()
        wait()
        self.pass_line(0)
        self.spread(0)

    def pass_line(self, d):
        self.line(d, lambda c: c.start(), True)

    def spread(self, i):
        s = self.p.arrivals[i]
        self.right(s).start()
        self.left(s).start()
        self.swap(0, s).start()

    def sides(self, i):
        s = self.p.arrivals[i]
        self.arrived(1, s)
        self.arrived(3, s)
        self.swap(1, s).start()
        self.swap(3, s).start()

    def far(self, i):
        self.far_copy(i).start()

    def opposite(self, i):
        s = self.p.arrivals[i]
        self.arrived(2, s)
        self.swap(2, s).start()

    def end(self):
        for i in range(self.p.nz):
            self.line(i, lambda c: c.wait_send(), False)
        here = self.p.at(rows=1 - self.p.r)
        column = self.w.at[0, :, :, pl.ds(0, self.fs)]
        for send in (self.right_send, self.left_send, self.far_send):
            remote(column, column, send, self.local, here).wait_send()
        whole = self.w.at[:, :, :, pl.ds(0, self.fs)]
        remote(whole, whole, self.swap_send, self.local, here).wait_send()


class Reduce:
    BY_LEFT = (1, 3)

    def __init__(self, places, mine_ref, got_ref, steps, inb, pool, sinks, extras, sems):
        self.p, self.mine, self.got, self.steps, self.inb, self.pool = places, mine_ref, got_ref, steps, inb, pool
        self.sinks, self.extras = sinks, extras
        self.load_sem, self.send, self.spare = sems
        self.order = [at for group in steps for at in group]
        self.sent = [at for at in self.order if at[0]]
        self.first = {group[0] for group in steps}
        self.last = {group[-1] for group in steps}

    def columns(self, s):
        nz, dz = self.p.nz, self.inb.shape[4]
        return pl.ds(pl.multiple_of((self.p.z + nz - s) % nz * dz, dz), dz)

    def loads(self, i):
        k, s = self.order[i]
        slot = i % 2
        at = self.columns(s)
        sources = [self.mine.at[k, :, :, at], self.got.at[k, :, :, at]] + self.extras(k, s)[0]
        return [pltpu.make_async_copy(src, self.inb.at[slot, j], self.load_sem.at[slot, j]) for j, src in enumerate(sources)]

    def begin(self, group):
        at = self.order.index(self.steps[group][0])
        for i in range(at, min(at + 2, at + len(self.steps[group]))):
            for c in self.loads(i):
                c.start()

    def sum_of(self, k, s, out):
        i = self.order.index((k, s))
        loads = self.loads(i)
        for c in loads:
            c.wait()
        for j in range(3):
            total = self.inb[i % 2, 0, j].astype(F32)
            for n in range(1, len(loads)):
                total = total + self.inb[i % 2, n, j].astype(F32)
            for ref in self.extras(k, s)[1]:
                total = total + ref[j].astype(F32)
            out[j] = total.astype(BF16)
        group = next(g for g in self.steps if (k, s) in g)
        if group.index((k, s)) + 2 < len(group):
            for c in self.loads(i + 2):
                c.start()

    def sender(self, n):
        k, s = self.sent[n]
        slot = n % self.pool.shape[0]
        left = k == 1 or (k == 2 and s in self.BY_LEFT)
        ref, recv = self.sinks[k]
        to = self.p.at(ha=self.p.left_to if left else self.p.right_to)
        return remote(self.pool.at[slot], ref.at[s], self.send.at[slot], recv.at[s], to)

    def wait_in(self, k, s):
        ref, recv = self.sinks[k]
        remote(ref.at[s], ref.at[s], self.spare, recv.at[s], self.p.at(ha=self.p.right_to)).wait_recv()

    def pass_on(self, k, s):
        n = self.sent.index((k, s))
        size = self.pool.shape[0]
        if n >= size:
            self.sender(n - size).wait_send()
        self.sum_of(k, s, self.pool.at[n % size])
        self.sender(n).start()

    def end(self):
        for n in range(max(0, len(self.sent) - self.pool.shape[0]), len(self.sent)):
            self.sender(n).wait_send()


EARLY = [[(1, 2), (1, 0)], [(2, 1), (2, 2), (2, 3), (2, 0)]]


def first_kernel(
    nz, len_ref, x_ref, gain_ref, wq_ref, wk_ref, wv_ref, fv_ref, cos_ref, sin_ref, wo_ref, gain_m_ref, dy_ref, own_ref,
    q_ref, k_ref, v_ref, o_ref, st_ref, nmmt_ref, mixed_ref, dh1_ref, da_ref, dgain_ref, mine_ref, got_ref, far_ref, b1_ref, w_ref,
    h1_ref, branch_ref, nmm_ref, nma_ref, dyt_ref, hbuf, wbuf, gbuf, inb, pool,
    wsem, gsem, gsend, grecv, load_sem, rsend, spare, far_recv, b1_recv, *sems,
):
    g = pl.program_id(0)
    places = Places(nz)
    gather = Gather(places, own_ref, w_ref, sems)
    fs, dz = own_ref.shape[1:]
    reduce = Reduce(
        places, mine_ref, got_ref, EARLY, inb, pool, {1: (b1_ref, b1_recv), 2: (far_ref, far_recv)}, lambda k, s: ([], []),
        (load_sem, rsend, spare),
    )

    @pl.when(g == 0)
    def _():
        gather.begin()
        forward_start(x_ref, gain_ref, nma_ref, h1_ref, st_ref)
        dyt_ref[...] = dy_ref[...].T
        branch_ref[...] = jnp.zeros_like(branch_ref)
        dh1_ref[...] = jnp.zeros_like(dh1_ref)

    @pl.when(g == 1)
    def _():
        gather.pass_line(1)
        gather.spread(1)

    @pl.when(g == 3)
    def _():
        gather.pass_line(2)
        gather.spread(2)
        gather.sides(0)

    @pl.when(g < STEPS)
    def _():
        forward_group(
            g, len_ref[0], nma_ref, wq_ref, wk_ref, wv_ref, fv_ref, cos_ref, sin_ref, wo_ref,
            q_ref, k_ref, v_ref, o_ref, st_ref, h1_ref,
        )

    starts = [pl.multiple_of((places.z + nz - s) % nz * dz, dz) for s in range(nz)]

    def loads(k):
        return [
            pltpu.make_async_copy(w_ref.at[k, s], wbuf.at[:, :, pl.ds(starts[s], dz)], wsem.at[s])
            for s in range(nz)
        ]

    def fetch(k):
        gather.all_swapped(k)
        for c in loads(k):
            c.start()

    def keep(k):
        return pltpu.make_async_copy(gbuf.at[0], mine_ref.at[k], gsem)

    def push(k):
        return remote(gbuf.at[1], got_ref.at[k], gsend, grecv.at[k], places.at(rows=1 - places.r))

    @pl.when(g == STEPS - 1)
    def _():
        gather.pass_line(3)
        gather.spread(3)
        gather.sides(1)
        forward_end(h1_ref, gain_m_ref, nmm_ref)
        nmmt_ref[...] = nmm_ref[...].T
        fetch(0)
        gather.far(0)
        gather.far(1)

    @pl.when(g >= STEPS)
    def _():
        k = g - STEPS
        for c in loads(k):
            c.wait()

        @pl.when(k > 0)
        def _():
            keep(k - 1).wait()

        for group, at in enumerate((2, 3)):
            @pl.when(k == at)
            def _():
                push(at - 1).wait_recv()
                reduce.begin(group)
                for step in EARLY[group]:
                    reduce.pass_on(*step)

        for c in range(2):
            rows = slice(c * fs, (c + 1) * fs)
            gate = nn(wbuf[0, rows, :], nmmt_ref[...])
            up = nn(wbuf[1, rows, :], nmmt_ref[...])
            dh = nn(wbuf[2, rows, :], dyt_ref[...])
            sg = sig(gate)
            silu = gate * sg
            hbuf[2, rows, :] = (silu * up).astype(BF16)
            hbuf[0, rows, :] = (dh * up * (sg * (1.0 + gate * (1.0 - sg)))).astype(BF16)
            hbuf[1, rows, :] = (dh * silu).astype(BF16)
        for at in range(0, SLOT, QB):
            rows = slice(at, at + QB)
            branch_ref[rows, :] += tn(hbuf[2, :, rows], wbuf[2])
            dh1_ref[rows, :] += tn(hbuf[0, :, rows], wbuf[0]) + tn(hbuf[1, :, rows], wbuf[1])

        @pl.when(k == 0)
        def _():
            gather.sides(2)
            gather.sides(3)
            gather.far(2)
            gather.far(3)
            fetch(1)

        @pl.when(k == 1)
        def _():
            for i in range(4):
                gather.opposite(i)
            fetch(2)

        @pl.when(k == 2)
        def _():
            fetch(3)

        @pl.when(k > 0)
        def _():
            push(k - 1).wait_send()

        for c in (1, 0):
            rows = slice(c * fs, (c + 1) * fs)
            gbuf[c, 0] = nn(hbuf[0, rows, :], nmm_ref[...]).astype(BF16)
            gbuf[c, 1] = nn(hbuf[1, rows, :], nmm_ref[...]).astype(BF16)
            gbuf[c, 2] = nn(hbuf[2, rows, :], dy_ref[...]).astype(BF16)
            if c == 0:
                keep(k).start()
            else:
                push(k).start()

    @pl.when(g == pl.num_programs(0) - 1)
    def _():
        total = jnp.zeros(dgain_ref.shape, F32)
        for at in range(0, SLOT, QB):
            rows = slice(at, at + QB)
            h1 = h1_ref[rows, :]
            mixed_ref[rows, :] = (h1 + branch_ref[rows, :]).astype(BF16)
            dv, dgain = norm_back(h1, gain_m_ref[...], dh1_ref[rows, :])
            dh1 = dy_ref[rows, :].astype(F32) + dv
            dh1_ref[rows, :] = dh1
            da_ref[rows, :] = dh1.astype(BF16)
            total = total + dgain
        dgain_ref[...] = total
        nmmt_ref[...] = nma_ref[...].T
        keep(3).wait()
        push(3).wait_send()
        push(0).wait_recv()
        push(3).wait_recv()
        for group in EARLY:
            for step in group:
                reduce.wait_in(*step)
        reduce.end()
        gather.end()


def first_half(length, x, gain, wq, wk, wv, fv, cos, sin, wo, gain_m, dy, own, nz):
    tok = x.shape[0]
    fs, dz = own.shape[1:]
    sds = jax.ShapeDtypeStruct
    once = dict(pipeline_mode=pl.Buffered(1))
    step = lambda g: jnp.minimum(g, STEPS - 1)
    full = pl.BlockSpec((tok, D), lambda g: (0, 0), **once)
    blk = pl.BlockSpec((tok, GW), lambda g: (0, step(g)))
    wblk = pl.BlockSpec((D, GW), lambda g: (0, step(g)))
    vec = pl.BlockSpec((1, D), lambda g: (0, 0), **once)
    tab = pl.BlockSpec((tok, 128), lambda g: (0, 0), **once)
    hbm = pl.BlockSpec(memory_space=pl.ANY)
    sem = pltpu.SemaphoreType.DMA
    piece = (3, fs, dz)
    return pl.pallas_call(
        functools.partial(first_kernel, nz),
        grid=(STEPS + 4,),
        in_specs=[
            pl.BlockSpec(memory_space=pltpu.SMEM), full, vec, wblk, wblk, wblk, blk, tab, tab,
            pl.BlockSpec((GW, D), lambda g: (step(g), 0)), vec, full, hbm,
        ],
        out_specs=[blk, blk, blk, blk, tab, full, full, full, full, vec, hbm, hbm, hbm, hbm, hbm],
        out_shape=[sds((tok, D), BF16)] * 4
        + [sds((tok, 128), BF16), sds((D, tok), BF16), sds((tok, D), BF16), sds((tok, D), F32), sds((tok, D), BF16), sds((1, D), F32)]
        + [sds((4, 3, fs, D), BF16)] * 2
        + [sds((nz, *piece), BF16)] * 2
        + [sds((4, nz, 3, 2 * fs, dz), BF16)],
        scratch_shapes=[
            pltpu.VMEM((tok, D), F32), pltpu.VMEM((tok, D), F32),
            pltpu.VMEM((tok, D), BF16), pltpu.VMEM((D, tok), BF16), pltpu.VMEM((D, tok), BF16),
            pltpu.VMEM((3, 2 * fs, tok), BF16), pltpu.VMEM((3, 2 * fs, D), BF16), pltpu.VMEM((2, 3, fs, D), BF16),
            pltpu.VMEM((2, 2, *piece), BF16), pltpu.VMEM((3, *piece), BF16),
            sem((nz,)), sem, sem, sem((4,)), sem((2, 2)), sem((3,)), sem, sem((nz,)), sem((nz,)),
            sem((4, nz)), sem((4,)), sem((2, nz)), sem, sem, sem, sem, sem,
        ],
        compiler_params=pltpu.CompilerParams(vmem_limit_bytes=63 * MIB, collective_id=1, has_side_effects=True),
        cost_estimate=pl.CostEstimate(flops=84 * 10**9, bytes_accessed=80 * 10**6, transcendentals=10**7),
        name="first_half",
    )(length, x, gain, wq, wk, wv, fv, cos, sin, wo, gain_m, dy, own)


MOVES = {
    (0, 0, 0): [("pass", 3, 1), ("pass", 1, 1), (4, 0)],
    (0, 1, 0): [("pass", 3, 2)],
    (0, 2, 0): [(4, 1), (0, 0)],
    (1, 0, 0): [(0, 1), ("total", 1)],
    (1, 1, 0): [(0, 2), (4, 2)],
    (1, 2, 0): [(1, 0)],
    (2, 0, 0): [(0, 3), (1, 1), ("pass", 3, 3), ("pass", 1, 3), (4, 3)],
    (2, 1, 0): [(0, 4), (1, 2)],
    (2, 2, 0): [(4, 4), (0, 5), (2, 0), ("total", 2)],
    (3, 0, 0): [(2, 1), (1, 3), ("pass", 3, 0), (0, 6), (2, 2)],
    (3, 1, 0): [(1, 4), (4, 5), (0, 7)],
    (3, 2, 0): [(2, 3), (3, 0), (1, 5), (4, 6), (3, 1)],
}
TAIL = [
    [("total", 0), (2, 4)],
    [(1, 6)],
    [("total", 3), (3, 2), (2, 5), (4, 7)],
    [(1, 7), (3, 3), (2, 6), (2, 7)],
]
SEQUENCE = [what for at in sorted(MOVES) for what in MOVES[at]] + [what for moves in TAIL for what in moves]
LATE = [[what[1:] if what[0] == "pass" else (0, what[1]) for what in SEQUENCE if what[0] in ("pass", "total")]]


class Spread:
    def __init__(self, places, m, x, far, r1, r3, zin, piece, y, send, recv, local):
        self.p, self.m, self.x, self.far, self.r1, self.r3, self.zin, self.piece, self.y = places, m, x, far, r1, r3, zin, piece, y
        self.send, self.recv, self.local = send, recv, local
        self.half = D // 2
        self.block = self.half // 4
        self.small = self.block // places.nz
        self.to_left = self.block - self.small

    def own_half(self):
        return pl.multiple_of(self.p.r * self.half, self.half)

    def place_of(self, k):
        return (self.p.a, self.p.left_to, self.p.far_to, self.p.right_to)[k]

    def in_x(self, k, at=0, size=None):
        return pl.ds(pl.multiple_of(self.place_of(k) * self.block + at, self.small), size or self.block)

    def rows(self, k, at=0, size=None):
        return pl.ds(pl.multiple_of(self.p.r * self.half + self.place_of(k) * self.block + at, self.small), size or self.block)

    def small_rows(self, z):
        return pl.ds(pl.multiple_of(self.p.r * self.half + self.p.a * self.block + z * self.small, self.small), self.small)

    def copy(self, stage, src, dst, device):
        return remote(src, dst, self.send, self.recv.at[stage], device)

    def left(self):
        return self.p.at(ha=self.p.left_to)

    def right(self):
        return self.p.at(ha=self.p.right_to)

    def sibling(self):
        return self.p.at(rows=1 - self.p.r)

    def copies(self, stage):
        p, m, y = self.p, self.m, self.y
        h = self.to_left
        others = range(1, p.nz)
        if stage == 0:
            other = pl.ds(pl.multiple_of((1 - p.r) * self.half, self.half), self.half)
            return [(m.at[:, other], self.x, self.sibling())]
        if stage == 1:
            return [
                (m.at[:, self.rows(2, 0, h)], self.far.at[:, pl.ds(0, h)], self.left()),
                (m.at[:, self.rows(2, h, self.block - h)], self.far.at[:, pl.ds(h, self.block - h)], self.right()),
            ]
        if stage == 2:
            return [(m.at[:, self.rows(1)], self.r1, self.left()), (m.at[:, self.rows(3)], self.r3, self.right())]
        if stage == 3:
            to = [(p.z + p.nz - s) % p.nz for s in others]
            return [(m.at[:, self.small_rows(z)], self.zin.at[s], p.at(ma=z)) for s, z in zip(others, to)]
        if stage == 4:
            return [(self.piece, y.at[:, self.small_rows(p.z)], p.at(ma=(p.z + s) % p.nz)) for s in others]
        if stage == 5:
            here = y.at[:, self.rows(0)]
            return [(here, here, self.right()), (here, here, self.left())]
        if stage == 6:
            cut = self.block - h
            first, second = y.at[:, self.rows(1, 0, cut)], y.at[:, self.rows(3, cut, h)]
            return [(first, first, self.right()), (second, second, self.left())]
        here = y.at[:, pl.ds(self.own_half(), self.half)]
        return [(here, here, self.sibling())]

    def amount(self, stage):
        return (self.half, self.block, 2 * self.block, self.block - self.small, self.block - self.small, 2 * self.block, self.block, self.half)[stage]

    def keep(self):
        return pltpu.make_async_copy(self.piece, self.y.at[:, self.small_rows(self.p.z)], self.local)

    def wait_for(self, stage):
        these = self.m.at[:, pl.ds(0, self.amount(stage))]
        self.copy(stage, these, these, self.sibling()).wait_recv()

    def add(self, at, *others):
        for j in range(self.m.shape[0]):
            total = self.m[j, at, :].astype(F32)
            for ref, place in others:
                total = total + ref[j, place, :].astype(F32)
            self.m[j, at, :] = total.astype(BF16)

    def run(self, stage):
        p = self.p
        h = self.to_left
        rest = self.block - h
        if stage == 1:
            self.wait_for(0)
            self.add(self.rows(2), (self.x, self.in_x(2)))
        elif stage == 2:
            self.wait_for(1)
            self.add(self.rows(1, 0, h), (self.x, self.in_x(1, 0, h)), (self.far, pl.ds(0, h)))
            self.add(self.rows(1, h, rest), (self.x, self.in_x(1, h, rest)))
            self.add(self.rows(3, 0, h), (self.x, self.in_x(3, 0, h)))
            self.add(self.rows(3, h, rest), (self.x, self.in_x(3, h, rest)), (self.far, pl.ds(h, rest)))
        elif stage == 3:
            self.wait_for(2)
            whole = pl.ds(0, self.block)
            self.add(self.rows(0), (self.x, self.in_x(0)), (self.r1, whole), (self.r3, whole))
        elif stage == 4:
            self.wait_for(3)
            for j in range(self.m.shape[0]):
                total = self.m[j, self.small_rows(p.z), :].astype(F32)
                for s in range(1, p.nz):
                    total = total + self.zin[s, j].astype(F32)
                self.piece[j] = total.astype(BF16)
            self.keep().start()
        elif stage == 5:
            self.wait_for(4)
            self.keep().wait()
        elif stage == 6:
            self.wait_for(5)
        elif stage == 7:
            self.wait_for(6)
        for c in self.copies(stage):
            self.copy(stage, *c).start()

    def end(self):
        self.wait_for(7)
        left = sum(self.amount(stage) for stage in range(8))
        while left:
            these = self.m.at[:, pl.ds(0, min(left, D))]
            self.copy(0, these, these, self.sibling()).wait_send()
            left -= min(left, D)


class Gains:
    def __init__(self, places, own, twin, ring, line, send, recv):
        self.p, self.own, self.twin, self.ring, self.line, self.send, self.recv = places, own, twin, ring, line, send, recv

    def to_twin(self):
        return [remote(self.own, self.twin, self.send.at[0], self.recv.at[0], self.p.at(rows=1 - self.p.r))]

    def round_ring(self):
        p, at = self.p, self.ring.at[self.p.a]
        return [remote(at, at, self.send.at[i], self.recv.at[i], p.at(ha=to)) for i, to in ((1, p.right_to), (2, p.left_to), (3, p.far_to))]

    def along_line(self):
        p, at = self.p, self.line.at[self.p.z]
        return [remote(at, at, self.send.at[3 + s], self.recv.at[3 + s], p.at(ma=(p.z + s) % p.nz)) for s in range(1, p.nz)]

    def run(self, stage):
        if stage == 0:
            sends = self.to_twin()
        elif stage == 1:
            for c in self.to_twin():
                c.wait_recv()
            self.ring[pl.ds(self.p.a, 1)] = (self.own[...] + self.twin[...])[None]
            sends = self.round_ring()
        else:
            for c in self.round_ring():
                c.wait_recv()
            self.line[pl.ds(self.p.z, 1)] = (self.ring[0] + self.ring[1] + self.ring[2] + self.ring[3])[None]
            sends = self.along_line()
        for c in sends:
            c.start()

    def end(self, out_ref):
        for c in self.along_line():
            c.wait_recv()
        total = self.line[0]
        for s in range(1, self.p.nz):
            total = total + self.line[s]
        out_ref[...] = total
        for c in self.to_twin() + self.round_ring() + self.along_line():
            c.wait_send()


def second_kernel(
    nz, len_ref, da_ref, wo_ref, q_ref, k_ref, v_ref, o_ref, st_ref, nmt_ref, cos_ref, sin_ref, wq_ref, wk_ref, wv_ref,
    gain_ref, dgm_ref, x_ref, dh1_ref, attn_ref, mine_ref, got_ref, far_ref, b1_ref,
    gt_ref, gf_ref, gains_ref, ywo_ref, y_ref, tiles_ref,
    dq_acc, dq_ref, dk_ref, dv_ref, xbuf, hbuf, tile_sem,
    mo, xo, faro, r1o, r3o, zo, po, mg, xg, farg, r1g, r3g, zg, pg,
    inb, pool, tot, b1_in, b3_in, z_in, gown, gtwin, gring, gline,
    ar_send, ar_recv, ar_local, g_send, g_recv,
    first_sem, load_sem, rsend, spare, b1_recv, b3_recv, z_send, z_recv, swap_send, swap_recv,
):
    g = pl.program_id(0)
    p = Places(nz)

    def extras(block, s):
        if block == 0:
            early = (1, s) in EARLY[0]
            return [b1_ref.at[s]] if early else [], [b3_in.at[s]] if early else [b1_in.at[s], b3_in.at[s]]
        return [far_ref.at[s]] if (s in Reduce.BY_LEFT) == (block == 1) else [], []

    reduce = Reduce(
        p, mine_ref, got_ref, LATE, inb, pool, {1: (b1_in, b1_recv), 3: (b3_in, b3_recv)}, extras, (load_sem, rsend, spare)
    )

    def to_owner(s):
        return remote(tot.at[s], z_in.at[s], z_send.at[s], z_recv.at[s], p.at(ma=(p.z + nz - s) % nz))

    def total_of(s):
        if (1, s) not in EARLY[0]:
            reduce.wait_in(1, s)
        reduce.wait_in(3, s)
        reduce.sum_of(0, s, tot.at[s])
        if s:
            to_owner(s).start()

    def tile_copies():
        return (
            pltpu.make_async_copy(tot.at[0], tiles_ref.at[p.r], spare),
            remote(tot.at[0], tiles_ref.at[p.r], swap_send, swap_recv, p.at(rows=1 - p.r)),
        )

    def finish():
        for s in range(1, nz):
            to_owner(s).wait_recv()
        for j in range(3):
            total = tot[0, j].astype(F32)
            for s in range(1, nz):
                total = total + z_in[s, j].astype(F32)
            tot[0, j] = total.astype(BF16)
        for c in tile_copies():
            c.start()

    sets = mg.shape[0]
    width = mg.shape[3]
    chunks = [
        Spread(
            p, *(v.at[i % sets] for v in (mg, xg, farg, r1g, r3g, zg, pg)), y_ref.at[:, :, pl.ds(i * width, width)],
            ar_send.at[i], ar_recv.at[i], ar_local.at[i],
        )
        for i in range(STEPS)
    ]
    chunks.append(Spread(p, mo, xo, faro, r1o, r3o, zo, po, ywo_ref, ar_send.at[STEPS], ar_recv.at[STEPS], ar_local.at[STEPS]))
    gains = Gains(p, gown, gtwin, gring, gline, g_send, g_recv)

    def move(what):
        if what[0] == "pass":
            reduce.pass_on(*what[1:])
        elif what[0] == "total":
            total_of(what[1])
        else:
            chunks[what[0]].run(what[1])

    def between(pair, kb):
        for at in range(STEPS):
            moves = MOVES.get((at, pair, kb))
            if moves:
                @pl.when(g == at)
                def _():
                    for what in moves:
                        move(what)

    @pl.when(g == 0)
    def _():
        wait = p.meet(
            [p.at(ma=(p.z + s) % nz) for s in range(1, nz)] + [p.at(ha=to) for to in (p.right_to, p.left_to, p.far_to)] + [p.at(rows=1 - p.r)]
        )
        spots = [(i // 3, i % 3) for i in range(4)]
        fills = [
            pltpu.make_async_copy(attn_ref.at[:, pl.ds(i * width, width)], mg.at[spots[i]], first_sem.at[i])
            for i in range(4)
        ]
        for c in fills:
            c.start()
        reduce.begin(0)
        gt_ref[...] = jnp.zeros_like(gt_ref)
        for i in range(4):
            fills[i].wait()
            mo[0, pl.ds(i * width, width), :] = tn(mg[spots[i]], da_ref[...]).astype(BF16)
        wait()

    backward_group(
        g, len_ref[0], da_ref, wo_ref, q_ref, k_ref, v_ref, o_ref, st_ref, cos_ref, sin_ref,
        dq_ref, dk_ref, dv_ref, gf_ref, dq_acc, between,
    )
    for i in range(sets, STEPS):
        @pl.when(g == i)
        def _():
            chunks[i - sets].end()

    for j, ref in enumerate((dq_ref, dk_ref, dv_ref)):
        mg[g % sets, j] = nn(nmt_ref[...], ref[...]).astype(BF16)

    between(2, 0)
    gt_ref[...] += nt(dq_ref[...], wq_ref[...]) + nt(dk_ref[...], wk_ref[...]) + nt(dv_ref[...], wv_ref[...])

    @pl.when(g == STEPS - 1)
    def _():
        def loads(i):
            rows = pl.ds(i * QB, QB)
            return [
                pltpu.make_async_copy(src.at[rows], buf.at[i % 2], tile_sem.at[i % 2, j])
                for j, (src, buf) in enumerate(((x_ref, xbuf), (dh1_ref, hbuf)))
            ]

        tiles = SLOT // QB
        for c in loads(0):
            c.start()
        total = jnp.zeros(gain_ref.shape, F32)
        for i in range(tiles):
            if i + 1 < tiles:
                for c in loads(i + 1):
                    c.start()
            for what in TAIL[i]:
                move(what)
            for c in loads(i):
                c.wait()
            rows = slice(i * QB, (i + 1) * QB)
            dv, dgain = norm_back(xbuf[i % 2].astype(F32), gain_ref[...], gt_ref[rows, :])
            gt_ref[rows, :] = hbuf[i % 2] + dv
            total = total + dgain
        gown[...] = jnp.concatenate([total, dgm_ref[...], jnp.zeros((6, D), F32)], axis=0)
        gains.run(0)
        move((3, 4))
        gains.run(1)
        move((3, 5))
        gains.run(2)
        finish()
        move((3, 6))
        move((3, 7))
        gains.end(gains_ref)
        for i in [STEPS] + list(range(max(0, STEPS - sets), STEPS)):
            chunks[i].end()
        for c in tile_copies():
            c.wait()
        for s in range(1, nz):
            to_owner(s).wait_send()
        reduce.end()


def second_half(length, da, wo, q, k, v, o, st, nmat, cos, sin, wq, wk, wv, gain, dgm, x, dh1, mine, got, far, b1):
    tok = x.shape[0]
    nz, _, fs, dz = far.shape
    sds = jax.ShapeDtypeStruct
    once = dict(pipeline_mode=pl.Buffered(1))
    full = pl.BlockSpec((tok, D), lambda g: (0, 0), **once)
    blk = pl.BlockSpec((tok, GW), lambda g: (0, g))
    wblk = pl.BlockSpec((D, GW), lambda g: (0, g))
    vec = pl.BlockSpec((1, D), lambda g: (0, 0), **once)
    tab = pl.BlockSpec((tok, 128), lambda g: (0, 0), **once)
    hbm = pl.BlockSpec(memory_space=pl.ANY)
    sem = pltpu.SemaphoreType.DMA
    vmem = lambda *shape: pltpu.VMEM(shape, BF16)
    half = D // 2
    block = half // 4
    small = block // nz
    sets = 3
    piece = (3, fs, dz)

    def buffers(n, lead, width):
        return [
            vmem(*n, lead, D, width), vmem(*n, lead, half, width), vmem(*n, lead, block, width), vmem(*n, lead, block, width),
            vmem(*n, lead, block, width), vmem(*n, nz, lead, small, width), vmem(*n, lead, small, width),
        ]

    return pl.pallas_call(
        functools.partial(second_kernel, nz),
        grid=(STEPS,),
        in_specs=[
            pl.BlockSpec(memory_space=pltpu.SMEM), full, pl.BlockSpec((GW, D), lambda g: (g, 0)), blk, blk, blk, blk, tab, full,
            tab, tab, wblk, wblk, wblk, vec, vec, *[hbm] * 7,
        ],
        out_specs=[full, blk, pl.BlockSpec((8, D), lambda g: (0, 0), **once), hbm, hbm, hbm],
        out_shape=[
            sds((tok, D), F32), sds((tok, D), F32), sds((8, D), F32), sds((1, D, D), BF16), sds((3, D, D), BF16), sds((2, *piece), BF16),
        ],
        scratch_shapes=[
            pltpu.VMEM((tok, GW), F32), vmem(tok, GW), vmem(tok, GW), vmem(tok, GW), vmem(2, QB, D), pltpu.VMEM((2, QB, D), F32), sem((2, 2)),
            *buffers((), 1, D), *buffers((sets,), 3, GW),
            vmem(2, 3, *piece), vmem(4, *piece), vmem(nz, *piece), vmem(nz, *piece), vmem(nz, *piece), vmem(nz, *piece),
            pltpu.VMEM((8, D), F32), pltpu.VMEM((8, D), F32), pltpu.VMEM((4, 8, D), F32), pltpu.VMEM((nz, 8, D), F32),
            sem((STEPS + 1,)), sem((STEPS + 1, 8)), sem((STEPS + 1,)), sem((3 + nz,)), sem((3 + nz,)),
            sem((4,)), sem((2, 3)), sem((4,)), sem, sem((nz,)), sem((nz,)), sem((nz,)), sem((nz,)), sem, sem,
        ],
        compiler_params=pltpu.CompilerParams(vmem_limit_bytes=63 * MIB, collective_id=2, has_side_effects=True),
        cost_estimate=pl.CostEstimate(flops=50 * 10**9, bytes_accessed=80 * 10**6, transcendentals=10**7),
        name="second_half",
    )(length, da, wo, q, k, v, o, st, nmat, cos, sin, wq, wk, wv, gain, dgm, x, dh1, o, mine, got, far, b1)


def mlp_out_kernel(nk, nc, nz, zs_ref, w_ref, hs_ref, dgs_ref, dus_ref, h1_ref, gain_ref, dy_ref, mixed_ref, dh1_ref, da_ref, dgain_ref, branch_ref, dnm_ref):
    fs, dz = w_ref.shape[4:]
    i = pl.program_id(0)
    for s in range(nz):
        b = d = None
        for k in range(nk):
            for c in range(nc):
                rows = pl.ds(c * fs, fs)
                b_one = tn(hs_ref[k, rows, :], w_ref[k, c, s, 2])
                d_one = tn(dgs_ref[k, rows, :], w_ref[k, c, s, 0]) + tn(dus_ref[k, rows, :], w_ref[k, c, s, 1])
                b, d = (b_one, d_one) if b is None else (b + b_one, d + d_one)
        at = pl.ds(pl.multiple_of(zs_ref[s] * dz, dz), dz)
        branch_ref[:, at] = b
        dnm_ref[:, at] = d
    h1 = h1_ref[...]
    mixed_ref[...] = (h1 + branch_ref[...]).astype(BF16)
    dv, dgain = norm_back(h1, gain_ref[...], dnm_ref[...])
    dh1 = dy_ref[...].astype(F32) + dv
    dh1_ref[...] = dh1
    da_ref[...] = dh1.astype(BF16)

    @pl.when(i == 0)
    def _():
        dgain_ref[...] = jnp.zeros_like(dgain_ref)

    dgain_ref[...] += dgain


def mlp_out(zs, w, hs, dgs, dus, h1, gain, dy):
    nk, nc, nz = w.shape[:3]
    tok = h1.shape[0]
    tile = 256
    wspec = pl.BlockSpec(w.shape, lambda i: (0,) * 6, pipeline_mode=pl.Buffered(1))
    hspec = pl.BlockSpec((nk, hs.shape[1], tile), lambda i: (0, 0, i))
    row = pl.BlockSpec((tile, D), lambda i: (i, 0))
    vec = pl.BlockSpec((1, D), lambda i: (0, 0))
    sds = jax.ShapeDtypeStruct
    return pl.pallas_call(
        functools.partial(mlp_out_kernel, nk, nc, nz),
        grid=(tok // tile,),
        in_specs=[pl.BlockSpec(memory_space=pltpu.SMEM), wspec, hspec, hspec, hspec, row, vec, row],
        out_specs=[row, row, row, vec],
        out_shape=[sds((tok, D), BF16), sds((tok, D), F32), sds((tok, D), BF16), sds((1, D), F32)],
        scratch_shapes=[pltpu.VMEM((tile, D), F32)] * 2,
        compiler_params=pltpu.CompilerParams(vmem_limit_bytes=58 * MIB),
        cost_estimate=pl.CostEstimate(flops=18 * 10**9, bytes_accessed=45 * 10**6, transcendentals=0),
        name="mlp_out",
    )(zs, w, hs, dgs, dus, h1, gain, dy)


def tokens_kernel(n, *refs):
    parts, (wq_ref, wk_ref, wv_ref, x_ref, gain_ref, dh1_ref, out_ref, dgain_ref) = refs[: 3 * n], refs[3 * n :]
    i = pl.program_id(0)
    total = None
    for j, w_ref in enumerate((wq_ref, wk_ref, wv_ref)):
        d = parts[j * n][...] if n == 1 else jnp.concatenate([r[...] for r in parts[j * n : (j + 1) * n]], axis=1)
        t = nt(d, w_ref[...])
        total = t if total is None else total + t
    dv, dgain = norm_back(x_ref[...].astype(F32), gain_ref[...], total)
    out_ref[...] = dh1_ref[...] + dv

    @pl.when(i == 0)
    def _():
        dgain_ref[...] = jnp.zeros_like(dgain_ref)

    dgain_ref[...] += dgain


def tokens_grad(dqs, dks, dvs, wq, wk, wv, x, gain, dh1):
    n = len(dqs)
    tok = x.shape[0]
    tile = 256
    row = pl.BlockSpec((tile, D), lambda i: (i, 0))
    full = pl.BlockSpec((D, D), lambda i: (0, 0))
    vec = pl.BlockSpec((1, D), lambda i: (0, 0))
    sds = jax.ShapeDtypeStruct
    return pl.pallas_call(
        functools.partial(tokens_kernel, n),
        grid=(tok // tile,),
        in_specs=[pl.BlockSpec((tile, d.shape[1]), lambda i: (i, 0)) for d in (*dqs, *dks, *dvs)] + [full, full, full, row, vec, row],
        out_specs=[row, vec],
        out_shape=[sds((tok, D), F32), sds((1, D), F32)],
        compiler_params=pltpu.CompilerParams(vmem_limit_bytes=40 * MIB),
        cost_estimate=pl.CostEstimate(flops=7 * 10**9, bytes_accessed=24 * 10**6, transcendentals=0),
        name="tokens_grad",
    )(*dqs, *dks, *dvs, wq, wk, wv, x, gain, dh1)
def body(
    paired, tokens, first_values, lengths, w_query, w_key, w_value, w_out, norm_attn, norm_mlp, w_gate, w_up, w_down, grad_out
):
    nz = lax.axis_size("ma")
    r = lax.axis_index("rows")
    cos, sin = (jnp.asarray(t) for t in rope_tables())
    gain_a, gain_m = norm_attn[None], norm_mlp[None]
    tile = jnp.stack([w_gate.T, w_up.T, w_down])
    if paired:
        fs = tile.shape[1] // 2
        own = lax.dynamic_slice_in_dim(tile, r * fs, fs, axis=1)
        q, k, v, o, st, nmat, mixed, dh1, da, dgain_m, mine, got, far, b1, _ = first_half(
            lengths, tokens, gain_a, w_query, w_key, w_value, first_values, cos, sin, w_out, gain_m, grad_out, own, nz
        )
        grad_tokens, grad_first, gains, grad_wout, grads, tiles = second_half(
            lengths, da, w_out, q, k, v, o, st, nmat, cos, sin, w_query, w_key, w_value, gain_a, dgain_m, tokens, dh1,
            mine, got, far, b1,
        )
        gain_grads = gains[0], gains[1]
        grad_wout = grad_wout[0].astype(F32)
        grad_q, grad_k, grad_v = (grads[j].astype(F32) for j in range(3))
        tiles = tiles.transpose(1, 0, 2, 3).reshape(tile.shape).astype(F32)
    else:
        w = lax.all_gather(lax.all_gather(tile, "ma", axis=0), "ha", axis=0)[:, None]
        zs = jnp.arange(nz, dtype=jnp.int32)
        q, k, v, o, st, nma, h1, nmm = attention_forward(
            lengths, tokens, gain_a, w_query, w_key, w_value, first_values, cos, sin, w_out, gain_m
        )
        nmat, ot, nmmt, dyt = prepare(nma, o, nmm, grad_out)
        done = [mlp_block(zs, [[w[i, 0, j] for j in range(nz)]], nmmt, dyt, nmm, grad_out) for i in range(w.shape[0])]
        hs, dgs, dus, mine = (jnp.stack([d[j] for d in done]) for j in range(4))
        mixed, dh1, da, dgain_m = mlp_out(zs, w, hs, dgs, dus, h1, gain_m, grad_out)
        dq, dk, dv, grad_first, grads = attention_backward(
            0, H // GROUP, lengths, da, w_out, q, k, v, o, st, nmat, cos, sin
        )
        grad_tokens, dgain_a = tokens_grad([dq], [dk], [dv], w_query, w_key, w_value, tokens, gain_a, dh1)
        part = lax.psum_scatter(lax.psum_scatter(mine, "ha", scatter_dimension=0), "ma", scatter_dimension=0)
        tiles = lax.psum(part, "rows").astype(F32)
        grad_wout, grads, *gains = lax.psum((wout_grad(ot, da), grads, dgain_a, dgain_m), ("rows", "ha", "ma"))
        grad_wout = grad_wout.astype(F32)
        grad_q, grad_k, grad_v = (grads[j].astype(F32) for j in range(3))
        gain_grads = [v[0] for v in gains]
    return (
        mixed, grad_tokens, 0.5 * grad_first, grad_q, grad_k, grad_v, grad_wout, gain_grads[0], gain_grads[1],
        tiles[0].T, tiles[1].T, tiles[2],
    )


def solution(mesh):
    tok = P(("rows", "ha", "ma"), None)
    gate, down = P("ma", "ha"), P("ha", "ma")
    return jax.shard_map(
        functools.partial(body, mesh.shape["rows"] == 2),
        mesh=mesh,
        in_specs=(tok, tok, P(("rows", "ha", "ma")), P(), P(), P(), P(), P(), P(), gate, gate, down, tok),
        out_specs=(tok, tok, tok, P(), P(), P(), P(), P(), P(), gate, gate, down),
        check_vma=False,
    )
```
